32 devices in a mesh: seq: 8 (over z, x), grp: 4 (over y, core).
Axes of the slice: x: 2, y: 2, z: 4, core: 2. Of those that a mesh axis runs over, the one named last changes fastest.
Arguments:
- tokens: bfloat16 [4, 1024, 768], P('grp', 'seq'), may hold values from -20 to 20
- out_grad: bfloat16 [4, 1024, 768], P('grp', 'seq'), may hold values from -6 to 6
- norm_gain: float32 [2, 768], replicated, may hold values from 0.25 to 1.75
- norm_bias: float32 [2, 768], replicated, may hold values from -3 to 3
- in_weight: bfloat16 [768, 2304], replicated, may hold values from -0.21875 to 0.21875
- in_bias: float32 [2304], replicated, may hold values from -3 to 3
- conv_weight: float32 [3, 2304], replicated, may hold values from -3 to 3
- conv_bias: float32 [2304], replicated, may hold values from -3 to 3
- filt_first: float32 [33, 64], replicated, may hold values from -1 to 1
- filt_hidden: float32 [2, 64, 64], replicated, may hold values from -0.75 to 0.75
- filt_bias: float32 [3, 64], replicated, may hold values from -3 to 3
- filt_freq: float32 [3, 64], replicated, may hold values from 2 to 10
- filt_last: float32 [64, 768], replicated, may hold values from -0.1875 to 0.1875
- decay_rates: float32 [768], replicated, may hold values from 0 to 0.034, as said below
- skip_scale: float32 [768], replicated, may hold values from -4 to 4
- out_weight: bfloat16 [768, 768], replicated, may hold values from -0.21875 to 0.21875
- out_bias: float32 [768], replicated, may hold values from -3 to 3
- up_weight: bfloat16 [768, 3072], replicated, may hold values from -0.21875 to 0.21875
- up_bias: float32 [3072], replicated, may hold values from -3 to 3
- down_weight: bfloat16 [3072, 768], replicated, may hold values from -0.109375 to 0.109375
- down_bias: float32 [768], replicated, may hold values from -3 to 3
Outputs:
- output: float32 [4, 1024, 768], P('grp', 'seq')
- grad_tokens: float32 [4, 1024, 768], P('grp', 'seq')
- grad_norm_gain: float32 [2, 768], replicated
- grad_norm_bias: float32 [2, 768], replicated
- grad_in_weight: float32 [1769472], P(('seq', 'grp'))
- grad_in_bias: float32 [2304], replicated
- grad_conv_weight: float32 [3, 2304], replicated
- grad_conv_bias: float32 [2304], replicated
- grad_filt_first: float32 [33, 64], replicated
- grad_filt_hidden: float32 [2, 64, 64], replicated
- grad_filt_bias: float32 [3, 64], replicated
- grad_filt_freq: float32 [3, 64], replicated
- grad_filt_last: float32 [64, 768], replicated
- grad_decay_rates: float32 [768], replicated
- grad_skip_scale: float32 [768], replicated
- grad_out_weight: float32 [589824], P(('seq', 'grp'))
- grad_out_bias: float32 [768], replicated
- grad_up_weight: float32 [2359296], P(('seq', 'grp'))
- grad_up_bias: float32 [3072], replicated
- grad_down_weight: float32 [2359296], P(('seq', 'grp'))
- grad_down_bias: float32 [768], replicated
The draws below stay inside these ranges and needn't reach their ends.
Inputs may be any that keep to these rules, and one draw needn't show every extreme that they name: `decay_rates`: every rate is positive.
All inputs are finite; a program needn't handle non-finite values.
Results may differ from the reference program's by a relative error of at most 0.0097.
Values may be sent and summed in bfloat16 or wider, within the bound.
A program may use at most 192 MiB of HBM per device.

```python
import math
import jax
import jax.numpy as jnp
from jax import lax

D = 768
FF = 3072
FILT = 64
EMB = 33
LEN = 1024
SEQS = 4


def draw_tokens(key, part):
    key = jax.random.fold_in(key, 11)
    key_base, key_scale = jax.random.split(key, 2)
    base_values = jnp.clip(jax.random.normal(key_base, (SEQS, LEN, D), jnp.float32), -4.0, 4.0)
    scale_low = 0.5
    scale_high = 4.0
    scales = jnp.exp(jax.random.uniform(key_scale, (SEQS, LEN, 1), jnp.float32, math.log(scale_low), math.log(scale_high)))
    return jnp.clip(base_values * scales, -20.0, 20.0).astype(jnp.bfloat16)


def draw_decay_rates(key, part):
    key = jax.random.fold_in(key, 12)
    key_pick, key_slow, key_fast = jax.random.split(key, 3)
    slow_share = 0.5
    slow_pick = jax.random.bernoulli(key_pick, slow_share, (D,))
    slow_rate = jnp.exp(jax.random.uniform(key_slow, (D,), jnp.float32, math.log(0.1 / LEN), math.log(1.0 / LEN)))
    fast_rate = jnp.exp(jax.random.uniform(key_fast, (D,), jnp.float32, math.log(1.0 / LEN), math.log(1.0 / 30.0)))
    return jnp.where(slow_pick, slow_rate, fast_rate).astype(jnp.float32)


def steps_of(key, shape, pieces, smallest, largest):
    def one(axis_at, parts):
        heights = jax.random.uniform(jax.random.fold_in(jax.random.fold_in(key, 6), axis_at), (parts,), jnp.float32, smallest / len(pieces), largest / len(pieces))
        return jnp.repeat(jnp.exp(heights), shape[axis_at] // parts).reshape((-1,) + (1,) * (len(shape) - axis_at - 1))

    level = one(*pieces[0])
    for cut in pieces[1:]:
        level = level * one(*cut)
    return level


def normal_values(own_key, shape, width, limit, cuts=(), held_as=jnp.bfloat16):
    values = jax.random.normal(own_key, shape, jnp.float32) * width
    if len(cuts) > 0:
        values = steps_of(own_key, shape, cuts, -0.22, 0.18) * values
    return jnp.clip(values, min=-limit, max=limit).astype(held_as)


def setup_inputs(seed: int = 0) -> dict:
    key_of = jax.random.split(jax.random.key(seed), 22)
    tokens = draw_tokens(jax.random.fold_in(key_of[21], 71), 0)
    out_grad = normal_values(key_of[1], (SEQS, LEN, D), 1.0, 6.0, ((0, 4), (1, 8)))
    norm_gain = jnp.clip(1.0 + 0.15 * jax.random.normal(key_of[2], (2, D), jnp.float32), 0.25, 1.75)
    norm_bias = normal_values(key_of[3], (2, D), 0.3, 3.0, (), jnp.float32)
    in_weight = normal_values(key_of[4], (D, 3 * D), D ** -0.5, 0.21875)
    in_bias = normal_values(key_of[5], (3 * D,), 0.3, 3.0, (), jnp.float32)
    conv_weight = normal_values(key_of[6], (3, 3 * D), 0.6, 3.0, (), jnp.float32)
    conv_bias = normal_values(key_of[7], (3 * D,), 0.3, 3.0, (), jnp.float32)
    filt_first = normal_values(key_of[8], (EMB, FILT), EMB ** -0.5, 1.0, (), jnp.float32)
    filt_hidden = normal_values(key_of[9], (2, FILT, FILT), FILT ** -0.5, 0.75, (), jnp.float32)
    filt_bias = normal_values(key_of[10], (3, FILT), 0.5, 3.0, (), jnp.float32)
    filt_freq = jnp.clip(jnp.exp(jax.random.uniform(key_of[11], (3, FILT), jnp.float32, math.log(2.0), math.log(10.0))), 2.0, 10.0)
    filt_last = normal_values(key_of[12], (FILT, D), LEN ** -0.5, 0.1875, (), jnp.float32)
    decay_rates = draw_decay_rates(jax.random.fold_in(key_of[21], 71), 0)
    skip_scale = normal_values(key_of[14], (D,), 1.0, 4.0, (), jnp.float32)
    out_weight = normal_values(key_of[15], (D, D), D ** -0.5, 0.21875)
    out_bias = normal_values(key_of[16], (D,), 0.3, 3.0, (), jnp.float32)
    up_weight = normal_values(key_of[17], (D, FF), D ** -0.5, 0.21875)
    up_bias = normal_values(key_of[18], (FF,), 0.3, 3.0, (), jnp.float32)
    down_weight = normal_values(key_of[19], (FF, D), FF ** -0.5, 0.109375)
    down_bias = normal_values(key_of[20], (D,), 0.3, 3.0, (), jnp.float32)
    return dict(tokens=tokens, out_grad=out_grad, norm_gain=norm_gain, norm_bias=norm_bias, in_weight=in_weight, in_bias=in_bias, conv_weight=conv_weight, conv_bias=conv_bias, filt_first=filt_first, filt_hidden=filt_hidden, filt_bias=filt_bias, filt_freq=filt_freq, filt_last=filt_last, decay_rates=decay_rates, skip_scale=skip_scale, out_weight=out_weight, out_bias=out_bias, up_weight=up_weight, up_bias=up_bias, down_weight=down_weight, down_bias=down_bias)


@jax.custom_vjp
def low(v):
    return lax.optimization_barrier(v.astype(jnp.bfloat16)).astype(jnp.float32)

@jax.custom_vjp
def low_back(v):
    return v

def low_keep(v):
    return (low(v), None)

def low_pass(kept, grad):
    return (grad,)

def back_keep(v):
    return (v, None)

def back_low(kept, grad):
    return (low(grad),)
low.defvjp(low_keep, low_pass)
low_back.defvjp(back_keep, back_low)
epsilon = 1e-05

def highest(left_mat, right_mat):
    return jnp.dot(left_mat, right_mat, precision=lax.Precision.HIGHEST, preferred_element_type=jnp.float32)

def layer_norm(values, gain_row, shift_row):
    row_mean = lax.optimization_barrier(jnp.mean(values, axis=-1, keepdims=True))
    centred = values - row_mean
    inv_std = lax.rsqrt(lax.optimization_barrier(jnp.mean(centred * centred, axis=-1, keepdims=True)) + epsilon)
    return centred * inv_std * gain_row + shift_row

def smooth(values):
    return jax.nn.gelu(values, approximate=False)

def filter_rows(filt_first, filt_hidden, filt_bias, filt_freq, filt_last, decay_rates, positions, length):
    place = positions.astype(jnp.float32)
    bands = (filt_first.shape[0] - 1) // 2
    band = 0.0001 + jnp.arange(bands, dtype=jnp.float32) * ((bands - 1 - 0.0001) / (bands - 1))
    omega = place[:, None] * (2.0 * math.pi / length)
    phase = omega * band[None, :]
    feats = jnp.concatenate([place[:, None] / (length - 1), jnp.cos(phase), -jnp.sin(phase)], axis=1)
    act_one = jnp.sin(filt_freq[0] * (highest(feats, filt_first) + filt_bias[0]))
    act_two = jnp.sin(filt_freq[1] * (highest(act_one, filt_hidden[0]) + filt_bias[1]))
    act_three = jnp.sin(filt_freq[2] * (highest(act_two, filt_hidden[1]) + filt_bias[2]))
    window = jnp.exp(-decay_rates[None, :] * jnp.maximum(place, 0.0)[:, None])
    return highest(act_three, filt_last) * window

def one_sequence(inputs, norm_gain, norm_bias, in_weight, in_bias, conv_weight, conv_bias, filt_first, filt_hidden, filt_bias, filt_freq, filt_last, decay_rates, skip_scale, out_weight, out_bias, up_weight, up_bias, down_weight, down_bias):
    length = inputs.shape[0]
    model_width = inputs.shape[1]
    normed1 = low(layer_norm(inputs, norm_gain[0], norm_bias[0]))
    projected = low_back(low(highest(normed1, in_weight) + in_bias))
    padded = jnp.concatenate([jnp.zeros((2, projected.shape[1]), jnp.float32), projected], axis=0)
    mixed_conv = conv_weight[0] * padded[:length] + conv_weight[1] * padded[1:length + 1] + conv_weight[2] * padded[2:] + conv_bias
    outer_part = mixed_conv[:, :model_width]
    inner_part = mixed_conv[:, model_width:2 * model_width]
    value_part = mixed_conv[:, 2 * model_width:]
    gated = low(inner_part * value_part)
    filter_taps = filter_rows(filt_first, filt_hidden, filt_bias, filt_freq, filt_last, decay_rates, jnp.arange(length, dtype=jnp.int32), length)
    fft_size = 2 * length
    spectrum = jnp.fft.rfft(gated, n=fft_size, axis=0) * jnp.fft.rfft(filter_taps, n=fft_size, axis=0)
    conv_out = low_back(jnp.fft.irfft(spectrum, n=fft_size, axis=0)[:length])
    summed = conv_out + skip_scale * gated
    mixed_out = low(outer_part * summed)
    residual = inputs + low_back(highest(mixed_out, out_weight) + out_bias)
    normed2 = low(layer_norm(residual, norm_gain[1], norm_bias[1]))
    pre_act = low_back(highest(normed2, up_weight) + up_bias)
    act_val = low(smooth(pre_act))
    return residual + low_back(highest(act_val, down_weight) + down_bias)

def whole_batch(inputs, *weights):
    axes_in = (0,) + (None,) * len(weights)
    return jax.vmap(one_sequence, in_axes=axes_in)(inputs, *weights)

def reference(tokens, out_grad, norm_gain, norm_bias, in_weight, in_bias, conv_weight, conv_bias, filt_first, filt_hidden, filt_bias, filt_freq, filt_last, decay_rates, skip_scale, out_weight, out_bias, up_weight, up_bias, down_weight, down_bias):
    weights = [norm_gain, norm_bias, in_weight, in_bias, conv_weight, conv_bias, filt_first, filt_hidden, filt_bias, filt_freq, filt_last, decay_rates, skip_scale, out_weight, out_bias, up_weight, up_bias, down_weight, down_bias]
    weights = [item.astype(jnp.float32) for item in weights]
    result, pull_back = jax.vjp(whole_batch, tokens.astype(jnp.float32), *weights)
    grads = pull_back(out_grad.astype(jnp.float32))
    return (result, grads[0], grads[1], grads[2], grads[3].reshape(-1), grads[4], grads[5], grads[6], grads[7], grads[8], grads[9], grads[10], grads[11], grads[12], grads[13], grads[14].reshape(-1), grads[15], grads[16].reshape(-1), grads[17], grads[18].reshape(-1), grads[19])
```

```python
import math

import jax
import jax.numpy as jnp
import ml_dtypes
import numpy as np
from jax import lax
from jax.experimental import pallas as pl
from jax.experimental.pallas import tpu as pltpu
from jax.sharding import PartitionSpec as P

epsilon = 1e-05


def shifted(array, axis, by):
    peers = lax.axis_size(axis)
    pairs = [(i, i + by) for i in range(peers) if 0 <= i + by < peers]
    return lax.ppermute(array, axis, pairs)


def highest(left_mat, right_mat):
    return jnp.dot(
        left_mat, right_mat, precision=lax.Precision.HIGHEST, preferred_element_type=jnp.float32
    )


def highest_t(left_mat, right_mat):
    return lax.dot_general(
        left_mat,
        right_mat,
        (((0,), (0,)), ((), ())),
        precision=lax.Precision.HIGHEST,
        preferred_element_type=jnp.float32,
    )


def rows_t(left_mat, right_mat):
    return lax.dot_general(
        left_mat, right_mat, (((0,), (0,)), ((), ())), preferred_element_type=jnp.float32
    )


def back_mul(grad_in, weight_mat):
    return lax.dot_general(
        grad_in, weight_mat, (((1,), (1,)), ((), ())), preferred_element_type=jnp.float32
    )


def layer_norm(values, gain_row, shift_row):
    row_mean = jnp.mean(values, axis=-1, keepdims=True)
    centred = values - row_mean
    inv_std = lax.rsqrt(jnp.mean(centred * centred, axis=-1, keepdims=True) + epsilon)
    normed = centred * inv_std
    return (normed * gain_row + shift_row, normed, inv_std)


def norm_back(grad_in, normed, inv_std, gain_row):
    scaled = grad_in * gain_row
    centred_grad = (
        scaled
        - jnp.mean(scaled, axis=-1, keepdims=True)
        - normed * jnp.mean(scaled * normed, axis=-1, keepdims=True)
    )
    return (centred_grad * inv_std, jnp.sum(grad_in * normed, axis=0), jnp.sum(grad_in, axis=0))


def smooth(values):
    return jax.nn.gelu(values, approximate=False)


def filter_rows(params, positions, length):
    filt_first, filt_hidden, filt_bias, filt_freq, filt_last, decay_rates = params
    place = positions.astype(jnp.float32)
    bands = (filt_first.shape[0] - 1) // 2
    band = 0.0001 + jnp.arange(bands, dtype=jnp.float32) * ((bands - 1 - 0.0001) / (bands - 1))
    omega = place[:, None] * (2.0 * math.pi / length)
    phase = omega * band[None, :]
    feats = jnp.concatenate(
        [place[:, None] / (length - 1), jnp.cos(phase), -jnp.sin(phase)], axis=1
    )
    act_one = jnp.sin(filt_freq[0] * (highest(feats, filt_first) + filt_bias[0]))
    act_two = jnp.sin(filt_freq[1] * (highest(act_one, filt_hidden[0]) + filt_bias[1]))
    act_three = jnp.sin(filt_freq[2] * (highest(act_two, filt_hidden[1]) + filt_bias[2]))
    window = jnp.exp(-decay_rates[None, :] * jnp.maximum(place, 0.0)[:, None])
    return highest(act_three, filt_last) * window


def body(
    tokens,
    out_grad,
    norm_gain,
    norm_bias,
    in_weight,
    in_bias,
    conv_weight,
    conv_bias,
    filt_first,
    filt_hidden,
    filt_bias,
    filt_freq,
    filt_last,
    decay_rates,
    skip_scale,
    out_weight,
    out_bias,
    up_weight,
    up_bias,
    down_weight,
    down_bias,
):
    row_count = tokens.shape[1]
    model_width = tokens.shape[2]
    seq_count = lax.axis_size("seq")
    length = row_count * seq_count
    fft_span = 2 * row_count
    fparams = (filt_first, filt_hidden, filt_bias, filt_freq, filt_last, decay_rates)
    fft_grid = jnp.arange(fft_span, dtype=jnp.int32)
    angles = (fft_grid[:, None] * fft_grid[None, :] % fft_span).astype(jnp.float32) * (
        2.0 * math.pi / fft_span
    )
    cos_full = jnp.cos(angles)
    sin_full = jnp.sin(angles)
    cos_left = cos_full[:, :row_count]
    sin_left = sin_full[:, :row_count]
    cos_low = cos_full[row_count:, :]
    sin_low = sin_full[row_count:, :]

    def segment(params, lag_step):
        positions = (lag_step - 1) * row_count + fft_grid
        keep_mask = (positions >= 0).astype(jnp.float32)
        return filter_rows(params, positions, length) * keep_mask[:, None]

    def forward_add(lag_step, source, totals):
        filter_taps = segment(fparams, lag_step)
        g_re = highest(cos_full, filter_taps)
        g_im = -highest(sin_full, filter_taps)
        source_f = source.astype(jnp.float32)
        s_re = highest(cos_left, source_f)
        s_im = -highest(sin_left, source_f)
        return (totals[0] + g_re * s_re - g_im * s_im, totals[1] + g_re * s_im + g_im * s_re)

    inputs = tokens[0].astype(jnp.float32)
    normed1, hat_one, std_one = layer_norm(inputs, norm_gain[0], norm_bias[0])
    normed1_b = normed1.astype(jnp.bfloat16)
    projected = (
        jnp.dot(normed1_b, in_weight, preferred_element_type=jnp.float32) + in_bias
    ).astype(jnp.bfloat16)
    before = shifted(projected[row_count - 2 :], "seq", 1)
    padded = jnp.concatenate([before, projected], axis=0).astype(jnp.float32)
    mixed_conv = (
        conv_weight[0] * padded[:row_count]
        + conv_weight[1] * padded[1 : row_count + 1]
        + conv_weight[2] * padded[2:]
        + conv_bias
    )
    outer_part = mixed_conv[:, :model_width]
    inner_part = mixed_conv[:, model_width : 2 * model_width]
    value_part = mixed_conv[:, 2 * model_width :]
    gated_b = (inner_part * value_part).astype(jnp.bfloat16)
    gated_f = gated_b.astype(jnp.float32)
    zero_totals = (
        jnp.zeros((fft_span, model_width), jnp.float32),
        jnp.zeros((fft_span, model_width), jnp.float32),
    )
    first_pass = forward_add(0, gated_b, zero_totals)

    def forward_step(lag_step, loop_carry):
        source, tot_re, tot_im = loop_carry
        source = shifted(source, "seq", 1)
        tot_re, tot_im = forward_add(lag_step, source, (tot_re, tot_im))
        return (source, tot_re, tot_im)

    unused_src, tot_re, tot_im = lax.fori_loop(
        1, seq_count, forward_step, (gated_b, first_pass[0], first_pass[1])
    )
    conv_out = (highest(cos_low, tot_re) - highest(sin_low, tot_im)) / fft_span
    summed = conv_out + skip_scale * gated_f
    mixed_out_b = (outer_part * summed).astype(jnp.bfloat16)
    residual = (
        inputs + jnp.dot(mixed_out_b, out_weight, preferred_element_type=jnp.float32) + out_bias
    )
    normed2, hat_two, std_two = layer_norm(residual, norm_gain[1], norm_bias[1])
    normed2_b = normed2.astype(jnp.bfloat16)
    pre_act = jnp.dot(normed2_b, up_weight, preferred_element_type=jnp.float32) + up_bias
    act_val, gelu_back = jax.vjp(smooth, pre_act)
    act_b = act_val.astype(jnp.bfloat16)
    result = residual + jnp.dot(act_b, down_weight, preferred_element_type=jnp.float32) + down_bias
    grad_out_b = out_grad[0]
    grad_out_f = grad_out_b.astype(jnp.float32)
    g_down = rows_t(act_b, grad_out_b)
    g_down_bias = jnp.sum(grad_out_f, axis=0)
    g_act = back_mul(grad_out_b, down_weight)
    g_pre_b = gelu_back(g_act)[0].astype(jnp.bfloat16)
    g_up = rows_t(normed2_b, g_pre_b)
    g_up_bias = jnp.sum(g_pre_b.astype(jnp.float32), axis=0)
    g_norm_two = back_mul(g_pre_b, up_weight)
    g_res_norm, g_gain_two, g_shift_two = norm_back(g_norm_two, hat_two, std_two, norm_gain[1])
    g_resid = grad_out_f + g_res_norm
    g_resid_b = g_resid.astype(jnp.bfloat16)
    g_outw = rows_t(mixed_out_b, g_resid_b)
    g_out_bias = jnp.sum(g_resid_b.astype(jnp.float32), axis=0)
    g_mixed = back_mul(g_resid_b, out_weight)
    g_outer = g_mixed * summed
    g_summed = g_mixed * outer_part
    g_skip = jnp.sum(g_summed * gated_f, axis=0)
    g_conv_b = g_summed.astype(jnp.bfloat16)
    v_re = highest(cos_left, gated_f)
    v_im = -highest(sin_left, gated_f)

    def backward_add(lag_step, source, loop_carry):
        tot_re, tot_im, grad_acc = loop_carry
        source_f = source.astype(jnp.float32)
        d_re = highest_t(cos_low, source_f) / fft_span
        d_im = -highest_t(sin_low, source_f) / fft_span

        def lag_taps(params):
            return segment(params, lag_step)

        filter_taps, taps_pull = jax.vjp(lag_taps, fparams)
        g_re = highest(cos_full, filter_taps)
        g_im = -highest(sin_full, filter_taps)
        tot_re = tot_re + g_re * d_re + g_im * d_im
        tot_im = tot_im - g_im * d_re + g_re * d_im
        s_re = v_re * d_re + v_im * d_im
        s_im = v_re * d_im - v_im * d_re
        d_taps = highest_t(cos_full, s_re) - highest_t(sin_full, s_im)
        more_grads = taps_pull(d_taps)[0]
        grad_acc = jax.tree.map(jnp.add, grad_acc, more_grads)
        return (tot_re, tot_im, grad_acc)

    zero_grads = jax.tree.map(jnp.zeros_like, fparams)
    start_carry = (zero_totals[0], zero_totals[1], zero_grads)
    first_back = backward_add(0, g_conv_b, start_carry)

    def backward_step(lag_step, loop_carry):
        source, tot_re, tot_im, grad_acc = loop_carry
        source = shifted(source, "seq", -1)
        tot_re, tot_im, grad_acc = backward_add(lag_step, source, (tot_re, tot_im, grad_acc))
        return (source, tot_re, tot_im, grad_acc)

    unused_src, back_re, back_im, cycle_grads = lax.fori_loop(
        1, seq_count, backward_step, (g_conv_b,) + first_back
    )
    g_long = highest_t(cos_left, back_re) - highest_t(sin_left, back_im)
    g_gated = g_summed * skip_scale + g_long
    g_mix = jnp.concatenate([g_outer, g_gated * value_part, g_gated * inner_part], axis=1)
    g_conv_bias = jnp.sum(g_mix, axis=0)
    g_conv_w = jnp.stack(
        [
            jnp.sum(g_mix * padded[tap_index : tap_index + row_count], axis=0)
            for tap_index in range(3)
        ]
    )
    g_pad = (
        jnp.pad(conv_weight[0] * g_mix, ((0, 2), (0, 0)))
        + jnp.pad(conv_weight[1] * g_mix, ((1, 1), (0, 0)))
        + jnp.pad(conv_weight[2] * g_mix, ((2, 0), (0, 0)))
    )
    after_rows = shifted(g_pad[:2], "seq", -1)
    g_proj_b = (g_pad[2:] + jnp.pad(after_rows, ((row_count - 2, 0), (0, 0)))).astype(jnp.bfloat16)
    g_inw = rows_t(normed1_b, g_proj_b)
    g_in_bias = jnp.sum(g_proj_b.astype(jnp.float32), axis=0)
    g_norm_one = back_mul(g_proj_b, in_weight)
    g_in_norm, g_gain_one, g_shift_one = norm_back(g_norm_one, hat_one, std_one, norm_gain[0])
    g_tokens = g_resid + g_in_norm
    small_grads = lax.psum(
        (
            jnp.stack([g_gain_one, g_gain_two]),
            jnp.stack([g_shift_one, g_shift_two]),
            g_in_bias,
            g_conv_w,
            g_conv_bias,
            cycle_grads[0],
            cycle_grads[1],
            cycle_grads[2],
            cycle_grads[3],
            cycle_grads[4],
            cycle_grads[5],
            g_skip,
            g_out_bias,
            g_up_bias,
            g_down_bias,
        ),
        ("seq", "grp"),
    )
    large_grads = (
        lax.psum_scatter(g_inw.reshape(-1), ("seq", "grp"), scatter_dimension=0, tiled=True),
        lax.psum_scatter(g_outw.reshape(-1), ("seq", "grp"), scatter_dimension=0, tiled=True),
        lax.psum_scatter(g_up.reshape(-1), ("seq", "grp"), scatter_dimension=0, tiled=True),
        lax.psum_scatter(g_down.reshape(-1), ("seq", "grp"), scatter_dimension=0, tiled=True),
    )
    return (
        result[None],
        g_tokens[None],
        small_grads[0],
        small_grads[1],
        large_grads[0],
        small_grads[2],
        small_grads[3],
        small_grads[4],
        small_grads[5],
        small_grads[6],
        small_grads[7],
        small_grads[8],
        small_grads[9],
        small_grads[10],
        small_grads[11],
        large_grads[1],
        small_grads[12],
        large_grads[2],
        small_grads[13],
        large_grads[3],
        small_grads[14],
    )


f32 = jnp.float32
bf16 = jnp.bfloat16
MESH_ID = pl.DeviceIdType.MESH
HIGH = lax.Precision.HIGHEST
ROWS = 128
HALO = 16


def nn(a, b):
    return jnp.dot(a, b, preferred_element_type=f32)


def nt(a, b):
    return lax.dot_general(a, b, (((1,), (1,)), ((), ())), preferred_element_type=f32)


def nn_high(a, b):
    return jnp.dot(a, b, precision=HIGH, preferred_element_type=f32)


def nt_high(a, b):
    return lax.dot_general(
        a, b, (((1,), (1,)), ((), ())), precision=HIGH, preferred_element_type=f32
    )


def tn_high(a, b):
    return lax.dot_general(
        a, b, (((0,), (0,)), ((), ())), precision=HIGH, preferred_element_type=f32
    )


def two(v):
    high = v.astype(bf16)
    return high, (v - high.astype(f32)).astype(bf16)


def sin_cos(v):
    k = jnp.floor(v * (1.0 / math.pi) + 0.5)
    r = ((v - k * 3.140625) - k * 0.0009670257568359375) - k * 6.2771141529083252e-07
    sign = 1.0 - 2.0 * (k - 2.0 * jnp.floor(k * 0.5))
    q = r * r
    s = 1.0 / math.factorial(13)
    for order in (11, 9, 7, 5, 3):
        s = 1.0 / math.factorial(order) - s * q
    s = r - r * q * s
    c = 1.0 / math.factorial(12)
    for order in (10, 8, 6, 4, 2):
        c = 1.0 / math.factorial(order) - c * q
    c = 1.0 - q * c
    return s * sign, c * sign


def gelu_both(v):
    a = jnp.abs(v)
    t = 1.0 / (1.0 + (0.3275911 / math.sqrt(2.0)) * a)
    poly = t * (
        0.254829592
        + t * (-0.284496736 + t * (1.421413741 + t * (-1.453152027 + t * 1.061405429)))
    )
    bell = jnp.exp(-0.5 * v * v)
    tail = 0.5 * poly * bell
    phi = jnp.where(v >= 0, 1.0 - tail, tail)
    return v * phi, phi + v * bell * (1.0 / math.sqrt(2.0 * math.pi))


def col_sum(v):
    return jnp.sum(v, axis=0, keepdims=True)


def row_mean(v):
    return jnp.mean(v, axis=1, keepdims=True)


def norm_rows(v):
    centred = v - row_mean(v)
    inv = lax.rsqrt(row_mean(centred * centred) + epsilon)
    return centred * inv, inv


def norm_rows_back(e, hat, inv, gain):
    k = e * gain
    return (k - row_mean(k) - hat * row_mean(k * hat)) * inv


def fourier_tables():
    bins = np.arange(128) + 0.5
    angle = 2.0 * np.pi * bins[:, None] * np.arange(256)[None, :] / 256
    full = np.concatenate([np.cos(angle), -np.sin(angle)], axis=0).astype(np.float32)
    out = []
    for mat in (full, full.T):
        high = mat.astype(ml_dtypes.bfloat16)
        out += [high, (mat - high.astype(np.float32)).astype(ml_dtypes.bfloat16)]
    return np.stack(out)


def feature_table(length, bands):
    place = np.arange(length)
    band = 1e-4 + np.arange(bands) * ((bands - 1 - 1e-4) / (bands - 1))
    phase = band[:, None] * (2.0 * np.pi * place / length)[None, :]
    return np.concatenate(
        [(place / (length - 1))[None], np.cos(phase), -np.sin(phase)], axis=0
    ).astype(np.float32)


AT_GAIN, AT_SHIFT, AT_IN, AT_CONVW, AT_CONVB = 0, 12, 24, 42, 96
AT_SKIP, AT_OUTB, AT_UPB, AT_DOWNB, AT_HID, AT_FIRST = 114, 120, 126, 150, 156, 220


def step_kernel(
    tokens, out_grad, in_w_h, out_w_h, up_w_h, down_w_h, tables_h, feats,
    norm_gain, norm_bias, in_b, conv_w, conv_b, filt_first, filt_hidden, filt_bias,
    filt_freq, filt_last, decay, skip, out_b, up_b, down_b,
    o_out, o_gtok, o_gin, o_gout, o_gup, o_gdown, o_small,
    in_w, out_w, up_w, down_w, tables,
    tok, n1, hat1, std1, pp, outer, inner, value, gf,
    stage, gat, xs, es, ys, co_in, taps, wind, hwin,
    a1, a2, a3, c1, c2, c3, u1, u2, u3,
    g_act, act, summed, hat2, std2, resid, g_resid, g_sum, g_outer,
    at_down, at_up, at_in, at_out, lh_down, lh_up, lh_in, lh_out,
    rh_down, rh_up, rh_in, rh_out,
    s1a, k1a, r1a, s2a, r2a, zsa, zra, s1b, k1b, r1b, s2b, r2b, zsb, zrb,
    gc_in, gl_in, gm, gtap, dpre,
    sm, smr, fl, flr, ag,
    f_gin, f_gout, f_gup, f_gdown, f_out, f_gtok,
    ld, a2a_s, a2a_r, halo_s, halo_r, pair_s, pair_r,
    p1_s, p1_r, p2_s, p2_r, z_s, z_r, sm_s, sm_r, fl_s, fl_r, ag_s, ag_r, st,
):
    s = lax.axis_index("seq")
    g = lax.axis_index("grp")
    me = s * 4 + g
    z, x = lax.div(s, 2), lax.rem(s, 2)
    y, c = lax.div(g, 2), lax.rem(g, 2)
    other = g + 1 - 2 * c
    x_step, y_step = 1 - 2 * x, 2 * (1 - 2 * y)
    first = (s + (1 - c) * x_step, g + c * y_step)
    second = (s + c * x_step, g + (1 - c) * y_step)
    b1 = (1 - c) * x + c * y
    b2 = (1 - c) * y + c * x

    def at(index, size):
        return pl.ds(pl.multiple_of(index * size, size), size)

    def remote(src, dst, ss, rs, where):
        return pltpu.make_async_remote_copy(
            src_ref=src,
            dst_ref=dst,
            send_sem=ss,
            recv_sem=rs,
            device_id=where,
            device_id_type=MESH_ID,
        )

    bar = pltpu.get_barrier_semaphore()

    @pl.loop(1, 32)
    def _(k):
        t = lax.rem(me + k, 32)
        pl.semaphore_signal(
            bar, inc=1, device_id=(lax.div(t, 4), lax.rem(t, 4)), device_id_type=MESH_ID
        )

    loads = [
        pltpu.make_async_copy(tokens.at[0], tok.at[pl.ds(HALO, ROWS)], ld.at[0]),
        pltpu.make_async_copy(in_w_h, in_w, ld.at[1]),
        pltpu.make_async_copy(tables_h, tables, ld.at[2]),
        pltpu.make_async_copy(out_grad.at[0], rh_down.at[pl.ds(0, ROWS)], ld.at[3]),
        pltpu.make_async_copy(down_w_h, down_w, ld.at[4]),
        pltpu.make_async_copy(out_w_h, out_w, ld.at[5]),
        pltpu.make_async_copy(up_w_h, up_w, ld.at[6]),
    ]
    for copy in loads:
        copy.start()

    def pair(index, src, dst):
        return remote(src, dst, pair_s.at[index], pair_r.at[index], (s, other))

    half = pl.ds(ROWS, ROWS)
    pairs = [
        pair(0, rh_down.at[pl.ds(0, ROWS)], rh_down.at[half]),
        pair(1, at_in.at[1 - c], lh_in.at[:, half]),
        pair(2, at_down.at[1 - c], lh_down.at[:, half]),
        pair(3, at_out.at[1 - c], lh_out.at[:, half]),
        pair(4, at_up.at[1 - c], lh_up.at[:, half]),
        pair(5, rh_up.at[pl.ds(0, ROWS)], rh_up.at[half]),
        pair(6, rh_out.at[pl.ds(0, ROWS)], rh_out.at[half]),
        pair(7, rh_in.at[pl.ds(0, ROWS)], rh_in.at[half]),
    ]

    def order_rows(v, size, halves):
        t = jnp.transpose(v)
        for core in range(2):
            blocks = []
            for i1 in range(2):
                for i2 in range(2):
                    ix, iy = (i1, i2) if core == 0 else (i2, i1)
                    for iz in range(4):
                        at_row = size * (iz * 8 + ix * 4 + iy * 2 + core)
                        blocks.append(t[at_row : at_row + size])
            halves[core] = jnp.concatenate(blocks, axis=0).astype(bf16)

    loads[0].wait()
    hat, inv = norm_rows(tok[pl.ds(HALO, ROWS)].astype(f32))
    hat1[...] = hat
    std1[...] = inv
    own_norm = (hat * norm_gain[0:1] + norm_bias[0:1]).astype(bf16)
    n1[pl.ds(HALO, ROWS)] = own_norm
    loads[3].wait()
    pl.semaphore_wait(bar, 31)

    last_rows = remote(
        tok.at[pl.ds(ROWS, HALO)], tok.at[pl.ds(0, HALO)], halo_s.at[0], halo_r.at[0], (s + 1, g)
    )

    @pl.when(s < 7)
    def _():
        last_rows.start()

    pairs[0].start()
    order_rows(own_norm.astype(f32), 24, at_in)
    lh_in[:, pl.ds(0, ROWS)] = at_in[c]
    pairs[1].start()

    @pl.when(s > 0)
    def _():
        last_rows.wait_recv()

    @pl.when(s == 0)
    def _():
        tok[pl.ds(0, HALO)] = jnp.zeros((HALO, tok.shape[1]), bf16)

    hat, inv = norm_rows(tok[pl.ds(0, HALO)].astype(f32))
    n1[pl.ds(0, HALO)] = (hat * norm_gain[0:1] + norm_bias[0:1]).astype(bf16)
    loads[1].wait()
    inside = jnp.where(s > 0, 1.0, 0.0).astype(f32)
    for part, dest in enumerate((outer, inner, value)):
        cols = pl.ds(768 * part, 768)
        proj = (nn(n1[...], in_w[:, cols]) + in_b[:, cols]).astype(bf16).astype(f32)
        pp[pl.ds(0, HALO), cols] = proj[:HALO] * inside
        pp[pl.ds(HALO, ROWS), cols] = proj[HALO:]
        dest[...] = (
            conv_w[0:1, cols] * pp[pl.ds(HALO - 2, ROWS), cols]
            + conv_w[1:2, cols] * pp[pl.ds(HALO - 1, ROWS), cols]
            + conv_w[2:3, cols] * pp[pl.ds(HALO, ROWS), cols]
            + conv_b[:, cols]
        )
    gated = (inner[...] * value[...]).astype(bf16).astype(f32)
    gf[...] = gated

    def spread(v, which):
        pad = jnp.zeros((ROWS, 32), f32)
        for j in range(8):
            piece = jnp.concatenate([v[:, 96 * j : 96 * j + 96], pad], axis=1)
            stage[which, :, 128 * j : 128 * j + 128] = piece.astype(bf16)

    def trade(which, dst):
        @pl.loop(1, 8)
        def _(k):
            peer = lax.rem(s + k, 8)
            remote(
                stage.at[which, :, at(peer, 128)],
                dst.at[:, at(s, 128)],
                a2a_s.at[which, k - 1],
                a2a_r.at[which, k - 1],
                (peer, g),
            ).start()

        dst[:, at(s, 128)] = stage[which, :, at(s, 128)]

    def arrive(which, dst):
        @pl.loop(1, 8)
        def _(k):
            peer = lax.rem(s + 8 - k, 8)
            remote(
                stage.at[which, :, at(peer, 128)],
                dst.at[:, at(peer, 128)],
                a2a_s.at[which, k - 1],
                a2a_r.at[which, k - 1],
                (peer, g),
            ).wait_recv()

    spread(gated, 0)
    trade(0, gat)

    loads[2].wait()
    bias_cols = jnp.transpose(filt_bias[...])
    freq_cols = jnp.transpose(filt_freq[...])
    below = feats[...]
    for i, (u_ref, a_ref, c_ref) in enumerate(((u1, a1, c1), (u2, a2, c2), (u3, a3, c3))):
        weights = filt_first[...] if i == 0 else filt_hidden[i - 1]
        u = tn_high(weights, below) + bias_cols[:, i : i + 1]
        u_ref[...] = u
        below, cosine = sin_cos(freq_cols[:, i : i + 1] * u)
        a_ref[...] = below
        c_ref[...] = cosine

    back = lax.rem(768 - 96 * s, 768)
    lane = lax.broadcasted_iota(jnp.int32, (1, 128), 1)
    live = lane < 96

    def my_lanes(v):
        return jnp.where(live, pltpu.roll(v, back, axis=1)[:, :128], 0.0)

    last = my_lanes(filt_last[...])
    rate = my_lanes(jnp.broadcast_to(decay[...], (8, 768)))[0:1]
    hwin[:, pl.ds(0, 128)] = jnp.zeros((512, 128), bf16)
    for b in range(8):
        rows = pl.ds(128 * b, 128)
        place = lax.broadcasted_iota(jnp.int32, (128, 128), 0).astype(f32) + 128.0 * b
        window = jnp.exp(-rate * place)
        tap = tn_high(a3[:, rows], last) * window
        wind[rows] = window
        taps[rows] = tap
        high, low = two(tap)
        hwin[pl.ds(128, 128), rows] = high
        hwin[pl.ds(384, 128), rows] = low
        if b < 7:
            after = pl.ds(128 * b + 128, 128)
            hwin[pl.ds(0, 128), after] = high
            hwin[pl.ds(256, 128), after] = low

    def table_mul(which, rows, v):
        high, low = two(v)
        return (
            nn(tables[which, rows], high)
            + nn(tables[which, rows], low)
            + nn(tables[which + 1, rows], high)
        )

    es[...] = (
        nn(tables[0], hwin[pl.ds(0, 256)])
        + nn(tables[0], hwin[pl.ds(256, 256)])
        + nn(tables[1], hwin[pl.ds(0, 256)])
    )

    arrive(0, gat)
    xs[...] = nn(tables[0, :, 0:128], gat[...]) + nn(tables[1, :, 0:128], gat[...])

    def pick(ref, tile, b):
        lanes = pl.ds(128 * b, 128)
        return ref[at(tile, 8), lanes], ref[pl.ds(pl.multiple_of(128 + tile * 8, 8), 8), lanes]

    def keep(ref, tile, b, pair_of):
        lanes = pl.ds(128 * b, 128)
        ref[at(tile, 8), lanes] = pair_of[0]
        ref[pl.ds(pl.multiple_of(128 + tile * 8, 8), 8), lanes] = pair_of[1]

    @pl.loop(0, 16)
    def _(tile):
        e = [pick(es, tile, b) for b in range(8)]
        v = [pick(xs, tile, b) for b in range(8)]
        for b in range(8):
            re, im = 0.0, 0.0
            for lag in range(b + 1):
                er, ei = e[lag]
                vr, vi = v[b - lag]
                re = re + er * vr - ei * vi
                im = im + er * vi + ei * vr
            keep(ys, tile, b, (re, im))

    conv = table_mul(2, pl.ds(128, 128), ys[...]) * (1.0 / 128.0)
    stage[1] = conv.astype(bf16)
    trade(1, co_in)

    loads[4].wait()
    for t in range(4):
        cols = pl.ds(768 * t, 768)
        g_act[:, cols] = nt(rh_down[pl.ds(0, ROWS)], down_w[cols])

    def gathered(ref):
        return jnp.concatenate(
            [ref[:, 128 * j : 128 * j + 96].astype(f32) for j in range(8)], axis=1
        )

    arrive(1, co_in)
    sum_f = gathered(co_in) + skip[...] * gf[...]
    summed[...] = sum_f
    mixed = (outer[...] * sum_f).astype(bf16)
    loads[5].wait()
    res = tok[pl.ds(HALO, ROWS)].astype(f32) + nn(mixed, out_w[...]) + out_b[...]
    resid[...] = res
    hat, inv = norm_rows(res)
    hat2[...] = hat
    std2[...] = inv
    n2 = (hat * norm_gain[1:2] + norm_bias[1:2]).astype(bf16)
    loads[6].wait()
    for t in range(4):
        cols = pl.ds(768 * t, 768)
        act_f, slope = gelu_both(nn(n2, up_w[:, cols]) + up_b[:, cols])
        act_b = act_f.astype(bf16)
        act[:, cols] = act_b
        rh_up[pl.ds(0, ROWS), cols] = (g_act[:, cols] * slope).astype(bf16)
        turned = jnp.transpose(act_b.astype(f32)).astype(bf16)
        for ix in range(2):
            for iy in range(2):
                for core in range(2):
                    i1, i2 = (ix, iy) if core == 0 else (iy, ix)
                    src = 96 * (ix * 4 + iy * 2 + core)
                    at_down[core, pl.ds(i1 * 768 + i2 * 384 + t * 96, 96)] = turned[src : src + 96]
    pairs[2].start()
    lh_down[:, pl.ds(0, ROWS)] = at_down[c]

    def one_a(p):
        return remote(s1a.at[p], r1a.at[p], p1_s.at[p], p1_r.at[p], first)

    def two_a(p):
        return remote(s2a.at[p], r2a.at[p], p2_s.at[p], p2_r.at[p], second)

    def zed_a(p, k):
        to = lax.rem(z + k, 4)
        return remote(
            zsa.at[p, to], zra.at[p, k - 1], z_s.at[p, k - 1], z_r.at[p, k - 1], (to * 2 + x, g)
        )

    def one_b(p):
        return remote(s1b.at[p], r1b.at[p], p1_s.at[8 + p], p1_r.at[8 + p], first)

    def two_b(p):
        return remote(s2b.at[p], r2b.at[p], p2_s.at[8 + p], p2_r.at[8 + p], second)

    def zed_b(p, k):
        to = lax.rem(z + k, 4)
        return remote(
            zsb.at[p, to],
            zrb.at[p, k - 1],
            z_s.at[8 + p, k - 1],
            z_r.at[8 + p, k - 1],
            (to * 2 + x, g),
        )

    def make_a(p0, count, lh, rh):
        @pl.loop(0, count)
        def _(p):
            s1a[p0 + p] = nn(lh[at(1 - b1, 192)], rh[:, at(p, 768)]).astype(bf16)
            one_a(p0 + p).start()

        @pl.loop(0, count)
        def _(p):
            k1a[p0 + p] = nn(lh[at(b1, 192)], rh[:, at(p, 768)]).astype(bf16)

    def ph1_a(p):
        one_a(p).wait_recv()
        rows = at(1 - b2, 96)
        s2a[p] = (k1a[p, rows].astype(f32) + r1a[p, rows].astype(f32)).astype(bf16)
        two_a(p).start()

    def ph2_a(p):
        two_a(p).wait_recv()
        rows = at(b2, 96)
        v = k1a[p, rows].astype(f32) + r1a[p, rows].astype(f32) + r2a[p].astype(f32)
        for iz in range(4):
            block = v[24 * iz : 24 * iz + 24]
            zsa[p, iz] = jnp.concatenate([block[:, :384], block[:, 384:]], axis=0).astype(bf16)
        for k in range(1, 4):
            zed_a(p, k).start()

    def ph3_a(p, dest, base, per_row):
        for k in range(1, 4):
            zed_a(p, k).wait_recv()
        v = zsa[p, z].astype(f32)
        for k in range(3):
            v = v + zra[p, k].astype(f32)
        for h in range(2):
            for j in range(3):
                dest[pl.ds(base + 3 * h + j, 24, stride=per_row)] = v[
                    24 * h : 24 * h + 24, 128 * j : 128 * j + 128
                ]

    def ph1_b(p):
        one_b(p).wait_recv()
        rows = at(1 - b2, 384)
        s2b[p] = (k1b[p, rows].astype(f32) + r1b[p, rows].astype(f32)).astype(bf16)
        two_b(p).start()

    def ph2_b(p):
        two_b(p).wait_recv()
        rows = at(b2, 384)
        v = k1b[p, rows].astype(f32) + r1b[p, rows].astype(f32) + r2b[p].astype(f32)
        for iz in range(4):
            zsb[p, iz] = v[96 * iz : 96 * iz + 96].astype(bf16)
        for k in range(1, 4):
            zed_b(p, k).start()

    def ph3_b(p):
        for k in range(1, 4):
            zed_b(p, k).wait_recv()
        v = zsb[p, z].astype(f32)
        for k in range(3):
            v = v + zrb[p, k].astype(f32)
        for j in range(2):
            f_gdown[pl.ds(2 * p + j, 96, stride=6)] = v[:, 128 * j : 128 * j + 128]

    order_rows(mixed.astype(f32), 24, at_out)
    pairs[3].start()
    lh_out[:, pl.ds(0, ROWS)] = at_out[c]
    order_rows(n2.astype(f32), 24, at_up)
    pairs[4].start()
    lh_up[:, pl.ds(0, ROWS)] = at_up[c]
    pairs[5].start()

    pairs[0].wait_recv()
    pairs[2].wait_recv()

    for p in range(3):
        s1b[p] = nn(lh_down[at(1 - b1, 768)], rh_down[:, 256 * p : 256 * p + 256]).astype(bf16)
        one_b(p).start()

    e = nt(rh_up[pl.ds(0, ROWS)], up_w[...])

    def put(row, v):
        for j in range(v.shape[1] // 128):
            sm[row + j : row + j + 1] = v[:, 128 * j : 128 * j + 128]

    hat = hat2[...]
    put(AT_GAIN + 6, col_sum(e * hat))
    put(AT_SHIFT + 6, col_sum(e))
    grad_f = rh_down[pl.ds(0, ROWS)].astype(f32)
    put(AT_DOWNB, col_sum(grad_f))
    put(AT_UPB, col_sum(rh_up[pl.ds(0, ROWS)].astype(f32)))
    g_res = grad_f + norm_rows_back(e, hat, std2[...], norm_gain[1:2])
    g_resid[...] = g_res
    g_res_b = g_res.astype(bf16)
    rh_out[pl.ds(0, ROWS)] = g_res_b
    pairs[6].start()
    put(AT_OUTB, col_sum(g_res_b.astype(f32)))
    g_mixed = nt(g_res_b, out_w[...])
    g_outer[...] = g_mixed * summed[...]
    g_summed = g_mixed * outer[...]
    g_sum[...] = g_summed
    spread(g_summed, 2)
    trade(2, gc_in)
    put(AT_SKIP, col_sum(g_summed * gf[...]))

    pairs[4].wait_recv()
    pairs[5].wait_recv()
    make_a(0, 4, lh_up, rh_up)
    for p in range(3):
        k1b[p] = nn(lh_down[at(b1, 768)], rh_down[:, 256 * p : 256 * p + 256]).astype(bf16)
    pairs[3].wait_recv()
    pairs[6].wait_recv()
    make_a(4, 1, lh_out, rh_out)
    ph1_b(0)

    arrive(2, gc_in)
    ys[...] = (nn(tables[0, :, 128:256], gc_in[...]) + nn(tables[1, :, 128:256], gc_in[...])) * (
        1.0 / 128.0
    )

    @pl.loop(0, 16)
    def _(tile):
        e = [pick(es, tile, b) for b in range(8)]
        d = [pick(ys, tile, b) for b in range(8)]
        for b in range(8):
            re, im = 0.0, 0.0
            for lag in range(8 - b):
                er, ei = e[lag]
                dr, di = d[b + lag]
                re = re + er * dr + ei * di
                im = im + er * di - ei * dr
            keep(es, tile, b, (re, im))

    g_long = table_mul(2, pl.ds(0, 128), es[...])
    stage[3] = g_long.astype(bf16)
    trade(3, gl_in)

    f_out[...] = resid[...] + nn(act[...], down_w[...]) + down_b[...]
    store_out = pltpu.make_async_copy(f_out, o_out, st.at[0])
    store_out.start()
    ph1_b(1)

    @pl.loop(0, 16)
    def _(tile):
        v = [pick(xs, tile, b) for b in range(8)]
        d = [pick(ys, tile, b) for b in range(8)]
        for lag in range(8):
            re, im = 0.0, 0.0
            for b in range(8 - lag):
                vr, vi = v[b]
                dr, di = d[b + lag]
                re = re + vr * dr + vi * di
                im = im + vr * di - vi * dr
            keep(xs, tile, lag, (re, im))

    gtap[...] = table_mul(2, pl.ds(0, 256), xs[...])
    g_rate = jnp.zeros((1, 128), f32)
    for b in range(8):
        rows = pl.ds(128 * b, 128)
        gt = gtap[pl.ds(128, 128), rows]
        if b < 7:
            gt = gt + gtap[pl.ds(0, 128), pl.ds(128 * b + 128, 128)]
        place = lax.broadcasted_iota(jnp.int32, (128, 128), 0).astype(f32) + 128.0 * b
        g_rate = g_rate - col_sum(place * taps[rows] * gt)
        dpre[rows] = gt * wind[rows]
    g_last = nn_high(a3[...], dpre[...])
    decay_rows = jnp.concatenate(
        [pltpu.roll(jnp.broadcast_to(g_rate, (8, 128)), 96 - 32 * j, axis=1)[0:1] for j in range(3)]
        + [jnp.zeros((61, 128), f32)],
        axis=0,
    )
    g_last = jnp.where(live, g_last, decay_rows)
    for j in range(4):
        fl[j] = g_last[16 * j : 16 * j + 16]
    ones = jnp.ones((8, 1024), f32)
    g_a = nt_high(last, dpre[...])
    for i, (u_ref, c_ref, a_ref) in enumerate(((u3, c3, a2), (u2, c2, a1), (u1, c1, None))):
        layer = 2 - i
        g_arg = g_a * c_ref[...]
        g_freq = nt_high(ones, g_arg * u_ref[...])[0:1]
        g_u = g_arg * freq_cols[:, layer : layer + 1]
        g_bias = nt_high(ones, g_u)[0:1]
        sm[AT_FIRST + layer : AT_FIRST + layer + 1, 64:128] = g_bias
        sm[AT_FIRST + 3 + layer : AT_FIRST + 4 + layer, 64:128] = g_freq
        if layer > 0:
            g_w = nt_high(a_ref[...], g_u)
            sm[pl.ds(AT_HID, 64), 64 * (layer - 1) : 64 * layer] = g_w
            g_a = nn_high(filt_hidden[layer - 1], g_u)
        else:
            sm[pl.ds(AT_FIRST, 33), 0:64] = nt_high(feats[...], g_u)

    ph1_b(2)

    arrive(3, gl_in)
    g_gated = skip[...] * g_sum[...] + gathered(gl_in)
    mixes = (g_outer[...], g_gated * value[...], g_gated * inner[...])
    for part in range(3):
        gm[pl.ds(0, ROWS), 768 * part : 768 * part + 768] = mixes[part]
    first_rows = remote(
        gm.at[pl.ds(0, 8)], gm.at[pl.ds(ROWS, 8)], halo_s.at[1], halo_r.at[1], (s - 1, g)
    )

    @pl.when(s > 0)
    def _():
        first_rows.start()

    for part in range(3):
        cols = pl.ds(768 * part, 768)
        mix = gm[pl.ds(0, ROWS), cols]
        put(AT_CONVB + 6 * part, col_sum(mix))
        for tap in range(3):
            put(
                AT_CONVW + 18 * tap + 6 * part,
                col_sum(mix * pp[pl.ds(HALO - 2 + tap, ROWS), cols]),
            )

    @pl.when(s < 7)
    def _():
        first_rows.wait_recv()

    @pl.when(s == 7)
    def _():
        gm[pl.ds(ROWS, 8)] = jnp.zeros((8, gm.shape[1]), f32)

    for part in range(3):
        cols = pl.ds(768 * part, 768)
        g_proj = (
            conv_w[0:1, cols] * gm[pl.ds(2, ROWS), cols]
            + conv_w[1:2, cols] * gm[pl.ds(1, ROWS), cols]
            + conv_w[2:3, cols] * gm[pl.ds(0, ROWS), cols]
        ).astype(bf16)
        rh_in[pl.ds(0, ROWS), cols] = g_proj
        put(AT_IN + 6 * part, col_sum(g_proj.astype(f32)))
    pairs[7].start()
    e = nt(rh_in[pl.ds(0, ROWS)], in_w[...])
    hat = hat1[...]
    put(AT_GAIN, col_sum(e * hat))
    put(AT_SHIFT, col_sum(e))

    @pl.loop(1, 32)
    def _(k):
        t = lax.rem(me + k, 32)
        remote(
            sm.at[at(t, 8)],
            smr.at[k],
            sm_s.at[k],
            sm_r.at[k],
            (lax.div(t, 4), lax.rem(t, 4)),
        ).start()

    @pl.loop(1, 4)
    def _(k):
        t = lax.rem(g + k, 4)
        remote(fl.at[t], flr.at[k], fl_s.at[k], fl_r.at[k], (s, t)).start()

    pairs[1].wait_recv()
    pairs[7].wait_recv()
    make_a(5, 3, lh_in, rh_in)
    f_gtok[...] = g_resid[...] + norm_rows_back(e, hat, std1[...], norm_gain[0:1])
    store_tok = pltpu.make_async_copy(f_gtok, o_gtok, st.at[1])
    store_tok.start()

    for p in range(3):
        ph2_b(p)

    @pl.loop(0, 5)
    def _(p):
        ph1_a(p)

    @pl.loop(1, 32)
    def _(k):
        remote(sm.at[pl.ds(0, 8)], smr.at[k], sm_s.at[k], sm_r.at[k], (s, other)).wait_recv()

    @pl.loop(1, 4)
    def _(k):
        remote(fl.at[0], flr.at[k], fl_s.at[k], fl_r.at[k], (s, other)).wait_recv()

    smr[0] = sm[at(me, 8)]
    flr[0] = fl[g]
    ag[me, pl.ds(0, 8)] = jnp.sum(smr[...], axis=0)
    ag[me, pl.ds(8, 16)] = jnp.sum(flr[...], axis=0)

    @pl.loop(1, 32)
    def _(k):
        t = lax.rem(me + k, 32)
        remote(
            ag.at[me], ag.at[me], ag_s.at[k], ag_r.at[k], (lax.div(t, 4), lax.rem(t, 4))
        ).start()

    for p in range(3):
        ph3_b(p)

    @pl.loop(0, 5)
    def _(p):
        ph2_a(p)

    @pl.loop(5, 8)
    def _(p):
        ph1_a(p)

    @pl.loop(0, 4)
    def _(p):
        ph3_a(p, f_gup, 6 * p, 24)

    ph3_a(4, f_gout, 0, 6)

    stores = [
        store_out,
        store_tok,
        pltpu.make_async_copy(f_gdown, o_gdown, st.at[2]),
        pltpu.make_async_copy(f_gup, o_gup, st.at[3]),
        pltpu.make_async_copy(f_gout, o_gout, st.at[4]),
        pltpu.make_async_copy(f_gin, o_gin, st.at[5]),
        pltpu.make_async_copy(ag, o_small, st.at[6]),
    ]
    for copy in stores[2:5]:
        copy.start()

    @pl.loop(5, 8)
    def _(p):
        ph2_a(p)

    @pl.loop(1, 32)
    def _(k):
        t = lax.rem(me + 32 - k, 32)
        remote(ag.at[t], ag.at[t], ag_s.at[k], ag_r.at[k], (s, other)).wait_recv()

    stores[6].start()

    @pl.loop(0, 3)
    def _(p):
        ph3_a(5 + p, f_gin, 6 * p, 18)

    stores[5].start()

    @pl.when(s < 7)
    def _():
        last_rows.wait_send()

    @pl.when(s > 0)
    def _():
        first_rows.wait_send()

    for copy in pairs:
        copy.wait_send()

    @pl.loop(0, 4)
    def _(which):
        @pl.loop(1, 8)
        def _(k):
            remote(
                stage.at[which, :, pl.ds(0, 128)],
                gat.at[:, pl.ds(0, 128)],
                a2a_s.at[which, k - 1],
                a2a_r.at[which, k - 1],
                (s, other),
            ).wait_send()

    @pl.loop(0, 8)
    def _(p):
        one_a(p).wait_send()
        two_a(p).wait_send()
        for k in range(1, 4):
            zed_a(p, k).wait_send()

    @pl.loop(0, 3)
    def _(p):
        one_b(p).wait_send()
        two_b(p).wait_send()
        for k in range(1, 4):
            zed_b(p, k).wait_send()

    @pl.loop(1, 32)
    def _(k):
        remote(sm.at[pl.ds(0, 8)], smr.at[k], sm_s.at[k], sm_r.at[k], (s, other)).wait_send()
        remote(ag.at[me], ag.at[me], ag_s.at[k], ag_r.at[k], (s, other)).wait_send()

    @pl.loop(1, 4)
    def _(k):
        remote(fl.at[0], flr.at[k], fl_s.at[k], fl_r.at[k], (s, other)).wait_send()

    for copy in stores:
        copy.wait()


def finish_kernel(
    i_out, i_gtok, i_gin, i_gout, i_gup, i_gdown, small,
    out, gtok, gain, shift, gin, in_b, conv_w, conv_b, first, hidden, bias, freq,
    last, decay, skip, gout, out_b, gup, up_b, gdown, down_b, sem,
):
    copies = [
        pltpu.make_async_copy(a, b, sem.at[i])
        for i, (a, b) in enumerate(
            (
                (i_out, out.at[0]),
                (i_gtok, gtok.at[0]),
                (i_gin, gin),
                (i_gout, gout),
                (i_gup, gup),
                (i_gdown, gdown),
            )
        )
    ]
    for copy in copies:
        copy.start()

    def row(at_row):
        return small[at_row // 8, at_row % 8 : at_row % 8 + 1, :]

    def fetch(at_row, dest, dest_row, wide):
        for j in range(wide):
            dest[dest_row : dest_row + 1, 128 * j : 128 * j + 128] = row(at_row + j)

    for i in range(2):
        fetch(AT_GAIN + 6 * i, gain, i, 6)
        fetch(AT_SHIFT + 6 * i, shift, i, 6)
    for i in range(3):
        fetch(AT_CONVW + 18 * i, conv_w, i, 18)
    fetch(AT_IN, in_b, 0, 18)
    fetch(AT_CONVB, conv_b, 0, 18)
    fetch(AT_SKIP, skip, 0, 6)
    fetch(AT_OUTB, out_b, 0, 6)
    fetch(AT_UPB, up_b, 0, 24)
    fetch(AT_DOWNB, down_b, 0, 6)
    rows = jnp.concatenate([small[i, 0:8, :] for i in range(32)], axis=0)
    for i in range(2):
        hidden[i] = rows[AT_HID : AT_HID + 64, 64 * i : 64 * i + 64]
    first[...] = rows[AT_FIRST : AT_FIRST + 33, 0:64]
    bias[...] = rows[AT_FIRST : AT_FIRST + 3, 64:128]
    freq[...] = rows[AT_FIRST + 3 : AT_FIRST + 6, 64:128]
    lasts, rates = [], []
    for i in range(8):
        mine = jnp.concatenate([small[4 * i + j, 8:24, :] for j in range(4)], axis=0)
        lasts.append(mine[:, :96])
        rates += [mine[j : j + 1, 96:128] for j in range(3)]
    last[...] = jnp.concatenate(lasts, axis=1)
    decay[...] = jnp.concatenate(rates, axis=1)
    for copy in copies:
        copy.wait()


def one_kernel_body(tokens, out_grad, norm_gain, norm_bias, in_weight, in_bias, conv_weight, conv_bias,
                    filt_first, filt_hidden, filt_bias, filt_freq, filt_last, decay_rates, skip_scale,
                    out_weight, out_bias, up_weight, up_bias, down_weight, down_bias):
    width, hidden = up_weight.shape
    length = tokens.shape[1] * lax.axis_size("seq")
    any_spec = pl.BlockSpec(memory_space=pl.ANY)
    vmem_spec = pl.BlockSpec(memory_space=pltpu.VMEM)

    def row(v):
        return v.reshape(1, -1)

    def vm(*shape, dtype=f32):
        return pltpu.VMEM(shape, dtype)

    def vb(*shape):
        return pltpu.VMEM(shape, bf16)

    def dma(*shape):
        return pltpu.SemaphoreType.DMA(shape)

    def shape(*dims):
        return jax.ShapeDtypeStruct(dims, f32)

    scratch = [
        vb(width, 3 * width), vb(width, width), vb(width, hidden), vb(hidden, width), vb(4, 256, 256),
        vb(144, width), vb(144, width), vm(128, width), vm(128, 1), vm(144, 3 * width),
        vm(128, width), vm(128, width), vm(128, width), vm(128, width),
        vb(4, 128, 1024), vb(128, 1024), vm(256, 1024), vm(256, 1024), vm(256, 1024), vb(128, 1024),
        vm(1024, 128), vm(1024, 128), vb(512, 1024),
        vm(64, 1024), vm(64, 1024), vm(64, 1024), vm(64, 1024), vm(64, 1024), vm(64, 1024),
        vm(64, 1024), vm(64, 1024), vm(64, 1024),
        vm(128, hidden), vb(128, hidden), vm(128, width), vm(128, width), vm(128, 1),
        vm(128, width), vm(128, width), vm(128, width), vm(128, width),
        vb(2, 1536, 128), vb(2, 384, 128), vb(2, 384, 128), vb(2, 384, 128),
        vb(1536, 256), vb(384, 256), vb(384, 256), vb(384, 256),
        vb(256, width), vb(256, hidden), vb(256, 3 * width), vb(256, width),
        vb(8, 192, 768), vb(8, 192, 768), vb(8, 192, 768), vb(8, 96, 768), vb(8, 96, 768),
        vb(8, 4, 48, 384), vb(8, 3, 48, 384),
        vb(3, 768, 256), vb(3, 768, 256), vb(3, 768, 256), vb(3, 384, 256), vb(3, 384, 256),
        vb(3, 4, 96, 256), vb(3, 3, 96, 256),
        vb(128, 1024), vb(128, 1024), vm(136, 3 * width), vm(256, 1024), vm(1024, 128),
        vm(256, 128), vm(32, 8, 128), vm(4, 16, 128), vm(4, 16, 128), vm(32, 24, 128),
        vm(432, 128), vm(144, 128), vm(576, 128), vm(576, 128), vm(128, width), vm(128, width),
        dma(7), dma(4, 7), dma(4, 7), dma(2), dma(2), dma(8), dma(8),
        dma(11), dma(11), dma(11), dma(11), dma(11, 3), dma(11, 3),
        dma(32), dma(32), dma(4), dma(4), dma(32), dma(32), dma(7),
    ]
    outs = pl.pallas_call(
        step_kernel,
        out_shape=[
            shape(128, width), shape(128, width), shape(432, 128), shape(144, 128),
            shape(576, 128), shape(576, 128), shape(32, 24, 128),
        ],
        in_specs=[any_spec] * 7 + [vmem_spec] * 16,
        out_specs=[any_spec] * 7,
        scratch_shapes=scratch,
        compiler_params=pltpu.CompilerParams(
            collective_id=0, has_side_effects=True, vmem_limit_bytes=62 * 1024 * 1024
        ),
        name="hyena_step",
    )(
        tokens, out_grad, in_weight, out_weight, up_weight, down_weight,
        jnp.asarray(fourier_tables()),
        jnp.asarray(feature_table(length, (filt_first.shape[0] - 1) // 2)),
        norm_gain, norm_bias, row(in_bias), conv_weight, row(conv_bias), filt_first, filt_hidden,
        filt_bias, filt_freq, filt_last, row(decay_rates), row(skip_scale), row(out_bias),
        row(up_bias), row(down_bias),
    )
    done = pl.pallas_call(
        finish_kernel,
        out_shape=[
            shape(1, 128, width), shape(1, 128, width), shape(2, width), shape(2, width), shape(432, 128),
            shape(1, 3 * width), shape(3, 3 * width), shape(1, 3 * width), shape(33, 64), shape(2, 64, 64),
            shape(3, 64), shape(3, 64), shape(64, width), shape(1, width), shape(1, width), shape(144, 128),
            shape(1, width), shape(576, 128), shape(1, hidden), shape(576, 128), shape(1, width),
        ],
        in_specs=[any_spec] * 6 + [vmem_spec],
        out_specs=[any_spec, any_spec, vmem_spec, vmem_spec, any_spec]
        + [vmem_spec] * 10
        + [any_spec, vmem_spec, any_spec, vmem_spec, any_spec, vmem_spec],
        scratch_shapes=[dma(6)],
        name="hyena_finish",
    )(*outs)
    flat = (4, 5, 7, 13, 14, 15, 16, 17, 18, 19, 20)
    return tuple(v.reshape(-1) if i in flat else v for i, v in enumerate(done))


def solution(mesh):
    small_mesh = mesh.shape["seq"] == 8 and mesh.shape["grp"] == 4
    return jax.shard_map(
        one_kernel_body if small_mesh else body,
        mesh=mesh,
        in_specs=(P("grp", "seq", None), P("grp", "seq", None)) + (P(),) * 19,
        out_specs=(
            P("grp", "seq", None),
            P("grp", "seq", None),
            P(),
            P(),
            P(("seq", "grp")),
        )
        + (P(),) * 10
        + (P(("seq", "grp")), P(), P(("seq", "grp")), P(), P(("seq", "grp")), P()),
        check_vma=False,
    )
```

```python
import math

import jax
import jax.numpy as jnp
import ml_dtypes
import numpy as np
from jax import lax
from jax.experimental import pallas as pl
from jax.experimental.pallas import tpu as pltpu
from jax.sharding import PartitionSpec as P

epsilon = 1e-05


def shifted(array, axis, by):
    peers = lax.axis_size(axis)
    pairs = [(i, i + by) for i in range(peers) if 0 <= i + by < peers]
    return lax.ppermute(array, axis, pairs)


def highest(left_mat, right_mat):
    return jnp.dot(
        left_mat, right_mat, precision=lax.Precision.HIGHEST, preferred_element_type=jnp.float32
    )


def highest_t(left_mat, right_mat):
    return lax.dot_general(
        left_mat,
        right_mat,
        (((0,), (0,)), ((), ())),
        precision=lax.Precision.HIGHEST,
        preferred_element_type=jnp.float32,
    )


def rows_t(left_mat, right_mat):
    return lax.dot_general(
        left_mat, right_mat, (((0,), (0,)), ((), ())), preferred_element_type=jnp.float32
    )


def back_mul(grad_in, weight_mat):
    return lax.dot_general(
        grad_in, weight_mat, (((1,), (1,)), ((), ())), preferred_element_type=jnp.float32
    )


def layer_norm(values, gain_row, shift_row):
    row_mean = jnp.mean(values, axis=-1, keepdims=True)
    centred = values - row_mean
    inv_std = lax.rsqrt(jnp.mean(centred * centred, axis=-1, keepdims=True) + epsilon)
    normed = centred * inv_std
    return (normed * gain_row + shift_row, normed, inv_std)


def norm_back(grad_in, normed, inv_std, gain_row):
    scaled = grad_in * gain_row
    centred_grad = (
        scaled
        - jnp.mean(scaled, axis=-1, keepdims=True)
        - normed * jnp.mean(scaled * normed, axis=-1, keepdims=True)
    )
    return (centred_grad * inv_std, jnp.sum(grad_in * normed, axis=0), jnp.sum(grad_in, axis=0))


def smooth(values):
    return jax.nn.gelu(values, approximate=False)


def filter_rows(params, positions, length):
    filt_first, filt_hidden, filt_bias, filt_freq, filt_last, decay_rates = params
    place = positions.astype(jnp.float32)
    bands = (filt_first.shape[0] - 1) // 2
    band = 0.0001 + jnp.arange(bands, dtype=jnp.float32) * ((bands - 1 - 0.0001) / (bands - 1))
    omega = place[:, None] * (2.0 * math.pi / length)
    phase = omega * band[None, :]
    feats = jnp.concatenate(
        [place[:, None] / (length - 1), jnp.cos(phase), -jnp.sin(phase)], axis=1
    )
    act_one = jnp.sin(filt_freq[0] * (highest(feats, filt_first) + filt_bias[0]))
    act_two = jnp.sin(filt_freq[1] * (highest(act_one, filt_hidden[0]) + filt_bias[1]))
    act_three = jnp.sin(filt_freq[2] * (highest(act_two, filt_hidden[1]) + filt_bias[2]))
    window = jnp.exp(-decay_rates[None, :] * jnp.maximum(place, 0.0)[:, None])
    return highest(act_three, filt_last) * window


def body(
    tokens,
    out_grad,
    norm_gain,
    norm_bias,
    in_weight,
    in_bias,
    conv_weight,
    conv_bias,
    filt_first,
    filt_hidden,
    filt_bias,
    filt_freq,
    filt_last,
    decay_rates,
    skip_scale,
    out_weight,
    out_bias,
    up_weight,
    up_bias,
    down_weight,
    down_bias,
):
    row_count = tokens.shape[1]
    model_width = tokens.shape[2]
    seq_count = lax.axis_size("seq")
    length = row_count * seq_count
    fft_span = 2 * row_count
    fparams = (filt_first, filt_hidden, filt_bias, filt_freq, filt_last, decay_rates)
    fft_grid = jnp.arange(fft_span, dtype=jnp.int32)
    angles = (fft_grid[:, None] * fft_grid[None, :] % fft_span).astype(jnp.float32) * (
        2.0 * math.pi / fft_span
    )
    cos_full = jnp.cos(angles)
    sin_full = jnp.sin(angles)
    cos_left = cos_full[:, :row_count]
    sin_left = sin_full[:, :row_count]
    cos_low = cos_full[row_count:, :]
    sin_low = sin_full[row_count:, :]

    def segment(params, lag_step):
        positions = (lag_step - 1) * row_count + fft_grid
        keep_mask = (positions >= 0).astype(jnp.float32)
        return filter_rows(params, positions, length) * keep_mask[:, None]

    def forward_add(lag_step, source, totals):
        filter_taps = segment(fparams, lag_step)
        g_re = highest(cos_full, filter_taps)
        g_im = -highest(sin_full, filter_taps)
        source_f = source.astype(jnp.float32)
        s_re = highest(cos_left, source_f)
        s_im = -highest(sin_left, source_f)
        return (totals[0] + g_re * s_re - g_im * s_im, totals[1] + g_re * s_im + g_im * s_re)

    inputs = tokens[0].astype(jnp.float32)
    normed1, hat_one, std_one = layer_norm(inputs, norm_gain[0], norm_bias[0])
    normed1_b = normed1.astype(jnp.bfloat16)
    projected = (
        jnp.dot(normed1_b, in_weight, preferred_element_type=jnp.float32) + in_bias
    ).astype(jnp.bfloat16)
    before = shifted(projected[row_count - 2 :], "seq", 1)
    padded = jnp.concatenate([before, projected], axis=0).astype(jnp.float32)
    mixed_conv = (
        conv_weight[0] * padded[:row_count]
        + conv_weight[1] * padded[1 : row_count + 1]
        + conv_weight[2] * padded[2:]
        + conv_bias
    )
    outer_part = mixed_conv[:, :model_width]
    inner_part = mixed_conv[:, model_width : 2 * model_width]
    value_part = mixed_conv[:, 2 * model_width :]
    gated_b = (inner_part * value_part).astype(jnp.bfloat16)
    gated_f = gated_b.astype(jnp.float32)
    zero_totals = (
        jnp.zeros((fft_span, model_width), jnp.float32),
        jnp.zeros((fft_span, model_width), jnp.float32),
    )
    first_pass = forward_add(0, gated_b, zero_totals)

    def forward_step(lag_step, loop_carry):
        source, tot_re, tot_im = loop_carry
        source = shifted(source, "seq", 1)
        tot_re, tot_im = forward_add(lag_step, source, (tot_re, tot_im))
        return (source, tot_re, tot_im)

    unused_src, tot_re, tot_im = lax.fori_loop(
        1, seq_count, forward_step, (gated_b, first_pass[0], first_pass[1])
    )
    conv_out = (highest(cos_low, tot_re) - highest(sin_low, tot_im)) / fft_span
    summed = conv_out + skip_scale * gated_f
    mixed_out_b = (outer_part * summed).astype(jnp.bfloat16)
    residual = (
        inputs + jnp.dot(mixed_out_b, out_weight, preferred_element_type=jnp.float32) + out_bias
    )
    normed2, hat_two, std_two = layer_norm(residual, norm_gain[1], norm_bias[1])
    normed2_b = normed2.astype(jnp.bfloat16)
    pre_act = jnp.dot(normed2_b, up_weight, preferred_element_type=jnp.float32) + up_bias
    act_val, gelu_back = jax.vjp(smooth, pre_act)
    act_b = act_val.astype(jnp.bfloat16)
    result = residual + jnp.dot(act_b, down_weight, preferred_element_type=jnp.float32) + down_bias
    grad_out_b = out_grad[0]
    grad_out_f = grad_out_b.astype(jnp.float32)
    g_down = rows_t(act_b, grad_out_b)
    g_down_bias = jnp.sum(grad_out_f, axis=0)
    g_act = back_mul(grad_out_b, down_weight)
    g_pre_b = gelu_back(g_act)[0].astype(jnp.bfloat16)
    g_up = rows_t(normed2_b, g_pre_b)
    g_up_bias = jnp.sum(g_pre_b.astype(jnp.float32), axis=0)
    g_norm_two = back_mul(g_pre_b, up_weight)
    g_res_norm, g_gain_two, g_shift_two = norm_back(g_norm_two, hat_two, std_two, norm_gain[1])
    g_resid = grad_out_f + g_res_norm
    g_resid_b = g_resid.astype(jnp.bfloat16)
    g_outw = rows_t(mixed_out_b, g_resid_b)
    g_out_bias = jnp.sum(g_resid_b.astype(jnp.float32), axis=0)
    g_mixed = back_mul(g_resid_b, out_weight)
    g_outer = g_mixed * summed
    g_summed = g_mixed * outer_part
    g_skip = jnp.sum(g_summed * gated_f, axis=0)
    g_conv_b = g_summed.astype(jnp.bfloat16)
    v_re = highest(cos_left, gated_f)
    v_im = -highest(sin_left, gated_f)

    def backward_add(lag_step, source, loop_carry):
        tot_re, tot_im, grad_acc = loop_carry
        source_f = source.astype(jnp.float32)
        d_re = highest_t(cos_low, source_f) / fft_span
        d_im = -highest_t(sin_low, source_f) / fft_span

        def lag_taps(params):
            return segment(params, lag_step)

        filter_taps, taps_pull = jax.vjp(lag_taps, fparams)
        g_re = highest(cos_full, filter_taps)
        g_im = -highest(sin_full, filter_taps)
        tot_re = tot_re + g_re * d_re + g_im * d_im
        tot_im = tot_im - g_im * d_re + g_re * d_im
        s_re = v_re * d_re + v_im * d_im
        s_im = v_re * d_im - v_im * d_re
        d_taps = highest_t(cos_full, s_re) - highest_t(sin_full, s_im)
        more_grads = taps_pull(d_taps)[0]
        grad_acc = jax.tree.map(jnp.add, grad_acc, more_grads)
        return (tot_re, tot_im, grad_acc)

    zero_grads = jax.tree.map(jnp.zeros_like, fparams)
    start_carry = (zero_totals[0], zero_totals[1], zero_grads)
    first_back = backward_add(0, g_conv_b, start_carry)

    def backward_step(lag_step, loop_carry):
        source, tot_re, tot_im, grad_acc = loop_carry
        source = shifted(source, "seq", -1)
        tot_re, tot_im, grad_acc = backward_add(lag_step, source, (tot_re, tot_im, grad_acc))
        return (source, tot_re, tot_im, grad_acc)

    unused_src, back_re, back_im, cycle_grads = lax.fori_loop(
        1, seq_count, backward_step, (g_conv_b,) + first_back
    )
    g_long = highest_t(cos_left, back_re) - highest_t(sin_left, back_im)
    g_gated = g_summed * skip_scale + g_long
    g_mix = jnp.concatenate([g_outer, g_gated * value_part, g_gated * inner_part], axis=1)
    g_conv_bias = jnp.sum(g_mix, axis=0)
    g_conv_w = jnp.stack(
        [
            jnp.sum(g_mix * padded[tap_index : tap_index + row_count], axis=0)
            for tap_index in range(3)
        ]
    )
    g_pad = (
        jnp.pad(conv_weight[0] * g_mix, ((0, 2), (0, 0)))
        + jnp.pad(conv_weight[1] * g_mix, ((1, 1), (0, 0)))
        + jnp.pad(conv_weight[2] * g_mix, ((2, 0), (0, 0)))
    )
    after_rows = shifted(g_pad[:2], "seq", -1)
    g_proj_b = (g_pad[2:] + jnp.pad(after_rows, ((row_count - 2, 0), (0, 0)))).astype(jnp.bfloat16)
    g_inw = rows_t(normed1_b, g_proj_b)
    g_in_bias = jnp.sum(g_proj_b.astype(jnp.float32), axis=0)
    g_norm_one = back_mul(g_proj_b, in_weight)
    g_in_norm, g_gain_one, g_shift_one = norm_back(g_norm_one, hat_one, std_one, norm_gain[0])
    g_tokens = g_resid + g_in_norm
    small_grads = lax.psum(
        (
            jnp.stack([g_gain_one, g_gain_two]),
            jnp.stack([g_shift_one, g_shift_two]),
            g_in_bias,
            g_conv_w,
            g_conv_bias,
            cycle_grads[0],
            cycle_grads[1],
            cycle_grads[2],
            cycle_grads[3],
            cycle_grads[4],
            cycle_grads[5],
            g_skip,
            g_out_bias,
            g_up_bias,
            g_down_bias,
        ),
        ("seq", "grp"),
    )
    large_grads = (
        lax.psum_scatter(g_inw.reshape(-1), ("seq", "grp"), scatter_dimension=0, tiled=True),
        lax.psum_scatter(g_outw.reshape(-1), ("seq", "grp"), scatter_dimension=0, tiled=True),
        lax.psum_scatter(g_up.reshape(-1), ("seq", "grp"), scatter_dimension=0, tiled=True),
        lax.psum_scatter(g_down.reshape(-1), ("seq", "grp"), scatter_dimension=0, tiled=True),
    )
    return (
        result[None],
        g_tokens[None],
        small_grads[0],
        small_grads[1],
        large_grads[0],
        small_grads[2],
        small_grads[3],
        small_grads[4],
        small_grads[5],
        small_grads[6],
        small_grads[7],
        small_grads[8],
        small_grads[9],
        small_grads[10],
        small_grads[11],
        large_grads[1],
        small_grads[12],
        large_grads[2],
        small_grads[13],
        large_grads[3],
        small_grads[14],
    )


f32 = jnp.float32
bf16 = jnp.bfloat16
MESH_ID = pl.DeviceIdType.MESH
HIGH = lax.Precision.HIGHEST
ROWS = 128
HALO = 16


def nn(a, b):
    return jnp.dot(a, b, preferred_element_type=f32)


def nt(a, b):
    return lax.dot_general(a, b, (((1,), (1,)), ((), ())), preferred_element_type=f32)


def nn_high(a, b):
    return jnp.dot(a, b, precision=HIGH, preferred_element_type=f32)


def nt_high(a, b):
    return lax.dot_general(
        a, b, (((1,), (1,)), ((), ())), precision=HIGH, preferred_element_type=f32
    )


def tn_high(a, b):
    return lax.dot_general(
        a, b, (((0,), (0,)), ((), ())), precision=HIGH, preferred_element_type=f32
    )


def two(v):
    high = v.astype(bf16)
    return high, (v - high.astype(f32)).astype(bf16)


def sin_cos(v):
    k = jnp.floor(v * (1.0 / math.pi) + 0.5)
    r = ((v - k * 3.140625) - k * 0.0009670257568359375) - k * 6.2771141529083252e-07
    sign = 1.0 - 2.0 * (k - 2.0 * jnp.floor(k * 0.5))
    q = r * r
    s = 1.0 / math.factorial(13)
    for order in (11, 9, 7, 5, 3):
        s = 1.0 / math.factorial(order) - s * q
    s = r - r * q * s
    c = 1.0 / math.factorial(12)
    for order in (10, 8, 6, 4, 2):
        c = 1.0 / math.factorial(order) - c * q
    c = 1.0 - q * c
    return s * sign, c * sign


def gelu_both(v):
    a = jnp.abs(v)
    t = 1.0 / (1.0 + (0.3275911 / math.sqrt(2.0)) * a)
    poly = t * (
        0.254829592
        + t * (-0.284496736 + t * (1.421413741 + t * (-1.453152027 + t * 1.061405429)))
    )
    bell = jnp.exp(-0.5 * v * v)
    tail = 0.5 * poly * bell
    phi = jnp.where(v >= 0, 1.0 - tail, tail)
    return v * phi, phi + v * bell * (1.0 / math.sqrt(2.0 * math.pi))


def col_sum(v):
    return jnp.sum(v, axis=0, keepdims=True)


def row_mean(v):
    return jnp.mean(v, axis=1, keepdims=True)


def norm_rows(v):
    centred = v - row_mean(v)
    inv = lax.rsqrt(row_mean(centred * centred) + epsilon)
    return centred * inv, inv


def norm_rows_back(e, hat, inv, gain):
    k = e * gain
    return (k - row_mean(k) - hat * row_mean(k * hat)) * inv


def fourier_tables():
    bins = np.arange(128) + 0.5
    angle = 2.0 * np.pi * bins[:, None] * np.arange(256)[None, :] / 256
    full = np.concatenate([np.cos(angle), -np.sin(angle)], axis=0).astype(np.float32)
    out = []
    for mat in (full, full.T):
        high = mat.astype(ml_dtypes.bfloat16)
        out += [high, (mat - high.astype(np.float32)).astype(ml_dtypes.bfloat16)]
    return np.stack(out)


def feature_table(length, bands):
    place = np.arange(length)
    band = 1e-4 + np.arange(bands) * ((bands - 1 - 1e-4) / (bands - 1))
    phase = band[:, None] * (2.0 * np.pi * place / length)[None, :]
    return np.concatenate(
        [(place / (length - 1))[None], np.cos(phase), -np.sin(phase)], axis=0
    ).astype(np.float32)


AT_GAIN, AT_SHIFT, AT_IN, AT_CONVW, AT_CONVB = 0, 12, 24, 42, 96
AT_SKIP, AT_OUTB, AT_UPB, AT_DOWNB, AT_HID, AT_FIRST = 114, 120, 126, 150, 156, 220


def step_kernel(
    tokens, out_grad, in_w_h, out_w_h, up_w_h, down_w_h, tables_h, feats,
    norm_gain, norm_bias, in_b1, conv_w, conv_b1, filt_first, filt_hidden, filt_bias,
    filt_freq, filt_last, decay1, skip1, out_b1, up_b1, down_b1,
    o_out, o_gtok, o_gin, o_gout, o_gup, o_gdown, o_small,
    in_w, out_w, up_w, down_w, tables, in_b, conv_b, decay, skip, out_b, up_b, down_b,
    tok, n1, hat1, std1, pp, outer, inner, value, gf,
    stage, gat, xs, es, ys, co_in, taps, wind, hwin,
    a1, a2, a3, c1, c2, c3, u1, u2, u3,
    g_act, act, summed, hat2, std2, resid, g_resid, g_sum, g_outer,
    at_down, at_up, at_in, at_out, lh_down, lh_up, lh_in, lh_out,
    rh_down, rh_up, rh_in, rh_out,
    s1a, k1a, r1a, s2a, r2a, zsa, zra, s1b, k1b, r1b, s2b, r2b, zsb, zrb,
    gc_in, gl_in, gm, gtap, dpre,
    sm, smr, fl, flr, ag,
    f_gin, f_gout, f_gup, f_gdown, f_out, f_gtok,
    ld, a2a_s, a2a_r, halo_s, halo_r, pair_s, pair_r,
    p1_s, p1_r, p2_s, p2_r, z_s, z_r, sm_s, sm_r, fl_s, fl_r, ag_s, ag_r, st,
):
    s = lax.axis_index("seq")
    g = lax.axis_index("grp")
    me = s * 4 + g
    z, x = lax.div(s, 2), lax.rem(s, 2)
    y, c = lax.div(g, 2), lax.rem(g, 2)
    other = g + 1 - 2 * c
    x_step, y_step = 1 - 2 * x, 2 * (1 - 2 * y)
    first = (s + (1 - c) * x_step, g + c * y_step)
    second = (s + c * x_step, g + (1 - c) * y_step)
    b1 = (1 - c) * x + c * y
    b2 = (1 - c) * y + c * x

    def at(index, size):
        return pl.ds(pl.multiple_of(index * size, size), size)

    def remote(src, dst, ss, rs, where):
        return pltpu.make_async_remote_copy(
            src_ref=src,
            dst_ref=dst,
            send_sem=ss,
            recv_sem=rs,
            device_id=where,
            device_id_type=MESH_ID,
        )

    bar = pltpu.get_barrier_semaphore()

    @pl.loop(1, 32)
    def _(k):
        t = lax.rem(me + k, 32)
        pl.semaphore_signal(
            bar, inc=1, device_id=(lax.div(t, 4), lax.rem(t, 4)), device_id_type=MESH_ID
        )

    loads = [
        pltpu.make_async_copy(tokens.at[0], tok.at[pl.ds(HALO, ROWS)], ld.at[0]),
        pltpu.make_async_copy(in_w_h, in_w, ld.at[1]),
        pltpu.make_async_copy(tables_h, tables, ld.at[2]),
        pltpu.make_async_copy(out_grad.at[0], rh_down.at[pl.ds(0, ROWS)], ld.at[3]),
        pltpu.make_async_copy(down_w_h, down_w, ld.at[4]),
        pltpu.make_async_copy(out_w_h, out_w, ld.at[5]),
        pltpu.make_async_copy(up_w_h, up_w, ld.at[6]),
    ]
    for copy in loads:
        copy.start()

    for line, flat in (
        (in_b, in_b1), (conv_b, conv_b1), (decay, decay1), (skip, skip1),
        (out_b, out_b1), (up_b, up_b1), (down_b, down_b1),
    ):
        line[...] = flat[...].reshape(line.shape)

    def pair(index, src, dst):
        return remote(src, dst, pair_s.at[index], pair_r.at[index], (s, other))

    half = pl.ds(ROWS, ROWS)
    pairs = [
        pair(0, rh_down.at[pl.ds(0, ROWS)], rh_down.at[half]),
        pair(1, at_in.at[1 - c], lh_in.at[:, half]),
        pair(2, at_down.at[1 - c], lh_down.at[:, half]),
        pair(3, at_out.at[1 - c], lh_out.at[:, half]),
        pair(4, at_up.at[1 - c], lh_up.at[:, half]),
        pair(5, rh_up.at[pl.ds(0, ROWS)], rh_up.at[half]),
        pair(6, rh_out.at[pl.ds(0, ROWS)], rh_out.at[half]),
        pair(7, rh_in.at[pl.ds(0, ROWS)], rh_in.at[half]),
    ]

    def order_rows(v, size, halves):
        t = jnp.transpose(v)
        for core in range(2):
            blocks = []
            for i1 in range(2):
                for i2 in range(2):
                    ix, iy = (i1, i2) if core == 0 else (i2, i1)
                    for iz in range(4):
                        at_row = size * (iz * 8 + ix * 4 + iy * 2 + core)
                        blocks.append(t[at_row : at_row + size])
            halves[core] = jnp.concatenate(blocks, axis=0).astype(bf16)

    loads[0].wait()
    hat, inv = norm_rows(tok[pl.ds(HALO, ROWS)].astype(f32))
    hat1[...] = hat
    std1[...] = inv
    own_norm = (hat * norm_gain[0:1] + norm_bias[0:1]).astype(bf16)
    n1[pl.ds(HALO, ROWS)] = own_norm
    loads[3].wait()
    pl.semaphore_wait(bar, 31)

    last_rows = remote(
        tok.at[pl.ds(ROWS, HALO)], tok.at[pl.ds(0, HALO)], halo_s.at[0], halo_r.at[0], (s + 1, g)
    )

    @pl.when(s < 7)
    def _():
        last_rows.start()

    pairs[0].start()
    order_rows(own_norm.astype(f32), 24, at_in)
    lh_in[:, pl.ds(0, ROWS)] = at_in[c]
    pairs[1].start()

    @pl.when(s > 0)
    def _():
        last_rows.wait_recv()

    @pl.when(s == 0)
    def _():
        tok[pl.ds(0, HALO)] = jnp.zeros((HALO, tok.shape[1]), bf16)

    hat, inv = norm_rows(tok[pl.ds(0, HALO)].astype(f32))
    n1[pl.ds(0, HALO)] = (hat * norm_gain[0:1] + norm_bias[0:1]).astype(bf16)
    loads[1].wait()
    inside = jnp.where(s > 0, 1.0, 0.0).astype(f32)
    for part, dest in enumerate((outer, inner, value)):
        cols = pl.ds(768 * part, 768)
        proj = (nn(n1[...], in_w[:, cols]) + in_b[:, cols]).astype(bf16).astype(f32)
        pp[pl.ds(0, HALO), cols] = proj[:HALO] * inside
        pp[pl.ds(HALO, ROWS), cols] = proj[HALO:]
        dest[...] = (
            conv_w[0:1, cols] * pp[pl.ds(HALO - 2, ROWS), cols]
            + conv_w[1:2, cols] * pp[pl.ds(HALO - 1, ROWS), cols]
            + conv_w[2:3, cols] * pp[pl.ds(HALO, ROWS), cols]
            + conv_b[:, cols]
        )
    gated = (inner[...] * value[...]).astype(bf16).astype(f32)
    gf[...] = gated

    def spread(v, which):
        pad = jnp.zeros((ROWS, 32), f32)
        for j in range(8):
            piece = jnp.concatenate([v[:, 96 * j : 96 * j + 96], pad], axis=1)
            stage[which, :, 128 * j : 128 * j + 128] = piece.astype(bf16)

    def trade(which, dst):
        @pl.loop(1, 8)
        def _(k):
            peer = lax.rem(s + k, 8)
            remote(
                stage.at[which, :, at(peer, 128)],
                dst.at[:, at(s, 128)],
                a2a_s.at[which, k - 1],
                a2a_r.at[which, k - 1],
                (peer, g),
            ).start()

        dst[:, at(s, 128)] = stage[which, :, at(s, 128)]

    def arrive(which, dst):
        @pl.loop(1, 8)
        def _(k):
            peer = lax.rem(s + 8 - k, 8)
            remote(
                stage.at[which, :, at(peer, 128)],
                dst.at[:, at(peer, 128)],
                a2a_s.at[which, k - 1],
                a2a_r.at[which, k - 1],
                (peer, g),
            ).wait_recv()

    spread(gated, 0)
    trade(0, gat)

    loads[2].wait()
    bias_cols = jnp.transpose(filt_bias[...])
    freq_cols = jnp.transpose(filt_freq[...])
    below = feats[...]
    for i, (u_ref, a_ref, c_ref) in enumerate(((u1, a1, c1), (u2, a2, c2), (u3, a3, c3))):
        weights = filt_first[...] if i == 0 else filt_hidden[i - 1]
        u = tn_high(weights, below) + bias_cols[:, i : i + 1]
        u_ref[...] = u
        below, cosine = sin_cos(freq_cols[:, i : i + 1] * u)
        a_ref[...] = below
        c_ref[...] = cosine

    back = lax.rem(768 - 96 * s, 768)
    lane = lax.broadcasted_iota(jnp.int32, (1, 128), 1)
    live = lane < 96

    def my_lanes(v):
        return jnp.where(live, pltpu.roll(v, back, axis=1)[:, :128], 0.0)

    last = my_lanes(filt_last[...])
    rate = my_lanes(jnp.broadcast_to(decay[...], (8, 768)))[0:1]
    hwin[:, pl.ds(0, 128)] = jnp.zeros((512, 128), bf16)
    for b in range(8):
        rows = pl.ds(128 * b, 128)
        place = lax.broadcasted_iota(jnp.int32, (128, 128), 0).astype(f32) + 128.0 * b
        window = jnp.exp(-rate * place)
        tap = tn_high(a3[:, rows], last) * window
        wind[rows] = window
        taps[rows] = tap
        high, low = two(tap)
        hwin[pl.ds(128, 128), rows] = high
        hwin[pl.ds(384, 128), rows] = low
        if b < 7:
            after = pl.ds(128 * b + 128, 128)
            hwin[pl.ds(0, 128), after] = high
            hwin[pl.ds(256, 128), after] = low

    def table_mul(which, rows, v):
        high, low = two(v)
        return (
            nn(tables[which, rows], high)
            + nn(tables[which, rows], low)
            + nn(tables[which + 1, rows], high)
        )

    es[...] = (
        nn(tables[0], hwin[pl.ds(0, 256)])
        + nn(tables[0], hwin[pl.ds(256, 256)])
        + nn(tables[1], hwin[pl.ds(0, 256)])
    )

    arrive(0, gat)
    xs[...] = nn(tables[0, :, 0:128], gat[...]) + nn(tables[1, :, 0:128], gat[...])

    def pick(ref, tile, b):
        lanes = pl.ds(128 * b, 128)
        return ref[at(tile, 8), lanes], ref[pl.ds(pl.multiple_of(128 + tile * 8, 8), 8), lanes]

    def keep(ref, tile, b, pair_of):
        lanes = pl.ds(128 * b, 128)
        ref[at(tile, 8), lanes] = pair_of[0]
        ref[pl.ds(pl.multiple_of(128 + tile * 8, 8), 8), lanes] = pair_of[1]

    @pl.loop(0, 16)
    def _(tile):
        e = [pick(es, tile, b) for b in range(8)]
        v = [pick(xs, tile, b) for b in range(8)]
        for b in range(8):
            re, im = 0.0, 0.0
            for lag in range(b + 1):
                er, ei = e[lag]
                vr, vi = v[b - lag]
                re = re + er * vr - ei * vi
                im = im + er * vi + ei * vr
            keep(ys, tile, b, (re, im))

    conv = table_mul(2, pl.ds(128, 128), ys[...]) * (1.0 / 128.0)
    stage[1] = conv.astype(bf16)
    trade(1, co_in)

    loads[4].wait()
    for t in range(4):
        cols = pl.ds(768 * t, 768)
        g_act[:, cols] = nt(rh_down[pl.ds(0, ROWS)], down_w[cols])

    def gathered(ref):
        return jnp.concatenate(
            [ref[:, 128 * j : 128 * j + 96].astype(f32) for j in range(8)], axis=1
        )

    arrive(1, co_in)
    sum_f = gathered(co_in) + skip[...] * gf[...]
    summed[...] = sum_f
    mixed = (outer[...] * sum_f).astype(bf16)
    loads[5].wait()
    res = tok[pl.ds(HALO, ROWS)].astype(f32) + nn(mixed, out_w[...]) + out_b[...]
    resid[...] = res
    hat, inv = norm_rows(res)
    hat2[...] = hat
    std2[...] = inv
    n2 = (hat * norm_gain[1:2] + norm_bias[1:2]).astype(bf16)
    loads[6].wait()
    for t in range(4):
        cols = pl.ds(768 * t, 768)
        act_f, slope = gelu_both(nn(n2, up_w[:, cols]) + up_b[:, cols])
        act_b = act_f.astype(bf16)
        act[:, cols] = act_b
        rh_up[pl.ds(0, ROWS), cols] = (g_act[:, cols] * slope).astype(bf16)
        turned = jnp.transpose(act_b.astype(f32)).astype(bf16)
        for ix in range(2):
            for iy in range(2):
                for core in range(2):
                    i1, i2 = (ix, iy) if core == 0 else (iy, ix)
                    src = 96 * (ix * 4 + iy * 2 + core)
                    at_down[core, pl.ds(i1 * 768 + i2 * 384 + t * 96, 96)] = turned[src : src + 96]
    pairs[2].start()
    lh_down[:, pl.ds(0, ROWS)] = at_down[c]

    def one_a(p):
        return remote(s1a.at[p], r1a.at[p], p1_s.at[p], p1_r.at[p], first)

    def two_a(p):
        return remote(s2a.at[p], r2a.at[p], p2_s.at[p], p2_r.at[p], second)

    def zed_a(p, k):
        to = lax.rem(z + k, 4)
        return remote(
            zsa.at[p, to], zra.at[p, k - 1], z_s.at[p, k - 1], z_r.at[p, k - 1], (to * 2 + x, g)
        )

    def one_b(p):
        return remote(s1b.at[p], r1b.at[p], p1_s.at[8 + p], p1_r.at[8 + p], first)

    def two_b(p):
        return remote(s2b.at[p], r2b.at[p], p2_s.at[8 + p], p2_r.at[8 + p], second)

    def zed_b(p, k):
        to = lax.rem(z + k, 4)
        return remote(
            zsb.at[p, to],
            zrb.at[p, k - 1],
            z_s.at[8 + p, k - 1],
            z_r.at[8 + p, k - 1],
            (to * 2 + x, g),
        )

    def make_a(p0, count, lh, rh):
        @pl.loop(0, count)
        def _(p):
            s1a[p0 + p] = nn(lh[at(1 - b1, 192)], rh[:, at(p, 768)]).astype(bf16)
            one_a(p0 + p).start()

        @pl.loop(0, count)
        def _(p):
            k1a[p0 + p] = nn(lh[at(b1, 192)], rh[:, at(p, 768)]).astype(bf16)

    def ph1_a(p):
        one_a(p).wait_recv()
        rows = at(1 - b2, 96)
        s2a[p] = (k1a[p, rows].astype(f32) + r1a[p, rows].astype(f32)).astype(bf16)
        two_a(p).start()

    def ph2_a(p):
        two_a(p).wait_recv()
        rows = at(b2, 96)
        v = k1a[p, rows].astype(f32) + r1a[p, rows].astype(f32) + r2a[p].astype(f32)
        for iz in range(4):
            block = v[24 * iz : 24 * iz + 24]
            zsa[p, iz] = jnp.concatenate([block[:, :384], block[:, 384:]], axis=0).astype(bf16)
        for k in range(1, 4):
            zed_a(p, k).start()

    def ph3_a(p, dest, base, per_row):
        for k in range(1, 4):
            zed_a(p, k).wait_recv()
        v = zsa[p, z].astype(f32)
        for k in range(3):
            v = v + zra[p, k].astype(f32)
        for h in range(2):
            for j in range(3):
                dest[pl.ds(base + 3 * h + j, 24, stride=per_row)] = v[
                    24 * h : 24 * h + 24, 128 * j : 128 * j + 128
                ]

    def ph1_b(p):
        one_b(p).wait_recv()
        rows = at(1 - b2, 384)
        s2b[p] = (k1b[p, rows].astype(f32) + r1b[p, rows].astype(f32)).astype(bf16)
        two_b(p).start()

    def ph2_b(p):
        two_b(p).wait_recv()
        rows = at(b2, 384)
        v = k1b[p, rows].astype(f32) + r1b[p, rows].astype(f32) + r2b[p].astype(f32)
        for iz in range(4):
            zsb[p, iz] = v[96 * iz : 96 * iz + 96].astype(bf16)
        for k in range(1, 4):
            zed_b(p, k).start()

    def ph3_b(p):
        for k in range(1, 4):
            zed_b(p, k).wait_recv()
        v = zsb[p, z].astype(f32)
        for k in range(3):
            v = v + zrb[p, k].astype(f32)
        for j in range(2):
            f_gdown[pl.ds(2 * p + j, 96, stride=6)] = v[:, 128 * j : 128 * j + 128]

    order_rows(mixed.astype(f32), 24, at_out)
    pairs[3].start()
    lh_out[:, pl.ds(0, ROWS)] = at_out[c]
    order_rows(n2.astype(f32), 24, at_up)
    pairs[4].start()
    lh_up[:, pl.ds(0, ROWS)] = at_up[c]
    pairs[5].start()

    pairs[0].wait_recv()
    pairs[2].wait_recv()

    for p in range(3):
        s1b[p] = nn(lh_down[at(1 - b1, 768)], rh_down[:, 256 * p : 256 * p + 256]).astype(bf16)
        one_b(p).start()

    e = nt(rh_up[pl.ds(0, ROWS)], up_w[...])

    def put(row, v):
        for j in range(v.shape[1] // 128):
            sm[row + j : row + j + 1] = v[:, 128 * j : 128 * j + 128]

    hat = hat2[...]
    put(AT_GAIN + 6, col_sum(e * hat))
    put(AT_SHIFT + 6, col_sum(e))
    grad_f = rh_down[pl.ds(0, ROWS)].astype(f32)
    put(AT_DOWNB, col_sum(grad_f))
    put(AT_UPB, col_sum(rh_up[pl.ds(0, ROWS)].astype(f32)))
    g_res = grad_f + norm_rows_back(e, hat, std2[...], norm_gain[1:2])
    g_resid[...] = g_res
    g_res_b = g_res.astype(bf16)
    rh_out[pl.ds(0, ROWS)] = g_res_b
    pairs[6].start()
    put(AT_OUTB, col_sum(g_res_b.astype(f32)))
    g_mixed = nt(g_res_b, out_w[...])
    g_outer[...] = g_mixed * summed[...]
    g_summed = g_mixed * outer[...]
    g_sum[...] = g_summed
    spread(g_summed, 2)
    trade(2, gc_in)
    put(AT_SKIP, col_sum(g_summed * gf[...]))

    pairs[4].wait_recv()
    pairs[5].wait_recv()
    make_a(0, 4, lh_up, rh_up)
    for p in range(3):
        k1b[p] = nn(lh_down[at(b1, 768)], rh_down[:, 256 * p : 256 * p + 256]).astype(bf16)
    pairs[3].wait_recv()
    pairs[6].wait_recv()
    make_a(4, 1, lh_out, rh_out)
    ph1_b(0)

    arrive(2, gc_in)
    ys[...] = (nn(tables[0, :, 128:256], gc_in[...]) + nn(tables[1, :, 128:256], gc_in[...])) * (
        1.0 / 128.0
    )

    @pl.loop(0, 16)
    def _(tile):
        e = [pick(es, tile, b) for b in range(8)]
        d = [pick(ys, tile, b) for b in range(8)]
        for b in range(8):
            re, im = 0.0, 0.0
            for lag in range(8 - b):
                er, ei = e[lag]
                dr, di = d[b + lag]
                re = re + er * dr + ei * di
                im = im + er * di - ei * dr
            keep(es, tile, b, (re, im))

    g_long = table_mul(2, pl.ds(0, 128), es[...])
    stage[3] = g_long.astype(bf16)
    trade(3, gl_in)

    f_out[...] = resid[...] + nn(act[...], down_w[...]) + down_b[...]
    store_out = pltpu.make_async_copy(f_out, o_out, st.at[0])
    store_out.start()
    ph1_b(1)

    @pl.loop(0, 16)
    def _(tile):
        v = [pick(xs, tile, b) for b in range(8)]
        d = [pick(ys, tile, b) for b in range(8)]
        for lag in range(8):
            re, im = 0.0, 0.0
            for b in range(8 - lag):
                vr, vi = v[b]
                dr, di = d[b + lag]
                re = re + vr * dr + vi * di
                im = im + vr * di - vi * dr
            keep(xs, tile, lag, (re, im))

    gtap[...] = table_mul(2, pl.ds(0, 256), xs[...])
    g_rate = jnp.zeros((1, 128), f32)
    for b in range(8):
        rows = pl.ds(128 * b, 128)
        gt = gtap[pl.ds(128, 128), rows]
        if b < 7:
            gt = gt + gtap[pl.ds(0, 128), pl.ds(128 * b + 128, 128)]
        place = lax.broadcasted_iota(jnp.int32, (128, 128), 0).astype(f32) + 128.0 * b
        g_rate = g_rate - col_sum(place * taps[rows] * gt)
        dpre[rows] = gt * wind[rows]
    g_last = nn_high(a3[...], dpre[...])
    decay_rows = jnp.concatenate(
        [pltpu.roll(jnp.broadcast_to(g_rate, (8, 128)), 96 - 32 * j, axis=1)[0:1] for j in range(3)]
        + [jnp.zeros((61, 128), f32)],
        axis=0,
    )
    g_last = jnp.where(live, g_last, decay_rows)
    for j in range(4):
        fl[j] = g_last[16 * j : 16 * j + 16]
    ones = jnp.ones((8, 1024), f32)
    g_a = nt_high(last, dpre[...])
    for i, (u_ref, c_ref, a_ref) in enumerate(((u3, c3, a2), (u2, c2, a1), (u1, c1, None))):
        layer = 2 - i
        g_arg = g_a * c_ref[...]
        g_freq = nt_high(ones, g_arg * u_ref[...])[0:1]
        g_u = g_arg * freq_cols[:, layer : layer + 1]
        g_bias = nt_high(ones, g_u)[0:1]
        sm[AT_FIRST + layer : AT_FIRST + layer + 1, 64:128] = g_bias
        sm[AT_FIRST + 3 + layer : AT_FIRST + 4 + layer, 64:128] = g_freq
        if layer > 0:
            g_w = nt_high(a_ref[...], g_u)
            sm[pl.ds(AT_HID, 64), 64 * (layer - 1) : 64 * layer] = g_w
            g_a = nn_high(filt_hidden[layer - 1], g_u)
        else:
            sm[pl.ds(AT_FIRST, 33), 0:64] = nt_high(feats[...], g_u)

    ph1_b(2)

    arrive(3, gl_in)
    g_gated = skip[...] * g_sum[...] + gathered(gl_in)
    mixes = (g_outer[...], g_gated * value[...], g_gated * inner[...])
    for part in range(3):
        gm[pl.ds(0, ROWS), 768 * part : 768 * part + 768] = mixes[part]
    first_rows = remote(
        gm.at[pl.ds(0, 8)], gm.at[pl.ds(ROWS, 8)], halo_s.at[1], halo_r.at[1], (s - 1, g)
    )

    @pl.when(s > 0)
    def _():
        first_rows.start()

    for part in range(3):
        cols = pl.ds(768 * part, 768)
        mix = gm[pl.ds(0, ROWS), cols]
        put(AT_CONVB + 6 * part, col_sum(mix))
        for tap in range(3):
            put(
                AT_CONVW + 18 * tap + 6 * part,
                col_sum(mix * pp[pl.ds(HALO - 2 + tap, ROWS), cols]),
            )

    @pl.when(s < 7)
    def _():
        first_rows.wait_recv()

    @pl.when(s == 7)
    def _():
        gm[pl.ds(ROWS, 8)] = jnp.zeros((8, gm.shape[1]), f32)

    for part in range(3):
        cols = pl.ds(768 * part, 768)
        g_proj = (
            conv_w[0:1, cols] * gm[pl.ds(2, ROWS), cols]
            + conv_w[1:2, cols] * gm[pl.ds(1, ROWS), cols]
            + conv_w[2:3, cols] * gm[pl.ds(0, ROWS), cols]
        ).astype(bf16)
        rh_in[pl.ds(0, ROWS), cols] = g_proj
        put(AT_IN + 6 * part, col_sum(g_proj.astype(f32)))
    pairs[7].start()
    e = nt(rh_in[pl.ds(0, ROWS)], in_w[...])
    hat = hat1[...]
    put(AT_GAIN, col_sum(e * hat))
    put(AT_SHIFT, col_sum(e))

    @pl.loop(1, 32)
    def _(k):
        t = lax.rem(me + k, 32)
        remote(
            sm.at[at(t, 8)],
            smr.at[k],
            sm_s.at[k],
            sm_r.at[k],
            (lax.div(t, 4), lax.rem(t, 4)),
        ).start()

    @pl.loop(1, 4)
    def _(k):
        t = lax.rem(g + k, 4)
        remote(fl.at[t], flr.at[k], fl_s.at[k], fl_r.at[k], (s, t)).start()

    pairs[1].wait_recv()
    pairs[7].wait_recv()
    make_a(5, 3, lh_in, rh_in)
    f_gtok[...] = g_resid[...] + norm_rows_back(e, hat, std1[...], norm_gain[0:1])
    store_tok = pltpu.make_async_copy(f_gtok, o_gtok, st.at[1])
    store_tok.start()

    for p in range(3):
        ph2_b(p)

    @pl.loop(0, 5)
    def _(p):
        ph1_a(p)

    @pl.loop(1, 32)
    def _(k):
        remote(sm.at[pl.ds(0, 8)], smr.at[k], sm_s.at[k], sm_r.at[k], (s, other)).wait_recv()

    @pl.loop(1, 4)
    def _(k):
        remote(fl.at[0], flr.at[k], fl_s.at[k], fl_r.at[k], (s, other)).wait_recv()

    smr[0] = sm[at(me, 8)]
    flr[0] = fl[g]
    ag[me, pl.ds(0, 8)] = jnp.sum(smr[...], axis=0)
    ag[me, pl.ds(8, 16)] = jnp.sum(flr[...], axis=0)

    @pl.loop(1, 32)
    def _(k):
        t = lax.rem(me + k, 32)
        remote(
            ag.at[me], ag.at[me], ag_s.at[k], ag_r.at[k], (lax.div(t, 4), lax.rem(t, 4))
        ).start()

    for p in range(3):
        ph3_b(p)

    @pl.loop(0, 5)
    def _(p):
        ph2_a(p)

    @pl.loop(5, 8)
    def _(p):
        ph1_a(p)

    @pl.loop(0, 4)
    def _(p):
        ph3_a(p, f_gup, 6 * p, 24)

    ph3_a(4, f_gout, 0, 6)

    stores = [
        store_out,
        store_tok,
        pltpu.make_async_copy(f_gdown, o_gdown, st.at[2]),
        pltpu.make_async_copy(f_gup, o_gup, st.at[3]),
        pltpu.make_async_copy(f_gout, o_gout, st.at[4]),
        pltpu.make_async_copy(f_gin, o_gin, st.at[5]),
        pltpu.make_async_copy(ag, o_small, st.at[6]),
    ]
    for copy in stores[2:5]:
        copy.start()

    @pl.loop(5, 8)
    def _(p):
        ph2_a(p)

    @pl.loop(1, 32)
    def _(k):
        t = lax.rem(me + 32 - k, 32)
        remote(ag.at[t], ag.at[t], ag_s.at[k], ag_r.at[k], (s, other)).wait_recv()

    stores[6].start()

    @pl.loop(0, 3)
    def _(p):
        ph3_a(5 + p, f_gin, 6 * p, 18)

    stores[5].start()

    @pl.when(s < 7)
    def _():
        last_rows.wait_send()

    @pl.when(s > 0)
    def _():
        first_rows.wait_send()

    for copy in pairs:
        copy.wait_send()

    @pl.loop(0, 4)
    def _(which):
        @pl.loop(1, 8)
        def _(k):
            remote(
                stage.at[which, :, pl.ds(0, 128)],
                gat.at[:, pl.ds(0, 128)],
                a2a_s.at[which, k - 1],
                a2a_r.at[which, k - 1],
                (s, other),
            ).wait_send()

    @pl.loop(0, 8)
    def _(p):
        one_a(p).wait_send()
        two_a(p).wait_send()
        for k in range(1, 4):
            zed_a(p, k).wait_send()

    @pl.loop(0, 3)
    def _(p):
        one_b(p).wait_send()
        two_b(p).wait_send()
        for k in range(1, 4):
            zed_b(p, k).wait_send()

    @pl.loop(1, 32)
    def _(k):
        remote(sm.at[pl.ds(0, 8)], smr.at[k], sm_s.at[k], sm_r.at[k], (s, other)).wait_send()
        remote(ag.at[me], ag.at[me], ag_s.at[k], ag_r.at[k], (s, other)).wait_send()

    @pl.loop(1, 4)
    def _(k):
        remote(fl.at[0], flr.at[k], fl_s.at[k], fl_r.at[k], (s, other)).wait_send()

    for copy in stores:
        copy.wait()


def finish_kernel(
    i_out, i_gtok, i_gin, i_gout, i_gup, i_gdown, i_small,
    out, gtok, gain, shift, gin, in_b, conv_w, conv_b, first, hidden, bias, freq,
    last, decay, skip, gout, out_b, gup, up_b, gdown, down_b,
    h_out, h_gtok, h_gin, h_gout, h_gup, h_gdown, small, sem_in, sem_out,
):
    bulk = (
        (i_small, small, None),
        (i_out, h_out, out.at[0]),
        (i_gtok, h_gtok, gtok.at[0]),
        (i_gin, h_gin, gin),
        (i_gout, h_gout, gout),
        (i_gup, h_gup, gup),
        (i_gdown, h_gdown, gdown),
    )
    enter = [pltpu.make_async_copy(a, b, sem_in.at[i]) for i, (a, b, _) in enumerate(bulk)]
    leave = [
        pltpu.make_async_copy(b, d, sem_out.at[i]) for i, (_, b, d) in enumerate(bulk) if i > 0
    ]
    for copy in enter:
        copy.start()
    for i in range(6):
        enter[i + 1].wait()
        leave[i].start()
    enter[0].wait()
    rows = jnp.concatenate([small[i, 0:8, :] for i in range(32)], axis=0)

    def fetch(at_row, dest, dest_row, wide):
        for j in range(wide):
            dest[dest_row : dest_row + 1, 128 * j : 128 * j + 128] = rows[at_row + j : at_row + j + 1]

    def line(at_row, dest):
        dest[...] = rows[at_row : at_row + dest.shape[0] // 128].reshape(dest.shape[0])

    for i in range(2):
        fetch(AT_GAIN + 6 * i, gain, i, 6)
        fetch(AT_SHIFT + 6 * i, shift, i, 6)
    for i in range(3):
        fetch(AT_CONVW + 18 * i, conv_w, i, 18)
    line(AT_IN, in_b)
    line(AT_CONVB, conv_b)
    line(AT_SKIP, skip)
    line(AT_OUTB, out_b)
    line(AT_UPB, up_b)
    line(AT_DOWNB, down_b)
    for i in range(2):
        hidden[i] = rows[AT_HID : AT_HID + 64, 64 * i : 64 * i + 64]
    first[...] = rows[AT_FIRST : AT_FIRST + 33, 0:64]
    bias[...] = rows[AT_FIRST : AT_FIRST + 3, 64:128]
    freq[...] = rows[AT_FIRST + 3 : AT_FIRST + 6, 64:128]
    lasts, rates = [], []
    for i in range(8):
        mine = jnp.concatenate([small[4 * i + j, 8:24, :] for j in range(4)], axis=0)
        lasts.append(mine[:, :96])
        rates += [mine[j : j + 1, 96:128] for j in range(3)]
    last[...] = jnp.concatenate(lasts, axis=1)
    rate = jnp.concatenate(rates, axis=1)
    decay[...] = jnp.concatenate(
        [rate[:, 128 * j : 128 * j + 128] for j in range(6)], axis=0
    ).reshape(768)
    for copy in leave:
        copy.wait()


def one_kernel_body(tokens, out_grad, norm_gain, norm_bias, in_weight, in_bias, conv_weight, conv_bias,
                    filt_first, filt_hidden, filt_bias, filt_freq, filt_last, decay_rates, skip_scale,
                    out_weight, out_bias, up_weight, up_bias, down_weight, down_bias):
    width, hidden = up_weight.shape
    length = tokens.shape[1] * lax.axis_size("seq")
    any_spec = pl.BlockSpec(memory_space=pl.ANY)
    vmem_spec = pl.BlockSpec(memory_space=pltpu.VMEM)

    def vm(*shape, dtype=f32):
        return pltpu.VMEM(shape, dtype)

    def vb(*shape):
        return pltpu.VMEM(shape, bf16)

    def dma(*shape):
        return pltpu.SemaphoreType.DMA(shape)

    def shape(*dims):
        return jax.ShapeDtypeStruct(dims, f32)

    scratch = [
        vb(width, 3 * width), vb(width, width), vb(width, hidden), vb(hidden, width), vb(4, 256, 256),
        vm(1, 3 * width), vm(1, 3 * width), vm(1, width), vm(1, width), vm(1, width), vm(1, hidden), vm(1, width),
        vb(144, width), vb(144, width), vm(128, width), vm(128, 1), vm(144, 3 * width),
        vm(128, width), vm(128, width), vm(128, width), vm(128, width),
        vb(4, 128, 1024), vb(128, 1024), vm(256, 1024), vm(256, 1024), vm(256, 1024), vb(128, 1024),
        vm(1024, 128), vm(1024, 128), vb(512, 1024),
        vm(64, 1024), vm(64, 1024), vm(64, 1024), vm(64, 1024), vm(64, 1024), vm(64, 1024),
        vm(64, 1024), vm(64, 1024), vm(64, 1024),
        vm(128, hidden), vb(128, hidden), vm(128, width), vm(128, width), vm(128, 1),
        vm(128, width), vm(128, width), vm(128, width), vm(128, width),
        vb(2, 1536, 128), vb(2, 384, 128), vb(2, 384, 128), vb(2, 384, 128),
        vb(1536, 256), vb(384, 256), vb(384, 256), vb(384, 256),
        vb(256, width), vb(256, hidden), vb(256, 3 * width), vb(256, width),
        vb(8, 192, 768), vb(8, 192, 768), vb(8, 192, 768), vb(8, 96, 768), vb(8, 96, 768),
        vb(8, 4, 48, 384), vb(8, 3, 48, 384),
        vb(3, 768, 256), vb(3, 768, 256), vb(3, 768, 256), vb(3, 384, 256), vb(3, 384, 256),
        vb(3, 4, 96, 256), vb(3, 3, 96, 256),
        vb(128, 1024), vb(128, 1024), vm(136, 3 * width), vm(256, 1024), vm(1024, 128),
        vm(256, 128), vm(32, 8, 128), vm(4, 16, 128), vm(4, 16, 128), vm(32, 24, 128),
        vm(432, 128), vm(144, 128), vm(576, 128), vm(576, 128), vm(128, width), vm(128, width),
        dma(7), dma(4, 7), dma(4, 7), dma(2), dma(2), dma(8), dma(8),
        dma(11), dma(11), dma(11), dma(11), dma(11, 3), dma(11, 3),
        dma(32), dma(32), dma(4), dma(4), dma(32), dma(32), dma(7),
    ]
    outs = pl.pallas_call(
        step_kernel,
        out_shape=[
            shape(128, width), shape(128, width), shape(432, 128), shape(144, 128),
            shape(576, 128), shape(576, 128), shape(32, 24, 128),
        ],
        in_specs=[any_spec] * 7 + [vmem_spec] * 16,
        out_specs=[any_spec] * 7,
        scratch_shapes=scratch,
        compiler_params=pltpu.CompilerParams(
            collective_id=0, has_side_effects=True, vmem_limit_bytes=62 * 1024 * 1024
        ),
        name="hyena_step",
    )(
        tokens, out_grad, in_weight, out_weight, up_weight, down_weight,
        jnp.asarray(fourier_tables()),
        jnp.asarray(feature_table(length, (filt_first.shape[0] - 1) // 2)),
        norm_gain, norm_bias, in_bias, conv_weight, conv_bias, filt_first, filt_hidden,
        filt_bias, filt_freq, filt_last, decay_rates, skip_scale, out_bias, up_bias, down_bias,
    )
    done = pl.pallas_call(
        finish_kernel,
        out_shape=[
            shape(1, 128, width), shape(1, 128, width), shape(2, width), shape(2, width), shape(432, 128),
            shape(3 * width), shape(3, 3 * width), shape(3 * width), shape(33, 64), shape(2, 64, 64),
            shape(3, 64), shape(3, 64), shape(64, width), shape(width), shape(width), shape(144, 128),
            shape(width), shape(576, 128), shape(hidden), shape(576, 128), shape(width),
        ],
        in_specs=[any_spec] * 7,
        out_specs=[any_spec, any_spec, vmem_spec, vmem_spec, any_spec]
        + [vmem_spec] * 10
        + [any_spec, vmem_spec, any_spec, vmem_spec, any_spec, vmem_spec],
        scratch_shapes=[
            vm(128, width), vm(128, width), vm(432, 128), vm(144, 128), vm(576, 128), vm(576, 128),
            vm(32, 24, 128), dma(7), dma(7),
        ],
        compiler_params=pltpu.CompilerParams(vmem_limit_bytes=32 * 1024 * 1024),
        name="hyena_finish",
    )(*outs)
    flat = (4, 15, 17, 19)
    return tuple(v.reshape(-1) if i in flat else v for i, v in enumerate(done))


def solution(mesh):
    small_mesh = mesh.shape["seq"] == 8 and mesh.shape["grp"] == 4
    return jax.shard_map(
        one_kernel_body if small_mesh else body,
        mesh=mesh,
        in_specs=(P("grp", "seq", None), P("grp", "seq", None)) + (P(),) * 19,
        out_specs=(
            P("grp", "seq", None),
            P("grp", "seq", None),
            P(),
            P(),
            P(("seq", "grp")),
        )
        + (P(),) * 10
        + (P(("seq", "grp")), P(), P(("seq", "grp")), P(), P(("seq", "grp")), P()),
        check_vma=False,
    )
```

```python
import math
import types

import jax
import jax.numpy as jnp
import ml_dtypes
import numpy as np
from jax import lax
from jax.experimental import pallas as pl
from jax.experimental.pallas import tpu as pltpu
from jax.sharding import PartitionSpec as P

epsilon = 1e-05


def shifted(array, axis, by):
    peers = lax.axis_size(axis)
    pairs = [(i, i + by) for i in range(peers) if 0 <= i + by < peers]
    return lax.ppermute(array, axis, pairs)


def highest(left_mat, right_mat):
    return jnp.dot(
        left_mat, right_mat, precision=lax.Precision.HIGHEST, preferred_element_type=jnp.float32
    )


def highest_t(left_mat, right_mat):
    return lax.dot_general(
        left_mat,
        right_mat,
        (((0,), (0,)), ((), ())),
        precision=lax.Precision.HIGHEST,
        preferred_element_type=jnp.float32,
    )


def rows_t(left_mat, right_mat):
    return lax.dot_general(
        left_mat, right_mat, (((0,), (0,)), ((), ())), preferred_element_type=jnp.float32
    )


def back_mul(grad_in, weight_mat):
    return lax.dot_general(
        grad_in, weight_mat, (((1,), (1,)), ((), ())), preferred_element_type=jnp.float32
    )


def layer_norm(values, gain_row, shift_row):
    row_mean = jnp.mean(values, axis=-1, keepdims=True)
    centred = values - row_mean
    inv_std = lax.rsqrt(jnp.mean(centred * centred, axis=-1, keepdims=True) + epsilon)
    normed = centred * inv_std
    return (normed * gain_row + shift_row, normed, inv_std)


def norm_back(grad_in, normed, inv_std, gain_row):
    scaled = grad_in * gain_row
    centred_grad = (
        scaled
        - jnp.mean(scaled, axis=-1, keepdims=True)
        - normed * jnp.mean(scaled * normed, axis=-1, keepdims=True)
    )
    return (centred_grad * inv_std, jnp.sum(grad_in * normed, axis=0), jnp.sum(grad_in, axis=0))


def smooth(values):
    return jax.nn.gelu(values, approximate=False)


def filter_rows(params, positions, length):
    filt_first, filt_hidden, filt_bias, filt_freq, filt_last, decay_rates = params
    place = positions.astype(jnp.float32)
    bands = (filt_first.shape[0] - 1) // 2
    band = 0.0001 + jnp.arange(bands, dtype=jnp.float32) * ((bands - 1 - 0.0001) / (bands - 1))
    omega = place[:, None] * (2.0 * math.pi / length)
    phase = omega * band[None, :]
    feats = jnp.concatenate(
        [place[:, None] / (length - 1), jnp.cos(phase), -jnp.sin(phase)], axis=1
    )
    act_one = jnp.sin(filt_freq[0] * (highest(feats, filt_first) + filt_bias[0]))
    act_two = jnp.sin(filt_freq[1] * (highest(act_one, filt_hidden[0]) + filt_bias[1]))
    act_three = jnp.sin(filt_freq[2] * (highest(act_two, filt_hidden[1]) + filt_bias[2]))
    window = jnp.exp(-decay_rates[None, :] * jnp.maximum(place, 0.0)[:, None])
    return highest(act_three, filt_last) * window


def body(
    tokens,
    out_grad,
    norm_gain,
    norm_bias,
    in_weight,
    in_bias,
    conv_weight,
    conv_bias,
    filt_first,
    filt_hidden,
    filt_bias,
    filt_freq,
    filt_last,
    decay_rates,
    skip_scale,
    out_weight,
    out_bias,
    up_weight,
    up_bias,
    down_weight,
    down_bias,
):
    row_count = tokens.shape[1]
    model_width = tokens.shape[2]
    seq_count = lax.axis_size("seq")
    length = row_count * seq_count
    fft_span = 2 * row_count
    fparams = (filt_first, filt_hidden, filt_bias, filt_freq, filt_last, decay_rates)
    fft_grid = jnp.arange(fft_span, dtype=jnp.int32)
    angles = (fft_grid[:, None] * fft_grid[None, :] % fft_span).astype(jnp.float32) * (
        2.0 * math.pi / fft_span
    )
    cos_full = jnp.cos(angles)
    sin_full = jnp.sin(angles)
    cos_left = cos_full[:, :row_count]
    sin_left = sin_full[:, :row_count]
    cos_low = cos_full[row_count:, :]
    sin_low = sin_full[row_count:, :]

    def segment(params, lag_step):
        positions = (lag_step - 1) * row_count + fft_grid
        keep_mask = (positions >= 0).astype(jnp.float32)
        return filter_rows(params, positions, length) * keep_mask[:, None]

    def forward_add(lag_step, source, totals):
        filter_taps = segment(fparams, lag_step)
        g_re = highest(cos_full, filter_taps)
        g_im = -highest(sin_full, filter_taps)
        source_f = source.astype(jnp.float32)
        s_re = highest(cos_left, source_f)
        s_im = -highest(sin_left, source_f)
        return (totals[0] + g_re * s_re - g_im * s_im, totals[1] + g_re * s_im + g_im * s_re)

    inputs = tokens[0].astype(jnp.float32)
    normed1, hat_one, std_one = layer_norm(inputs, norm_gain[0], norm_bias[0])
    normed1_b = normed1.astype(jnp.bfloat16)
    projected = (
        jnp.dot(normed1_b, in_weight, preferred_element_type=jnp.float32) + in_bias
    ).astype(jnp.bfloat16)
    before = shifted(projected[row_count - 2 :], "seq", 1)
    padded = jnp.concatenate([before, projected], axis=0).astype(jnp.float32)
    mixed_conv = (
        conv_weight[0] * padded[:row_count]
        + conv_weight[1] * padded[1 : row_count + 1]
        + conv_weight[2] * padded[2:]
        + conv_bias
    )
    outer_part = mixed_conv[:, :model_width]
    inner_part = mixed_conv[:, model_width : 2 * model_width]
    value_part = mixed_conv[:, 2 * model_width :]
    gated_b = (inner_part * value_part).astype(jnp.bfloat16)
    gated_f = gated_b.astype(jnp.float32)
    zero_totals = (
        jnp.zeros((fft_span, model_width), jnp.float32),
        jnp.zeros((fft_span, model_width), jnp.float32),
    )
    first_pass = forward_add(0, gated_b, zero_totals)

    def forward_step(lag_step, loop_carry):
        source, tot_re, tot_im = loop_carry
        source = shifted(source, "seq", 1)
        tot_re, tot_im = forward_add(lag_step, source, (tot_re, tot_im))
        return (source, tot_re, tot_im)

    unused_src, tot_re, tot_im = lax.fori_loop(
        1, seq_count, forward_step, (gated_b, first_pass[0], first_pass[1])
    )
    conv_out = (highest(cos_low, tot_re) - highest(sin_low, tot_im)) / fft_span
    summed = conv_out + skip_scale * gated_f
    mixed_out_b = (outer_part * summed).astype(jnp.bfloat16)
    residual = (
        inputs + jnp.dot(mixed_out_b, out_weight, preferred_element_type=jnp.float32) + out_bias
    )
    normed2, hat_two, std_two = layer_norm(residual, norm_gain[1], norm_bias[1])
    normed2_b = normed2.astype(jnp.bfloat16)
    pre_act = jnp.dot(normed2_b, up_weight, preferred_element_type=jnp.float32) + up_bias
    act_val, gelu_back = jax.vjp(smooth, pre_act)
    act_b = act_val.astype(jnp.bfloat16)
    result = residual + jnp.dot(act_b, down_weight, preferred_element_type=jnp.float32) + down_bias
    grad_out_b = out_grad[0]
    grad_out_f = grad_out_b.astype(jnp.float32)
    g_down = rows_t(act_b, grad_out_b)
    g_down_bias = jnp.sum(grad_out_f, axis=0)
    g_act = back_mul(grad_out_b, down_weight)
    g_pre_b = gelu_back(g_act)[0].astype(jnp.bfloat16)
    g_up = rows_t(normed2_b, g_pre_b)
    g_up_bias = jnp.sum(g_pre_b.astype(jnp.float32), axis=0)
    g_norm_two = back_mul(g_pre_b, up_weight)
    g_res_norm, g_gain_two, g_shift_two = norm_back(g_norm_two, hat_two, std_two, norm_gain[1])
    g_resid = grad_out_f + g_res_norm
    g_resid_b = g_resid.astype(jnp.bfloat16)
    g_outw = rows_t(mixed_out_b, g_resid_b)
    g_out_bias = jnp.sum(g_resid_b.astype(jnp.float32), axis=0)
    g_mixed = back_mul(g_resid_b, out_weight)
    g_outer = g_mixed * summed
    g_summed = g_mixed * outer_part
    g_skip = jnp.sum(g_summed * gated_f, axis=0)
    g_conv_b = g_summed.astype(jnp.bfloat16)
    v_re = highest(cos_left, gated_f)
    v_im = -highest(sin_left, gated_f)

    def backward_add(lag_step, source, loop_carry):
        tot_re, tot_im, grad_acc = loop_carry
        source_f = source.astype(jnp.float32)
        d_re = highest_t(cos_low, source_f) / fft_span
        d_im = -highest_t(sin_low, source_f) / fft_span

        def lag_taps(params):
            return segment(params, lag_step)

        filter_taps, taps_pull = jax.vjp(lag_taps, fparams)
        g_re = highest(cos_full, filter_taps)
        g_im = -highest(sin_full, filter_taps)
        tot_re = tot_re + g_re * d_re + g_im * d_im
        tot_im = tot_im - g_im * d_re + g_re * d_im
        s_re = v_re * d_re + v_im * d_im
        s_im = v_re * d_im - v_im * d_re
        d_taps = highest_t(cos_full, s_re) - highest_t(sin_full, s_im)
        more_grads = taps_pull(d_taps)[0]
        grad_acc = jax.tree.map(jnp.add, grad_acc, more_grads)
        return (tot_re, tot_im, grad_acc)

    zero_grads = jax.tree.map(jnp.zeros_like, fparams)
    start_carry = (zero_totals[0], zero_totals[1], zero_grads)
    first_back = backward_add(0, g_conv_b, start_carry)

    def backward_step(lag_step, loop_carry):
        source, tot_re, tot_im, grad_acc = loop_carry
        source = shifted(source, "seq", -1)
        tot_re, tot_im, grad_acc = backward_add(lag_step, source, (tot_re, tot_im, grad_acc))
        return (source, tot_re, tot_im, grad_acc)

    unused_src, back_re, back_im, cycle_grads = lax.fori_loop(
        1, seq_count, backward_step, (g_conv_b,) + first_back
    )
    g_long = highest_t(cos_left, back_re) - highest_t(sin_left, back_im)
    g_gated = g_summed * skip_scale + g_long
    g_mix = jnp.concatenate([g_outer, g_gated * value_part, g_gated * inner_part], axis=1)
    g_conv_bias = jnp.sum(g_mix, axis=0)
    g_conv_w = jnp.stack(
        [
            jnp.sum(g_mix * padded[tap_index : tap_index + row_count], axis=0)
            for tap_index in range(3)
        ]
    )
    g_pad = (
        jnp.pad(conv_weight[0] * g_mix, ((0, 2), (0, 0)))
        + jnp.pad(conv_weight[1] * g_mix, ((1, 1), (0, 0)))
        + jnp.pad(conv_weight[2] * g_mix, ((2, 0), (0, 0)))
    )
    after_rows = shifted(g_pad[:2], "seq", -1)
    g_proj_b = (g_pad[2:] + jnp.pad(after_rows, ((row_count - 2, 0), (0, 0)))).astype(jnp.bfloat16)
    g_inw = rows_t(normed1_b, g_proj_b)
    g_in_bias = jnp.sum(g_proj_b.astype(jnp.float32), axis=0)
    g_norm_one = back_mul(g_proj_b, in_weight)
    g_in_norm, g_gain_one, g_shift_one = norm_back(g_norm_one, hat_one, std_one, norm_gain[0])
    g_tokens = g_resid + g_in_norm
    small_grads = lax.psum(
        (
            jnp.stack([g_gain_one, g_gain_two]),
            jnp.stack([g_shift_one, g_shift_two]),
            g_in_bias,
            g_conv_w,
            g_conv_bias,
            cycle_grads[0],
            cycle_grads[1],
            cycle_grads[2],
            cycle_grads[3],
            cycle_grads[4],
            cycle_grads[5],
            g_skip,
            g_out_bias,
            g_up_bias,
            g_down_bias,
        ),
        ("seq", "grp"),
    )
    large_grads = (
        lax.psum_scatter(g_inw.reshape(-1), ("seq", "grp"), scatter_dimension=0, tiled=True),
        lax.psum_scatter(g_outw.reshape(-1), ("seq", "grp"), scatter_dimension=0, tiled=True),
        lax.psum_scatter(g_up.reshape(-1), ("seq", "grp"), scatter_dimension=0, tiled=True),
        lax.psum_scatter(g_down.reshape(-1), ("seq", "grp"), scatter_dimension=0, tiled=True),
    )
    return (
        result[None],
        g_tokens[None],
        small_grads[0],
        small_grads[1],
        large_grads[0],
        small_grads[2],
        small_grads[3],
        small_grads[4],
        small_grads[5],
        small_grads[6],
        small_grads[7],
        small_grads[8],
        small_grads[9],
        small_grads[10],
        small_grads[11],
        large_grads[1],
        small_grads[12],
        large_grads[2],
        small_grads[13],
        large_grads[3],
        small_grads[14],
    )


f32 = jnp.float32
bf16 = jnp.bfloat16
MESH_ID = pl.DeviceIdType.MESH
HIGH = lax.Precision.HIGHEST
ROWS = 128
HALO = 16


def nn(a, b):
    return jnp.dot(a, b, preferred_element_type=f32)


def nt(a, b):
    return lax.dot_general(a, b, (((1,), (1,)), ((), ())), preferred_element_type=f32)


def nn_high(a, b):
    return jnp.dot(a, b, precision=HIGH, preferred_element_type=f32)


def nt_high(a, b):
    return lax.dot_general(
        a, b, (((1,), (1,)), ((), ())), precision=HIGH, preferred_element_type=f32
    )


def tn_high(a, b):
    return lax.dot_general(
        a, b, (((0,), (0,)), ((), ())), precision=HIGH, preferred_element_type=f32
    )


def two(v):
    high = v.astype(bf16)
    return high, (v - high.astype(f32)).astype(bf16)


def sin_cos(v):
    k = jnp.floor(v * (1.0 / math.pi) + 0.5)
    r = ((v - k * 3.140625) - k * 0.0009670257568359375) - k * 6.2771141529083252e-07
    sign = 1.0 - 2.0 * (k - 2.0 * jnp.floor(k * 0.5))
    q = r * r
    s = 1.0 / math.factorial(13)
    for order in (11, 9, 7, 5, 3):
        s = 1.0 / math.factorial(order) - s * q
    s = r - r * q * s
    c = 1.0 / math.factorial(12)
    for order in (10, 8, 6, 4, 2):
        c = 1.0 / math.factorial(order) - c * q
    c = 1.0 - q * c
    return s * sign, c * sign


def gelu_both(v):
    a = jnp.abs(v)
    t = 1.0 / (1.0 + (0.3275911 / math.sqrt(2.0)) * a)
    poly = t * (
        0.254829592
        + t * (-0.284496736 + t * (1.421413741 + t * (-1.453152027 + t * 1.061405429)))
    )
    bell = jnp.exp(-0.5 * v * v)
    tail = 0.5 * poly * bell
    phi = jnp.where(v >= 0, 1.0 - tail, tail)
    return v * phi, phi + v * bell * (1.0 / math.sqrt(2.0 * math.pi))


def col_sum(v):
    return jnp.sum(v, axis=0, keepdims=True)


def row_mean(v):
    return jnp.mean(v, axis=1, keepdims=True)


def norm_rows(v):
    centred = v - row_mean(v)
    inv = lax.rsqrt(row_mean(centred * centred) + epsilon)
    return centred * inv, inv


def norm_rows_back(e, hat, inv, gain):
    k = e * gain
    return (k - row_mean(k) - hat * row_mean(k * hat)) * inv


def fourier_tables():
    bins = np.arange(128) + 0.5
    angle = 2.0 * np.pi * bins[:, None] * np.arange(256)[None, :] / 256
    full = np.concatenate([np.cos(angle), -np.sin(angle)], axis=0).astype(np.float32)
    out = []
    for mat in (full, full.T):
        high = mat.astype(ml_dtypes.bfloat16)
        out += [high, (mat - high.astype(np.float32)).astype(ml_dtypes.bfloat16)]
    return np.stack(out)


def feature_table(length, bands):
    place = np.arange(length)
    band = 1e-4 + np.arange(bands) * ((bands - 1 - 1e-4) / (bands - 1))
    phase = band[:, None] * (2.0 * np.pi * place / length)[None, :]
    return np.concatenate(
        [(place / (length - 1))[None], np.cos(phase), -np.sin(phase)], axis=0
    ).astype(np.float32)


AT_HID, AT_FIRST, AT_GAIN, AT_SHIFT, AT_IN, AT_CONVW, AT_CONVB = 0, 64, 97, 109, 121, 139, 193
AT_SKIP, AT_OUTB, AT_UPB, AT_DOWNB = 211, 217, 223, 247

SMALL_ARGS = (
    ("norm_gain", (2, 768)), ("norm_bias", (2, 768)), ("in_b1", (2304,)), ("conv_w", (3, 2304)),
    ("conv_b1", (2304,)), ("feats", (33, 1024)), ("filt_first", (33, 64)), ("filt_hidden", (2, 64, 64)),
    ("filt_bias", (3, 64)), ("filt_freq", (3, 64)), ("filt_last", (64, 768)), ("decay1", (768,)),
    ("skip1", (768,)), ("out_b1", (768,)), ("up_b1", (3072,)), ("down_b1", (768,)),
)

SCRATCH = (
    ("in_w", (768, 2304), bf16), ("out_w", (768, 768), bf16), ("up_w", (768, 3072), bf16),
    ("down_w", (3072, 768), bf16), ("tables", (4, 256, 256), bf16),
    ("in_b", (1, 2304), f32), ("conv_b", (1, 2304), f32), ("skip", (1, 768), f32),
    ("out_b", (1, 768), f32), ("up_b", (1, 3072), f32), ("down_b", (1, 768), f32),
    ("tok", (144, 768), bf16), ("n1", (144, 768), bf16), ("hat1", (128, 768), f32),
    ("std1", (128, 1), f32), ("pp", (144, 2304), f32), ("outer", (128, 768), f32),
    ("inner", (128, 768), f32), ("value", (128, 768), f32), ("gf", (128, 768), f32),
    ("stage", (4, 768, 128), bf16), ("gat", (768, 128), bf16), ("co_in", (768, 128), bf16),
    ("gc_in", (768, 128), bf16), ("gl_in", (768, 128), bf16),
    ("xs", (768, 256), f32), ("es", (768, 256), f32), ("ys", (768, 256), f32),
    ("gtap", (768, 256), f32), ("hw_high", (768, 256), bf16), ("hw_low", (768, 256), bf16),
    ("taps", (96, 1024), f32), ("wind", (96, 1024), f32), ("dpre", (96, 1024), f32),
    ("last_t", (768, 64), f32), ("rate_t", (768, 8), f32),
    ("a1", (64, 1024), f32), ("a2", (64, 1024), f32), ("a3", (64, 1024), f32),
    ("c1", (64, 1024), f32), ("c2", (64, 1024), f32), ("c3", (64, 1024), f32),
    ("u1", (64, 1024), f32), ("u2", (64, 1024), f32), ("u3", (64, 1024), f32),
    ("g_act", (128, 3072), f32), ("act", (128, 3072), bf16), ("summed", (128, 768), f32),
    ("hat2", (128, 768), f32), ("std2", (128, 1), f32), ("resid", (128, 768), f32),
    ("g_resid", (128, 768), f32), ("g_sum", (128, 768), f32), ("g_outer", (128, 768), f32),
    ("gm", (136, 2304), f32),
    ("at_down", (2, 1536, 128), bf16), ("at_up", (2, 384, 128), bf16), ("at_in", (2, 384, 128), bf16),
    ("at_out", (2, 384, 128), bf16), ("lh_down", (768, 512), bf16), ("lh_up", (384, 256), bf16),
    ("lh_in", (384, 256), bf16), ("lh_out", (384, 256), bf16), ("rh_down", (512, 768), bf16),
    ("rh_up", (256, 3072), bf16), ("rh_in", (256, 2304), bf16), ("rh_out", (256, 768), bf16),
    ("s1a", (8, 192, 768), bf16), ("k1a", (8, 192, 768), f32), ("r1a", (8, 192, 768), bf16),
    ("s2a", (8, 96, 768), bf16), ("r2a", (8, 96, 768), bf16), ("zsa", (8, 4, 48, 384), bf16),
    ("zra", (8, 3, 48, 384), bf16), ("s2b", (3, 384, 256), bf16), ("k2b", (3, 384, 256), f32),
    ("r2b", (3, 384, 256), bf16), ("zsb", (3, 4, 96, 256), bf16), ("zrb", (3, 3, 96, 256), bf16),
    ("smf", (4, 88, 128), f32), ("q_in", (3, 88, 128), f32), ("q_sum", (88, 128), f32),
    ("o_in", (7, 8, 128), f32), ("ag", (4, 8, 32, 128), f32),
    ("f_gin", (432, 128), f32), ("f_gout", (144, 128), f32), ("f_gup", (576, 128), f32),
    ("f_gdown", (576, 128), f32), ("f_out", (128, 768), f32), ("f_gtok", (128, 768), f32),
)

SEMAPHORES = (
    ("ld", (8,)), ("ls", (16,)), ("a2a_s", (4, 7)), ("a2a_r", (4, 7)), ("halo_s", (2,)), ("halo_r", (2,)),
    ("pair_s", (12,)), ("pair_r", (12,)), ("p1_s", (8,)), ("p1_r", (8,)), ("p2_s", (11,)),
    ("p2_r", (11,)), ("z_s", (11, 3)), ("z_r", (11, 3)), ("q_s", (3,)), ("q_r", (3,)),
    ("o_s", (7,)), ("o_r", (7,)), ("ag_s", (10,)), ("ag_r", (10,)), ("st", (7,)),
)


def step_kernel(*refs):
    names = ["tokens", "out_grad", "in_w_h", "out_w_h", "up_w_h", "down_w_h", "tables_h"]
    names += ["h_" + name for name, _ in SMALL_ARGS]
    names += ["o_out", "o_gtok", "o_gin", "o_gout", "o_gup", "o_gdown", "o_small"]
    names += [name for name, _ in SMALL_ARGS]
    names += [name for name, _, _ in SCRATCH] + [name for name, _ in SEMAPHORES]
    r = types.SimpleNamespace(**dict(zip(names, refs, strict=True)))

    s = lax.axis_index("seq")
    g = lax.axis_index("grp")
    z, x = lax.div(s, 2), lax.rem(s, 2)
    y, c = lax.div(g, 2), lax.rem(g, 2)
    other = g + 1 - 2 * c
    x_step, y_step = 1 - 2 * x, 2 * (1 - 2 * y)
    first = (s + (1 - c) * x_step, g + c * y_step)
    second = (s + c * x_step, g + (1 - c) * y_step)
    cross = (s + c * x_step, other + (1 - c) * y_step)
    b1 = (1 - c) * x + c * y
    b2 = (1 - c) * y + c * x

    def at(index, size):
        return pl.ds(pl.multiple_of(index * size, size), size)

    def remote(src, dst, ss, rs, where):
        return pltpu.make_async_remote_copy(
            src_ref=src,
            dst_ref=dst,
            send_sem=ss,
            recv_sem=rs,
            device_id=where,
            device_id_type=MESH_ID,
        )

    bar = pltpu.get_barrier_semaphore()

    @pl.loop(1, 8)
    def _(k):
        pl.semaphore_signal(
            bar, inc=1, device_id=(lax.rem(s + k, 8), g), device_id_type=MESH_ID
        )

    @pl.loop(1, 4)
    def _(k):
        pl.semaphore_signal(
            bar, inc=1, device_id=(s, lax.rem(g + k, 4)), device_id_type=MESH_ID
        )

    pl.semaphore_signal(bar, inc=1, device_id=(s + x_step, other), device_id_type=MESH_ID)

    own = pl.ds(0, ROWS)
    loads = [
        pltpu.make_async_copy(r.tokens.at[0], r.tok.at[pl.ds(HALO, ROWS)], r.ld.at[0]),
        pltpu.make_async_copy(r.in_w_h, r.in_w, r.ld.at[1]),
        pltpu.make_async_copy(r.out_grad.at[0], r.rh_down.at[own], r.ld.at[2]),
        pltpu.make_async_copy(r.tables_h, r.tables, r.ld.at[3]),
        pltpu.make_async_copy(r.down_w_h, r.down_w, r.ld.at[4]),
        pltpu.make_async_copy(r.out_w_h, r.out_w, r.ld.at[5]),
        pltpu.make_async_copy(r.up_w_h, r.up_w, r.ld.at[6]),
    ]
    small_loads = [
        pltpu.make_async_copy(getattr(r, "h_" + name), getattr(r, name), r.ls.at[i])
        for i, (name, _) in enumerate(SMALL_ARGS)
    ]
    loads[0].start()
    for copy in small_loads[:2]:
        copy.start()
    loads[1].start()
    for copy in small_loads[2:]:
        copy.start()
    loads[2].start()
    loads[3].start()

    def share(index, src, dst, where):
        return remote(src, dst, r.pair_s.at[index], r.pair_r.at[index], where)

    block2, block3, block4 = pl.ds(ROWS, ROWS), pl.ds(2 * ROWS, ROWS), pl.ds(3 * ROWS, ROWS)
    shares = [
        share(0, r.rh_down.at[own], r.rh_down.at[block2], (s, other)),
        share(1, r.rh_down.at[own], r.rh_down.at[block3], first),
        share(2, r.rh_down.at[own], r.rh_down.at[block4], cross),
        share(3, r.at_down.at[1 - c, at(b2, 768)], r.lh_down.at[:, block2], (s, other)),
        share(4, r.at_down.at[c, at(1 - b1, 768)], r.lh_down.at[:, block3], first),
        share(5, r.at_down.at[1 - c, at(1 - b2, 768)], r.lh_down.at[:, block4], cross),
        share(6, r.at_in.at[1 - c], r.lh_in.at[:, block2], (s, other)),
        share(7, r.at_out.at[1 - c], r.lh_out.at[:, block2], (s, other)),
        share(8, r.at_up.at[1 - c], r.lh_up.at[:, block2], (s, other)),
        share(9, r.rh_up.at[own], r.rh_up.at[block2], (s, other)),
        share(10, r.rh_out.at[own], r.rh_out.at[block2], (s, other)),
        share(11, r.rh_in.at[own], r.rh_in.at[block2], (s, other)),
    ]

    def order_rows(v, halves):
        t = jnp.transpose(v)
        for core in range(2):
            blocks = []
            for i1 in range(2):
                for i2 in range(2):
                    ix, iy = (i1, i2) if core == 0 else (i2, i1)
                    for iz in range(4):
                        at_row = 24 * (iz * 8 + ix * 4 + iy * 2 + core)
                        blocks.append(t[at_row : at_row + 24])
            halves[core] = jnp.concatenate(blocks, axis=0).astype(bf16)

    loads[0].wait()
    hat, inv = norm_rows(r.tok[pl.ds(HALO, ROWS)].astype(f32))
    r.hat1[...] = hat
    r.std1[...] = inv
    small_loads[0].wait()
    small_loads[1].wait()
    own_norm = (hat * r.norm_gain[0:1] + r.norm_bias[0:1]).astype(bf16)
    r.n1[pl.ds(HALO, ROWS)] = own_norm
    pl.semaphore_wait(bar, 11)
    last_rows = remote(
        r.tok.at[pl.ds(ROWS, HALO)],
        r.tok.at[pl.ds(0, HALO)],
        r.halo_s.at[0],
        r.halo_r.at[0],
        (s + 1, g),
    )

    @pl.when(s < 7)
    def _():
        last_rows.start()

    order_rows(own_norm.astype(f32), r.at_in)
    r.lh_in[:, own] = r.at_in[c]
    for copy in small_loads[2:]:
        copy.wait()
    for line, flat in (
        (r.in_b, r.in_b1), (r.conv_b, r.conv_b1), (r.skip, r.skip1),
        (r.out_b, r.out_b1), (r.up_b, r.up_b1), (r.down_b, r.down_b1),
    ):
        line[...] = flat[...].reshape(line.shape)

    @pl.when(s > 0)
    def _():
        last_rows.wait_recv()

    @pl.when(s == 0)
    def _():
        r.tok[pl.ds(0, HALO)] = jnp.zeros((HALO, r.tok.shape[1]), bf16)

    hat, inv = norm_rows(r.tok[pl.ds(0, HALO)].astype(f32))
    r.n1[pl.ds(0, HALO)] = (hat * r.norm_gain[0:1] + r.norm_bias[0:1]).astype(bf16)
    loads[1].wait()
    for copy in loads[4:]:
        copy.start()
    inside = jnp.where(s > 0, 1.0, 0.0).astype(f32)
    for part, dest in enumerate((r.outer, r.inner, r.value)):
        cols = pl.ds(768 * part, 768)
        proj = (nn(r.n1[...], r.in_w[:, cols]) + r.in_b[:, cols]).astype(bf16).astype(f32)
        r.pp[pl.ds(0, HALO), cols] = proj[:HALO] * inside
        r.pp[pl.ds(HALO, ROWS), cols] = proj[HALO:]
        dest[...] = (
            r.conv_w[0:1, cols] * r.pp[pl.ds(HALO - 2, ROWS), cols]
            + r.conv_w[1:2, cols] * r.pp[pl.ds(HALO - 1, ROWS), cols]
            + r.conv_w[2:3, cols] * r.pp[pl.ds(HALO, ROWS), cols]
            + r.conv_b[:, cols]
        )
    gated = (r.inner[...] * r.value[...]).astype(bf16).astype(f32)
    r.gf[...] = gated

    def trade(which, dst):
        @pl.loop(1, 8)
        def _(k):
            peer = lax.rem(s + k, 8)
            remote(
                r.stage.at[which, at(peer, 96)],
                dst.at[at(s, 96)],
                r.a2a_s.at[which, k - 1],
                r.a2a_r.at[which, k - 1],
                (peer, g),
            ).start()

        dst[at(s, 96)] = r.stage[which, at(s, 96)]

    def arrive(which, dst):
        @pl.loop(1, 8)
        def _(k):
            peer = lax.rem(s + 8 - k, 8)
            remote(
                r.stage.at[which, at(peer, 96)],
                dst.at[at(peer, 96)],
                r.a2a_s.at[which, k - 1],
                r.a2a_r.at[which, k - 1],
                (peer, g),
            ).wait_recv()

    r.stage[0] = jnp.transpose(gated).astype(bf16)
    trade(0, r.gat)

    bias_cols = jnp.transpose(r.filt_bias[...])
    freq_cols = jnp.transpose(r.filt_freq[...])
    below = r.feats[...]
    for i, (u_ref, a_ref, c_ref) in enumerate(
        ((r.u1, r.a1, r.c1), (r.u2, r.a2, r.c2), (r.u3, r.a3, r.c3))
    ):
        weights = r.filt_first[...] if i == 0 else r.filt_hidden[i - 1]
        u = tn_high(weights, below) + bias_cols[:, i : i + 1]
        u_ref[...] = u
        below, cosine = sin_cos(freq_cols[:, i : i + 1] * u)
        a_ref[...] = below
        c_ref[...] = cosine

    r.last_t[...] = jnp.transpose(r.filt_last[...])
    r.rate_t[...] = jnp.transpose(jnp.broadcast_to(r.decay1[...].reshape(1, 768), (8, 768)))
    last = r.last_t[at(s, 96)]
    rate = r.rate_t[at(s, 96), 0:1]
    place = lax.broadcasted_iota(jnp.int32, (1, 1024), 1).astype(f32)
    r.wind[...] = jnp.exp(-rate * place)
    r.taps[...] = nn_high(last, r.a3[...]) * r.wind[...]
    r.hw_high[pl.ds(0, 96), own] = jnp.zeros((96, 128), bf16)
    r.hw_low[pl.ds(0, 96), own] = jnp.zeros((96, 128), bf16)
    for b in range(8):
        high, low = two(r.taps[:, 128 * b : 128 * b + 128])
        for half, ref in ((high, r.hw_high), (low, r.hw_low)):
            ref[96 * b : 96 * b + 96, 128:256] = half
            if b < 7:
                ref[96 * b + 96 : 96 * b + 192, 0:128] = half

    def by_table(v, which, rows, cols):
        high, low = two(v)
        table = r.tables[which, rows, cols]
        return nn(high, table) + nn(low, table) + nn(high, r.tables[which + 1, rows, cols])

    every = pl.ds(0, 256)
    low_half, high_half = pl.ds(0, 128), pl.ds(128, 128)
    loads[3].wait()
    r.es[...] = (
        nn(r.hw_high[...], r.tables[2])
        + nn(r.hw_low[...], r.tables[2])
        + nn(r.hw_high[...], r.tables[3])
    )
    loads[2].wait()
    for copy in shares[0:3]:
        copy.start()
    shares[6].start()

    arrive(0, r.gat)
    r.xs[...] = nn(r.gat[...], r.tables[2, low_half]) + nn(r.gat[...], r.tables[3, low_half])

    def pick(ref, tile, b):
        rows = pl.ds(pl.multiple_of(96 * b + 8 * tile, 8), 8)
        return ref[rows, low_half], ref[rows, high_half]

    def keep(ref, tile, b, pair_of):
        rows = pl.ds(pl.multiple_of(96 * b + 8 * tile, 8), 8)
        ref[rows, low_half] = pair_of[0]
        ref[rows, high_half] = pair_of[1]

    @pl.loop(0, 12)
    def _(tile):
        e = [pick(r.es, tile, b) for b in range(8)]
        v = [pick(r.xs, tile, b) for b in range(8)]
        for b in range(8):
            re, im = 0.0, 0.0
            for lag in range(b + 1):
                er, ei = e[lag]
                vr, vi = v[b - lag]
                re = re + er * vr - ei * vi
                im = im + er * vi + ei * vr
            keep(r.ys, tile, b, (re, im))

    conv = by_table(r.ys[...], 0, every, high_half) * (1.0 / 128.0)
    r.stage[1] = conv.astype(bf16)
    trade(1, r.co_in)

    loads[4].wait()
    for t in range(4):
        cols = pl.ds(768 * t, 768)
        r.g_act[:, cols] = nt(r.rh_down[own], r.down_w[cols])

    arrive(1, r.co_in)
    sum_f = jnp.transpose(r.co_in[...].astype(f32)) + r.skip[...] * r.gf[...]
    r.summed[...] = sum_f
    mixed = (r.outer[...] * sum_f).astype(bf16)
    loads[5].wait()
    res = r.tok[pl.ds(HALO, ROWS)].astype(f32) + nn(mixed, r.out_w[...]) + r.out_b[...]
    r.resid[...] = res
    hat, inv = norm_rows(res)
    r.hat2[...] = hat
    r.std2[...] = inv
    n2 = (hat * r.norm_gain[1:2] + r.norm_bias[1:2]).astype(bf16)
    loads[6].wait()
    for t in range(4):
        cols = pl.ds(768 * t, 768)
        act_f, slope = gelu_both(nn(n2, r.up_w[:, cols]) + r.up_b[:, cols])
        act_b = act_f.astype(bf16)
        r.act[:, cols] = act_b
        r.rh_up[own, cols] = (r.g_act[:, cols] * slope).astype(bf16)
        turned = jnp.transpose(act_b.astype(f32)).astype(bf16)
        for ix in range(2):
            for iy in range(2):
                for core in range(2):
                    i1, i2 = (ix, iy) if core == 0 else (iy, ix)
                    src = 96 * (ix * 4 + iy * 2 + core)
                    r.at_down[core, pl.ds(i1 * 768 + i2 * 384 + t * 96, 96)] = turned[src : src + 96]
    for copy in shares[3:6]:
        copy.start()
    shares[9].start()
    order_rows(n2.astype(f32), r.at_up)
    shares[8].start()
    r.lh_up[:, own] = r.at_up[c]
    order_rows(mixed.astype(f32), r.at_out)
    shares[7].start()
    r.lh_out[:, own] = r.at_out[c]
    r.lh_down[:, own] = r.at_down[c, at(b1, 768)]

    def one_a(p):
        return remote(r.s1a.at[p], r.r1a.at[p], r.p1_s.at[p], r.p1_r.at[p], first)

    def two_a(p):
        return remote(r.s2a.at[p], r.r2a.at[p], r.p2_s.at[p], r.p2_r.at[p], second)

    def zed_a(p, k):
        to = lax.rem(z + k, 4)
        return remote(
            r.zsa.at[p, to],
            r.zra.at[p, k - 1],
            r.z_s.at[p, k - 1],
            r.z_r.at[p, k - 1],
            (to * 2 + x, g),
        )

    def two_b(p):
        return remote(r.s2b.at[p], r.r2b.at[p], r.p2_s.at[8 + p], r.p2_r.at[8 + p], second)

    def zed_b(p, k):
        to = lax.rem(z + k, 4)
        return remote(
            r.zsb.at[p, to],
            r.zrb.at[p, k - 1],
            r.z_s.at[8 + p, k - 1],
            r.z_r.at[8 + p, k - 1],
            (to * 2 + x, g),
        )

    def send_a(p0, count, lh, rh):
        @pl.loop(0, count)
        def _(p):
            r.s1a[p0 + p] = nn(lh[at(1 - b1, 192)], rh[:, at(p, 768)]).astype(bf16)
            one_a(p0 + p).start()

    def stay_a(p0, count, lh, rh):
        @pl.loop(0, count)
        def _(p):
            r.k1a[p0 + p] = nn(lh[at(b1, 192)], rh[:, at(p, 768)])

    def ph1_a(p):
        one_a(p).wait_recv()
        rows = at(1 - b2, 96)
        r.s2a[p] = (r.k1a[p, rows] + r.r1a[p, rows].astype(f32)).astype(bf16)
        two_a(p).start()

    def ph2_a(p):
        two_a(p).wait_recv()
        rows = at(b2, 96)
        v = r.k1a[p, rows] + r.r1a[p, rows].astype(f32) + r.r2a[p].astype(f32)
        for iz in range(4):
            block = v[24 * iz : 24 * iz + 24]
            r.zsa[p, iz] = jnp.concatenate([block[:, :384], block[:, 384:]], axis=0).astype(bf16)
        for k in range(1, 4):
            zed_a(p, k).start()

    def ph3_a(p, dest, base, per_row):
        for k in range(1, 4):
            zed_a(p, k).wait_recv()
        v = r.zsa[p, z].astype(f32)
        for k in range(3):
            v = v + r.zra[p, k].astype(f32)
        for h in range(2):
            for j in range(3):
                dest[pl.ds(base + 3 * h + j, 24, stride=per_row)] = v[
                    24 * h : 24 * h + 24, 128 * j : 128 * j + 128
                ]

    def ph2_b(p):
        two_b(p).wait_recv()
        v = r.k2b[p] + r.r2b[p].astype(f32)
        for iz in range(4):
            r.zsb[p, iz] = v[96 * iz : 96 * iz + 96].astype(bf16)
        for k in range(1, 4):
            zed_b(p, k).start()

    def ph3_b(p):
        for k in range(1, 4):
            zed_b(p, k).wait_recv()
        v = r.zsb[p, z].astype(f32)
        for k in range(3):
            v = v + r.zrb[p, k].astype(f32)
        for j in range(2):
            r.f_gdown[pl.ds(2 * p + j, 96, stride=6)] = v[:, 128 * j : 128 * j + 128]

    def put(row, v):
        for j in range(v.shape[1] // 128):
            part, line = divmod(row + j, 64)
            r.smf[part, line : line + 1] = v[:, 128 * j : 128 * j + 128]

    e = nt(r.rh_up[own], r.up_w[...])
    hat = r.hat2[...]
    grad_f = r.rh_down[own].astype(f32)
    g_res = grad_f + norm_rows_back(e, hat, r.std2[...], r.norm_gain[1:2])
    r.g_resid[...] = g_res
    g_res_b = g_res.astype(bf16)
    r.rh_out[own] = g_res_b
    shares[10].start()
    g_mixed = nt(g_res_b, r.out_w[...])
    r.g_outer[...] = g_mixed * r.summed[...]
    g_summed = g_mixed * r.outer[...]
    r.g_sum[...] = g_summed
    r.stage[2] = jnp.transpose(g_summed).astype(bf16)
    trade(2, r.gc_in)

    shares[8].wait_recv()
    shares[9].wait_recv()
    send_a(0, 4, r.lh_up, r.rh_up)
    for copy in shares[0:6]:
        copy.wait_recv()
    for p in range(3):
        cols = pl.ds(256 * p, 256)
        r.s2b[p] = nn(r.lh_down[at(1 - b2, 384)], r.rh_down[:, cols]).astype(bf16)
        two_b(p).start()
    shares[7].wait_recv()
    shares[10].wait_recv()
    send_a(4, 1, r.lh_out, r.rh_out)
    for p in range(3):
        r.k2b[p] = nn(r.lh_down[at(b2, 384)], r.rh_down[:, 256 * p : 256 * p + 256])
    put(AT_GAIN + 6, col_sum(e * hat))
    put(AT_SHIFT + 6, col_sum(e))
    put(AT_DOWNB, col_sum(grad_f))
    put(AT_UPB, col_sum(r.rh_up[own].astype(f32)))
    put(AT_OUTB, col_sum(g_res_b.astype(f32)))
    put(AT_SKIP, col_sum(g_summed * r.gf[...]))

    arrive(2, r.gc_in)
    r.ys[...] = (
        nn(r.gc_in[...], r.tables[2, high_half]) + nn(r.gc_in[...], r.tables[3, high_half])
    ) * (1.0 / 128.0)

    @pl.loop(0, 12)
    def _(tile):
        e = [pick(r.es, tile, b) for b in range(8)]
        d = [pick(r.ys, tile, b) for b in range(8)]
        for b in range(8):
            re, im = 0.0, 0.0
            for lag in range(8 - b):
                er, ei = e[lag]
                dr, di = d[b + lag]
                re = re + er * dr + ei * di
                im = im + er * di - ei * dr
            keep(r.es, tile, b, (re, im))

    g_long = by_table(r.es[...], 0, every, low_half)
    r.stage[3] = g_long.astype(bf16)
    trade(3, r.gl_in)

    stay_a(0, 4, r.lh_up, r.rh_up)
    stay_a(4, 1, r.lh_out, r.rh_out)
    r.f_out[...] = r.resid[...] + nn(r.act[...], r.down_w[...]) + r.down_b[...]
    store_out = pltpu.make_async_copy(r.f_out, r.o_out, r.st.at[0])
    store_out.start()
    ph1_a(0)

    arrive(3, r.gl_in)
    g_gated = r.skip[...] * r.g_sum[...] + jnp.transpose(r.gl_in[...].astype(f32))
    mixes = (r.g_outer[...], g_gated * r.value[...], g_gated * r.inner[...])
    for part in range(3):
        r.gm[own, 768 * part : 768 * part + 768] = mixes[part]
    first_rows = remote(
        r.gm.at[pl.ds(0, 8)], r.gm.at[pl.ds(ROWS, 8)], r.halo_s.at[1], r.halo_r.at[1], (s - 1, g)
    )

    @pl.when(s > 0)
    def _():
        first_rows.start()

    for part in range(3):
        cols = pl.ds(768 * part, 768)
        mix = r.gm[own, cols]
        put(AT_CONVB + 6 * part, col_sum(mix))
        for tap in range(3):
            put(
                AT_CONVW + 18 * tap + 6 * part,
                col_sum(mix * r.pp[pl.ds(HALO - 2 + tap, ROWS), cols]),
            )

    ph1_a(1)

    @pl.when(s < 7)
    def _():
        first_rows.wait_recv()

    @pl.when(s == 7)
    def _():
        r.gm[pl.ds(ROWS, 8)] = jnp.zeros((8, r.gm.shape[1]), f32)

    for part in range(3):
        cols = pl.ds(768 * part, 768)
        r.rh_in[own, cols] = (
            r.conv_w[0:1, cols] * r.gm[pl.ds(2, ROWS), cols]
            + r.conv_w[1:2, cols] * r.gm[pl.ds(1, ROWS), cols]
            + r.conv_w[2:3, cols] * r.gm[pl.ds(0, ROWS), cols]
        ).astype(bf16)
    shares[11].start()
    e = nt(r.rh_in[own], r.in_w[...])
    shares[6].wait_recv()
    shares[11].wait_recv()
    send_a(5, 3, r.lh_in, r.rh_in)
    ph1_a(2)
    stay_a(5, 3, r.lh_in, r.rh_in)
    for p in range(3):
        ph2_b(p)
    hat = r.hat1[...]
    put(AT_IN, col_sum(r.rh_in[own].astype(f32)))
    put(AT_GAIN, col_sum(e * hat))
    put(AT_SHIFT, col_sum(e))
    r.f_gtok[...] = r.g_resid[...] + norm_rows_back(e, hat, r.std1[...], r.norm_gain[0:1])
    store_tok = pltpu.make_async_copy(r.f_gtok, r.o_gtok, r.st.at[1])
    store_tok.start()
    ph1_a(3)

    @pl.loop(0, 12)
    def _(tile):
        v = [pick(r.xs, tile, b) for b in range(8)]
        d = [pick(r.ys, tile, b) for b in range(8)]
        for lag in range(8):
            re, im = 0.0, 0.0
            for b in range(8 - lag):
                vr, vi = v[b]
                dr, di = d[b + lag]
                re = re + vr * dr + vi * di
                im = im + vr * di - vi * dr
            keep(r.xs, tile, lag, (re, im))

    r.gtap[...] = by_table(r.xs[...], 0, every, every)
    ph1_a(4)
    for b in range(8):
        cols = pl.ds(128 * b, 128)
        gt = r.gtap[96 * b : 96 * b + 96, 128:256]
        if b < 7:
            gt = gt + r.gtap[96 * b + 96 : 96 * b + 192, 0:128]
        r.dpre[:, cols] = gt * r.wind[:, cols]
        r.taps[:, cols] = r.taps[:, cols] * gt
    g_rate = -jnp.sum(r.taps[...] * place, axis=1, keepdims=True)
    g_last = nt_high(r.dpre[...], r.a3[...])
    for j in range(4):
        r.smf[j, 64:88, 0:64] = g_last[24 * j : 24 * j + 24]
        r.smf[j, 64:88, 64:65] = g_rate[24 * j : 24 * j + 24]
    ones = jnp.ones((8, 1024), f32)
    g_a = tn_high(last, r.dpre[...])
    for i, (u_ref, c_ref, a_ref) in enumerate(
        ((r.u3, r.c3, r.a2), (r.u2, r.c2, r.a1), (r.u1, r.c1, None))
    ):
        layer = 2 - i
        g_arg = g_a * c_ref[...]
        g_freq = nt_high(ones, g_arg * u_ref[...])[0:1]
        g_u = g_arg * freq_cols[:, layer : layer + 1]
        g_bias = nt_high(ones, g_u)[0:1]
        r.smf[1, layer : layer + 1, 64:128] = g_bias
        r.smf[1, 3 + layer : 4 + layer, 64:128] = g_freq
        if layer > 0:
            r.smf[0, 0:64, 64 * (layer - 1) : 64 * layer] = nt_high(a_ref[...], g_u)
            g_a = nn_high(r.filt_hidden[layer - 1], g_u)
        else:
            r.smf[1, 0:33, 0:64] = nt_high(r.feats[...], g_u)

    def quarter(k):
        t = lax.rem(g + k, 4)
        return remote(r.smf.at[t], r.q_in.at[k - 1], r.q_s.at[k - 1], r.q_r.at[k - 1], (s, t))

    def eighth(k):
        t = lax.rem(s + k, 8)
        return remote(
            r.q_sum.at[at(t, 8)], r.o_in.at[k - 1], r.o_s.at[k - 1], r.o_r.at[k - 1], (t, g)
        )

    def spread(k, back):
        t = lax.rem(s + k, 8)
        mine = lax.rem(s + 8 - k, 8) if back else s
        slot = r.ag.at[g, mine]
        return remote(slot, slot, r.ag_s.at[k - 1], r.ag_r.at[k - 1], (t, g))

    over_y = g + y_step
    first_slot, second_slot = r.ag.at[g], r.ag.at[over_y]
    y_send = remote(first_slot, first_slot, r.ag_s.at[7], r.ag_r.at[7], (s, over_y))
    y_back = remote(second_slot, second_slot, r.ag_s.at[7], r.ag_r.at[7], (s, over_y))
    c_send = [
        remote(slot, slot, r.ag_s.at[8 + i], r.ag_r.at[8 + i], (s, other))
        for i, slot in enumerate((first_slot, second_slot))
    ]
    third_slot, fourth_slot = r.ag.at[other], r.ag.at[other + y_step]
    c_back = [
        remote(slot, slot, r.ag_s.at[8 + i], r.ag_r.at[8 + i], (s, other))
        for i, slot in enumerate((third_slot, fourth_slot))
    ]

    for k in range(1, 4):
        quarter(k).start()

    @pl.loop(0, 3)
    def _(p):
        ph2_a(p)

    for k in range(1, 4):
        quarter(k).wait_recv()
    r.q_sum[...] = r.smf[g] + r.q_in[0] + r.q_in[1] + r.q_in[2]

    @pl.loop(1, 8)
    def _(k):
        eighth(k).start()

    @pl.loop(5, 8)
    def _(p):
        ph1_a(p)

    ph2_a(3)
    ph2_a(4)

    @pl.loop(1, 8)
    def _(k):
        eighth(k).wait_recv()

    r.ag[g, s, pl.ds(0, 8)] = r.q_sum[at(s, 8)] + jnp.sum(r.o_in[...], axis=0)
    r.ag[g, s, pl.ds(8, 24)] = r.q_sum[pl.ds(64, 24)]

    @pl.loop(1, 8)
    def _(k):
        spread(k, False).start()

    for p in range(3):
        ph3_b(p)

    @pl.loop(1, 8)
    def _(k):
        spread(k, True).wait_recv()

    y_send.start()

    @pl.loop(0, 4)
    def _(p):
        ph3_a(p, r.f_gup, 6 * p, 24)

    @pl.loop(5, 8)
    def _(p):
        ph2_a(p)

    ph3_a(4, r.f_gout, 0, 6)
    y_back.wait_recv()
    for copy in c_send:
        copy.start()

    stores = [
        store_out,
        store_tok,
        pltpu.make_async_copy(r.f_gdown, r.o_gdown, r.st.at[2]),
        pltpu.make_async_copy(r.f_gup, r.o_gup, r.st.at[3]),
        pltpu.make_async_copy(r.f_gout, r.o_gout, r.st.at[4]),
        pltpu.make_async_copy(r.f_gin, r.o_gin, r.st.at[5]),
        pltpu.make_async_copy(r.ag, r.o_small, r.st.at[6]),
    ]
    for copy in stores[2:5]:
        copy.start()
    for copy in c_back:
        copy.wait_recv()
    stores[6].start()

    @pl.loop(0, 3)
    def _(p):
        ph3_a(5 + p, r.f_gin, 6 * p, 18)

    stores[5].start()

    @pl.when(s < 7)
    def _():
        last_rows.wait_send()

    @pl.when(s > 0)
    def _():
        first_rows.wait_send()

    for copy in shares:
        copy.wait_send()

    @pl.loop(0, 4)
    def _(which):
        @pl.loop(1, 8)
        def _(k):
            remote(
                r.stage.at[which, pl.ds(0, 96)],
                r.gat.at[pl.ds(0, 96)],
                r.a2a_s.at[which, k - 1],
                r.a2a_r.at[which, k - 1],
                (s, other),
            ).wait_send()

    @pl.loop(0, 8)
    def _(p):
        one_a(p).wait_send()
        two_a(p).wait_send()
        for k in range(1, 4):
            zed_a(p, k).wait_send()

    @pl.loop(0, 3)
    def _(p):
        two_b(p).wait_send()
        for k in range(1, 4):
            zed_b(p, k).wait_send()

    for k in range(1, 4):
        quarter(k).wait_send()

    @pl.loop(1, 8)
    def _(k):
        eighth(k).wait_send()
        spread(k, False).wait_send()

    y_send.wait_send()
    for copy in c_send:
        copy.wait_send()
    for copy in stores:
        copy.wait()


def finish_kernel(
    i_out, i_gtok, i_gin, i_gout, i_gup, i_gdown, i_small,
    out, gtok, gain, shift, gin, in_b, conv_w, conv_b, first, hidden, bias, freq,
    last, decay, skip, gout, out_b, gup, up_b, gdown, down_b,
    h_out, h_gtok, h_gin, h_gout, h_gup, h_gdown, small, sem_in, sem_out,
):
    bulk = (
        (i_small, small, None),
        (i_out, h_out, out.at[0]),
        (i_gtok, h_gtok, gtok.at[0]),
        (i_gin, h_gin, gin),
        (i_gout, h_gout, gout),
        (i_gup, h_gup, gup),
        (i_gdown, h_gdown, gdown),
    )
    enter = [pltpu.make_async_copy(a, b, sem_in.at[i]) for i, (a, b, _) in enumerate(bulk)]
    leave = [
        pltpu.make_async_copy(b, d, sem_out.at[i]) for i, (_, b, d) in enumerate(bulk) if i > 0
    ]
    for copy in enter:
        copy.start()
    for i in range(6):
        enter[i + 1].wait()
        leave[i].start()
    enter[0].wait()
    rows = jnp.concatenate([small[i, j, 0:8, :] for i in range(4) for j in range(8)], axis=0)

    def fetch(at_row, dest, dest_row, wide):
        for j in range(wide):
            dest[dest_row : dest_row + 1, 128 * j : 128 * j + 128] = rows[at_row + j : at_row + j + 1]

    def line(at_row, dest):
        dest[...] = rows[at_row : at_row + dest.shape[0] // 128].reshape(dest.shape[0])

    for i in range(2):
        fetch(AT_GAIN + 6 * i, gain, i, 6)
        fetch(AT_SHIFT + 6 * i, shift, i, 6)
        hidden[i] = rows[AT_HID : AT_HID + 64, 64 * i : 64 * i + 64]
    for i in range(3):
        fetch(AT_CONVW + 18 * i, conv_w, i, 18)
    line(AT_IN, in_b)
    line(AT_CONVB, conv_b)
    line(AT_SKIP, skip)
    line(AT_OUTB, out_b)
    line(AT_UPB, up_b)
    line(AT_DOWNB, down_b)
    first[...] = rows[AT_FIRST : AT_FIRST + 33, 0:64]
    bias[...] = rows[AT_FIRST : AT_FIRST + 3, 64:128]
    freq[...] = rows[AT_FIRST + 3 : AT_FIRST + 6, 64:128]
    channels = jnp.transpose(
        jnp.concatenate([small[j, i, 8:32, :] for i in range(8) for j in range(4)], axis=0)
    )
    last[...] = channels[0:64]
    decay[...] = channels[64:65].reshape(768)
    for copy in leave:
        copy.wait()


def one_kernel_body(tokens, out_grad, norm_gain, norm_bias, in_weight, in_bias, conv_weight, conv_bias,
                    filt_first, filt_hidden, filt_bias, filt_freq, filt_last, decay_rates, skip_scale,
                    out_weight, out_bias, up_weight, up_bias, down_weight, down_bias):
    width, hidden = up_weight.shape
    length = tokens.shape[1] * lax.axis_size("seq")
    any_spec = pl.BlockSpec(memory_space=pl.ANY)
    vmem_spec = pl.BlockSpec(memory_space=pltpu.VMEM)

    def vm(*shape, dtype=f32):
        return pltpu.VMEM(shape, dtype)

    def dma(*shape):
        return pltpu.SemaphoreType.DMA(shape)

    def shape(*dims):
        return jax.ShapeDtypeStruct(dims, f32)

    outs = pl.pallas_call(
        step_kernel,
        out_shape=[
            shape(128, width), shape(128, width), shape(432, 128), shape(144, 128),
            shape(576, 128), shape(576, 128), shape(4, 8, 32, 128),
        ],
        in_specs=[any_spec] * 23,
        out_specs=[any_spec] * 7,
        scratch_shapes=[vm(*dims) for _, dims in SMALL_ARGS]
        + [vm(*dims, dtype=dtype) for _, dims, dtype in SCRATCH]
        + [dma(*dims) for _, dims in SEMAPHORES],
        compiler_params=pltpu.CompilerParams(
            collective_id=0, has_side_effects=True, vmem_limit_bytes=62 * 1024 * 1024
        ),
        name="hyena_step",
    )(
        tokens, out_grad, in_weight, out_weight, up_weight, down_weight,
        jnp.asarray(fourier_tables()),
        norm_gain, norm_bias, in_bias, conv_weight, conv_bias,
        jnp.asarray(feature_table(length, (filt_first.shape[0] - 1) // 2)),
        filt_first, filt_hidden, filt_bias, filt_freq, filt_last, decay_rates, skip_scale, out_bias,
        up_bias, down_bias,
    )
    done = pl.pallas_call(
        finish_kernel,
        out_shape=[
            shape(1, 128, width), shape(1, 128, width), shape(2, width), shape(2, width), shape(432, 128),
            shape(3 * width), shape(3, 3 * width), shape(3 * width), shape(33, 64), shape(2, 64, 64),
            shape(3, 64), shape(3, 64), shape(64, width), shape(width), shape(width), shape(144, 128),
            shape(width), shape(576, 128), shape(hidden), shape(576, 128), shape(width),
        ],
        in_specs=[any_spec] * 7,
        out_specs=[any_spec, any_spec, vmem_spec, vmem_spec, any_spec]
        + [vmem_spec] * 10
        + [any_spec, vmem_spec, any_spec, vmem_spec, any_spec, vmem_spec],
        scratch_shapes=[
            vm(128, width), vm(128, width), vm(432, 128), vm(144, 128), vm(576, 128), vm(576, 128),
            vm(4, 8, 32, 128), dma(7), dma(7),
        ],
        compiler_params=pltpu.CompilerParams(vmem_limit_bytes=60 * 1024 * 1024),
        name="hyena_finish",
    )(*outs)
    flat = (4, 15, 17, 19)
    return tuple(v.reshape(-1) if i in flat else v for i, v in enumerate(done))


def solution(mesh):
    small_mesh = mesh.shape["seq"] == 8 and mesh.shape["grp"] == 4
    return jax.shard_map(
        one_kernel_body if small_mesh else body,
        mesh=mesh,
        in_specs=(P("grp", "seq", None), P("grp", "seq", None)) + (P(),) * 19,
        out_specs=(
            P("grp", "seq", None),
            P("grp", "seq", None),
            P(),
            P(),
            P(("seq", "grp")),
        )
        + (P(),) * 10
        + (P(("seq", "grp")), P(), P(("seq", "grp")), P(), P(("seq", "grp")), P()),
        check_vma=False,
    )
```

```python
import math
import types

import jax
import jax.numpy as jnp
import ml_dtypes
import numpy as np
from jax import lax
from jax.experimental import pallas as pl
from jax.experimental.pallas import tpu as pltpu
from jax.sharding import PartitionSpec as P

epsilon = 1e-05


def shifted(array, axis, by):
    peers = lax.axis_size(axis)
    pairs = [(i, i + by) for i in range(peers) if 0 <= i + by < peers]
    return lax.ppermute(array, axis, pairs)


def highest(left_mat, right_mat):
    return jnp.dot(
        left_mat, right_mat, precision=lax.Precision.HIGHEST, preferred_element_type=jnp.float32
    )


def highest_t(left_mat, right_mat):
    return lax.dot_general(
        left_mat,
        right_mat,
        (((0,), (0,)), ((), ())),
        precision=lax.Precision.HIGHEST,
        preferred_element_type=jnp.float32,
    )


def rows_t(left_mat, right_mat):
    return lax.dot_general(
        left_mat, right_mat, (((0,), (0,)), ((), ())), preferred_element_type=jnp.float32
    )


def back_mul(grad_in, weight_mat):
    return lax.dot_general(
        grad_in, weight_mat, (((1,), (1,)), ((), ())), preferred_element_type=jnp.float32
    )


def layer_norm(values, gain_row, shift_row):
    row_mean = jnp.mean(values, axis=-1, keepdims=True)
    centred = values - row_mean
    inv_std = lax.rsqrt(jnp.mean(centred * centred, axis=-1, keepdims=True) + epsilon)
    normed = centred * inv_std
    return (normed * gain_row + shift_row, normed, inv_std)


def norm_back(grad_in, normed, inv_std, gain_row):
    scaled = grad_in * gain_row
    centred_grad = (
        scaled
        - jnp.mean(scaled, axis=-1, keepdims=True)
        - normed * jnp.mean(scaled * normed, axis=-1, keepdims=True)
    )
    return (centred_grad * inv_std, jnp.sum(grad_in * normed, axis=0), jnp.sum(grad_in, axis=0))


def smooth(values):
    return jax.nn.gelu(values, approximate=False)


def filter_rows(params, positions, length):
    filt_first, filt_hidden, filt_bias, filt_freq, filt_last, decay_rates = params
    place = positions.astype(jnp.float32)
    bands = (filt_first.shape[0] - 1) // 2
    band = 0.0001 + jnp.arange(bands, dtype=jnp.float32) * ((bands - 1 - 0.0001) / (bands - 1))
    omega = place[:, None] * (2.0 * math.pi / length)
    phase = omega * band[None, :]
    feats = jnp.concatenate(
        [place[:, None] / (length - 1), jnp.cos(phase), -jnp.sin(phase)], axis=1
    )
    act_one = jnp.sin(filt_freq[0] * (highest(feats, filt_first) + filt_bias[0]))
    act_two = jnp.sin(filt_freq[1] * (highest(act_one, filt_hidden[0]) + filt_bias[1]))
    act_three = jnp.sin(filt_freq[2] * (highest(act_two, filt_hidden[1]) + filt_bias[2]))
    window = jnp.exp(-decay_rates[None, :] * jnp.maximum(place, 0.0)[:, None])
    return highest(act_three, filt_last) * window


def body(
    tokens,
    out_grad,
    norm_gain,
    norm_bias,
    in_weight,
    in_bias,
    conv_weight,
    conv_bias,
    filt_first,
    filt_hidden,
    filt_bias,
    filt_freq,
    filt_last,
    decay_rates,
    skip_scale,
    out_weight,
    out_bias,
    up_weight,
    up_bias,
    down_weight,
    down_bias,
):
    row_count = tokens.shape[1]
    model_width = tokens.shape[2]
    seq_count = lax.axis_size("seq")
    length = row_count * seq_count
    fft_span = 2 * row_count
    fparams = (filt_first, filt_hidden, filt_bias, filt_freq, filt_last, decay_rates)
    fft_grid = jnp.arange(fft_span, dtype=jnp.int32)
    angles = (fft_grid[:, None] * fft_grid[None, :] % fft_span).astype(jnp.float32) * (
        2.0 * math.pi / fft_span
    )
    cos_full = jnp.cos(angles)
    sin_full = jnp.sin(angles)
    cos_left = cos_full[:, :row_count]
    sin_left = sin_full[:, :row_count]
    cos_low = cos_full[row_count:, :]
    sin_low = sin_full[row_count:, :]

    def segment(params, lag_step):
        positions = (lag_step - 1) * row_count + fft_grid
        keep_mask = (positions >= 0).astype(jnp.float32)
        return filter_rows(params, positions, length) * keep_mask[:, None]

    def forward_add(lag_step, source, totals):
        filter_taps = segment(fparams, lag_step)
        g_re = highest(cos_full, filter_taps)
        g_im = -highest(sin_full, filter_taps)
        source_f = source.astype(jnp.float32)
        s_re = highest(cos_left, source_f)
        s_im = -highest(sin_left, source_f)
        return (totals[0] + g_re * s_re - g_im * s_im, totals[1] + g_re * s_im + g_im * s_re)

    inputs = tokens[0].astype(jnp.float32)
    normed1, hat_one, std_one = layer_norm(inputs, norm_gain[0], norm_bias[0])
    normed1_b = normed1.astype(jnp.bfloat16)
    projected = (
        jnp.dot(normed1_b, in_weight, preferred_element_type=jnp.float32) + in_bias
    ).astype(jnp.bfloat16)
    before = shifted(projected[row_count - 2 :], "seq", 1)
    padded = jnp.concatenate([before, projected], axis=0).astype(jnp.float32)
    mixed_conv = (
        conv_weight[0] * padded[:row_count]
        + conv_weight[1] * padded[1 : row_count + 1]
        + conv_weight[2] * padded[2:]
        + conv_bias
    )
    outer_part = mixed_conv[:, :model_width]
    inner_part = mixed_conv[:, model_width : 2 * model_width]
    value_part = mixed_conv[:, 2 * model_width :]
    gated_b = (inner_part * value_part).astype(jnp.bfloat16)
    gated_f = gated_b.astype(jnp.float32)
    zero_totals = (
        jnp.zeros((fft_span, model_width), jnp.float32),
        jnp.zeros((fft_span, model_width), jnp.float32),
    )
    first_pass = forward_add(0, gated_b, zero_totals)

    def forward_step(lag_step, loop_carry):
        source, tot_re, tot_im = loop_carry
        source = shifted(source, "seq", 1)
        tot_re, tot_im = forward_add(lag_step, source, (tot_re, tot_im))
        return (source, tot_re, tot_im)

    unused_src, tot_re, tot_im = lax.fori_loop(
        1, seq_count, forward_step, (gated_b, first_pass[0], first_pass[1])
    )
    conv_out = (highest(cos_low, tot_re) - highest(sin_low, tot_im)) / fft_span
    summed = conv_out + skip_scale * gated_f
    mixed_out_b = (outer_part * summed).astype(jnp.bfloat16)
    residual = (
        inputs + jnp.dot(mixed_out_b, out_weight, preferred_element_type=jnp.float32) + out_bias
    )
    normed2, hat_two, std_two = layer_norm(residual, norm_gain[1], norm_bias[1])
    normed2_b = normed2.astype(jnp.bfloat16)
    pre_act = jnp.dot(normed2_b, up_weight, preferred_element_type=jnp.float32) + up_bias
    act_val, gelu_back = jax.vjp(smooth, pre_act)
    act_b = act_val.astype(jnp.bfloat16)
    result = residual + jnp.dot(act_b, down_weight, preferred_element_type=jnp.float32) + down_bias
    grad_out_b = out_grad[0]
    grad_out_f = grad_out_b.astype(jnp.float32)
    g_down = rows_t(act_b, grad_out_b)
    g_down_bias = jnp.sum(grad_out_f, axis=0)
    g_act = back_mul(grad_out_b, down_weight)
    g_pre_b = gelu_back(g_act)[0].astype(jnp.bfloat16)
    g_up = rows_t(normed2_b, g_pre_b)
    g_up_bias = jnp.sum(g_pre_b.astype(jnp.float32), axis=0)
    g_norm_two = back_mul(g_pre_b, up_weight)
    g_res_norm, g_gain_two, g_shift_two = norm_back(g_norm_two, hat_two, std_two, norm_gain[1])
    g_resid = grad_out_f + g_res_norm
    g_resid_b = g_resid.astype(jnp.bfloat16)
    g_outw = rows_t(mixed_out_b, g_resid_b)
    g_out_bias = jnp.sum(g_resid_b.astype(jnp.float32), axis=0)
    g_mixed = back_mul(g_resid_b, out_weight)
    g_outer = g_mixed * summed
    g_summed = g_mixed * outer_part
    g_skip = jnp.sum(g_summed * gated_f, axis=0)
    g_conv_b = g_summed.astype(jnp.bfloat16)
    v_re = highest(cos_left, gated_f)
    v_im = -highest(sin_left, gated_f)

    def backward_add(lag_step, source, loop_carry):
        tot_re, tot_im, grad_acc = loop_carry
        source_f = source.astype(jnp.float32)
        d_re = highest_t(cos_low, source_f) / fft_span
        d_im = -highest_t(sin_low, source_f) / fft_span

        def lag_taps(params):
            return segment(params, lag_step)

        filter_taps, taps_pull = jax.vjp(lag_taps, fparams)
        g_re = highest(cos_full, filter_taps)
        g_im = -highest(sin_full, filter_taps)
        tot_re = tot_re + g_re * d_re + g_im * d_im
        tot_im = tot_im - g_im * d_re + g_re * d_im
        s_re = v_re * d_re + v_im * d_im
        s_im = v_re * d_im - v_im * d_re
        d_taps = highest_t(cos_full, s_re) - highest_t(sin_full, s_im)
        more_grads = taps_pull(d_taps)[0]
        grad_acc = jax.tree.map(jnp.add, grad_acc, more_grads)
        return (tot_re, tot_im, grad_acc)

    zero_grads = jax.tree.map(jnp.zeros_like, fparams)
    start_carry = (zero_totals[0], zero_totals[1], zero_grads)
    first_back = backward_add(0, g_conv_b, start_carry)

    def backward_step(lag_step, loop_carry):
        source, tot_re, tot_im, grad_acc = loop_carry
        source = shifted(source, "seq", -1)
        tot_re, tot_im, grad_acc = backward_add(lag_step, source, (tot_re, tot_im, grad_acc))
        return (source, tot_re, tot_im, grad_acc)

    unused_src, back_re, back_im, cycle_grads = lax.fori_loop(
        1, seq_count, backward_step, (g_conv_b,) + first_back
    )
    g_long = highest_t(cos_left, back_re) - highest_t(sin_left, back_im)
    g_gated = g_summed * skip_scale + g_long
    g_mix = jnp.concatenate([g_outer, g_gated * value_part, g_gated * inner_part], axis=1)
    g_conv_bias = jnp.sum(g_mix, axis=0)
    g_conv_w = jnp.stack(
        [
            jnp.sum(g_mix * padded[tap_index : tap_index + row_count], axis=0)
            for tap_index in range(3)
        ]
    )
    g_pad = (
        jnp.pad(conv_weight[0] * g_mix, ((0, 2), (0, 0)))
        + jnp.pad(conv_weight[1] * g_mix, ((1, 1), (0, 0)))
        + jnp.pad(conv_weight[2] * g_mix, ((2, 0), (0, 0)))
    )
    after_rows = shifted(g_pad[:2], "seq", -1)
    g_proj_b = (g_pad[2:] + jnp.pad(after_rows, ((row_count - 2, 0), (0, 0)))).astype(jnp.bfloat16)
    g_inw = rows_t(normed1_b, g_proj_b)
    g_in_bias = jnp.sum(g_proj_b.astype(jnp.float32), axis=0)
    g_norm_one = back_mul(g_proj_b, in_weight)
    g_in_norm, g_gain_one, g_shift_one = norm_back(g_norm_one, hat_one, std_one, norm_gain[0])
    g_tokens = g_resid + g_in_norm
    small_grads = lax.psum(
        (
            jnp.stack([g_gain_one, g_gain_two]),
            jnp.stack([g_shift_one, g_shift_two]),
            g_in_bias,
            g_conv_w,
            g_conv_bias,
            cycle_grads[0],
            cycle_grads[1],
            cycle_grads[2],
            cycle_grads[3],
            cycle_grads[4],
            cycle_grads[5],
            g_skip,
            g_out_bias,
            g_up_bias,
            g_down_bias,
        ),
        ("seq", "grp"),
    )
    large_grads = (
        lax.psum_scatter(g_inw.reshape(-1), ("seq", "grp"), scatter_dimension=0, tiled=True),
        lax.psum_scatter(g_outw.reshape(-1), ("seq", "grp"), scatter_dimension=0, tiled=True),
        lax.psum_scatter(g_up.reshape(-1), ("seq", "grp"), scatter_dimension=0, tiled=True),
        lax.psum_scatter(g_down.reshape(-1), ("seq", "grp"), scatter_dimension=0, tiled=True),
    )
    return (
        result[None],
        g_tokens[None],
        small_grads[0],
        small_grads[1],
        large_grads[0],
        small_grads[2],
        small_grads[3],
        small_grads[4],
        small_grads[5],
        small_grads[6],
        small_grads[7],
        small_grads[8],
        small_grads[9],
        small_grads[10],
        small_grads[11],
        large_grads[1],
        small_grads[12],
        large_grads[2],
        small_grads[13],
        large_grads[3],
        small_grads[14],
    )


f32 = jnp.float32
bf16 = jnp.bfloat16
MESH_ID = pl.DeviceIdType.MESH
HIGH = lax.Precision.HIGHEST
ROWS = 128
HALO = 16


def nn(a, b):
    return jnp.dot(a, b, preferred_element_type=f32)


def nt(a, b):
    return lax.dot_general(a, b, (((1,), (1,)), ((), ())), preferred_element_type=f32)


def nn_high(a, b):
    return jnp.dot(a, b, precision=HIGH, preferred_element_type=f32)


def nt_high(a, b):
    return lax.dot_general(
        a, b, (((1,), (1,)), ((), ())), precision=HIGH, preferred_element_type=f32
    )


def tn_high(a, b):
    return lax.dot_general(
        a, b, (((0,), (0,)), ((), ())), precision=HIGH, preferred_element_type=f32
    )


def two(v):
    high = v.astype(bf16)
    return high, (v - high.astype(f32)).astype(bf16)


def sin_cos(v):
    k = jnp.floor(v * (1.0 / math.pi) + 0.5)
    r = ((v - k * 3.140625) - k * 0.0009670257568359375) - k * 6.2771141529083252e-07
    sign = 1.0 - 2.0 * (k - 2.0 * jnp.floor(k * 0.5))
    q = r * r
    s = 1.0 / math.factorial(13)
    for order in (11, 9, 7, 5, 3):
        s = 1.0 / math.factorial(order) - s * q
    s = r - r * q * s
    c = 1.0 / math.factorial(12)
    for order in (10, 8, 6, 4, 2):
        c = 1.0 / math.factorial(order) - c * q
    c = 1.0 - q * c
    return s * sign, c * sign


def gelu_both(v):
    a = jnp.abs(v)
    t = 1.0 / (1.0 + (0.3275911 / math.sqrt(2.0)) * a)
    poly = t * (
        0.254829592
        + t * (-0.284496736 + t * (1.421413741 + t * (-1.453152027 + t * 1.061405429)))
    )
    bell = jnp.exp(-0.5 * v * v)
    tail = 0.5 * poly * bell
    phi = jnp.where(v >= 0, 1.0 - tail, tail)
    return v * phi, phi + v * bell * (1.0 / math.sqrt(2.0 * math.pi))


def col_sum(v):
    return jnp.sum(v, axis=0, keepdims=True)


def row_mean(v):
    return jnp.mean(v, axis=1, keepdims=True)


def norm_rows(v):
    centred = v - row_mean(v)
    inv = lax.rsqrt(row_mean(centred * centred) + epsilon)
    return centred * inv, inv


def norm_rows_back(e, hat, inv, gain):
    k = e * gain
    return (k - row_mean(k) - hat * row_mean(k * hat)) * inv


def fourier_tables():
    bins = np.arange(128) + 0.5
    angle = 2.0 * np.pi * bins[:, None] * np.arange(256)[None, :] / 256
    full = np.concatenate([np.cos(angle), -np.sin(angle)], axis=0).astype(np.float32)
    out = []
    for mat in (full, full.T):
        high = mat.astype(ml_dtypes.bfloat16)
        out += [high, (mat - high.astype(np.float32)).astype(ml_dtypes.bfloat16)]
    return np.stack(out)


def feature_table(length, bands):
    place = np.arange(length)
    band = 1e-4 + np.arange(bands) * ((bands - 1 - 1e-4) / (bands - 1))
    phase = band[:, None] * (2.0 * np.pi * place / length)[None, :]
    return np.concatenate(
        [(place / (length - 1))[None], np.cos(phase), -np.sin(phase)], axis=0
    ).astype(np.float32)


AT_HID, AT_FIRST, AT_GAIN, AT_SHIFT, AT_IN, AT_CONVW, AT_CONVB = 0, 64, 97, 109, 121, 139, 193
AT_SKIP, AT_OUTB, AT_UPB, AT_DOWNB = 211, 217, 223, 247

SMALL_ARGS = (
    ("norm_gain", (2, 768)), ("norm_bias", (2, 768)), ("in_b1", (2304,)), ("conv_w", (3, 2304)),
    ("conv_b1", (2304,)), ("feats", (33, 1024)), ("filt_first", (33, 64)), ("filt_hidden", (2, 64, 64)),
    ("filt_bias", (3, 64)), ("filt_freq", (3, 64)), ("filt_last", (64, 768)), ("decay1", (768,)),
    ("skip1", (768,)), ("out_b1", (768,)), ("up_b1", (3072,)), ("down_b1", (768,)),
)

SCRATCH = (
    ("in_w", (768, 2304), bf16), ("out_w", (768, 768), bf16), ("up_w", (768, 3072), bf16),
    ("down_w", (3072, 768), bf16), ("tables", (4, 256, 256), bf16),
    ("in_b", (1, 2304), f32), ("conv_b", (1, 2304), f32), ("skip", (1, 768), f32),
    ("out_b", (1, 768), f32), ("up_b", (1, 3072), f32), ("down_b", (1, 768), f32),
    ("tok", (144, 768), bf16), ("n1", (144, 768), bf16), ("hat1", (128, 768), f32),
    ("std1", (128, 1), f32), ("pp", (144, 2304), f32), ("outer", (128, 768), f32),
    ("inner", (128, 768), f32), ("value", (128, 768), f32), ("gf", (128, 768), f32),
    ("stage", (4, 768, 128), bf16), ("gat", (768, 128), bf16), ("co_in", (768, 128), bf16),
    ("gc_in", (768, 128), bf16), ("gl_in", (768, 128), bf16),
    ("xs", (768, 256), f32), ("es", (768, 256), f32), ("ys", (768, 256), f32),
    ("gtap", (768, 256), f32), ("hw_high", (768, 256), bf16), ("hw_low", (768, 256), bf16),
    ("taps", (96, 1024), f32), ("wind", (96, 1024), f32), ("dpre", (96, 1024), f32),
    ("last_t", (768, 64), f32), ("rate_t", (768, 8), f32),
    ("a1", (64, 1024), f32), ("a2", (64, 1024), f32), ("a3", (64, 1024), f32),
    ("c1", (64, 1024), f32), ("c2", (64, 1024), f32), ("c3", (64, 1024), f32),
    ("u1", (64, 1024), f32), ("u2", (64, 1024), f32), ("u3", (64, 1024), f32),
    ("g_act", (128, 3072), f32), ("act", (128, 3072), bf16), ("summed", (128, 768), f32),
    ("hat2", (128, 768), f32), ("std2", (128, 1), f32), ("resid", (128, 768), f32),
    ("g_resid", (128, 768), f32), ("g_sum", (128, 768), f32), ("g_outer", (128, 768), f32),
    ("gm", (136, 2304), f32),
    ("at_down", (2, 1536, 128), bf16), ("at_up", (2, 384, 128), bf16), ("at_in", (2, 384, 128), bf16),
    ("at_out", (2, 384, 128), bf16), ("lh_down", (768, 512), bf16), ("lh_up", (384, 256), bf16),
    ("lh_in", (384, 256), bf16), ("lh_out", (384, 256), bf16), ("rh_down", (512, 768), bf16),
    ("rh_up", (256, 3072), bf16), ("rh_in", (256, 2304), bf16), ("rh_out", (256, 768), bf16),
    ("s1a", (8, 192, 768), bf16), ("k1a", (8, 192, 768), f32), ("r1a", (8, 192, 768), bf16),
    ("s2a", (8, 96, 768), bf16), ("r2a", (8, 96, 768), bf16), ("s3a", (8, 4, 48, 384), bf16),
    ("r3a", (8, 2, 48, 384), bf16), ("s4a", (8, 48, 384), bf16), ("r4a", (8, 48, 384), bf16),
    ("s2b", (3, 384, 256), bf16), ("k2b", (3, 384, 256), f32), ("r2b", (3, 384, 256), bf16),
    ("s3b", (3, 4, 96, 256), bf16), ("r3b", (3, 2, 96, 256), bf16), ("s4b", (3, 96, 256), bf16),
    ("r4b", (3, 96, 256), bf16),
    ("smf", (4, 88, 128), f32), ("q_in", (3, 88, 128), f32), ("q_sum", (88, 128), f32),
    ("o_in", (7, 8, 128), f32), ("ag", (4, 8, 32, 128), f32),
    ("f_gin", (432, 128), f32), ("f_gout", (144, 128), f32), ("f_gup", (576, 128), f32),
    ("f_gdown", (576, 128), f32), ("f_out", (128, 768), f32), ("f_gtok", (128, 768), f32),
)

SEMAPHORES = (
    ("ld", (8,)), ("ls", (16,)), ("a2a_s", (4, 7)), ("a2a_r", (4, 7)), ("halo_s", (2,)), ("halo_r", (2,)),
    ("pair_s", (12,)), ("pair_r", (12,)), ("p1_s", (8,)), ("p1_r", (8,)), ("p2_s", (11,)),
    ("p2_r", (11,)), ("p3_s", (11,)), ("p3_r", (11,)), ("p4_s", (11,)), ("p4_r", (11,)), ("q_s", (3,)), ("q_r", (3,)),
    ("o_s", (7,)), ("o_r", (7,)), ("ag_s", (10,)), ("ag_r", (10,)), ("st", (7,)),
)


def step_kernel(*refs):
    names = ["tokens", "out_grad", "in_w_h", "out_w_h", "up_w_h", "down_w_h", "tables_h"]
    names += ["h_" + name for name, _ in SMALL_ARGS]
    names += ["o_out", "o_gtok", "o_gin", "o_gout", "o_gup", "o_gdown", "o_small"]
    names += [name for name, _ in SMALL_ARGS]
    names += [name for name, _, _ in SCRATCH] + [name for name, _ in SEMAPHORES]
    r = types.SimpleNamespace(**dict(zip(names, refs, strict=True)))

    s = lax.axis_index("seq")
    g = lax.axis_index("grp")
    z, x = lax.div(s, 2), lax.rem(s, 2)
    y, c = lax.div(g, 2), lax.rem(g, 2)
    other = g + 1 - 2 * c
    x_step, y_step = 1 - 2 * x, 2 * (1 - 2 * y)
    first = (s + (1 - c) * x_step, g + c * y_step)
    second = (s + c * x_step, g + (1 - c) * y_step)
    cross = (s + c * x_step, other + (1 - c) * y_step)
    b1 = (1 - c) * x + c * y
    b2 = (1 - c) * y + c * x
    z2, z1 = lax.div(z, 2), lax.rem(z, 2)
    near, far = (s + 2 - 4 * z1, g), (s + 4 - 8 * z2, g)

    def at(index, size):
        return pl.ds(pl.multiple_of(index * size, size), size)

    def remote(src, dst, ss, rs, where):
        return pltpu.make_async_remote_copy(
            src_ref=src,
            dst_ref=dst,
            send_sem=ss,
            recv_sem=rs,
            device_id=where,
            device_id_type=MESH_ID,
        )

    bar = pltpu.get_barrier_semaphore()

    @pl.loop(1, 8)
    def _(k):
        pl.semaphore_signal(
            bar, inc=1, device_id=(lax.rem(s + k, 8), g), device_id_type=MESH_ID
        )

    @pl.loop(1, 4)
    def _(k):
        pl.semaphore_signal(
            bar, inc=1, device_id=(s, lax.rem(g + k, 4)), device_id_type=MESH_ID
        )

    pl.semaphore_signal(bar, inc=1, device_id=(s + x_step, other), device_id_type=MESH_ID)

    own = pl.ds(0, ROWS)
    loads = [
        pltpu.make_async_copy(r.tokens.at[0], r.tok.at[pl.ds(HALO, ROWS)], r.ld.at[0]),
        pltpu.make_async_copy(r.in_w_h, r.in_w, r.ld.at[1]),
        pltpu.make_async_copy(r.out_grad.at[0], r.rh_down.at[own], r.ld.at[2]),
        pltpu.make_async_copy(r.tables_h, r.tables, r.ld.at[3]),
        pltpu.make_async_copy(r.down_w_h, r.down_w, r.ld.at[4]),
        pltpu.make_async_copy(r.out_w_h, r.out_w, r.ld.at[5]),
        pltpu.make_async_copy(r.up_w_h, r.up_w, r.ld.at[6]),
    ]
    small_loads = [
        pltpu.make_async_copy(getattr(r, "h_" + name), getattr(r, name), r.ls.at[i])
        for i, (name, _) in enumerate(SMALL_ARGS)
    ]
    loads[0].start()
    for copy in small_loads[:2]:
        copy.start()
    loads[1].start()
    for copy in small_loads[2:]:
        copy.start()
    loads[2].start()
    loads[3].start()

    def share(index, src, dst, where):
        return remote(src, dst, r.pair_s.at[index], r.pair_r.at[index], where)

    block2, block3, block4 = pl.ds(ROWS, ROWS), pl.ds(2 * ROWS, ROWS), pl.ds(3 * ROWS, ROWS)
    shares = [
        share(0, r.rh_down.at[own], r.rh_down.at[block2], (s, other)),
        share(1, r.rh_down.at[own], r.rh_down.at[block3], first),
        share(2, r.rh_down.at[own], r.rh_down.at[block4], cross),
        share(3, r.at_down.at[1 - c, at(b2, 768)], r.lh_down.at[:, block2], (s, other)),
        share(4, r.at_down.at[c, at(1 - b1, 768)], r.lh_down.at[:, block3], first),
        share(5, r.at_down.at[1 - c, at(1 - b2, 768)], r.lh_down.at[:, block4], cross),
        share(6, r.at_in.at[1 - c], r.lh_in.at[:, block2], (s, other)),
        share(7, r.at_out.at[1 - c], r.lh_out.at[:, block2], (s, other)),
        share(8, r.at_up.at[1 - c], r.lh_up.at[:, block2], (s, other)),
        share(9, r.rh_up.at[own], r.rh_up.at[block2], (s, other)),
        share(10, r.rh_out.at[own], r.rh_out.at[block2], (s, other)),
        share(11, r.rh_in.at[own], r.rh_in.at[block2], (s, other)),
    ]

    def order_rows(v, halves):
        t = jnp.transpose(v)
        for core in range(2):
            blocks = []
            for i1 in range(2):
                for i2 in range(2):
                    ix, iy = (i1, i2) if core == 0 else (i2, i1)
                    for iz in range(4):
                        at_row = 24 * (iz * 8 + ix * 4 + iy * 2 + core)
                        blocks.append(t[at_row : at_row + 24])
            halves[core] = jnp.concatenate(blocks, axis=0).astype(bf16)

    loads[0].wait()
    hat, inv = norm_rows(r.tok[pl.ds(HALO, ROWS)].astype(f32))
    r.hat1[...] = hat
    r.std1[...] = inv
    small_loads[0].wait()
    small_loads[1].wait()
    own_norm = (hat * r.norm_gain[0:1] + r.norm_bias[0:1]).astype(bf16)
    r.n1[pl.ds(HALO, ROWS)] = own_norm
    pl.semaphore_wait(bar, 11)
    last_rows = remote(
        r.tok.at[pl.ds(ROWS, HALO)],
        r.tok.at[pl.ds(0, HALO)],
        r.halo_s.at[0],
        r.halo_r.at[0],
        (s + 1, g),
    )

    @pl.when(s < 7)
    def _():
        last_rows.start()

    order_rows(own_norm.astype(f32), r.at_in)
    r.lh_in[:, own] = r.at_in[c]
    for copy in small_loads[2:]:
        copy.wait()
    for line, flat in (
        (r.in_b, r.in_b1), (r.conv_b, r.conv_b1), (r.skip, r.skip1),
        (r.out_b, r.out_b1), (r.up_b, r.up_b1), (r.down_b, r.down_b1),
    ):
        line[...] = flat[...].reshape(line.shape)

    @pl.when(s > 0)
    def _():
        last_rows.wait_recv()

    @pl.when(s == 0)
    def _():
        r.tok[pl.ds(0, HALO)] = jnp.zeros((HALO, r.tok.shape[1]), bf16)

    hat, inv = norm_rows(r.tok[pl.ds(0, HALO)].astype(f32))
    r.n1[pl.ds(0, HALO)] = (hat * r.norm_gain[0:1] + r.norm_bias[0:1]).astype(bf16)
    loads[1].wait()
    for copy in loads[4:]:
        copy.start()
    inside = jnp.where(s > 0, 1.0, 0.0).astype(f32)
    for part, dest in enumerate((r.outer, r.inner, r.value)):
        cols = pl.ds(768 * part, 768)
        proj = (nn(r.n1[...], r.in_w[:, cols]) + r.in_b[:, cols]).astype(bf16).astype(f32)
        r.pp[pl.ds(0, HALO), cols] = proj[:HALO] * inside
        r.pp[pl.ds(HALO, ROWS), cols] = proj[HALO:]
        dest[...] = (
            r.conv_w[0:1, cols] * r.pp[pl.ds(HALO - 2, ROWS), cols]
            + r.conv_w[1:2, cols] * r.pp[pl.ds(HALO - 1, ROWS), cols]
            + r.conv_w[2:3, cols] * r.pp[pl.ds(HALO, ROWS), cols]
            + r.conv_b[:, cols]
        )
    gated = (r.inner[...] * r.value[...]).astype(bf16).astype(f32)
    r.gf[...] = gated

    def trade(which, dst):
        @pl.loop(1, 8)
        def _(k):
            peer = lax.rem(s + k, 8)
            remote(
                r.stage.at[which, at(peer, 96)],
                dst.at[at(s, 96)],
                r.a2a_s.at[which, k - 1],
                r.a2a_r.at[which, k - 1],
                (peer, g),
            ).start()

        dst[at(s, 96)] = r.stage[which, at(s, 96)]

    def arrive(which, dst):
        @pl.loop(1, 8)
        def _(k):
            peer = lax.rem(s + 8 - k, 8)
            remote(
                r.stage.at[which, at(peer, 96)],
                dst.at[at(peer, 96)],
                r.a2a_s.at[which, k - 1],
                r.a2a_r.at[which, k - 1],
                (peer, g),
            ).wait_recv()

    r.stage[0] = jnp.transpose(gated).astype(bf16)
    trade(0, r.gat)

    bias_cols = jnp.transpose(r.filt_bias[...])
    freq_cols = jnp.transpose(r.filt_freq[...])
    below = r.feats[...]
    for i, (u_ref, a_ref, c_ref) in enumerate(
        ((r.u1, r.a1, r.c1), (r.u2, r.a2, r.c2), (r.u3, r.a3, r.c3))
    ):
        weights = r.filt_first[...] if i == 0 else r.filt_hidden[i - 1]
        u = tn_high(weights, below) + bias_cols[:, i : i + 1]
        u_ref[...] = u
        below, cosine = sin_cos(freq_cols[:, i : i + 1] * u)
        a_ref[...] = below
        c_ref[...] = cosine

    r.last_t[...] = jnp.transpose(r.filt_last[...])
    r.rate_t[...] = jnp.transpose(jnp.broadcast_to(r.decay1[...].reshape(1, 768), (8, 768)))
    last = r.last_t[at(s, 96)]
    rate = r.rate_t[at(s, 96), 0:1]
    place = lax.broadcasted_iota(jnp.int32, (1, 1024), 1).astype(f32)
    r.wind[...] = jnp.exp(-rate * place)
    r.taps[...] = nn_high(last, r.a3[...]) * r.wind[...]
    r.hw_high[pl.ds(0, 96), own] = jnp.zeros((96, 128), bf16)
    r.hw_low[pl.ds(0, 96), own] = jnp.zeros((96, 128), bf16)
    for b in range(8):
        high, low = two(r.taps[:, 128 * b : 128 * b + 128])
        for half, ref in ((high, r.hw_high), (low, r.hw_low)):
            ref[96 * b : 96 * b + 96, 128:256] = half
            if b < 7:
                ref[96 * b + 96 : 96 * b + 192, 0:128] = half

    def by_table(v, which, rows, cols):
        high, low = two(v)
        table = r.tables[which, rows, cols]
        return nn(high, table) + nn(low, table) + nn(high, r.tables[which + 1, rows, cols])

    every = pl.ds(0, 256)
    low_half, high_half = pl.ds(0, 128), pl.ds(128, 128)
    loads[3].wait()
    r.es[...] = (
        nn(r.hw_high[...], r.tables[2])
        + nn(r.hw_low[...], r.tables[2])
        + nn(r.hw_high[...], r.tables[3])
    )
    loads[2].wait()
    for copy in shares[0:3]:
        copy.start()
    shares[6].start()

    arrive(0, r.gat)
    r.xs[...] = nn(r.gat[...], r.tables[2, low_half]) + nn(r.gat[...], r.tables[3, low_half])

    def pick(ref, tile, b):
        rows = pl.ds(pl.multiple_of(96 * b + 8 * tile, 8), 8)
        return ref[rows, low_half], ref[rows, high_half]

    def keep(ref, tile, b, pair_of):
        rows = pl.ds(pl.multiple_of(96 * b + 8 * tile, 8), 8)
        ref[rows, low_half] = pair_of[0]
        ref[rows, high_half] = pair_of[1]

    @pl.loop(0, 12)
    def _(tile):
        e = [pick(r.es, tile, b) for b in range(8)]
        v = [pick(r.xs, tile, b) for b in range(8)]
        for b in range(8):
            re, im = 0.0, 0.0
            for lag in range(b + 1):
                er, ei = e[lag]
                vr, vi = v[b - lag]
                re = re + er * vr - ei * vi
                im = im + er * vi + ei * vr
            keep(r.ys, tile, b, (re, im))

    conv = by_table(r.ys[...], 0, every, high_half) * (1.0 / 128.0)
    r.stage[1] = conv.astype(bf16)
    trade(1, r.co_in)

    loads[4].wait()
    for t in range(4):
        cols = pl.ds(768 * t, 768)
        r.g_act[:, cols] = nt(r.rh_down[own], r.down_w[cols])

    arrive(1, r.co_in)
    sum_f = jnp.transpose(r.co_in[...].astype(f32)) + r.skip[...] * r.gf[...]
    r.summed[...] = sum_f
    mixed = (r.outer[...] * sum_f).astype(bf16)
    loads[5].wait()
    res = r.tok[pl.ds(HALO, ROWS)].astype(f32) + nn(mixed, r.out_w[...]) + r.out_b[...]
    r.resid[...] = res
    hat, inv = norm_rows(res)
    r.hat2[...] = hat
    r.std2[...] = inv
    n2 = (hat * r.norm_gain[1:2] + r.norm_bias[1:2]).astype(bf16)
    loads[6].wait()
    for t in range(4):
        cols = pl.ds(768 * t, 768)
        act_f, slope = gelu_both(nn(n2, r.up_w[:, cols]) + r.up_b[:, cols])
        act_b = act_f.astype(bf16)
        r.act[:, cols] = act_b
        r.rh_up[own, cols] = (r.g_act[:, cols] * slope).astype(bf16)
        turned = jnp.transpose(act_b.astype(f32)).astype(bf16)
        for ix in range(2):
            for iy in range(2):
                for core in range(2):
                    i1, i2 = (ix, iy) if core == 0 else (iy, ix)
                    src = 96 * (ix * 4 + iy * 2 + core)
                    r.at_down[core, pl.ds(i1 * 768 + i2 * 384 + t * 96, 96)] = turned[src : src + 96]
    for copy in shares[3:6]:
        copy.start()
    shares[9].start()
    order_rows(n2.astype(f32), r.at_up)
    shares[8].start()
    r.lh_up[:, own] = r.at_up[c]
    order_rows(mixed.astype(f32), r.at_out)
    shares[7].start()
    r.lh_out[:, own] = r.at_out[c]
    r.lh_down[:, own] = r.at_down[c, at(b1, 768)]

    def one_a(p):
        return remote(r.s1a.at[p], r.r1a.at[p], r.p1_s.at[p], r.p1_r.at[p], first)

    def two_a(p):
        return remote(r.s2a.at[p], r.r2a.at[p], r.p2_s.at[p], r.p2_r.at[p], second)

    def three_a(p):
        return remote(
            r.s3a.at[p, at(1 - z1, 2)], r.r3a.at[p], r.p3_s.at[p], r.p3_r.at[p], near
        )

    def four_a(p):
        return remote(r.s4a.at[p], r.r4a.at[p], r.p4_s.at[p], r.p4_r.at[p], far)

    def two_b(p):
        return remote(r.s2b.at[p], r.r2b.at[p], r.p2_s.at[8 + p], r.p2_r.at[8 + p], second)

    def three_b(p):
        return remote(
            r.s3b.at[p, at(1 - z1, 2)], r.r3b.at[p], r.p3_s.at[8 + p], r.p3_r.at[8 + p], near
        )

    def four_b(p):
        return remote(r.s4b.at[p], r.r4b.at[p], r.p4_s.at[8 + p], r.p4_r.at[8 + p], far)

    def make_a(p0, count, lh, rh):
        @pl.loop(0, count)
        def _(p):
            r.s1a[p0 + p] = nn(lh[at(1 - b1, 192)], rh[:, at(p, 768)]).astype(bf16)

    def stay_a(p0, count, lh, rh):
        @pl.loop(0, count)
        def _(p):
            r.k1a[p0 + p] = nn(lh[at(b1, 192)], rh[:, at(p, 768)])

    def ph1_a(p):
        one_a(p).wait_recv()
        rows = at(1 - b2, 96)
        r.s2a[p] = (r.k1a[p, rows] + r.r1a[p, rows].astype(f32)).astype(bf16)
        two_a(p).start()

    def ph2_a(p):
        two_a(p).wait_recv()
        rows = at(b2, 96)
        v = r.k1a[p, rows] + r.r1a[p, rows].astype(f32) + r.r2a[p].astype(f32)
        for iz in range(4):
            block = v[24 * iz : 24 * iz + 24]
            r.s3a[p, 2 * (iz % 2) + iz // 2] = jnp.concatenate(
                [block[:, :384], block[:, 384:]], axis=0
            ).astype(bf16)
        three_a(p).start()

    def ph3_a(p):
        three_a(p).wait_recv()
        r.s4a[p] = (
            r.s3a[p, 2 * z1 + 1 - z2].astype(f32) + r.r3a[p, 1 - z2].astype(f32)
        ).astype(bf16)
        four_a(p).start()

    def ph4_a(p, dest, base, per_row):
        four_a(p).wait_recv()
        v = r.s3a[p, 2 * z1 + z2].astype(f32) + r.r3a[p, z2].astype(f32) + r.r4a[p].astype(f32)
        for h in range(2):
            for j in range(3):
                dest[pl.ds(base + 3 * h + j, 24, stride=per_row)] = v[
                    24 * h : 24 * h + 24, 128 * j : 128 * j + 128
                ]

    def ph2_b(p):
        two_b(p).wait_recv()
        v = r.k2b[p] + r.r2b[p].astype(f32)
        for iz in range(4):
            r.s3b[p, 2 * (iz % 2) + iz // 2] = v[96 * iz : 96 * iz + 96].astype(bf16)
        three_b(p).start()

    def ph3_b(p):
        three_b(p).wait_recv()
        r.s4b[p] = (
            r.s3b[p, 2 * z1 + 1 - z2].astype(f32) + r.r3b[p, 1 - z2].astype(f32)
        ).astype(bf16)
        four_b(p).start()

    def ph4_b(p):
        four_b(p).wait_recv()
        v = r.s3b[p, 2 * z1 + z2].astype(f32) + r.r3b[p, z2].astype(f32) + r.r4b[p].astype(f32)
        for j in range(2):
            r.f_gdown[pl.ds(2 * p + j, 96, stride=6)] = v[:, 128 * j : 128 * j + 128]

    def put(row, v):
        for j in range(v.shape[1] // 128):
            part, line = divmod(row + j, 64)
            r.smf[part, line : line + 1] = v[:, 128 * j : 128 * j + 128]

    e = nt(r.rh_up[own], r.up_w[...])
    hat = r.hat2[...]
    grad_f = r.rh_down[own].astype(f32)
    g_res = grad_f + norm_rows_back(e, hat, r.std2[...], r.norm_gain[1:2])
    r.g_resid[...] = g_res
    g_res_b = g_res.astype(bf16)
    r.rh_out[own] = g_res_b
    shares[10].start()
    g_mixed = nt(g_res_b, r.out_w[...])
    r.g_outer[...] = g_mixed * r.summed[...]
    g_summed = g_mixed * r.outer[...]
    r.g_sum[...] = g_summed
    r.stage[2] = jnp.transpose(g_summed).astype(bf16)
    trade(2, r.gc_in)

    shares[8].wait_recv()
    shares[9].wait_recv()
    make_a(0, 4, r.lh_up, r.rh_up)
    one_a(0).start()
    for copy in shares[0:6]:
        copy.wait_recv()
    for p in range(3):
        cols = pl.ds(256 * p, 256)
        r.s2b[p] = nn(r.lh_down[at(1 - b2, 384)], r.rh_down[:, cols]).astype(bf16)
        if p == 0:
            two_b(p).start()
    for p in range(3):
        r.k2b[p] = nn(r.lh_down[at(b2, 384)], r.rh_down[:, 256 * p : 256 * p + 256])
    shares[7].wait_recv()
    shares[10].wait_recv()
    make_a(4, 1, r.lh_out, r.rh_out)
    put(AT_GAIN + 6, col_sum(e * hat))
    put(AT_SHIFT + 6, col_sum(e))
    put(AT_DOWNB, col_sum(grad_f))
    put(AT_UPB, col_sum(r.rh_up[own].astype(f32)))
    put(AT_OUTB, col_sum(g_res_b.astype(f32)))
    put(AT_SKIP, col_sum(g_summed * r.gf[...]))

    arrive(2, r.gc_in)
    r.ys[...] = (
        nn(r.gc_in[...], r.tables[2, high_half]) + nn(r.gc_in[...], r.tables[3, high_half])
    ) * (1.0 / 128.0)

    @pl.loop(0, 12)
    def _(tile):
        e = [pick(r.es, tile, b) for b in range(8)]
        d = [pick(r.ys, tile, b) for b in range(8)]
        for b in range(8):
            re, im = 0.0, 0.0
            for lag in range(8 - b):
                er, ei = e[lag]
                dr, di = d[b + lag]
                re = re + er * dr + ei * di
                im = im + er * di - ei * dr
            keep(r.es, tile, b, (re, im))

    g_long = by_table(r.es[...], 0, every, low_half)
    r.stage[3] = g_long.astype(bf16)
    trade(3, r.gl_in)

    one_a(1).start()
    two_b(1).start()
    stay_a(0, 4, r.lh_up, r.rh_up)
    stay_a(4, 1, r.lh_out, r.rh_out)
    ph2_b(0)
    ph1_a(0)
    r.f_out[...] = r.resid[...] + nn(r.act[...], r.down_w[...]) + r.down_b[...]
    store_out = pltpu.make_async_copy(r.f_out, r.o_out, r.st.at[0])
    store_out.start()

    arrive(3, r.gl_in)
    g_gated = r.skip[...] * r.g_sum[...] + jnp.transpose(r.gl_in[...].astype(f32))
    mixes = (r.g_outer[...], g_gated * r.value[...], g_gated * r.inner[...])
    for part in range(3):
        r.gm[own, 768 * part : 768 * part + 768] = mixes[part]
    first_rows = remote(
        r.gm.at[pl.ds(0, 8)], r.gm.at[pl.ds(ROWS, 8)], r.halo_s.at[1], r.halo_r.at[1], (s - 1, g)
    )

    @pl.when(s > 0)
    def _():
        first_rows.start()

    one_a(2).start()
    two_b(2).start()
    for part in range(3):
        cols = pl.ds(768 * part, 768)
        mix = r.gm[own, cols]
        put(AT_CONVB + 6 * part, col_sum(mix))
        for tap in range(3):
            put(
                AT_CONVW + 18 * tap + 6 * part,
                col_sum(mix * r.pp[pl.ds(HALO - 2 + tap, ROWS), cols]),
            )

    @pl.when(s < 7)
    def _():
        first_rows.wait_recv()

    @pl.when(s == 7)
    def _():
        r.gm[pl.ds(ROWS, 8)] = jnp.zeros((8, r.gm.shape[1]), f32)

    for part in range(3):
        cols = pl.ds(768 * part, 768)
        r.rh_in[own, cols] = (
            r.conv_w[0:1, cols] * r.gm[pl.ds(2, ROWS), cols]
            + r.conv_w[1:2, cols] * r.gm[pl.ds(1, ROWS), cols]
            + r.conv_w[2:3, cols] * r.gm[pl.ds(0, ROWS), cols]
        ).astype(bf16)
    shares[11].start()
    e = nt(r.rh_in[own], r.in_w[...])
    shares[6].wait_recv()
    shares[11].wait_recv()
    make_a(5, 3, r.lh_in, r.rh_in)
    for p in (5, 6, 7, 3, 4):
        one_a(p).start()
    ph1_a(1)
    ph2_b(1)
    ph3_b(0)
    stay_a(5, 3, r.lh_in, r.rh_in)
    ph1_a(2)
    ph2_b(2)
    hat = r.hat1[...]
    put(AT_IN, col_sum(r.rh_in[own].astype(f32)))
    put(AT_GAIN, col_sum(e * hat))
    put(AT_SHIFT, col_sum(e))
    r.f_gtok[...] = r.g_resid[...] + norm_rows_back(e, hat, r.std1[...], r.norm_gain[0:1])
    store_tok = pltpu.make_async_copy(r.f_gtok, r.o_gtok, r.st.at[1])
    store_tok.start()
    ph2_a(0)
    ph3_b(1)

    @pl.loop(0, 12)
    def _(tile):
        v = [pick(r.xs, tile, b) for b in range(8)]
        d = [pick(r.ys, tile, b) for b in range(8)]
        for lag in range(8):
            re, im = 0.0, 0.0
            for b in range(8 - lag):
                vr, vi = v[b]
                dr, di = d[b + lag]
                re = re + vr * dr + vi * di
                im = im + vr * di - vi * dr
            keep(r.xs, tile, lag, (re, im))

    r.gtap[...] = by_table(r.xs[...], 0, every, every)
    ph2_a(1)
    ph3_a(0)
    ph3_b(2)
    for b in range(8):
        cols = pl.ds(128 * b, 128)
        gt = r.gtap[96 * b : 96 * b + 96, 128:256]
        if b < 7:
            gt = gt + r.gtap[96 * b + 96 : 96 * b + 192, 0:128]
        r.dpre[:, cols] = gt * r.wind[:, cols]
        r.taps[:, cols] = r.taps[:, cols] * gt
    g_rate = -jnp.sum(r.taps[...] * place, axis=1, keepdims=True)
    g_last = nt_high(r.dpre[...], r.a3[...])
    for j in range(4):
        r.smf[j, 64:88, 0:64] = g_last[24 * j : 24 * j + 24]
        r.smf[j, 64:88, 64:65] = g_rate[24 * j : 24 * j + 24]
    ones = jnp.ones((8, 1024), f32)
    g_a = tn_high(last, r.dpre[...])
    for i, (u_ref, c_ref, a_ref) in enumerate(
        ((r.u3, r.c3, r.a2), (r.u2, r.c2, r.a1), (r.u1, r.c1, None))
    ):
        layer = 2 - i
        g_arg = g_a * c_ref[...]
        g_freq = nt_high(ones, g_arg * u_ref[...])[0:1]
        g_u = g_arg * freq_cols[:, layer : layer + 1]
        g_bias = nt_high(ones, g_u)[0:1]
        r.smf[1, layer : layer + 1, 64:128] = g_bias
        r.smf[1, 3 + layer : 4 + layer, 64:128] = g_freq
        if layer > 0:
            r.smf[0, 0:64, 64 * (layer - 1) : 64 * layer] = nt_high(a_ref[...], g_u)
            g_a = nn_high(r.filt_hidden[layer - 1], g_u)
        else:
            r.smf[1, 0:33, 0:64] = nt_high(r.feats[...], g_u)

    def quarter(k):
        t = lax.rem(g + k, 4)
        return remote(r.smf.at[t], r.q_in.at[k - 1], r.q_s.at[k - 1], r.q_r.at[k - 1], (s, t))

    def eighth(k):
        t = lax.rem(s + k, 8)
        return remote(
            r.q_sum.at[at(t, 8)], r.o_in.at[k - 1], r.o_s.at[k - 1], r.o_r.at[k - 1], (t, g)
        )

    def spread(k, back):
        t = lax.rem(s + k, 8)
        mine = lax.rem(s + 8 - k, 8) if back else s
        slot = r.ag.at[g, mine]
        return remote(slot, slot, r.ag_s.at[k - 1], r.ag_r.at[k - 1], (t, g))

    over_y = g + y_step
    first_slot, second_slot = r.ag.at[g], r.ag.at[over_y]
    y_send = remote(first_slot, first_slot, r.ag_s.at[7], r.ag_r.at[7], (s, over_y))
    y_back = remote(second_slot, second_slot, r.ag_s.at[7], r.ag_r.at[7], (s, over_y))
    c_send = [
        remote(slot, slot, r.ag_s.at[8 + i], r.ag_r.at[8 + i], (s, other))
        for i, slot in enumerate((first_slot, second_slot))
    ]
    third_slot, fourth_slot = r.ag.at[other], r.ag.at[other + y_step]
    c_back = [
        remote(slot, slot, r.ag_s.at[8 + i], r.ag_r.at[8 + i], (s, other))
        for i, slot in enumerate((third_slot, fourth_slot))
    ]

    for k in range(1, 4):
        quarter(k).start()

    ph2_a(2)
    ph3_a(1)
    ph1_a(5)
    ph1_a(6)
    for k in range(1, 4):
        quarter(k).wait_recv()
    r.q_sum[...] = r.smf[g] + r.q_in[0] + r.q_in[1] + r.q_in[2]

    @pl.loop(1, 8)
    def _(k):
        eighth(k).start()

    ph3_a(2)
    ph1_a(7)
    ph2_a(5)

    @pl.loop(1, 8)
    def _(k):
        eighth(k).wait_recv()

    r.ag[g, s, pl.ds(0, 8)] = r.q_sum[at(s, 8)] + jnp.sum(r.o_in[...], axis=0)
    r.ag[g, s, pl.ds(8, 24)] = r.q_sum[pl.ds(64, 24)]

    @pl.loop(1, 8)
    def _(k):
        spread(k, False).start()

    ph1_a(3)
    ph2_a(6)
    ph3_a(5)
    ph1_a(4)
    ph2_a(7)
    ph3_a(6)
    for p in range(3):
        ph4_b(p)

    @pl.loop(1, 8)
    def _(k):
        spread(k, True).wait_recv()

    y_send.start()

    @pl.loop(0, 3)
    def _(p):
        ph4_a(p, r.f_gup, 6 * p, 24)

    ph2_a(3)
    ph3_a(7)
    ph2_a(4)
    ph3_a(3)

    @pl.loop(0, 3)
    def _(p):
        ph4_a(5 + p, r.f_gin, 6 * p, 18)

    y_back.wait_recv()
    for copy in c_send:
        copy.start()
    ph3_a(4)

    stores = [
        store_out,
        store_tok,
        pltpu.make_async_copy(r.f_gdown, r.o_gdown, r.st.at[2]),
        pltpu.make_async_copy(r.f_gup, r.o_gup, r.st.at[3]),
        pltpu.make_async_copy(r.f_gout, r.o_gout, r.st.at[4]),
        pltpu.make_async_copy(r.f_gin, r.o_gin, r.st.at[5]),
        pltpu.make_async_copy(r.ag, r.o_small, r.st.at[6]),
    ]
    stores[2].start()
    stores[5].start()
    for copy in c_back:
        copy.wait_recv()
    stores[6].start()
    ph4_a(3, r.f_gup, 18, 24)
    stores[3].start()
    ph4_a(4, r.f_gout, 0, 6)
    stores[4].start()

    @pl.when(s < 7)
    def _():
        last_rows.wait_send()

    @pl.when(s > 0)
    def _():
        first_rows.wait_send()

    for copy in shares:
        copy.wait_send()

    @pl.loop(0, 4)
    def _(which):
        @pl.loop(1, 8)
        def _(k):
            remote(
                r.stage.at[which, pl.ds(0, 96)],
                r.gat.at[pl.ds(0, 96)],
                r.a2a_s.at[which, k - 1],
                r.a2a_r.at[which, k - 1],
                (s, other),
            ).wait_send()

    @pl.loop(0, 8)
    def _(p):
        one_a(p).wait_send()
        two_a(p).wait_send()
        three_a(p).wait_send()
        four_a(p).wait_send()

    @pl.loop(0, 3)
    def _(p):
        two_b(p).wait_send()
        three_b(p).wait_send()
        four_b(p).wait_send()

    for k in range(1, 4):
        quarter(k).wait_send()

    @pl.loop(1, 8)
    def _(k):
        eighth(k).wait_send()
        spread(k, False).wait_send()

    y_send.wait_send()
    for copy in c_send:
        copy.wait_send()
    for copy in stores:
        copy.wait()


def finish_kernel(
    i_out, i_gtok, i_gin, i_gout, i_gup, i_gdown, i_small,
    out, gtok, gain, shift, gin, in_b, conv_w, conv_b, first, hidden, bias, freq,
    last, decay, skip, gout, out_b, gup, up_b, gdown, down_b,
    h_out, h_gtok, h_gin, h_gout, h_gup, h_gdown, small, sem_in, sem_out,
):
    bulk = (
        (i_small, small, None),
        (i_out, h_out, out.at[0]),
        (i_gtok, h_gtok, gtok.at[0]),
        (i_gin, h_gin, gin),
        (i_gout, h_gout, gout),
        (i_gup, h_gup, gup),
        (i_gdown, h_gdown, gdown),
    )
    enter = [pltpu.make_async_copy(a, b, sem_in.at[i]) for i, (a, b, _) in enumerate(bulk)]
    leave = [
        pltpu.make_async_copy(b, d, sem_out.at[i]) for i, (_, b, d) in enumerate(bulk) if i > 0
    ]
    for copy in enter:
        copy.start()
    for i in range(6):
        enter[i + 1].wait()
        leave[i].start()
    enter[0].wait()
    rows = jnp.concatenate([small[i, j, 0:8, :] for i in range(4) for j in range(8)], axis=0)

    def fetch(at_row, dest, dest_row, wide):
        for j in range(wide):
            dest[dest_row : dest_row + 1, 128 * j : 128 * j + 128] = rows[at_row + j : at_row + j + 1]

    def line(at_row, dest):
        dest[...] = rows[at_row : at_row + dest.shape[0] // 128].reshape(dest.shape[0])

    for i in range(2):
        fetch(AT_GAIN + 6 * i, gain, i, 6)
        fetch(AT_SHIFT + 6 * i, shift, i, 6)
        hidden[i] = rows[AT_HID : AT_HID + 64, 64 * i : 64 * i + 64]
    for i in range(3):
        fetch(AT_CONVW + 18 * i, conv_w, i, 18)
    line(AT_IN, in_b)
    line(AT_CONVB, conv_b)
    line(AT_SKIP, skip)
    line(AT_OUTB, out_b)
    line(AT_UPB, up_b)
    line(AT_DOWNB, down_b)
    first[...] = rows[AT_FIRST : AT_FIRST + 33, 0:64]
    bias[...] = rows[AT_FIRST : AT_FIRST + 3, 64:128]
    freq[...] = rows[AT_FIRST + 3 : AT_FIRST + 6, 64:128]
    channels = jnp.transpose(
        jnp.concatenate([small[j, i, 8:32, :] for i in range(8) for j in range(4)], axis=0)
    )
    last[...] = channels[0:64]
    decay[...] = channels[64:65].reshape(768)
    for copy in leave:
        copy.wait()


def one_kernel_body(tokens, out_grad, norm_gain, norm_bias, in_weight, in_bias, conv_weight, conv_bias,
                    filt_first, filt_hidden, filt_bias, filt_freq, filt_last, decay_rates, skip_scale,
                    out_weight, out_bias, up_weight, up_bias, down_weight, down_bias):
    width, hidden = up_weight.shape
    length = tokens.shape[1] * lax.axis_size("seq")
    any_spec = pl.BlockSpec(memory_space=pl.ANY)
    vmem_spec = pl.BlockSpec(memory_space=pltpu.VMEM)

    def vm(*shape, dtype=f32):
        return pltpu.VMEM(shape, dtype)

    def dma(*shape):
        return pltpu.SemaphoreType.DMA(shape)

    def shape(*dims):
        return jax.ShapeDtypeStruct(dims, f32)

    outs = pl.pallas_call(
        step_kernel,
        out_shape=[
            shape(128, width), shape(128, width), shape(432, 128), shape(144, 128),
            shape(576, 128), shape(576, 128), shape(4, 8, 32, 128),
        ],
        in_specs=[any_spec] * 23,
        out_specs=[any_spec] * 7,
        scratch_shapes=[vm(*dims) for _, dims in SMALL_ARGS]
        + [vm(*dims, dtype=dtype) for _, dims, dtype in SCRATCH]
        + [dma(*dims) for _, dims in SEMAPHORES],
        compiler_params=pltpu.CompilerParams(
            collective_id=0, has_side_effects=True, vmem_limit_bytes=62 * 1024 * 1024
        ),
        name="hyena_step",
    )(
        tokens, out_grad, in_weight, out_weight, up_weight, down_weight,
        jnp.asarray(fourier_tables()),
        norm_gain, norm_bias, in_bias, conv_weight, conv_bias,
        jnp.asarray(feature_table(length, (filt_first.shape[0] - 1) // 2)),
        filt_first, filt_hidden, filt_bias, filt_freq, filt_last, decay_rates, skip_scale, out_bias,
        up_bias, down_bias,
    )
    done = pl.pallas_call(
        finish_kernel,
        out_shape=[
            shape(1, 128, width), shape(1, 128, width), shape(2, width), shape(2, width), shape(432, 128),
            shape(3 * width), shape(3, 3 * width), shape(3 * width), shape(33, 64), shape(2, 64, 64),
            shape(3, 64), shape(3, 64), shape(64, width), shape(width), shape(width), shape(144, 128),
            shape(width), shape(576, 128), shape(hidden), shape(576, 128), shape(width),
        ],
        in_specs=[any_spec] * 7,
        out_specs=[any_spec, any_spec, vmem_spec, vmem_spec, any_spec]
        + [vmem_spec] * 10
        + [any_spec, vmem_spec, any_spec, vmem_spec, any_spec, vmem_spec],
        scratch_shapes=[
            vm(128, width), vm(128, width), vm(432, 128), vm(144, 128), vm(576, 128), vm(576, 128),
            vm(4, 8, 32, 128), dma(7), dma(7),
        ],
        compiler_params=pltpu.CompilerParams(vmem_limit_bytes=60 * 1024 * 1024),
        name="hyena_finish",
    )(*outs)
    flat = (4, 15, 17, 19)
    return tuple(v.reshape(-1) if i in flat else v for i, v in enumerate(done))


def solution(mesh):
    small_mesh = mesh.shape["seq"] == 8 and mesh.shape["grp"] == 4
    return jax.shard_map(
        one_kernel_body if small_mesh else body,
        mesh=mesh,
        in_specs=(P("grp", "seq", None), P("grp", "seq", None)) + (P(),) * 19,
        out_specs=(
            P("grp", "seq", None),
            P("grp", "seq", None),
            P(),
            P(),
            P(("seq", "grp")),
        )
        + (P(),) * 10
        + (P(("seq", "grp")), P(), P(("seq", "grp")), P(), P(("seq", "grp")), P()),
        check_vma=False,
    )
```

```python
import math
import types

import jax
import jax.numpy as jnp
import ml_dtypes
import numpy as np
from jax import lax
from jax.experimental import pallas as pl
from jax.experimental.pallas import tpu as pltpu
from jax.sharding import PartitionSpec as P

epsilon = 1e-05


def shifted(array, axis, by):
    peers = lax.axis_size(axis)
    pairs = [(i, i + by) for i in range(peers) if 0 <= i + by < peers]
    return lax.ppermute(array, axis, pairs)


def highest(left_mat, right_mat):
    return jnp.dot(
        left_mat, right_mat, precision=lax.Precision.HIGHEST, preferred_element_type=jnp.float32
    )


def highest_t(left_mat, right_mat):
    return lax.dot_general(
        left_mat,
        right_mat,
        (((0,), (0,)), ((), ())),
        precision=lax.Precision.HIGHEST,
        preferred_element_type=jnp.float32,
    )


def rows_t(left_mat, right_mat):
    return lax.dot_general(
        left_mat, right_mat, (((0,), (0,)), ((), ())), preferred_element_type=jnp.float32
    )


def back_mul(grad_in, weight_mat):
    return lax.dot_general(
        grad_in, weight_mat, (((1,), (1,)), ((), ())), preferred_element_type=jnp.float32
    )


def layer_norm(values, gain_row, shift_row):
    row_mean = jnp.mean(values, axis=-1, keepdims=True)
    centred = values - row_mean
    inv_std = lax.rsqrt(jnp.mean(centred * centred, axis=-1, keepdims=True) + epsilon)
    normed = centred * inv_std
    return (normed * gain_row + shift_row, normed, inv_std)


def norm_back(grad_in, normed, inv_std, gain_row):
    scaled = grad_in * gain_row
    centred_grad = (
        scaled
        - jnp.mean(scaled, axis=-1, keepdims=True)
        - normed * jnp.mean(scaled * normed, axis=-1, keepdims=True)
    )
    return (centred_grad * inv_std, jnp.sum(grad_in * normed, axis=0), jnp.sum(grad_in, axis=0))


def smooth(values):
    return jax.nn.gelu(values, approximate=False)


def filter_rows(params, positions, length):
    filt_first, filt_hidden, filt_bias, filt_freq, filt_last, decay_rates = params
    place = positions.astype(jnp.float32)
    bands = (filt_first.shape[0] - 1) // 2
    band = 0.0001 + jnp.arange(bands, dtype=jnp.float32) * ((bands - 1 - 0.0001) / (bands - 1))
    omega = place[:, None] * (2.0 * math.pi / length)
    phase = omega * band[None, :]
    feats = jnp.concatenate(
        [place[:, None] / (length - 1), jnp.cos(phase), -jnp.sin(phase)], axis=1
    )
    act_one = jnp.sin(filt_freq[0] * (highest(feats, filt_first) + filt_bias[0]))
    act_two = jnp.sin(filt_freq[1] * (highest(act_one, filt_hidden[0]) + filt_bias[1]))
    act_three = jnp.sin(filt_freq[2] * (highest(act_two, filt_hidden[1]) + filt_bias[2]))
    window = jnp.exp(-decay_rates[None, :] * jnp.maximum(place, 0.0)[:, None])
    return highest(act_three, filt_last) * window


def body(
    tokens,
    out_grad,
    norm_gain,
    norm_bias,
    in_weight,
    in_bias,
    conv_weight,
    conv_bias,
    filt_first,
    filt_hidden,
    filt_bias,
    filt_freq,
    filt_last,
    decay_rates,
    skip_scale,
    out_weight,
    out_bias,
    up_weight,
    up_bias,
    down_weight,
    down_bias,
):
    row_count = tokens.shape[1]
    model_width = tokens.shape[2]
    seq_count = lax.axis_size("seq")
    length = row_count * seq_count
    fft_span = 2 * row_count
    fparams = (filt_first, filt_hidden, filt_bias, filt_freq, filt_last, decay_rates)
    fft_grid = jnp.arange(fft_span, dtype=jnp.int32)
    angles = (fft_grid[:, None] * fft_grid[None, :] % fft_span).astype(jnp.float32) * (
        2.0 * math.pi / fft_span
    )
    cos_full = jnp.cos(angles)
    sin_full = jnp.sin(angles)
    cos_left = cos_full[:, :row_count]
    sin_left = sin_full[:, :row_count]
    cos_low = cos_full[row_count:, :]
    sin_low = sin_full[row_count:, :]

    def segment(params, lag_step):
        positions = (lag_step - 1) * row_count + fft_grid
        keep_mask = (positions >= 0).astype(jnp.float32)
        return filter_rows(params, positions, length) * keep_mask[:, None]

    def forward_add(lag_step, source, totals):
        filter_taps = segment(fparams, lag_step)
        g_re = highest(cos_full, filter_taps)
        g_im = -highest(sin_full, filter_taps)
        source_f = source.astype(jnp.float32)
        s_re = highest(cos_left, source_f)
        s_im = -highest(sin_left, source_f)
        return (totals[0] + g_re * s_re - g_im * s_im, totals[1] + g_re * s_im + g_im * s_re)

    inputs = tokens[0].astype(jnp.float32)
    normed1, hat_one, std_one = layer_norm(inputs, norm_gain[0], norm_bias[0])
    normed1_b = normed1.astype(jnp.bfloat16)
    projected = (
        jnp.dot(normed1_b, in_weight, preferred_element_type=jnp.float32) + in_bias
    ).astype(jnp.bfloat16)
    before = shifted(projected[row_count - 2 :], "seq", 1)
    padded = jnp.concatenate([before, projected], axis=0).astype(jnp.float32)
    mixed_conv = (
        conv_weight[0] * padded[:row_count]
        + conv_weight[1] * padded[1 : row_count + 1]
        + conv_weight[2] * padded[2:]
        + conv_bias
    )
    outer_part = mixed_conv[:, :model_width]
    inner_part = mixed_conv[:, model_width : 2 * model_width]
    value_part = mixed_conv[:, 2 * model_width :]
    gated_b = (inner_part * value_part).astype(jnp.bfloat16)
    gated_f = gated_b.astype(jnp.float32)
    zero_totals = (
        jnp.zeros((fft_span, model_width), jnp.float32),
        jnp.zeros((fft_span, model_width), jnp.float32),
    )
    first_pass = forward_add(0, gated_b, zero_totals)

    def forward_step(lag_step, loop_carry):
        source, tot_re, tot_im = loop_carry
        source = shifted(source, "seq", 1)
        tot_re, tot_im = forward_add(lag_step, source, (tot_re, tot_im))
        return (source, tot_re, tot_im)

    unused_src, tot_re, tot_im = lax.fori_loop(
        1, seq_count, forward_step, (gated_b, first_pass[0], first_pass[1])
    )
    conv_out = (highest(cos_low, tot_re) - highest(sin_low, tot_im)) / fft_span
    summed = conv_out + skip_scale * gated_f
    mixed_out_b = (outer_part * summed).astype(jnp.bfloat16)
    residual = (
        inputs + jnp.dot(mixed_out_b, out_weight, preferred_element_type=jnp.float32) + out_bias
    )
    normed2, hat_two, std_two = layer_norm(residual, norm_gain[1], norm_bias[1])
    normed2_b = normed2.astype(jnp.bfloat16)
    pre_act = jnp.dot(normed2_b, up_weight, preferred_element_type=jnp.float32) + up_bias
    act_val, gelu_back = jax.vjp(smooth, pre_act)
    act_b = act_val.astype(jnp.bfloat16)
    result = residual + jnp.dot(act_b, down_weight, preferred_element_type=jnp.float32) + down_bias
    grad_out_b = out_grad[0]
    grad_out_f = grad_out_b.astype(jnp.float32)
    g_down = rows_t(act_b, grad_out_b)
    g_down_bias = jnp.sum(grad_out_f, axis=0)
    g_act = back_mul(grad_out_b, down_weight)
    g_pre_b = gelu_back(g_act)[0].astype(jnp.bfloat16)
    g_up = rows_t(normed2_b, g_pre_b)
    g_up_bias = jnp.sum(g_pre_b.astype(jnp.float32), axis=0)
    g_norm_two = back_mul(g_pre_b, up_weight)
    g_res_norm, g_gain_two, g_shift_two = norm_back(g_norm_two, hat_two, std_two, norm_gain[1])
    g_resid = grad_out_f + g_res_norm
    g_resid_b = g_resid.astype(jnp.bfloat16)
    g_outw = rows_t(mixed_out_b, g_resid_b)
    g_out_bias = jnp.sum(g_resid_b.astype(jnp.float32), axis=0)
    g_mixed = back_mul(g_resid_b, out_weight)
    g_outer = g_mixed * summed
    g_summed = g_mixed * outer_part
    g_skip = jnp.sum(g_summed * gated_f, axis=0)
    g_conv_b = g_summed.astype(jnp.bfloat16)
    v_re = highest(cos_left, gated_f)
    v_im = -highest(sin_left, gated_f)

    def backward_add(lag_step, source, loop_carry):
        tot_re, tot_im, grad_acc = loop_carry
        source_f = source.astype(jnp.float32)
        d_re = highest_t(cos_low, source_f) / fft_span
        d_im = -highest_t(sin_low, source_f) / fft_span

        def lag_taps(params):
            return segment(params, lag_step)

        filter_taps, taps_pull = jax.vjp(lag_taps, fparams)
        g_re = highest(cos_full, filter_taps)
        g_im = -highest(sin_full, filter_taps)
        tot_re = tot_re + g_re * d_re + g_im * d_im
        tot_im = tot_im - g_im * d_re + g_re * d_im
        s_re = v_re * d_re + v_im * d_im
        s_im = v_re * d_im - v_im * d_re
        d_taps = highest_t(cos_full, s_re) - highest_t(sin_full, s_im)
        more_grads = taps_pull(d_taps)[0]
        grad_acc = jax.tree.map(jnp.add, grad_acc, more_grads)
        return (tot_re, tot_im, grad_acc)

    zero_grads = jax.tree.map(jnp.zeros_like, fparams)
    start_carry = (zero_totals[0], zero_totals[1], zero_grads)
    first_back = backward_add(0, g_conv_b, start_carry)

    def backward_step(lag_step, loop_carry):
        source, tot_re, tot_im, grad_acc = loop_carry
        source = shifted(source, "seq", -1)
        tot_re, tot_im, grad_acc = backward_add(lag_step, source, (tot_re, tot_im, grad_acc))
        return (source, tot_re, tot_im, grad_acc)

    unused_src, back_re, back_im, cycle_grads = lax.fori_loop(
        1, seq_count, backward_step, (g_conv_b,) + first_back
    )
    g_long = highest_t(cos_left, back_re) - highest_t(sin_left, back_im)
    g_gated = g_summed * skip_scale + g_long
    g_mix = jnp.concatenate([g_outer, g_gated * value_part, g_gated * inner_part], axis=1)
    g_conv_bias = jnp.sum(g_mix, axis=0)
    g_conv_w = jnp.stack(
        [
            jnp.sum(g_mix * padded[tap_index : tap_index + row_count], axis=0)
            for tap_index in range(3)
        ]
    )
    g_pad = (
        jnp.pad(conv_weight[0] * g_mix, ((0, 2), (0, 0)))
        + jnp.pad(conv_weight[1] * g_mix, ((1, 1), (0, 0)))
        + jnp.pad(conv_weight[2] * g_mix, ((2, 0), (0, 0)))
    )
    after_rows = shifted(g_pad[:2], "seq", -1)
    g_proj_b = (g_pad[2:] + jnp.pad(after_rows, ((row_count - 2, 0), (0, 0)))).astype(jnp.bfloat16)
    g_inw = rows_t(normed1_b, g_proj_b)
    g_in_bias = jnp.sum(g_proj_b.astype(jnp.float32), axis=0)
    g_norm_one = back_mul(g_proj_b, in_weight)
    g_in_norm, g_gain_one, g_shift_one = norm_back(g_norm_one, hat_one, std_one, norm_gain[0])
    g_tokens = g_resid + g_in_norm
    small_grads = lax.psum(
        (
            jnp.stack([g_gain_one, g_gain_two]),
            jnp.stack([g_shift_one, g_shift_two]),
            g_in_bias,
            g_conv_w,
            g_conv_bias,
            cycle_grads[0],
            cycle_grads[1],
            cycle_grads[2],
            cycle_grads[3],
            cycle_grads[4],
            cycle_grads[5],
            g_skip,
            g_out_bias,
            g_up_bias,
            g_down_bias,
        ),
        ("seq", "grp"),
    )
    large_grads = (
        lax.psum_scatter(g_inw.reshape(-1), ("seq", "grp"), scatter_dimension=0, tiled=True),
        lax.psum_scatter(g_outw.reshape(-1), ("seq", "grp"), scatter_dimension=0, tiled=True),
        lax.psum_scatter(g_up.reshape(-1), ("seq", "grp"), scatter_dimension=0, tiled=True),
        lax.psum_scatter(g_down.reshape(-1), ("seq", "grp"), scatter_dimension=0, tiled=True),
    )
    return (
        result[None],
        g_tokens[None],
        small_grads[0],
        small_grads[1],
        large_grads[0],
        small_grads[2],
        small_grads[3],
        small_grads[4],
        small_grads[5],
        small_grads[6],
        small_grads[7],
        small_grads[8],
        small_grads[9],
        small_grads[10],
        small_grads[11],
        large_grads[1],
        small_grads[12],
        large_grads[2],
        small_grads[13],
        large_grads[3],
        small_grads[14],
    )


f32 = jnp.float32
bf16 = jnp.bfloat16
MESH_ID = pl.DeviceIdType.MESH
HIGH = lax.Precision.HIGHEST
ROWS = 128
HALO = 16


def nn(a, b):
    return jnp.dot(a, b, preferred_element_type=f32)


def nt(a, b):
    return lax.dot_general(a, b, (((1,), (1,)), ((), ())), preferred_element_type=f32)


def nn_high(a, b):
    return jnp.dot(a, b, precision=HIGH, preferred_element_type=f32)


def nt_high(a, b):
    return lax.dot_general(
        a, b, (((1,), (1,)), ((), ())), precision=HIGH, preferred_element_type=f32
    )


def tn_high(a, b):
    return lax.dot_general(
        a, b, (((0,), (0,)), ((), ())), precision=HIGH, preferred_element_type=f32
    )


def two(v):
    high = v.astype(bf16)
    return high, (v - high.astype(f32)).astype(bf16)


def sin_cos(v):
    k = jnp.floor(v * (1.0 / math.pi) + 0.5)
    r = ((v - k * 3.140625) - k * 0.0009670257568359375) - k * 6.2771141529083252e-07
    sign = 1.0 - 2.0 * (k - 2.0 * jnp.floor(k * 0.5))
    q = r * r
    s = 1.0 / math.factorial(13)
    for order in (11, 9, 7, 5, 3):
        s = 1.0 / math.factorial(order) - s * q
    s = r - r * q * s
    c = 1.0 / math.factorial(12)
    for order in (10, 8, 6, 4, 2):
        c = 1.0 / math.factorial(order) - c * q
    c = 1.0 - q * c
    return s * sign, c * sign


def gelu_both(v):
    a = jnp.abs(v)
    t = 1.0 / (1.0 + (0.3275911 / math.sqrt(2.0)) * a)
    poly = t * (
        0.254829592
        + t * (-0.284496736 + t * (1.421413741 + t * (-1.453152027 + t * 1.061405429)))
    )
    bell = jnp.exp(-0.5 * v * v)
    tail = 0.5 * poly * bell
    phi = jnp.where(v >= 0, 1.0 - tail, tail)
    return v * phi, phi + v * bell * (1.0 / math.sqrt(2.0 * math.pi))


def col_sum(v):
    return jnp.sum(v, axis=0, keepdims=True)


def row_mean(v):
    return jnp.mean(v, axis=1, keepdims=True)


def norm_rows(v):
    centred = v - row_mean(v)
    inv = lax.rsqrt(row_mean(centred * centred) + epsilon)
    return centred * inv, inv


def norm_rows_back(e, hat, inv, gain):
    k = e * gain
    return (k - row_mean(k) - hat * row_mean(k * hat)) * inv


def fourier_tables():
    bins = np.arange(128) + 0.5
    angle = 2.0 * np.pi * bins[:, None] * np.arange(256)[None, :] / 256
    full = np.concatenate([np.cos(angle), -np.sin(angle)], axis=0).astype(np.float32)
    out = []
    for mat in (full, full.T):
        high = mat.astype(ml_dtypes.bfloat16)
        out += [high, (mat - high.astype(np.float32)).astype(ml_dtypes.bfloat16)]
    return np.stack(out)


def feature_table(length, bands):
    place = np.arange(length)
    band = 1e-4 + np.arange(bands) * ((bands - 1 - 1e-4) / (bands - 1))
    phase = band[:, None] * (2.0 * np.pi * place / length)[None, :]
    return np.concatenate(
        [(place / (length - 1))[None], np.cos(phase), -np.sin(phase)], axis=0
    ).astype(np.float32)


AT_HID, AT_FIRST, AT_GAIN, AT_SHIFT, AT_IN, AT_CONVW, AT_CONVB = 0, 64, 97, 109, 121, 139, 193
AT_SKIP, AT_OUTB, AT_UPB, AT_DOWNB = 211, 217, 223, 247

SMALL_ARGS = (
    ("norm_gain", (2, 768)), ("norm_bias", (2, 768)), ("in_b1", (2304,)), ("conv_w", (3, 2304)),
    ("conv_b1", (2304,)), ("feats", (33, 1024)), ("filt_first", (33, 64)), ("filt_hidden", (2, 64, 64)),
    ("filt_bias", (3, 64)), ("filt_freq", (3, 64)), ("filt_last", (64, 768)), ("decay1", (768,)),
    ("skip1", (768,)), ("out_b1", (768,)), ("up_b1", (3072,)), ("down_b1", (768,)),
)

SCRATCH = (
    ("in_w", (768, 2304), bf16), ("out_w", (768, 768), bf16), ("up_w", (768, 3072), bf16),
    ("down_w", (3072, 768), bf16), ("tables", (4, 256, 256), bf16),
    ("in_b", (1, 2304), f32), ("conv_b", (1, 2304), f32), ("skip", (1, 768), f32),
    ("out_b", (1, 768), f32), ("up_b", (1, 3072), f32), ("down_b", (1, 768), f32),
    ("tok", (144, 768), bf16), ("n1", (144, 768), bf16), ("hat1", (128, 768), f32),
    ("std1", (128, 1), f32), ("pp", (144, 2304), f32), ("outer", (128, 768), f32),
    ("inner", (128, 768), f32), ("value", (128, 768), f32), ("gf", (128, 768), f32),
    ("stage", (4, 768, 128), bf16), ("gat", (768, 128), bf16), ("co_in", (768, 128), bf16),
    ("gc_in", (768, 128), bf16), ("gl_in", (768, 128), bf16),
    ("xs", (768, 256), f32), ("es", (768, 256), f32), ("ys", (768, 256), f32),
    ("hw_high", (768, 256), bf16), ("hw_low", (768, 256), bf16),
    ("taps", (96, 1024), f32), ("wind", (96, 1024), f32), ("dpre", (96, 1024), f32),
    ("last_t", (768, 64), f32), ("rate_t", (768, 8), f32),
    ("a1", (64, 1024), f32), ("a2", (64, 1024), f32), ("a3", (64, 1024), f32),
    ("c1", (64, 1024), f32), ("c2", (64, 1024), f32), ("c3", (64, 1024), f32),
    ("u1", (64, 1024), f32), ("u2", (64, 1024), f32), ("u3", (64, 1024), f32),
    ("g_act", (128, 3072), f32), ("act", (128, 3072), bf16), ("summed", (128, 768), f32),
    ("hat2", (128, 768), f32), ("std2", (128, 1), f32), ("resid", (128, 768), f32),
    ("g_resid", (128, 768), f32), ("g_sum", (128, 768), f32), ("g_outer", (128, 768), f32),
    ("gm", (136, 2304), f32),
    ("at_down", (2, 1536, 128), bf16), ("at_up", (2, 384, 128), bf16), ("at_upz", (2, 384, 128), bf16), ("at_in", (2, 384, 128), bf16),
    ("at_out", (2, 384, 128), bf16), ("lh_down", (768, 512), bf16), ("lh_up", (384, 256), bf16), ("lh_upz", (384, 256), bf16),
    ("lh_in", (384, 256), bf16), ("lh_out", (384, 256), bf16), ("rh_down", (512, 768), bf16),
    ("rh_up", (256, 3072), bf16), ("rh_in", (256, 2304), bf16), ("rh_out", (256, 768), bf16),
    ("s1a", (7, 192, 768), bf16), ("k1a", (7, 192, 768), f32), ("r1a", (7, 192, 768), bf16),
    ("s2a", (7, 96, 768), bf16), ("r2a", (7, 96, 768), bf16), ("s3a", (7, 4, 48, 384), bf16),
    ("r3a", (7, 2, 48, 384), bf16), ("s4a", (7, 48, 384), bf16), ("r4a", (7, 48, 384), bf16),
    ("s2b", (3, 384, 256), bf16), ("k2b", (3, 384, 256), f32), ("r2b", (3, 384, 256), bf16),
    ("s3b", (3, 4, 96, 256), bf16), ("r3b", (3, 2, 96, 256), bf16), ("s4b", (3, 96, 256), bf16),
    ("r4b", (3, 96, 256), bf16),
    ("s1z", (192, 768), bf16), ("k1z", (192, 768), f32), ("r1z", (192, 768), bf16),
    ("s2z", (96, 768), bf16), ("r2z", (96, 768), bf16), ("k3z", (48, 768), f32),
    ("s3z", (48, 768), bf16), ("r3z", (48, 768), bf16), ("k4z", (24, 768), f32),
    ("s4z", (48, 384), bf16), ("r4z", (48, 384), bf16),
    ("smf", (4, 88, 128), f32), ("q_in", (3, 88, 128), f32), ("q_sum", (88, 128), f32),
    ("o_in", (7, 8, 128), f32), ("ag", (4, 8, 32, 128), f32),
    ("f_gin", (432, 128), f32), ("f_gout", (144, 128), f32), ("f_gup", (576, 128), f32),
    ("f_gdown", (576, 128), f32),
)

SEMAPHORES = (
    ("ld", (8,)), ("ls", (16,)), ("a2a_s", (4, 7)), ("a2a_r", (4, 7)), ("halo_s", (2,)), ("halo_r", (2,)),
    ("pair_s", (13,)), ("pair_r", (13,)), ("p1_s", (8,)), ("p1_r", (8,)), ("p2_s", (11,)),
    ("p2_r", (11,)), ("p3_s", (11,)), ("p3_r", (11,)), ("p4_s", (11,)), ("p4_r", (11,)),
    ("zf_s", (4,)), ("zf_r", (4,)), ("q_s", (3,)), ("q_r", (3,)),
    ("o_s", (7,)), ("o_r", (7,)), ("ag_s", (10,)), ("ag_r", (10,)), ("st", (7,)),
)


def step_kernel(*refs):
    names = ["tokens", "out_grad", "in_w_h", "out_w_h", "up_w_h", "down_w_h", "tables_h"]
    names += ["h_" + name for name, _ in SMALL_ARGS]
    names += ["o_out", "o_gtok", "o_gin", "o_gout", "o_gup", "o_gdown", "o_small"]
    names += [name for name, _ in SMALL_ARGS]
    names += [name for name, _, _ in SCRATCH] + [name for name, _ in SEMAPHORES]
    r = types.SimpleNamespace(**dict(zip(names, refs, strict=True)))

    s = lax.axis_index("seq")
    g = lax.axis_index("grp")
    z, x = lax.div(s, 2), lax.rem(s, 2)
    y, c = lax.div(g, 2), lax.rem(g, 2)
    other = g + 1 - 2 * c
    x_step, y_step = 1 - 2 * x, 2 * (1 - 2 * y)
    first = (s + (1 - c) * x_step, g + c * y_step)
    second = (s + c * x_step, g + (1 - c) * y_step)
    cross = (s + c * x_step, other + (1 - c) * y_step)
    b1 = (1 - c) * x + c * y
    b2 = (1 - c) * y + c * x
    z2, z1 = lax.div(z, 2), lax.rem(z, 2)
    near, far = (s + 2 - 4 * z1, g), (s + 4 - 8 * z2, g)

    def at(index, size):
        return pl.ds(pl.multiple_of(index * size, size), size)

    def remote(src, dst, ss, rs, where):
        return pltpu.make_async_remote_copy(
            src_ref=src,
            dst_ref=dst,
            send_sem=ss,
            recv_sem=rs,
            device_id=where,
            device_id_type=MESH_ID,
        )

    bar = pltpu.get_barrier_semaphore()

    @pl.loop(1, 8)
    def _(k):
        pl.semaphore_signal(
            bar, inc=1, device_id=(lax.rem(s + k, 8), g), device_id_type=MESH_ID
        )

    @pl.loop(1, 4)
    def _(k):
        pl.semaphore_signal(
            bar, inc=1, device_id=(s, lax.rem(g + k, 4)), device_id_type=MESH_ID
        )

    pl.semaphore_signal(bar, inc=1, device_id=(s + x_step, other), device_id_type=MESH_ID)

    own = pl.ds(0, ROWS)
    loads = [
        pltpu.make_async_copy(r.tokens.at[0], r.tok.at[pl.ds(HALO, ROWS)], r.ld.at[0]),
        pltpu.make_async_copy(r.in_w_h, r.in_w, r.ld.at[1]),
        pltpu.make_async_copy(r.out_grad.at[0], r.rh_down.at[own], r.ld.at[2]),
        pltpu.make_async_copy(r.tables_h, r.tables, r.ld.at[3]),
        pltpu.make_async_copy(r.down_w_h, r.down_w, r.ld.at[4]),
        pltpu.make_async_copy(r.out_w_h, r.out_w, r.ld.at[5]),
        pltpu.make_async_copy(r.up_w_h, r.up_w, r.ld.at[6]),
    ]
    small_loads = [
        pltpu.make_async_copy(getattr(r, "h_" + name), getattr(r, name), r.ls.at[i])
        for i, (name, _) in enumerate(SMALL_ARGS)
    ]
    loads[0].start()
    for copy in small_loads[:2]:
        copy.start()
    loads[1].start()
    for copy in small_loads[2:]:
        copy.start()
    loads[2].start()
    loads[3].start()

    def share(index, src, dst, where):
        return remote(src, dst, r.pair_s.at[index], r.pair_r.at[index], where)

    block2, block3, block4 = pl.ds(ROWS, ROWS), pl.ds(2 * ROWS, ROWS), pl.ds(3 * ROWS, ROWS)
    shares = [
        share(0, r.rh_down.at[own], r.rh_down.at[block2], (s, other)),
        share(1, r.rh_down.at[own], r.rh_down.at[block3], first),
        share(2, r.rh_down.at[own], r.rh_down.at[block4], cross),
        share(3, r.at_down.at[1 - c, at(b2, 768)], r.lh_down.at[:, block2], (s, other)),
        share(4, r.at_down.at[c, at(1 - b1, 768)], r.lh_down.at[:, block3], first),
        share(5, r.at_down.at[1 - c, at(1 - b2, 768)], r.lh_down.at[:, block4], cross),
        share(6, r.at_in.at[1 - c], r.lh_in.at[:, block2], (s, other)),
        share(7, r.at_out.at[1 - c], r.lh_out.at[:, block2], (s, other)),
        share(8, r.at_up.at[1 - c], r.lh_up.at[:, block2], (s, other)),
        share(9, r.rh_up.at[own], r.rh_up.at[block2], (s, other)),
        share(10, r.rh_out.at[own], r.rh_out.at[block2], (s, other)),
        share(11, r.rh_in.at[own], r.rh_in.at[block2], (s, other)),
        share(12, r.at_upz.at[1 - c], r.lh_upz.at[:, block2], (s, other)),
    ]

    def order_rows(v, halves, z_halves=None):
        t = jnp.transpose(v)
        bits = [(i, j) for i in range(2) for j in range(2)]
        for core in range(2):

            def block(i1, i2, iz):
                ix, iy = (i1, i2) if core == 0 else (i2, i1)
                at_row = 24 * (iz * 8 + ix * 4 + iy * 2 + core)
                return t[at_row : at_row + 24]

            blocks = [block(i1, i2, iz) for i1, i2 in bits for iz in range(4)]
            halves[core] = jnp.concatenate(blocks, axis=0).astype(bf16)
            if z_halves is not None:
                blocks = [block(i1, i2, 2 * j2 + j1) for j1, j2 in bits for i1, i2 in bits]
                z_halves[core] = jnp.concatenate(blocks, axis=0).astype(bf16)

    loads[0].wait()
    hat, inv = norm_rows(r.tok[pl.ds(HALO, ROWS)].astype(f32))
    r.hat1[...] = hat
    r.std1[...] = inv
    small_loads[0].wait()
    small_loads[1].wait()
    own_norm = (hat * r.norm_gain[0:1] + r.norm_bias[0:1]).astype(bf16)
    r.n1[pl.ds(HALO, ROWS)] = own_norm
    pl.semaphore_wait(bar, 11)
    last_rows = remote(
        r.tok.at[pl.ds(ROWS, HALO)],
        r.tok.at[pl.ds(0, HALO)],
        r.halo_s.at[0],
        r.halo_r.at[0],
        (s + 1, g),
    )

    @pl.when(s < 7)
    def _():
        last_rows.start()

    order_rows(own_norm.astype(f32), r.at_in)
    r.lh_in[:, own] = r.at_in[c]
    for copy in small_loads[2:]:
        copy.wait()
    for line, flat in (
        (r.in_b, r.in_b1), (r.conv_b, r.conv_b1), (r.skip, r.skip1),
        (r.out_b, r.out_b1), (r.up_b, r.up_b1), (r.down_b, r.down_b1),
    ):
        line[...] = flat[...].reshape(line.shape)

    @pl.when(s > 0)
    def _():
        last_rows.wait_recv()

    @pl.when(s == 0)
    def _():
        r.tok[pl.ds(0, HALO)] = jnp.zeros((HALO, r.tok.shape[1]), bf16)

    hat, inv = norm_rows(r.tok[pl.ds(0, HALO)].astype(f32))
    r.n1[pl.ds(0, HALO)] = (hat * r.norm_gain[0:1] + r.norm_bias[0:1]).astype(bf16)
    loads[1].wait()
    for copy in loads[4:]:
        copy.start()
    inside = jnp.where(s > 0, 1.0, 0.0).astype(f32)
    for part, dest in enumerate((r.outer, r.inner, r.value)):
        cols = pl.ds(768 * part, 768)
        proj = (nn(r.n1[...], r.in_w[:, cols]) + r.in_b[:, cols]).astype(bf16).astype(f32)
        r.pp[pl.ds(0, HALO), cols] = proj[:HALO] * inside
        r.pp[pl.ds(HALO, ROWS), cols] = proj[HALO:]
        dest[...] = (
            r.conv_w[0:1, cols] * r.pp[pl.ds(HALO - 2, ROWS), cols]
            + r.conv_w[1:2, cols] * r.pp[pl.ds(HALO - 1, ROWS), cols]
            + r.conv_w[2:3, cols] * r.pp[pl.ds(HALO, ROWS), cols]
            + r.conv_b[:, cols]
        )
    gated = (r.inner[...] * r.value[...]).astype(bf16).astype(f32)
    r.gf[...] = gated

    def trade(which, dst):
        @pl.loop(1, 8)
        def _(k):
            peer = lax.rem(s + k, 8)
            remote(
                r.stage.at[which, at(peer, 96)],
                dst.at[at(s, 96)],
                r.a2a_s.at[which, k - 1],
                r.a2a_r.at[which, k - 1],
                (peer, g),
            ).start()

        dst[at(s, 96)] = r.stage[which, at(s, 96)]

    def arrive(which, dst):
        @pl.loop(1, 8)
        def _(k):
            peer = lax.rem(s + 8 - k, 8)
            remote(
                r.stage.at[which, at(peer, 96)],
                dst.at[at(peer, 96)],
                r.a2a_s.at[which, k - 1],
                r.a2a_r.at[which, k - 1],
                (peer, g),
            ).wait_recv()

    r.stage[0] = jnp.transpose(gated).astype(bf16)
    trade(0, r.gat)

    bias_cols = jnp.transpose(r.filt_bias[...])
    freq_cols = jnp.transpose(r.filt_freq[...])
    below = r.feats[...]
    for i, (u_ref, a_ref, c_ref) in enumerate(
        ((r.u1, r.a1, r.c1), (r.u2, r.a2, r.c2), (r.u3, r.a3, r.c3))
    ):
        weights = r.filt_first[...] if i == 0 else r.filt_hidden[i - 1]
        u = tn_high(weights, below) + bias_cols[:, i : i + 1]
        u_ref[...] = u
        below, cosine = sin_cos(freq_cols[:, i : i + 1] * u)
        a_ref[...] = below
        c_ref[...] = cosine

    r.last_t[...] = jnp.transpose(r.filt_last[...])
    r.rate_t[...] = jnp.transpose(jnp.broadcast_to(r.decay1[...].reshape(1, 768), (8, 768)))
    last = r.last_t[at(s, 96)]
    rate = r.rate_t[at(s, 96), 0:1]
    place = lax.broadcasted_iota(jnp.int32, (1, 1024), 1).astype(f32)
    r.wind[...] = jnp.exp(-rate * place)
    r.taps[...] = nn_high(last, r.a3[...]) * r.wind[...]
    r.hw_high[pl.ds(0, 96), own] = jnp.zeros((96, 128), bf16)
    r.hw_low[pl.ds(0, 96), own] = jnp.zeros((96, 128), bf16)
    for b in range(8):
        high, low = two(r.taps[:, 128 * b : 128 * b + 128])
        for half, ref in ((high, r.hw_high), (low, r.hw_low)):
            ref[96 * b : 96 * b + 96, 128:256] = half
            if b < 7:
                ref[96 * b + 96 : 96 * b + 192, 0:128] = half

    def by_table(v, which, rows, cols):
        high, low = two(v)
        table = r.tables[which, rows, cols]
        return nn(high, table) + nn(low, table) + nn(high, r.tables[which + 1, rows, cols])

    every = pl.ds(0, 256)
    low_half, high_half = pl.ds(0, 128), pl.ds(128, 128)
    loads[3].wait()
    r.es[...] = (
        nn(r.hw_high[...], r.tables[2])
        + nn(r.hw_low[...], r.tables[2])
        + nn(r.hw_high[...], r.tables[3])
    )
    loads[2].wait()
    for copy in shares[0:3]:
        copy.start()
    shares[6].start()

    arrive(0, r.gat)
    r.xs[...] = nn(r.gat[...], r.tables[2, low_half]) + nn(r.gat[...], r.tables[3, low_half])

    def pick(ref, tile, b):
        rows = pl.ds(pl.multiple_of(96 * b + 8 * tile, 8), 8)
        return ref[rows, low_half], ref[rows, high_half]

    def keep(ref, tile, b, pair_of):
        rows = pl.ds(pl.multiple_of(96 * b + 8 * tile, 8), 8)
        ref[rows, low_half] = pair_of[0]
        ref[rows, high_half] = pair_of[1]

    @pl.loop(0, 12)
    def _(tile):
        e = [pick(r.es, tile, b) for b in range(8)]
        v = [pick(r.xs, tile, b) for b in range(8)]
        for b in range(8):
            re, im = 0.0, 0.0
            for lag in range(b + 1):
                er, ei = e[lag]
                vr, vi = v[b - lag]
                re = re + er * vr - ei * vi
                im = im + er * vi + ei * vr
            keep(r.ys, tile, b, (re, im))

    conv = by_table(r.ys[...], 0, every, high_half) * (1.0 / 128.0)
    r.stage[1] = conv.astype(bf16)
    trade(1, r.co_in)

    loads[4].wait()
    for t in range(4):
        cols = pl.ds(768 * t, 768)
        r.g_act[:, cols] = nt(r.rh_down[own], r.down_w[cols])

    arrive(1, r.co_in)
    sum_f = jnp.transpose(r.co_in[...].astype(f32)) + r.skip[...] * r.gf[...]
    r.summed[...] = sum_f
    mixed = (r.outer[...] * sum_f).astype(bf16)
    loads[5].wait()
    res = r.tok[pl.ds(HALO, ROWS)].astype(f32) + nn(mixed, r.out_w[...]) + r.out_b[...]
    r.resid[...] = res
    hat, inv = norm_rows(res)
    r.hat2[...] = hat
    r.std2[...] = inv
    n2 = (hat * r.norm_gain[1:2] + r.norm_bias[1:2]).astype(bf16)
    loads[6].wait()
    for t in range(4):
        cols = pl.ds(768 * t, 768)
        act_f, slope = gelu_both(nn(n2, r.up_w[:, cols]) + r.up_b[:, cols])
        act_b = act_f.astype(bf16)
        r.act[:, cols] = act_b
        r.rh_up[own, cols] = (r.g_act[:, cols] * slope).astype(bf16)
        turned = jnp.transpose(act_b.astype(f32)).astype(bf16)
        for ix in range(2):
            for iy in range(2):
                for core in range(2):
                    i1, i2 = (ix, iy) if core == 0 else (iy, ix)
                    src = 96 * (ix * 4 + iy * 2 + core)
                    r.at_down[core, pl.ds(i1 * 768 + i2 * 384 + t * 96, 96)] = turned[src : src + 96]
    for copy in shares[3:6]:
        copy.start()
    shares[9].start()
    order_rows(n2.astype(f32), r.at_up, r.at_upz)
    shares[12].start()
    shares[8].start()
    r.lh_up[:, own] = r.at_up[c]
    r.lh_upz[:, own] = r.at_upz[c]
    order_rows(mixed.astype(f32), r.at_out)
    shares[7].start()
    r.lh_out[:, own] = r.at_out[c]
    r.lh_down[:, own] = r.at_down[c, at(b1, 768)]

    def one_a(p):
        return remote(r.s1a.at[p], r.r1a.at[p], r.p1_s.at[p], r.p1_r.at[p], first)

    def two_a(p):
        return remote(r.s2a.at[p], r.r2a.at[p], r.p2_s.at[p], r.p2_r.at[p], second)

    def three_a(p):
        return remote(
            r.s3a.at[p, at(1 - z1, 2)], r.r3a.at[p], r.p3_s.at[p], r.p3_r.at[p], near
        )

    def four_a(p):
        return remote(r.s4a.at[p], r.r4a.at[p], r.p4_s.at[p], r.p4_r.at[p], far)

    def two_b(p):
        return remote(r.s2b.at[p], r.r2b.at[p], r.p2_s.at[8 + p], r.p2_r.at[8 + p], second)

    def three_b(p):
        return remote(
            r.s3b.at[p, at(1 - z1, 2)], r.r3b.at[p], r.p3_s.at[8 + p], r.p3_r.at[8 + p], near
        )

    def four_b(p):
        return remote(r.s4b.at[p], r.r4b.at[p], r.p4_s.at[8 + p], r.p4_r.at[8 + p], far)

    def make_a(p0, count, lh, rh, c0=0):
        @pl.loop(0, count)
        def _(p):
            r.s1a[p0 + p] = nn(lh[at(1 - b1, 192)], rh[:, at(c0 + p, 768)]).astype(bf16)

    def stay_a(p0, count, lh, rh, c0=0):
        @pl.loop(0, count)
        def _(p):
            r.k1a[p0 + p] = nn(lh[at(b1, 192)], rh[:, at(c0 + p, 768)])

    def ph1_a(p):
        one_a(p).wait_recv()
        rows = at(1 - b2, 96)
        r.s2a[p] = (r.k1a[p, rows] + r.r1a[p, rows].astype(f32)).astype(bf16)
        two_a(p).start()

    def ph2_a(p):
        two_a(p).wait_recv()
        rows = at(b2, 96)
        v = r.k1a[p, rows] + r.r1a[p, rows].astype(f32) + r.r2a[p].astype(f32)
        for iz in range(4):
            block = v[24 * iz : 24 * iz + 24]
            r.s3a[p, 2 * (iz % 2) + iz // 2] = jnp.concatenate(
                [block[:, :384], block[:, 384:]], axis=0
            ).astype(bf16)
        three_a(p).start()

    def ph3_a(p):
        three_a(p).wait_recv()
        r.s4a[p] = (
            r.s3a[p, 2 * z1 + 1 - z2].astype(f32) + r.r3a[p, 1 - z2].astype(f32)
        ).astype(bf16)
        four_a(p).start()

    def ph4_a(p, dest, base, per_row):
        four_a(p).wait_recv()
        v = r.s3a[p, 2 * z1 + z2].astype(f32) + r.r3a[p, z2].astype(f32) + r.r4a[p].astype(f32)
        for h in range(2):
            for j in range(3):
                dest[pl.ds(base + 3 * h + j, 24, stride=per_row)] = v[
                    24 * h : 24 * h + 24, 128 * j : 128 * j + 128
                ]

    def ph2_b(p):
        two_b(p).wait_recv()
        v = r.k2b[p] + r.r2b[p].astype(f32)
        for iz in range(4):
            r.s3b[p, 2 * (iz % 2) + iz // 2] = v[96 * iz : 96 * iz + 96].astype(bf16)
        three_b(p).start()

    def ph3_b(p):
        three_b(p).wait_recv()
        r.s4b[p] = (
            r.s3b[p, 2 * z1 + 1 - z2].astype(f32) + r.r3b[p, 1 - z2].astype(f32)
        ).astype(bf16)
        four_b(p).start()

    def ph4_b(p):
        four_b(p).wait_recv()
        v = r.s3b[p, 2 * z1 + z2].astype(f32) + r.r3b[p, z2].astype(f32) + r.r4b[p].astype(f32)
        for j in range(2):
            r.f_gdown[pl.ds(2 * p + j, 96, stride=6)] = v[:, 128 * j : 128 * j + 128]

    hops = [
        remote(src, dst, r.zf_s.at[i], r.zf_r.at[i], where)
        for i, (src, dst, where) in enumerate(
            ((r.s1z, r.r1z, near), (r.s2z, r.r2z, far), (r.s3z, r.r3z, first), (r.s4z, r.r4z, second))
        )
    ]

    def zf1():
        r.s1z[...] = nn(r.lh_upz[at(1 - z1, 192)], r.rh_up[:, 0:768]).astype(bf16)
        hops[0].start()

    def zf2():
        hops[0].wait_recv()
        rows = at(1 - z2, 96)
        r.s2z[...] = (r.k1z[rows] + r.r1z[rows].astype(f32)).astype(bf16)
        hops[1].start()

    def zf3():
        hops[1].wait_recv()
        for ref, half in ((r.s3z, 1 - b1), (r.k3z, b1)):
            rows = pl.ds(pl.multiple_of(96 * z2 + 48 * half, 48), 48)
            v = r.k1z[rows] + r.r1z[rows].astype(f32) + r.r2z[at(half, 48)].astype(f32)
            ref[...] = v.astype(ref.dtype)
        hops[2].start()

    def zf4():
        hops[2].wait_recv()
        v = r.k3z[...] + r.r3z[...].astype(f32)
        lower, upper = v[:24], v[24:]
        sent = jnp.where(b2 == 0, upper, lower)
        r.k4z[...] = jnp.where(b2 == 0, lower, upper)
        r.s4z[...] = jnp.concatenate([sent[:, :384], sent[:, 384:]], axis=0).astype(bf16)
        hops[3].start()

    def zf5():
        hops[3].wait_recv()
        got = r.r4z[...].astype(f32)
        for h in range(2):
            for j in range(3):
                k = 3 * h + j
                r.f_gup[pl.ds(k, 24, stride=24)] = (
                    r.k4z[:, 128 * k : 128 * k + 128]
                    + got[24 * h : 24 * h + 24, 128 * j : 128 * j + 128]
                )

    def put(row, v):
        for j in range(v.shape[1] // 128):
            part, line = divmod(row + j, 64)
            r.smf[part, line : line + 1] = v[:, 128 * j : 128 * j + 128]

    e = nt(r.rh_up[own], r.up_w[...])
    hat = r.hat2[...]
    grad_f = r.rh_down[own].astype(f32)
    g_res = grad_f + norm_rows_back(e, hat, r.std2[...], r.norm_gain[1:2])
    r.g_resid[...] = g_res
    g_res_b = g_res.astype(bf16)
    r.rh_out[own] = g_res_b
    shares[10].start()
    g_mixed = nt(g_res_b, r.out_w[...])
    r.g_outer[...] = g_mixed * r.summed[...]
    g_summed = g_mixed * r.outer[...]
    r.g_sum[...] = g_summed
    r.stage[2] = jnp.transpose(g_summed).astype(bf16)
    trade(2, r.gc_in)

    shares[12].wait_recv()
    shares[9].wait_recv()
    zf1()
    shares[8].wait_recv()
    make_a(0, 3, r.lh_up, r.rh_up, 1)
    one_a(0).start()
    for copy in shares[0:6]:
        copy.wait_recv()
    for p in range(3):
        cols = pl.ds(256 * p, 256)
        r.s2b[p] = nn(r.lh_down[at(1 - b2, 384)], r.rh_down[:, cols]).astype(bf16)
        if p == 0:
            two_b(p).start()
    for p in range(3):
        r.k2b[p] = nn(r.lh_down[at(b2, 384)], r.rh_down[:, 256 * p : 256 * p + 256])
    shares[7].wait_recv()
    shares[10].wait_recv()
    make_a(3, 1, r.lh_out, r.rh_out)
    r.k1z[...] = nn(r.lh_upz[at(z1, 192)], r.rh_up[:, 0:768])
    put(AT_GAIN + 6, col_sum(e * hat))
    put(AT_SHIFT + 6, col_sum(e))
    put(AT_DOWNB, col_sum(grad_f))
    put(AT_UPB, col_sum(r.rh_up[own].astype(f32)))
    put(AT_OUTB, col_sum(g_res_b.astype(f32)))
    put(AT_SKIP, col_sum(g_summed * r.gf[...]))

    arrive(2, r.gc_in)
    r.ys[...] = (
        nn(r.gc_in[...], r.tables[2, high_half]) + nn(r.gc_in[...], r.tables[3, high_half])
    ) * (1.0 / 128.0)

    @pl.loop(0, 12)
    def _(tile):
        e = [pick(r.es, tile, b) for b in range(8)]
        d = [pick(r.ys, tile, b) for b in range(8)]
        for b in range(8):
            re, im = 0.0, 0.0
            for lag in range(8 - b):
                er, ei = e[lag]
                dr, di = d[b + lag]
                re = re + er * dr + ei * di
                im = im + er * di - ei * dr
            keep(r.es, tile, b, (re, im))

    g_long = by_table(r.es[...], 0, every, low_half)
    r.stage[3] = g_long.astype(bf16)
    trade(3, r.gl_in)

    one_a(1).start()
    two_b(1).start()
    zf2()
    stay_a(0, 3, r.lh_up, r.rh_up, 1)
    stay_a(3, 1, r.lh_out, r.rh_out)
    ph2_b(0)
    ph1_a(0)
    r.resid[...] = r.resid[...] + nn(r.act[...], r.down_w[...]) + r.down_b[...]
    store_out = pltpu.make_async_copy(r.resid, r.o_out, r.st.at[0])
    store_out.start()

    arrive(3, r.gl_in)
    g_gated = r.skip[...] * r.g_sum[...] + jnp.transpose(r.gl_in[...].astype(f32))
    mixes = (r.g_outer[...], g_gated * r.value[...], g_gated * r.inner[...])
    for part in range(3):
        r.gm[own, 768 * part : 768 * part + 768] = mixes[part]
    first_rows = remote(
        r.gm.at[pl.ds(0, 2)], r.gm.at[pl.ds(ROWS, 2)], r.halo_s.at[1], r.halo_r.at[1], (s - 1, g)
    )

    @pl.when(s > 0)
    def _():
        first_rows.start()

    one_a(2).start()
    two_b(2).start()
    for part in range(3):
        cols = pl.ds(768 * part, 768)
        mix = r.gm[own, cols]
        put(AT_CONVB + 6 * part, col_sum(mix))
        for tap in range(3):
            put(
                AT_CONVW + 18 * tap + 6 * part,
                col_sum(mix * r.pp[pl.ds(HALO - 2 + tap, ROWS), cols]),
            )

    @pl.when(s < 7)
    def _():
        first_rows.wait_recv()

    @pl.when(s == 7)
    def _():
        r.gm[pl.ds(ROWS, 8)] = jnp.zeros((8, r.gm.shape[1]), f32)

    for part in range(3):
        cols = pl.ds(768 * part, 768)
        r.rh_in[own, cols] = (
            r.conv_w[0:1, cols] * r.gm[pl.ds(2, ROWS), cols]
            + r.conv_w[1:2, cols] * r.gm[pl.ds(1, ROWS), cols]
            + r.conv_w[2:3, cols] * r.gm[pl.ds(0, ROWS), cols]
        ).astype(bf16)
    shares[11].start()
    e = nt(r.rh_in[own], r.in_w[...])
    shares[6].wait_recv()
    shares[11].wait_recv()
    make_a(4, 3, r.lh_in, r.rh_in)
    for p in (4, 5, 6):
        one_a(p).start()
    zf3()
    ph1_a(1)
    ph2_b(1)
    ph3_b(0)
    stay_a(4, 3, r.lh_in, r.rh_in)
    ph1_a(2)
    ph2_b(2)
    hat = r.hat1[...]
    put(AT_IN, col_sum(r.rh_in[own].astype(f32)))
    put(AT_GAIN, col_sum(e * hat))
    put(AT_SHIFT, col_sum(e))
    r.g_resid[...] = r.g_resid[...] + norm_rows_back(e, hat, r.std1[...], r.norm_gain[0:1])
    store_tok = pltpu.make_async_copy(r.g_resid, r.o_gtok, r.st.at[1])
    store_tok.start()
    ph2_a(0)
    ph3_b(1)

    @pl.loop(0, 12)
    def _(tile):
        v = [pick(r.xs, tile, b) for b in range(8)]
        d = [pick(r.ys, tile, b) for b in range(8)]
        for lag in range(8):
            re, im = 0.0, 0.0
            for b in range(8 - lag):
                vr, vi = v[b]
                dr, di = d[b + lag]
                re = re + vr * dr + vi * di
                im = im + vr * di - vi * dr
            keep(r.xs, tile, lag, (re, im))

    r.es[...] = by_table(r.xs[...], 0, every, every)
    ph1_a(4)
    ph2_a(1)
    ph3_a(0)
    ph3_b(2)
    for b in range(8):
        cols = pl.ds(128 * b, 128)
        gt = r.es[96 * b : 96 * b + 96, 128:256]
        if b < 7:
            gt = gt + r.es[96 * b + 96 : 96 * b + 192, 0:128]
        r.dpre[:, cols] = gt * r.wind[:, cols]
        r.taps[:, cols] = r.taps[:, cols] * gt
    g_rate = -jnp.sum(r.taps[...] * place, axis=1, keepdims=True)
    g_last = nt_high(r.dpre[...], r.a3[...])
    for j in range(4):
        r.smf[j, 64:88, 0:64] = g_last[24 * j : 24 * j + 24]
        r.smf[j, 64:88, 64:65] = g_rate[24 * j : 24 * j + 24]
    ones = jnp.ones((8, 1024), f32)
    g_a = tn_high(last, r.dpre[...])
    for i, (u_ref, c_ref, a_ref) in enumerate(
        ((r.u3, r.c3, r.a2), (r.u2, r.c2, r.a1), (r.u1, r.c1, None))
    ):
        layer = 2 - i
        g_arg = g_a * c_ref[...]
        g_freq = nt_high(ones, g_arg * u_ref[...])[0:1]
        g_u = g_arg * freq_cols[:, layer : layer + 1]
        g_bias = nt_high(ones, g_u)[0:1]
        r.smf[1, layer : layer + 1, 64:128] = g_bias
        r.smf[1, 3 + layer : 4 + layer, 64:128] = g_freq
        if layer > 0:
            r.smf[0, 0:64, 64 * (layer - 1) : 64 * layer] = nt_high(a_ref[...], g_u)
            g_a = nn_high(r.filt_hidden[layer - 1], g_u)
        else:
            r.smf[1, 0:33, 0:64] = nt_high(r.feats[...], g_u)

    def quarter(k):
        t = lax.rem(g + k, 4)
        return remote(r.smf.at[t], r.q_in.at[k - 1], r.q_s.at[k - 1], r.q_r.at[k - 1], (s, t))

    def eighth(k):
        t = lax.rem(s + k, 8)
        return remote(
            r.q_sum.at[at(t, 8)], r.o_in.at[k - 1], r.o_s.at[k - 1], r.o_r.at[k - 1], (t, g)
        )

    def spread(k, back):
        t = lax.rem(s + k, 8)
        mine = lax.rem(s + 8 - k, 8) if back else s
        slot = r.ag.at[g, mine]
        return remote(slot, slot, r.ag_s.at[k - 1], r.ag_r.at[k - 1], (t, g))

    over_y = g + y_step
    first_slot, second_slot = r.ag.at[g], r.ag.at[over_y]
    y_send = remote(first_slot, first_slot, r.ag_s.at[7], r.ag_r.at[7], (s, over_y))
    y_back = remote(second_slot, second_slot, r.ag_s.at[7], r.ag_r.at[7], (s, over_y))
    c_send = [
        remote(slot, slot, r.ag_s.at[8 + i], r.ag_r.at[8 + i], (s, other))
        for i, slot in enumerate((first_slot, second_slot))
    ]
    third_slot, fourth_slot = r.ag.at[other], r.ag.at[other + y_step]
    c_back = [
        remote(slot, slot, r.ag_s.at[8 + i], r.ag_r.at[8 + i], (s, other))
        for i, slot in enumerate((third_slot, fourth_slot))
    ]

    for k in range(1, 4):
        quarter(k).start()

    one_a(3).start()
    zf4()
    ph1_a(5)
    ph2_a(2)
    ph3_a(1)
    for k in range(1, 4):
        quarter(k).wait_recv()
    r.q_sum[...] = r.smf[g] + r.q_in[0] + r.q_in[1] + r.q_in[2]

    @pl.loop(1, 8)
    def _(k):
        eighth(k).start()

    ph2_a(4)
    ph1_a(6)
    ph3_a(2)

    @pl.loop(1, 8)
    def _(k):
        eighth(k).wait_recv()

    r.ag[g, s, pl.ds(0, 8)] = r.q_sum[at(s, 8)] + jnp.sum(r.o_in[...], axis=0)
    r.ag[g, s, pl.ds(8, 24)] = r.q_sum[pl.ds(64, 24)]

    @pl.loop(1, 8)
    def _(k):
        spread(k, False).start()

    ph2_a(5)
    ph3_a(4)
    ph1_a(3)
    ph2_a(6)
    ph3_a(5)
    for p in range(3):
        ph4_b(p)

    @pl.loop(1, 8)
    def _(k):
        spread(k, True).wait_recv()

    y_send.start()
    ph2_a(3)
    ph3_a(6)
    zf5()

    @pl.loop(0, 3)
    def _(p):
        ph4_a(p, r.f_gup, 6 * p + 6, 24)

    @pl.loop(0, 3)
    def _(p):
        ph4_a(4 + p, r.f_gin, 6 * p, 18)

    ph3_a(3)
    y_back.wait_recv()
    for copy in c_send:
        copy.start()

    stores = [
        store_out,
        store_tok,
        pltpu.make_async_copy(r.f_gdown, r.o_gdown, r.st.at[2]),
        pltpu.make_async_copy(r.f_gup, r.o_gup, r.st.at[3]),
        pltpu.make_async_copy(r.f_gout, r.o_gout, r.st.at[4]),
        pltpu.make_async_copy(r.f_gin, r.o_gin, r.st.at[5]),
        pltpu.make_async_copy(r.ag, r.o_small, r.st.at[6]),
    ]
    stores[2].start()
    stores[3].start()
    stores[5].start()
    for copy in c_back:
        copy.wait_recv()
    stores[6].start()
    ph4_a(3, r.f_gout, 0, 6)
    stores[4].start()

    @pl.when(s < 7)
    def _():
        last_rows.wait_send()

    @pl.when(s > 0)
    def _():
        first_rows.wait_send()

    for copy in shares:
        copy.wait_send()

    @pl.loop(0, 4)
    def _(which):
        @pl.loop(1, 8)
        def _(k):
            remote(
                r.stage.at[which, pl.ds(0, 96)],
                r.gat.at[pl.ds(0, 96)],
                r.a2a_s.at[which, k - 1],
                r.a2a_r.at[which, k - 1],
                (s, other),
            ).wait_send()

    for copy in hops:
        copy.wait_send()

    @pl.loop(0, 7)
    def _(p):
        one_a(p).wait_send()
        two_a(p).wait_send()
        three_a(p).wait_send()
        four_a(p).wait_send()

    @pl.loop(0, 3)
    def _(p):
        two_b(p).wait_send()
        three_b(p).wait_send()
        four_b(p).wait_send()

    for k in range(1, 4):
        quarter(k).wait_send()

    @pl.loop(1, 8)
    def _(k):
        eighth(k).wait_send()
        spread(k, False).wait_send()

    y_send.wait_send()
    for copy in c_send:
        copy.wait_send()
    for copy in stores:
        copy.wait()


def finish_kernel(
    i_out, i_gtok, i_gin, i_gout, i_gup, i_gdown, i_small,
    out, gtok, gain, shift, gin, in_b, conv_w, conv_b, first, hidden, bias, freq,
    last, decay, skip, gout, out_b, gup, up_b, gdown, down_b,
    h_out, h_gtok, h_gin, h_gout, h_gup, h_gdown, small, sem_in, sem_out,
):
    bulk = (
        (i_small, small, None),
        (i_out, h_out, out.at[0]),
        (i_gtok, h_gtok, gtok.at[0]),
        (i_gin, h_gin, gin),
        (i_gout, h_gout, gout),
        (i_gup, h_gup, gup),
        (i_gdown, h_gdown, gdown),
    )
    enter = [pltpu.make_async_copy(a, b, sem_in.at[i]) for i, (a, b, _) in enumerate(bulk)]
    leave = [
        pltpu.make_async_copy(b, d, sem_out.at[i]) for i, (_, b, d) in enumerate(bulk) if i > 0
    ]
    for copy in enter:
        copy.start()
    for i in range(6):
        enter[i + 1].wait()
        leave[i].start()
    enter[0].wait()
    rows = jnp.concatenate([small[i, j, 0:8, :] for i in range(4) for j in range(8)], axis=0)

    def fetch(at_row, dest, dest_row, wide):
        for j in range(wide):
            dest[dest_row : dest_row + 1, 128 * j : 128 * j + 128] = rows[at_row + j : at_row + j + 1]

    def line(at_row, dest):
        dest[...] = rows[at_row : at_row + dest.shape[0] // 128].reshape(dest.shape[0])

    for i in range(2):
        fetch(AT_GAIN + 6 * i, gain, i, 6)
        fetch(AT_SHIFT + 6 * i, shift, i, 6)
        hidden[i] = rows[AT_HID : AT_HID + 64, 64 * i : 64 * i + 64]
    for i in range(3):
        fetch(AT_CONVW + 18 * i, conv_w, i, 18)
    line(AT_IN, in_b)
    line(AT_CONVB, conv_b)
    line(AT_SKIP, skip)
    line(AT_OUTB, out_b)
    line(AT_UPB, up_b)
    line(AT_DOWNB, down_b)
    first[...] = rows[AT_FIRST : AT_FIRST + 33, 0:64]
    bias[...] = rows[AT_FIRST : AT_FIRST + 3, 64:128]
    freq[...] = rows[AT_FIRST + 3 : AT_FIRST + 6, 64:128]
    channels = jnp.transpose(
        jnp.concatenate([small[j, i, 8:32, :] for i in range(8) for j in range(4)], axis=0)
    )
    last[...] = channels[0:64]
    decay[...] = channels[64:65].reshape(768)
    for copy in leave:
        copy.wait()


def one_kernel_body(tokens, out_grad, norm_gain, norm_bias, in_weight, in_bias, conv_weight, conv_bias,
                    filt_first, filt_hidden, filt_bias, filt_freq, filt_last, decay_rates, skip_scale,
                    out_weight, out_bias, up_weight, up_bias, down_weight, down_bias):
    width, hidden = up_weight.shape
    length = tokens.shape[1] * lax.axis_size("seq")
    any_spec = pl.BlockSpec(memory_space=pl.ANY)
    vmem_spec = pl.BlockSpec(memory_space=pltpu.VMEM)

    def vm(*shape, dtype=f32):
        return pltpu.VMEM(shape, dtype)

    def dma(*shape):
        return pltpu.SemaphoreType.DMA(shape)

    def shape(*dims):
        return jax.ShapeDtypeStruct(dims, f32)

    outs = pl.pallas_call(
        step_kernel,
        out_shape=[
            shape(128, width), shape(128, width), shape(432, 128), shape(144, 128),
            shape(576, 128), shape(576, 128), shape(4, 8, 32, 128),
        ],
        in_specs=[any_spec] * 23,
        out_specs=[any_spec] * 7,
        scratch_shapes=[vm(*dims) for _, dims in SMALL_ARGS]
        + [vm(*dims, dtype=dtype) for _, dims, dtype in SCRATCH]
        + [dma(*dims) for _, dims in SEMAPHORES],
        compiler_params=pltpu.CompilerParams(
            collective_id=0, has_side_effects=True, vmem_limit_bytes=62 * 1024 * 1024
        ),
        name="hyena_step",
    )(
        tokens, out_grad, in_weight, out_weight, up_weight, down_weight,
        jnp.asarray(fourier_tables()),
        norm_gain, norm_bias, in_bias, conv_weight, conv_bias,
        jnp.asarray(feature_table(length, (filt_first.shape[0] - 1) // 2)),
        filt_first, filt_hidden, filt_bias, filt_freq, filt_last, decay_rates, skip_scale, out_bias,
        up_bias, down_bias,
    )
    done = pl.pallas_call(
        finish_kernel,
        out_shape=[
            shape(1, 128, width), shape(1, 128, width), shape(2, width), shape(2, width), shape(432, 128),
            shape(3 * width), shape(3, 3 * width), shape(3 * width), shape(33, 64), shape(2, 64, 64),
            shape(3, 64), shape(3, 64), shape(64, width), shape(width), shape(width), shape(144, 128),
            shape(width), shape(576, 128), shape(hidden), shape(576, 128), shape(width),
        ],
        in_specs=[any_spec] * 7,
        out_specs=[any_spec, any_spec, vmem_spec, vmem_spec, any_spec]
        + [vmem_spec] * 10
        + [any_spec, vmem_spec, any_spec, vmem_spec, any_spec, vmem_spec],
        scratch_shapes=[
            vm(128, width), vm(128, width), vm(432, 128), vm(144, 128), vm(576, 128), vm(576, 128),
            vm(4, 8, 32, 128), dma(7), dma(7),
        ],
        compiler_params=pltpu.CompilerParams(vmem_limit_bytes=60 * 1024 * 1024),
        name="hyena_finish",
    )(*outs)
    flat = (4, 15, 17, 19)
    return tuple(v.reshape(-1) if i in flat else v for i, v in enumerate(done))


def solution(mesh):
    small_mesh = mesh.shape["seq"] == 8 and mesh.shape["grp"] == 4
    return jax.shard_map(
        one_kernel_body if small_mesh else body,
        mesh=mesh,
        in_specs=(P("grp", "seq", None), P("grp", "seq", None)) + (P(),) * 19,
        out_specs=(
            P("grp", "seq", None),
            P("grp", "seq", None),
            P(),
            P(),
            P(("seq", "grp")),
        )
        + (P(),) * 10
        + (P(("seq", "grp")), P(), P(("seq", "grp")), P(), P(("seq", "grp")), P()),
        check_vma=False,
    )
```

```python
import math
import types

import jax
import jax.numpy as jnp
import ml_dtypes
import numpy as np
from jax import lax
from jax.experimental import pallas as pl
from jax.experimental.pallas import tpu as pltpu
from jax.sharding import PartitionSpec as P

epsilon = 1e-05


def shifted(array, axis, by):
    peers = lax.axis_size(axis)
    pairs = [(i, i + by) for i in range(peers) if 0 <= i + by < peers]
    return lax.ppermute(array, axis, pairs)


def highest(left_mat, right_mat):
    return jnp.dot(
        left_mat, right_mat, precision=lax.Precision.HIGHEST, preferred_element_type=jnp.float32
    )


def highest_t(left_mat, right_mat):
    return lax.dot_general(
        left_mat,
        right_mat,
        (((0,), (0,)), ((), ())),
        precision=lax.Precision.HIGHEST,
        preferred_element_type=jnp.float32,
    )


def rows_t(left_mat, right_mat):
    return lax.dot_general(
        left_mat, right_mat, (((0,), (0,)), ((), ())), preferred_element_type=jnp.float32
    )


def back_mul(grad_in, weight_mat):
    return lax.dot_general(
        grad_in, weight_mat, (((1,), (1,)), ((), ())), preferred_element_type=jnp.float32
    )


def layer_norm(values, gain_row, shift_row):
    row_mean = jnp.mean(values, axis=-1, keepdims=True)
    centred = values - row_mean
    inv_std = lax.rsqrt(jnp.mean(centred * centred, axis=-1, keepdims=True) + epsilon)
    normed = centred * inv_std
    return (normed * gain_row + shift_row, normed, inv_std)


def norm_back(grad_in, normed, inv_std, gain_row):
    scaled = grad_in * gain_row
    centred_grad = (
        scaled
        - jnp.mean(scaled, axis=-1, keepdims=True)
        - normed * jnp.mean(scaled * normed, axis=-1, keepdims=True)
    )
    return (centred_grad * inv_std, jnp.sum(grad_in * normed, axis=0), jnp.sum(grad_in, axis=0))


def smooth(values):
    return jax.nn.gelu(values, approximate=False)


def filter_rows(params, positions, length):
    filt_first, filt_hidden, filt_bias, filt_freq, filt_last, decay_rates = params
    place = positions.astype(jnp.float32)
    bands = (filt_first.shape[0] - 1) // 2
    band = 0.0001 + jnp.arange(bands, dtype=jnp.float32) * ((bands - 1 - 0.0001) / (bands - 1))
    omega = place[:, None] * (2.0 * math.pi / length)
    phase = omega * band[None, :]
    feats = jnp.concatenate(
        [place[:, None] / (length - 1), jnp.cos(phase), -jnp.sin(phase)], axis=1
    )
    act_one = jnp.sin(filt_freq[0] * (highest(feats, filt_first) + filt_bias[0]))
    act_two = jnp.sin(filt_freq[1] * (highest(act_one, filt_hidden[0]) + filt_bias[1]))
    act_three = jnp.sin(filt_freq[2] * (highest(act_two, filt_hidden[1]) + filt_bias[2]))
    window = jnp.exp(-decay_rates[None, :] * jnp.maximum(place, 0.0)[:, None])
    return highest(act_three, filt_last) * window


def body(
    tokens,
    out_grad,
    norm_gain,
    norm_bias,
    in_weight,
    in_bias,
    conv_weight,
    conv_bias,
    filt_first,
    filt_hidden,
    filt_bias,
    filt_freq,
    filt_last,
    decay_rates,
    skip_scale,
    out_weight,
    out_bias,
    up_weight,
    up_bias,
    down_weight,
    down_bias,
):
    row_count = tokens.shape[1]
    model_width = tokens.shape[2]
    seq_count = lax.axis_size("seq")
    length = row_count * seq_count
    fft_span = 2 * row_count
    fparams = (filt_first, filt_hidden, filt_bias, filt_freq, filt_last, decay_rates)
    fft_grid = jnp.arange(fft_span, dtype=jnp.int32)
    angles = (fft_grid[:, None] * fft_grid[None, :] % fft_span).astype(jnp.float32) * (
        2.0 * math.pi / fft_span
    )
    cos_full = jnp.cos(angles)
    sin_full = jnp.sin(angles)
    cos_left = cos_full[:, :row_count]
    sin_left = sin_full[:, :row_count]
    cos_low = cos_full[row_count:, :]
    sin_low = sin_full[row_count:, :]

    def segment(params, lag_step):
        positions = (lag_step - 1) * row_count + fft_grid
        keep_mask = (positions >= 0).astype(jnp.float32)
        return filter_rows(params, positions, length) * keep_mask[:, None]

    def forward_add(lag_step, source, totals):
        filter_taps = segment(fparams, lag_step)
        g_re = highest(cos_full, filter_taps)
        g_im = -highest(sin_full, filter_taps)
        source_f = source.astype(jnp.float32)
        s_re = highest(cos_left, source_f)
        s_im = -highest(sin_left, source_f)
        return (totals[0] + g_re * s_re - g_im * s_im, totals[1] + g_re * s_im + g_im * s_re)

    inputs = tokens[0].astype(jnp.float32)
    normed1, hat_one, std_one = layer_norm(inputs, norm_gain[0], norm_bias[0])
    normed1_b = normed1.astype(jnp.bfloat16)
    projected = (
        jnp.dot(normed1_b, in_weight, preferred_element_type=jnp.float32) + in_bias
    ).astype(jnp.bfloat16)
    before = shifted(projected[row_count - 2 :], "seq", 1)
    padded = jnp.concatenate([before, projected], axis=0).astype(jnp.float32)
    mixed_conv = (
        conv_weight[0] * padded[:row_count]
        + conv_weight[1] * padded[1 : row_count + 1]
        + conv_weight[2] * padded[2:]
        + conv_bias
    )
    outer_part = mixed_conv[:, :model_width]
    inner_part = mixed_conv[:, model_width : 2 * model_width]
    value_part = mixed_conv[:, 2 * model_width :]
    gated_b = (inner_part * value_part).astype(jnp.bfloat16)
    gated_f = gated_b.astype(jnp.float32)
    zero_totals = (
        jnp.zeros((fft_span, model_width), jnp.float32),
        jnp.zeros((fft_span, model_width), jnp.float32),
    )
    first_pass = forward_add(0, gated_b, zero_totals)

    def forward_step(lag_step, loop_carry):
        source, tot_re, tot_im = loop_carry
        source = shifted(source, "seq", 1)
        tot_re, tot_im = forward_add(lag_step, source, (tot_re, tot_im))
        return (source, tot_re, tot_im)

    unused_src, tot_re, tot_im = lax.fori_loop(
        1, seq_count, forward_step, (gated_b, first_pass[0], first_pass[1])
    )
    conv_out = (highest(cos_low, tot_re) - highest(sin_low, tot_im)) / fft_span
    summed = conv_out + skip_scale * gated_f
    mixed_out_b = (outer_part * summed).astype(jnp.bfloat16)
    residual = (
        inputs + jnp.dot(mixed_out_b, out_weight, preferred_element_type=jnp.float32) + out_bias
    )
    normed2, hat_two, std_two = layer_norm(residual, norm_gain[1], norm_bias[1])
    normed2_b = normed2.astype(jnp.bfloat16)
    pre_act = jnp.dot(normed2_b, up_weight, preferred_element_type=jnp.float32) + up_bias
    act_val, gelu_back = jax.vjp(smooth, pre_act)
    act_b = act_val.astype(jnp.bfloat16)
    result = residual + jnp.dot(act_b, down_weight, preferred_element_type=jnp.float32) + down_bias
    grad_out_b = out_grad[0]
    grad_out_f = grad_out_b.astype(jnp.float32)
    g_down = rows_t(act_b, grad_out_b)
    g_down_bias = jnp.sum(grad_out_f, axis=0)
    g_act = back_mul(grad_out_b, down_weight)
    g_pre_b = gelu_back(g_act)[0].astype(jnp.bfloat16)
    g_up = rows_t(normed2_b, g_pre_b)
    g_up_bias = jnp.sum(g_pre_b.astype(jnp.float32), axis=0)
    g_norm_two = back_mul(g_pre_b, up_weight)
    g_res_norm, g_gain_two, g_shift_two = norm_back(g_norm_two, hat_two, std_two, norm_gain[1])
    g_resid = grad_out_f + g_res_norm
    g_resid_b = g_resid.astype(jnp.bfloat16)
    g_outw = rows_t(mixed_out_b, g_resid_b)
    g_out_bias = jnp.sum(g_resid_b.astype(jnp.float32), axis=0)
    g_mixed = back_mul(g_resid_b, out_weight)
    g_outer = g_mixed * summed
    g_summed = g_mixed * outer_part
    g_skip = jnp.sum(g_summed * gated_f, axis=0)
    g_conv_b = g_summed.astype(jnp.bfloat16)
    v_re = highest(cos_left, gated_f)
    v_im = -highest(sin_left, gated_f)

    def backward_add(lag_step, source, loop_carry):
        tot_re, tot_im, grad_acc = loop_carry
        source_f = source.astype(jnp.float32)
        d_re = highest_t(cos_low, source_f) / fft_span
        d_im = -highest_t(sin_low, source_f) / fft_span

        def lag_taps(params):
            return segment(params, lag_step)

        filter_taps, taps_pull = jax.vjp(lag_taps, fparams)
        g_re = highest(cos_full, filter_taps)
        g_im = -highest(sin_full, filter_taps)
        tot_re = tot_re + g_re * d_re + g_im * d_im
        tot_im = tot_im - g_im * d_re + g_re * d_im
        s_re = v_re * d_re + v_im * d_im
        s_im = v_re * d_im - v_im * d_re
        d_taps = highest_t(cos_full, s_re) - highest_t(sin_full, s_im)
        more_grads = taps_pull(d_taps)[0]
        grad_acc = jax.tree.map(jnp.add, grad_acc, more_grads)
        return (tot_re, tot_im, grad_acc)

    zero_grads = jax.tree.map(jnp.zeros_like, fparams)
    start_carry = (zero_totals[0], zero_totals[1], zero_grads)
    first_back = backward_add(0, g_conv_b, start_carry)

    def backward_step(lag_step, loop_carry):
        source, tot_re, tot_im, grad_acc = loop_carry
        source = shifted(source, "seq", -1)
        tot_re, tot_im, grad_acc = backward_add(lag_step, source, (tot_re, tot_im, grad_acc))
        return (source, tot_re, tot_im, grad_acc)

    unused_src, back_re, back_im, cycle_grads = lax.fori_loop(
        1, seq_count, backward_step, (g_conv_b,) + first_back
    )
    g_long = highest_t(cos_left, back_re) - highest_t(sin_left, back_im)
    g_gated = g_summed * skip_scale + g_long
    g_mix = jnp.concatenate([g_outer, g_gated * value_part, g_gated * inner_part], axis=1)
    g_conv_bias = jnp.sum(g_mix, axis=0)
    g_conv_w = jnp.stack(
        [
            jnp.sum(g_mix * padded[tap_index : tap_index + row_count], axis=0)
            for tap_index in range(3)
        ]
    )
    g_pad = (
        jnp.pad(conv_weight[0] * g_mix, ((0, 2), (0, 0)))
        + jnp.pad(conv_weight[1] * g_mix, ((1, 1), (0, 0)))
        + jnp.pad(conv_weight[2] * g_mix, ((2, 0), (0, 0)))
    )
    after_rows = shifted(g_pad[:2], "seq", -1)
    g_proj_b = (g_pad[2:] + jnp.pad(after_rows, ((row_count - 2, 0), (0, 0)))).astype(jnp.bfloat16)
    g_inw = rows_t(normed1_b, g_proj_b)
    g_in_bias = jnp.sum(g_proj_b.astype(jnp.float32), axis=0)
    g_norm_one = back_mul(g_proj_b, in_weight)
    g_in_norm, g_gain_one, g_shift_one = norm_back(g_norm_one, hat_one, std_one, norm_gain[0])
    g_tokens = g_resid + g_in_norm
    small_grads = lax.psum(
        (
            jnp.stack([g_gain_one, g_gain_two]),
            jnp.stack([g_shift_one, g_shift_two]),
            g_in_bias,
            g_conv_w,
            g_conv_bias,
            cycle_grads[0],
            cycle_grads[1],
            cycle_grads[2],
            cycle_grads[3],
            cycle_grads[4],
            cycle_grads[5],
            g_skip,
            g_out_bias,
            g_up_bias,
            g_down_bias,
        ),
        ("seq", "grp"),
    )
    large_grads = (
        lax.psum_scatter(g_inw.reshape(-1), ("seq", "grp"), scatter_dimension=0, tiled=True),
        lax.psum_scatter(g_outw.reshape(-1), ("seq", "grp"), scatter_dimension=0, tiled=True),
        lax.psum_scatter(g_up.reshape(-1), ("seq", "grp"), scatter_dimension=0, tiled=True),
        lax.psum_scatter(g_down.reshape(-1), ("seq", "grp"), scatter_dimension=0, tiled=True),
    )
    return (
        result[None],
        g_tokens[None],
        small_grads[0],
        small_grads[1],
        large_grads[0],
        small_grads[2],
        small_grads[3],
        small_grads[4],
        small_grads[5],
        small_grads[6],
        small_grads[7],
        small_grads[8],
        small_grads[9],
        small_grads[10],
        small_grads[11],
        large_grads[1],
        small_grads[12],
        large_grads[2],
        small_grads[13],
        large_grads[3],
        small_grads[14],
    )


f32 = jnp.float32
bf16 = jnp.bfloat16
MESH_ID = pl.DeviceIdType.MESH
HIGH = lax.Precision.HIGHEST
ROWS = 128
HALO = 16


def nn(a, b):
    return jnp.dot(a, b, preferred_element_type=f32)


def nt(a, b):
    return lax.dot_general(a, b, (((1,), (1,)), ((), ())), preferred_element_type=f32)


def nn_high(a, b):
    return jnp.dot(a, b, precision=HIGH, preferred_element_type=f32)


def nt_high(a, b):
    return lax.dot_general(
        a, b, (((1,), (1,)), ((), ())), precision=HIGH, preferred_element_type=f32
    )


def tn_high(a, b):
    return lax.dot_general(
        a, b, (((0,), (0,)), ((), ())), precision=HIGH, preferred_element_type=f32
    )


def two(v):
    high = v.astype(bf16)
    return high, (v - high.astype(f32)).astype(bf16)


def sin_cos(v):
    k = jnp.floor(v * (1.0 / math.pi) + 0.5)
    r = ((v - k * 3.140625) - k * 0.0009670257568359375) - k * 6.2771141529083252e-07
    sign = 1.0 - 2.0 * (k - 2.0 * jnp.floor(k * 0.5))
    q = r * r
    s = 1.0 / math.factorial(13)
    for order in (11, 9, 7, 5, 3):
        s = 1.0 / math.factorial(order) - s * q
    s = r - r * q * s
    c = 1.0 / math.factorial(12)
    for order in (10, 8, 6, 4, 2):
        c = 1.0 / math.factorial(order) - c * q
    c = 1.0 - q * c
    return s * sign, c * sign


def gelu_both(v):
    a = jnp.abs(v)
    t = 1.0 / (1.0 + (0.3275911 / math.sqrt(2.0)) * a)
    poly = t * (
        0.254829592
        + t * (-0.284496736 + t * (1.421413741 + t * (-1.453152027 + t * 1.061405429)))
    )
    bell = jnp.exp(-0.5 * v * v)
    tail = 0.5 * poly * bell
    phi = jnp.where(v >= 0, 1.0 - tail, tail)
    return v * phi, phi + v * bell * (1.0 / math.sqrt(2.0 * math.pi))


def col_sum(v):
    return jnp.sum(v, axis=0, keepdims=True)


def row_mean(v):
    return jnp.mean(v, axis=1, keepdims=True)


def norm_rows(v):
    centred = v - row_mean(v)
    inv = lax.rsqrt(row_mean(centred * centred) + epsilon)
    return centred * inv, inv


def norm_rows_back(e, hat, inv, gain):
    k = e * gain
    return (k - row_mean(k) - hat * row_mean(k * hat)) * inv


def fourier_tables():
    bins = np.arange(128) + 0.5
    angle = 2.0 * np.pi * bins[:, None] * np.arange(256)[None, :] / 256
    full = np.concatenate([np.cos(angle), -np.sin(angle)], axis=0).astype(np.float32)
    out = []
    for mat in (full, full.T):
        high = mat.astype(ml_dtypes.bfloat16)
        out += [high, (mat - high.astype(np.float32)).astype(ml_dtypes.bfloat16)]
    return np.stack(out)


def feature_table(length, bands):
    place = np.arange(length)
    band = 1e-4 + np.arange(bands) * ((bands - 1 - 1e-4) / (bands - 1))
    phase = band[:, None] * (2.0 * np.pi * place / length)[None, :]
    return np.concatenate(
        [(place / (length - 1))[None], np.cos(phase), -np.sin(phase)], axis=0
    ).astype(np.float32)


AT_HID, AT_FIRST, AT_GAIN, AT_SHIFT, AT_IN, AT_CONVW, AT_CONVB = 0, 64, 97, 109, 121, 139, 193
AT_SKIP, AT_OUTB, AT_UPB, AT_DOWNB = 211, 217, 223, 247

SMALL_ARGS = (
    ("norm_gain", (2, 768)), ("norm_bias", (2, 768)), ("in_b1", (2304,)), ("conv_w", (3, 2304)),
    ("conv_b1", (2304,)), ("feats", (33, 1024)), ("filt_first", (33, 64)), ("filt_hidden", (2, 64, 64)),
    ("filt_bias", (3, 64)), ("filt_freq", (3, 64)), ("filt_last", (64, 768)), ("decay1", (768,)),
    ("skip1", (768,)), ("out_b1", (768,)), ("up_b1", (3072,)), ("down_b1", (768,)),
)

SCRATCH = (
    ("in_w", (768, 2304), bf16), ("out_w", (768, 768), bf16), ("up_w", (768, 3072), bf16),
    ("down_w", (3072, 768), bf16), ("tables", (4, 256, 256), bf16),
    ("in_b", (1, 2304), f32), ("conv_b", (1, 2304), f32), ("skip", (1, 768), f32),
    ("out_b", (1, 768), f32), ("up_b", (1, 3072), f32), ("down_b", (1, 768), f32),
    ("tok", (144, 768), bf16), ("n1", (144, 768), bf16), ("hat1", (128, 768), f32),
    ("std1", (128, 1), f32), ("pp", (144, 2304), f32), ("outer", (128, 768), f32),
    ("inner", (128, 768), f32), ("value", (128, 768), f32), ("gf", (128, 768), f32),
    ("stage", (4, 768, 128), bf16), ("gat", (768, 128), bf16), ("co_in", (768, 128), bf16),
    ("gc_in", (768, 128), bf16), ("gl_in", (768, 128), bf16),
    ("xs", (768, 256), f32), ("es", (768, 256), f32), ("ys", (768, 256), f32),
    ("hw_high", (768, 256), bf16), ("hw_low", (768, 256), bf16),
    ("taps", (96, 1024), f32), ("wind", (96, 1024), f32), ("dpre", (96, 1024), f32),
    ("last_t", (768, 64), f32), ("rate_t", (768, 8), f32),
    ("a1", (64, 1024), f32), ("a2", (64, 1024), f32), ("a3", (64, 1024), f32),
    ("c1", (64, 1024), f32), ("c2", (64, 1024), f32), ("c3", (64, 1024), f32),
    ("u1", (64, 1024), f32), ("u2", (64, 1024), f32), ("u3", (64, 1024), f32),
    ("g_act", (128, 3072), f32), ("act", (128, 3072), bf16), ("summed", (128, 768), f32),
    ("hat2", (128, 768), f32), ("std2", (128, 1), f32),
    ("g_sum", (128, 768), f32), ("g_outer", (128, 768), f32),
    ("gm", (136, 2304), f32),
    ("at_down", (2, 1536, 128), bf16), ("at_up", (2, 384, 128), bf16), ("at_upz", (2, 384, 128), bf16), ("at_in", (2, 384, 128), bf16),
    ("at_out", (2, 384, 128), bf16), ("lh_down", (768, 512), bf16), ("lh_up", (384, 256), bf16), ("lh_upz", (384, 256), bf16),
    ("lh_in", (384, 256), bf16), ("lh_out", (384, 256), bf16), ("rh_down", (512, 768), bf16),
    ("rh_up", (256, 3072), bf16), ("rh_in", (256, 2304), bf16), ("rh_out", (256, 768), bf16),
    ("s1a", (7, 192, 768), bf16), ("k1a", (7, 192, 768), f32), ("r1a", (7, 192, 768), bf16),
    ("s2a", (7, 96, 768), bf16), ("r2a", (7, 96, 768), bf16), ("s3a", (7, 4, 48, 384), bf16),
    ("r3a", (7, 2, 48, 384), bf16), ("s4a", (7, 48, 384), bf16), ("r4a", (7, 48, 384), bf16),
    ("s2b", (3, 384, 256), bf16), ("k2b", (3, 384, 256), f32), ("r2b", (3, 384, 256), bf16),
    ("s3b", (3, 4, 96, 256), bf16), ("r3b", (3, 2, 96, 256), bf16), ("s4b", (3, 96, 256), bf16),
    ("r4b", (3, 96, 256), bf16),
    ("s1z", (192, 768), bf16), ("k1z", (192, 768), f32), ("r1z", (192, 768), bf16),
    ("s2z", (96, 768), bf16), ("r2z", (96, 768), bf16), ("k3z", (48, 768), f32),
    ("s3z", (48, 768), bf16), ("r3z", (48, 768), bf16), ("k4z", (24, 768), f32),
    ("s4z", (48, 384), bf16), ("r4z", (48, 384), bf16),
    ("smf", (4, 88, 128), f32), ("q_in", (3, 88, 128), f32), ("q_sum", (88, 128), f32),
    ("o_in", (7, 8, 128), f32), ("ag", (4, 8, 32, 128), f32),

)

SEMAPHORES = (
    ("ld", (8,)), ("ls", (16,)), ("a2a_s", (4, 7)), ("a2a_r", (4, 7)), ("halo_s", (2,)), ("halo_r", (2,)),
    ("pair_s", (13,)), ("pair_r", (13,)), ("p1_s", (8,)), ("p1_r", (8,)), ("p2_s", (11,)),
    ("p2_r", (11,)), ("p3_s", (11,)), ("p3_r", (11,)), ("p4_s", (11,)), ("p4_r", (11,)),
    ("zf_s", (4,)), ("zf_r", (4,)), ("q_s", (3,)), ("q_r", (3,)),
    ("o_s", (7,)), ("o_r", (7,)), ("ag_s", (10,)), ("ag_r", (10,)),
)


def step_kernel(*refs):
    names = ["tokens", "out_grad", "in_w_h", "out_w_h", "up_w_h", "down_w_h", "tables_h"]
    names += ["h_" + name for name, _ in SMALL_ARGS]
    names += ["o_out", "o_gtok", "o_gin", "o_gout", "o_gup", "o_gdown", "o_small"]
    names += [name for name, _ in SMALL_ARGS]
    names += [name for name, _, _ in SCRATCH] + [name for name, _ in SEMAPHORES]
    r = types.SimpleNamespace(**dict(zip(names, refs, strict=True)))

    s = lax.axis_index("seq")
    g = lax.axis_index("grp")
    z, x = lax.div(s, 2), lax.rem(s, 2)
    y, c = lax.div(g, 2), lax.rem(g, 2)
    other = g + 1 - 2 * c
    x_step, y_step = 1 - 2 * x, 2 * (1 - 2 * y)
    first = (s + (1 - c) * x_step, g + c * y_step)
    second = (s + c * x_step, g + (1 - c) * y_step)
    cross = (s + c * x_step, other + (1 - c) * y_step)
    b1 = (1 - c) * x + c * y
    b2 = (1 - c) * y + c * x
    z2, z1 = lax.div(z, 2), lax.rem(z, 2)
    near, far = (s + 2 - 4 * z1, g), (s + 4 - 8 * z2, g)

    def at(index, size):
        return pl.ds(pl.multiple_of(index * size, size), size)

    def remote(src, dst, ss, rs, where):
        return pltpu.make_async_remote_copy(
            src_ref=src,
            dst_ref=dst,
            send_sem=ss,
            recv_sem=rs,
            device_id=where,
            device_id_type=MESH_ID,
        )

    bar = pltpu.get_barrier_semaphore()

    @pl.loop(1, 8)
    def _(k):
        pl.semaphore_signal(
            bar, inc=1, device_id=(lax.rem(s + k, 8), g), device_id_type=MESH_ID
        )

    @pl.loop(1, 4)
    def _(k):
        pl.semaphore_signal(
            bar, inc=1, device_id=(s, lax.rem(g + k, 4)), device_id_type=MESH_ID
        )

    pl.semaphore_signal(bar, inc=1, device_id=(s + x_step, other), device_id_type=MESH_ID)

    own = pl.ds(0, ROWS)
    loads = [
        pltpu.make_async_copy(r.tokens.at[0], r.tok.at[pl.ds(HALO, ROWS)], r.ld.at[0]),
        pltpu.make_async_copy(r.in_w_h, r.in_w, r.ld.at[1]),
        pltpu.make_async_copy(r.out_grad.at[0], r.rh_down.at[own], r.ld.at[2]),
        pltpu.make_async_copy(r.tables_h, r.tables, r.ld.at[3]),
        pltpu.make_async_copy(r.down_w_h, r.down_w, r.ld.at[4]),
        pltpu.make_async_copy(r.out_w_h, r.out_w, r.ld.at[5]),
        pltpu.make_async_copy(r.up_w_h, r.up_w, r.ld.at[6]),
    ]
    small_loads = [
        pltpu.make_async_copy(getattr(r, "h_" + name), getattr(r, name), r.ls.at[i])
        for i, (name, _) in enumerate(SMALL_ARGS)
    ]
    loads[0].start()
    for copy in small_loads[:2]:
        copy.start()
    loads[1].start()
    for copy in small_loads[2:]:
        copy.start()
    loads[2].start()
    loads[3].start()

    def share(index, src, dst, where):
        return remote(src, dst, r.pair_s.at[index], r.pair_r.at[index], where)

    block2, block3, block4 = pl.ds(ROWS, ROWS), pl.ds(2 * ROWS, ROWS), pl.ds(3 * ROWS, ROWS)
    shares = [
        share(0, r.rh_down.at[own], r.rh_down.at[block2], (s, other)),
        share(1, r.rh_down.at[own], r.rh_down.at[block3], first),
        share(2, r.rh_down.at[own], r.rh_down.at[block4], cross),
        share(3, r.at_down.at[1 - c, at(b2, 768)], r.lh_down.at[:, block2], (s, other)),
        share(4, r.at_down.at[c, at(1 - b1, 768)], r.lh_down.at[:, block3], first),
        share(5, r.at_down.at[1 - c, at(1 - b2, 768)], r.lh_down.at[:, block4], cross),
        share(6, r.at_in.at[1 - c], r.lh_in.at[:, block2], (s, other)),
        share(7, r.at_out.at[1 - c], r.lh_out.at[:, block2], (s, other)),
        share(8, r.at_up.at[1 - c], r.lh_up.at[:, block2], (s, other)),
        share(9, r.rh_up.at[own], r.rh_up.at[block2], (s, other)),
        share(10, r.rh_out.at[own], r.rh_out.at[block2], (s, other)),
        share(11, r.rh_in.at[own], r.rh_in.at[block2], (s, other)),
        share(12, r.at_upz.at[1 - c], r.lh_upz.at[:, block2], (s, other)),
    ]

    def order_rows(v, halves, z_halves=None):
        t = jnp.transpose(v)
        bits = [(i, j) for i in range(2) for j in range(2)]
        for core in range(2):

            def block(i1, i2, iz):
                ix, iy = (i1, i2) if core == 0 else (i2, i1)
                at_row = 24 * (iz * 8 + ix * 4 + iy * 2 + core)
                return t[at_row : at_row + 24]

            blocks = [block(i1, i2, iz) for i1, i2 in bits for iz in range(4)]
            halves[core] = jnp.concatenate(blocks, axis=0).astype(bf16)
            if z_halves is not None:
                blocks = [block(i1, i2, 2 * j2 + j1) for j1, j2 in bits for i1, i2 in bits]
                z_halves[core] = jnp.concatenate(blocks, axis=0).astype(bf16)

    loads[0].wait()
    hat, inv = norm_rows(r.tok[pl.ds(HALO, ROWS)].astype(f32))
    r.hat1[...] = hat
    r.std1[...] = inv
    small_loads[0].wait()
    small_loads[1].wait()
    own_norm = (hat * r.norm_gain[0:1] + r.norm_bias[0:1]).astype(bf16)
    r.n1[pl.ds(HALO, ROWS)] = own_norm
    pl.semaphore_wait(bar, 11)
    last_rows = remote(
        r.tok.at[pl.ds(ROWS, HALO)],
        r.tok.at[pl.ds(0, HALO)],
        r.halo_s.at[0],
        r.halo_r.at[0],
        (s + 1, g),
    )

    @pl.when(s < 7)
    def _():
        last_rows.start()

    order_rows(own_norm.astype(f32), r.at_in)
    r.lh_in[:, own] = r.at_in[c]
    for copy in small_loads[2:]:
        copy.wait()
    for line, flat in (
        (r.in_b, r.in_b1), (r.conv_b, r.conv_b1), (r.skip, r.skip1),
        (r.out_b, r.out_b1), (r.up_b, r.up_b1), (r.down_b, r.down_b1),
    ):
        line[...] = flat[...].reshape(line.shape)

    @pl.when(s > 0)
    def _():
        last_rows.wait_recv()

    @pl.when(s == 0)
    def _():
        r.tok[pl.ds(0, HALO)] = jnp.zeros((HALO, r.tok.shape[1]), bf16)

    hat, inv = norm_rows(r.tok[pl.ds(0, HALO)].astype(f32))
    r.n1[pl.ds(0, HALO)] = (hat * r.norm_gain[0:1] + r.norm_bias[0:1]).astype(bf16)
    loads[1].wait()
    for copy in loads[4:]:
        copy.start()
    inside = jnp.where(s > 0, 1.0, 0.0).astype(f32)
    for part, dest in enumerate((r.outer, r.inner, r.value)):
        cols = pl.ds(768 * part, 768)
        proj = (nn(r.n1[...], r.in_w[:, cols]) + r.in_b[:, cols]).astype(bf16).astype(f32)
        r.pp[pl.ds(0, HALO), cols] = proj[:HALO] * inside
        r.pp[pl.ds(HALO, ROWS), cols] = proj[HALO:]
        dest[...] = (
            r.conv_w[0:1, cols] * r.pp[pl.ds(HALO - 2, ROWS), cols]
            + r.conv_w[1:2, cols] * r.pp[pl.ds(HALO - 1, ROWS), cols]
            + r.conv_w[2:3, cols] * r.pp[pl.ds(HALO, ROWS), cols]
            + r.conv_b[:, cols]
        )
    gated = (r.inner[...] * r.value[...]).astype(bf16).astype(f32)
    r.gf[...] = gated

    across, over_two, next_z = 3 - z, lax.rem(z + 2, 4), z + 1 - 2 * z1
    peers = [
        2 * to_z + to_x
        for to_z, to_x in (
            (across, 1 - x), (across, x), (over_two, 1 - x), (over_two, x),
            (next_z, 1 - x), (next_z, x), (z, 1 - x),
        )
    ]

    def swap(which, k, dst, slot):
        return remote(
            r.stage.at[which, at(peers[k], 96)],
            dst.at[at(slot, 96)],
            r.a2a_s.at[which, k],
            r.a2a_r.at[which, k],
            (peers[k], g),
        )

    def trade(which, dst):
        for k in range(7):
            swap(which, k, dst, s).start()
        dst[at(s, 96)] = r.stage[which, at(s, 96)]

    def arrive(which, dst):
        for k in range(7):
            swap(which, k, dst, peers[k]).wait_recv()

    r.stage[0] = jnp.transpose(gated).astype(bf16)
    trade(0, r.gat)

    bias_cols = jnp.transpose(r.filt_bias[...])
    freq_cols = jnp.transpose(r.filt_freq[...])
    below = r.feats[...]
    for i, (u_ref, a_ref, c_ref) in enumerate(
        ((r.u1, r.a1, r.c1), (r.u2, r.a2, r.c2), (r.u3, r.a3, r.c3))
    ):
        weights = r.filt_first[...] if i == 0 else r.filt_hidden[i - 1]
        u = tn_high(weights, below) + bias_cols[:, i : i + 1]
        u_ref[...] = u
        below, cosine = sin_cos(freq_cols[:, i : i + 1] * u)
        a_ref[...] = below
        c_ref[...] = cosine

    r.last_t[...] = jnp.transpose(r.filt_last[...])
    r.rate_t[...] = jnp.transpose(jnp.broadcast_to(r.decay1[...].reshape(1, 768), (8, 768)))
    last = r.last_t[at(s, 96)]
    rate = r.rate_t[at(s, 96), 0:1]
    place = lax.broadcasted_iota(jnp.int32, (1, 1024), 1).astype(f32)
    r.wind[...] = jnp.exp(-rate * place)
    r.taps[...] = nn_high(last, r.a3[...]) * r.wind[...]
    r.hw_high[pl.ds(0, 96), own] = jnp.zeros((96, 128), bf16)
    r.hw_low[pl.ds(0, 96), own] = jnp.zeros((96, 128), bf16)
    for b in range(8):
        high, low = two(r.taps[:, 128 * b : 128 * b + 128])
        for half, ref in ((high, r.hw_high), (low, r.hw_low)):
            ref[96 * b : 96 * b + 96, 128:256] = half
            if b < 7:
                ref[96 * b + 96 : 96 * b + 192, 0:128] = half

    def by_table(v, which, rows, cols):
        high, low = two(v)
        table = r.tables[which, rows, cols]
        return nn(high, table) + nn(low, table) + nn(high, r.tables[which + 1, rows, cols])

    every = pl.ds(0, 256)
    low_half, high_half = pl.ds(0, 128), pl.ds(128, 128)
    loads[3].wait()
    r.es[...] = (
        nn(r.hw_high[...], r.tables[2])
        + nn(r.hw_low[...], r.tables[2])
        + nn(r.hw_high[...], r.tables[3])
    )
    loads[2].wait()
    for copy in shares[0:3]:
        copy.start()
    shares[6].start()

    arrive(0, r.gat)
    r.xs[...] = nn(r.gat[...], r.tables[2, low_half]) + nn(r.gat[...], r.tables[3, low_half])

    def pick(ref, tile, b):
        rows = pl.ds(pl.multiple_of(96 * b + 8 * tile, 8), 8)
        return ref[rows, low_half], ref[rows, high_half]

    def keep(ref, tile, b, pair_of):
        rows = pl.ds(pl.multiple_of(96 * b + 8 * tile, 8), 8)
        ref[rows, low_half] = pair_of[0]
        ref[rows, high_half] = pair_of[1]

    @pl.loop(0, 12)
    def _(tile):
        e = [pick(r.es, tile, b) for b in range(8)]
        v = [pick(r.xs, tile, b) for b in range(8)]
        for b in range(8):
            re, im = 0.0, 0.0
            for lag in range(b + 1):
                er, ei = e[lag]
                vr, vi = v[b - lag]
                re = re + er * vr - ei * vi
                im = im + er * vi + ei * vr
            keep(r.ys, tile, b, (re, im))

    conv = by_table(r.ys[...], 0, every, high_half) * (1.0 / 128.0)
    r.stage[1] = conv.astype(bf16)
    trade(1, r.co_in)

    loads[4].wait()
    for t in range(4):
        cols = pl.ds(768 * t, 768)
        r.g_act[:, cols] = nt(r.rh_down[own], r.down_w[cols])

    arrive(1, r.co_in)
    sum_f = jnp.transpose(r.co_in[...].astype(f32)) + r.skip[...] * r.gf[...]
    r.summed[...] = sum_f
    mixed = (r.outer[...] * sum_f).astype(bf16)
    loads[5].wait()
    res = r.tok[pl.ds(HALO, ROWS)].astype(f32) + nn(mixed, r.out_w[...]) + r.out_b[...]
    r.o_out[...] = res
    hat, inv = norm_rows(res)
    r.hat2[...] = hat
    r.std2[...] = inv
    n2 = (hat * r.norm_gain[1:2] + r.norm_bias[1:2]).astype(bf16)
    loads[6].wait()
    for t in range(4):
        cols = pl.ds(768 * t, 768)
        act_f, slope = gelu_both(nn(n2, r.up_w[:, cols]) + r.up_b[:, cols])
        act_b = act_f.astype(bf16)
        r.act[:, cols] = act_b
        r.rh_up[own, cols] = (r.g_act[:, cols] * slope).astype(bf16)
        turned = jnp.transpose(act_b.astype(f32)).astype(bf16)
        for ix in range(2):
            for iy in range(2):
                for core in range(2):
                    i1, i2 = (ix, iy) if core == 0 else (iy, ix)
                    src = 96 * (ix * 4 + iy * 2 + core)
                    r.at_down[core, pl.ds(i1 * 768 + i2 * 384 + t * 96, 96)] = turned[src : src + 96]
    for copy in shares[3:6]:
        copy.start()
    shares[9].start()
    order_rows(n2.astype(f32), r.at_up, r.at_upz)
    shares[12].start()
    shares[8].start()
    r.lh_up[:, own] = r.at_up[c]
    r.lh_upz[:, own] = r.at_upz[c]
    order_rows(mixed.astype(f32), r.at_out)
    shares[7].start()
    r.lh_out[:, own] = r.at_out[c]
    r.lh_down[:, own] = r.at_down[c, at(b1, 768)]

    def one_a(p):
        return remote(r.s1a.at[p], r.r1a.at[p], r.p1_s.at[p], r.p1_r.at[p], first)

    def two_a(p):
        return remote(r.s2a.at[p], r.r2a.at[p], r.p2_s.at[p], r.p2_r.at[p], second)

    def three_a(p):
        return remote(
            r.s3a.at[p, at(1 - z1, 2)], r.r3a.at[p], r.p3_s.at[p], r.p3_r.at[p], near
        )

    def four_a(p):
        return remote(r.s4a.at[p], r.r4a.at[p], r.p4_s.at[p], r.p4_r.at[p], far)

    def two_b(p):
        return remote(r.s2b.at[p], r.r2b.at[p], r.p2_s.at[8 + p], r.p2_r.at[8 + p], second)

    def three_b(p):
        return remote(
            r.s3b.at[p, at(1 - z1, 2)], r.r3b.at[p], r.p3_s.at[8 + p], r.p3_r.at[8 + p], near
        )

    def four_b(p):
        return remote(r.s4b.at[p], r.r4b.at[p], r.p4_s.at[8 + p], r.p4_r.at[8 + p], far)

    def make_a(p0, count, lh, rh, c0=0):
        @pl.loop(0, count)
        def _(p):
            r.s1a[p0 + p] = nn(lh[at(1 - b1, 192)], rh[:, at(c0 + p, 768)]).astype(bf16)

    def stay_a(p0, count, lh, rh, c0=0):
        @pl.loop(0, count)
        def _(p):
            r.k1a[p0 + p] = nn(lh[at(b1, 192)], rh[:, at(c0 + p, 768)])

    def ph1_a(p):
        one_a(p).wait_recv()
        rows = at(1 - b2, 96)
        r.s2a[p] = (r.k1a[p, rows] + r.r1a[p, rows].astype(f32)).astype(bf16)
        two_a(p).start()

    def ph2_a(p):
        two_a(p).wait_recv()
        rows = at(b2, 96)
        v = r.k1a[p, rows] + r.r1a[p, rows].astype(f32) + r.r2a[p].astype(f32)
        for iz in range(4):
            block = v[24 * iz : 24 * iz + 24]
            r.s3a[p, 2 * (iz % 2) + iz // 2] = jnp.concatenate(
                [block[:, :384], block[:, 384:]], axis=0
            ).astype(bf16)
        three_a(p).start()

    def ph3_a(p):
        three_a(p).wait_recv()
        r.s4a[p] = (
            r.s3a[p, 2 * z1 + 1 - z2].astype(f32) + r.r3a[p, 1 - z2].astype(f32)
        ).astype(bf16)
        four_a(p).start()

    def ph4_a(p, dest, base, per_row):
        four_a(p).wait_recv()
        v = r.s3a[p, 2 * z1 + z2].astype(f32) + r.r3a[p, z2].astype(f32) + r.r4a[p].astype(f32)
        for h in range(2):
            for j in range(3):
                dest[pl.ds(base + 3 * h + j, 24, stride=per_row)] = v[
                    24 * h : 24 * h + 24, 128 * j : 128 * j + 128
                ]

    def ph2_b(p):
        two_b(p).wait_recv()
        v = r.k2b[p] + r.r2b[p].astype(f32)
        for iz in range(4):
            r.s3b[p, 2 * (iz % 2) + iz // 2] = v[96 * iz : 96 * iz + 96].astype(bf16)
        three_b(p).start()

    def ph3_b(p):
        three_b(p).wait_recv()
        r.s4b[p] = (
            r.s3b[p, 2 * z1 + 1 - z2].astype(f32) + r.r3b[p, 1 - z2].astype(f32)
        ).astype(bf16)
        four_b(p).start()

    def ph4_b(p):
        four_b(p).wait_recv()
        v = r.s3b[p, 2 * z1 + z2].astype(f32) + r.r3b[p, z2].astype(f32) + r.r4b[p].astype(f32)
        for j in range(2):
            r.o_gdown[pl.ds(2 * p + j, 96, stride=6)] = v[:, 128 * j : 128 * j + 128]

    hops = [
        remote(src, dst, r.zf_s.at[i], r.zf_r.at[i], where)
        for i, (src, dst, where) in enumerate(
            ((r.s1z, r.r1z, near), (r.s2z, r.r2z, far), (r.s3z, r.r3z, first), (r.s4z, r.r4z, second))
        )
    ]

    def zf1():
        r.s1z[...] = nn(r.lh_upz[at(1 - z1, 192)], r.rh_up[:, 0:768]).astype(bf16)
        hops[0].start()

    def zf2():
        hops[0].wait_recv()
        rows = at(1 - z2, 96)
        r.s2z[...] = (r.k1z[rows] + r.r1z[rows].astype(f32)).astype(bf16)
        hops[1].start()

    def zf3():
        hops[1].wait_recv()
        for ref, half in ((r.s3z, 1 - b1), (r.k3z, b1)):
            rows = pl.ds(pl.multiple_of(96 * z2 + 48 * half, 48), 48)
            v = r.k1z[rows] + r.r1z[rows].astype(f32) + r.r2z[at(half, 48)].astype(f32)
            ref[...] = v.astype(ref.dtype)
        hops[2].start()

    def zf4():
        hops[2].wait_recv()
        v = r.k3z[...] + r.r3z[...].astype(f32)
        lower, upper = v[:24], v[24:]
        sent = jnp.where(b2 == 0, upper, lower)
        r.k4z[...] = jnp.where(b2 == 0, lower, upper)
        r.s4z[...] = jnp.concatenate([sent[:, :384], sent[:, 384:]], axis=0).astype(bf16)
        hops[3].start()

    def zf5():
        hops[3].wait_recv()
        got = r.r4z[...].astype(f32)
        for h in range(2):
            for j in range(3):
                k = 3 * h + j
                r.o_gup[pl.ds(k, 24, stride=24)] = (
                    r.k4z[:, 128 * k : 128 * k + 128]
                    + got[24 * h : 24 * h + 24, 128 * j : 128 * j + 128]
                )

    def put(row, v):
        for j in range(v.shape[1] // 128):
            part, line = divmod(row + j, 64)
            r.smf[part, line : line + 1] = v[:, 128 * j : 128 * j + 128]

    e = nt(r.rh_up[own], r.up_w[...])
    hat = r.hat2[...]
    grad_f = r.rh_down[own].astype(f32)
    g_res = grad_f + norm_rows_back(e, hat, r.std2[...], r.norm_gain[1:2])
    r.o_gtok[...] = g_res
    g_res_b = g_res.astype(bf16)
    r.rh_out[own] = g_res_b
    shares[10].start()
    g_mixed = nt(g_res_b, r.out_w[...])
    r.g_outer[...] = g_mixed * r.summed[...]
    g_summed = g_mixed * r.outer[...]
    r.g_sum[...] = g_summed
    r.stage[2] = jnp.transpose(g_summed).astype(bf16)
    trade(2, r.gc_in)

    def quarter(k):
        t = lax.rem(g + k, 4)
        return remote(r.smf.at[t], r.q_in.at[k - 1], r.q_s.at[k - 1], r.q_r.at[k - 1], (s, t))

    def eighth(k):
        t = peers[k]
        return remote(r.q_sum.at[at(t, 8)], r.o_in.at[k], r.o_s.at[k], r.o_r.at[k], (t, g))

    def spread(k, back):
        slot = r.ag.at[g, peers[k] if back else s]
        return remote(slot, slot, r.ag_s.at[k], r.ag_r.at[k], (peers[k], g))

    over_y = g + y_step
    first_slot, second_slot = r.ag.at[g], r.ag.at[over_y]
    y_send = remote(first_slot, first_slot, r.ag_s.at[7], r.ag_r.at[7], (s, over_y))
    y_back = remote(second_slot, second_slot, r.ag_s.at[7], r.ag_r.at[7], (s, over_y))
    c_send = [
        remote(slot, slot, r.ag_s.at[8 + i], r.ag_r.at[8 + i], (s, other))
        for i, slot in enumerate((first_slot, second_slot))
    ]
    third_slot, fourth_slot = r.ag.at[other], r.ag.at[other + y_step]
    c_back = [
        remote(slot, slot, r.ag_s.at[8 + i], r.ag_r.at[8 + i], (s, other))
        for i, slot in enumerate((third_slot, fourth_slot))
    ]

    put(AT_GAIN + 6, col_sum(e * hat))
    put(AT_SHIFT + 6, col_sum(e))
    put(AT_DOWNB, col_sum(grad_f))
    put(AT_UPB, col_sum(r.rh_up[own].astype(f32)))
    put(AT_OUTB, col_sum(g_res_b.astype(f32)))
    put(AT_SKIP, col_sum(g_summed * r.gf[...]))
    shares[8].wait_recv()
    shares[9].wait_recv()
    shares[12].wait_recv()
    r.s1z[...] = nn(r.lh_upz[at(1 - z1, 192)], r.rh_up[:, 0:768]).astype(bf16)
    hops[0].start()
    make_a(0, 3, r.lh_up, r.rh_up, 1)
    one_a(0).start()
    for copy in shares[0:6]:
        copy.wait_recv()
    for p in range(3):
        cols = pl.ds(256 * p, 256)
        r.s2b[p] = nn(r.lh_down[at(1 - b2, 384)], r.rh_down[:, cols]).astype(bf16)
    two_b(0).start()
    for p in range(3):
        cols = pl.ds(256 * p, 256)
        r.k2b[p] = nn(r.lh_down[at(b2, 384)], r.rh_down[:, cols])
    shares[7].wait_recv()
    shares[10].wait_recv()
    make_a(3, 1, r.lh_out, r.rh_out)
    r.k1z[...] = nn(r.lh_upz[at(z1, 192)], r.rh_up[:, 0:768])
    arrive(2, r.gc_in)
    r.ys[...] = (
        nn(r.gc_in[...], r.tables[2, high_half]) + nn(r.gc_in[...], r.tables[3, high_half])
    ) * (1.0 / 128.0)

    @pl.loop(0, 12)
    def _(tile):
        e = [pick(r.es, tile, b) for b in range(8)]
        d = [pick(r.ys, tile, b) for b in range(8)]
        for b in range(8):
            re, im = 0.0, 0.0
            for lag in range(8 - b):
                er, ei = e[lag]
                dr, di = d[b + lag]
                re = re + er * dr + ei * di
                im = im + er * di - ei * dr
            keep(r.es, tile, b, (re, im))

    g_long = by_table(r.es[...], 0, every, low_half)
    r.stage[3] = g_long.astype(bf16)
    trade(3, r.gl_in)
    one_a(1).start()
    two_b(1).start()
    zf2()
    stay_a(0, 3, r.lh_up, r.rh_up, 1)
    stay_a(3, 1, r.lh_out, r.rh_out)
    ph2_b(0)
    ph1_a(0)
    r.o_out[...] = r.o_out[...] + nn(r.act[...], r.down_w[...]) + r.down_b[...]
    arrive(3, r.gl_in)
    g_gated = r.skip[...] * r.g_sum[...] + jnp.transpose(r.gl_in[...].astype(f32))
    mixes = (r.g_outer[...], g_gated * r.value[...], g_gated * r.inner[...])
    for part in range(3):
        r.gm[own, 768 * part : 768 * part + 768] = mixes[part]
    first_rows = remote(
        r.gm.at[pl.ds(0, 2)], r.gm.at[pl.ds(ROWS, 2)], r.halo_s.at[1], r.halo_r.at[1], (s - 1, g)
    )

    @pl.when(s > 0)
    def _():
        first_rows.start()

    one_a(2).start()
    two_b(2).start()
    for part in range(3):
        cols = pl.ds(768 * part, 768)
        mix = r.gm[own, cols]
        put(AT_CONVB + 6 * part, col_sum(mix))
        for tap in range(3):
            put(
                AT_CONVW + 18 * tap + 6 * part,
                col_sum(mix * r.pp[pl.ds(HALO - 2 + tap, ROWS), cols]),
            )

    @pl.when(s < 7)
    def _():
        first_rows.wait_recv()

    @pl.when(s == 7)
    def _():
        r.gm[pl.ds(ROWS, 8)] = jnp.zeros((8, r.gm.shape[1]), f32)

    for part in range(3):
        cols = pl.ds(768 * part, 768)
        r.rh_in[own, cols] = (
            r.conv_w[0:1, cols] * r.gm[pl.ds(2, ROWS), cols]
            + r.conv_w[1:2, cols] * r.gm[pl.ds(1, ROWS), cols]
            + r.conv_w[2:3, cols] * r.gm[pl.ds(0, ROWS), cols]
        ).astype(bf16)
    shares[11].start()
    r.g_sum[...] = nt(r.rh_in[own], r.in_w[...])
    shares[6].wait_recv()
    shares[11].wait_recv()
    make_a(4, 3, r.lh_in, r.rh_in)
    one_a(4).start()
    one_a(5).start()
    one_a(6).start()
    zf3()
    ph1_a(1)
    ph2_b(1)
    ph3_b(0)
    stay_a(4, 3, r.lh_in, r.rh_in)
    ph1_a(2)
    ph2_b(2)
    e = r.g_sum[...]
    hat = r.hat1[...]
    put(AT_IN, col_sum(r.rh_in[own].astype(f32)))
    put(AT_GAIN, col_sum(e * hat))
    put(AT_SHIFT, col_sum(e))
    r.o_gtok[...] = r.o_gtok[...] + norm_rows_back(e, hat, r.std1[...], r.norm_gain[0:1])
    ph2_a(0)
    ph3_b(1)
    @pl.loop(0, 12)
    def _(tile):
        v = [pick(r.xs, tile, b) for b in range(8)]
        d = [pick(r.ys, tile, b) for b in range(8)]
        for lag in range(8):
            re, im = 0.0, 0.0
            for b in range(8 - lag):
                vr, vi = v[b]
                dr, di = d[b + lag]
                re = re + vr * dr + vi * di
                im = im + vr * di - vi * dr
            keep(r.xs, tile, lag, (re, im))

    r.es[...] = by_table(r.xs[...], 0, every, every)
    ph1_a(4)
    ph2_a(1)
    ph3_a(0)
    ph3_b(2)
    for b in range(8):
        cols = pl.ds(128 * b, 128)
        gt = r.es[96 * b : 96 * b + 96, 128:256]
        if b < 7:
            gt = gt + r.es[96 * b + 96 : 96 * b + 192, 0:128]
        r.dpre[:, cols] = gt * r.wind[:, cols]
        r.taps[:, cols] = r.taps[:, cols] * gt
    g_rate = -jnp.sum(r.taps[...] * place, axis=1, keepdims=True)
    g_last = nt_high(r.dpre[...], r.a3[...])
    for j in range(4):
        r.smf[j, 64:88, 0:64] = g_last[24 * j : 24 * j + 24]
        r.smf[j, 64:88, 64:65] = g_rate[24 * j : 24 * j + 24]
    ones = jnp.ones((8, 1024), f32)
    g_a = tn_high(last, r.dpre[...])
    for i, (u_ref, c_ref, a_ref) in enumerate(
        ((r.u3, r.c3, r.a2), (r.u2, r.c2, r.a1), (r.u1, r.c1, None))
    ):
        layer = 2 - i
        g_arg = g_a * c_ref[...]
        g_freq = nt_high(ones, g_arg * u_ref[...])[0:1]
        g_u = g_arg * freq_cols[:, layer : layer + 1]
        g_bias = nt_high(ones, g_u)[0:1]
        r.smf[1, layer : layer + 1, 64:128] = g_bias
        r.smf[1, 3 + layer : 4 + layer, 64:128] = g_freq
        if layer > 0:
            r.smf[0, 0:64, 64 * (layer - 1) : 64 * layer] = nt_high(a_ref[...], g_u)
            g_a = nn_high(r.filt_hidden[layer - 1], g_u)
        else:
            r.smf[1, 0:33, 0:64] = nt_high(r.feats[...], g_u)

    for k in range(1, 4):
        quarter(k).start()
    one_a(3).start()
    zf4()
    ph1_a(5)
    ph2_a(2)
    ph3_a(1)
    for k in range(1, 4):
        quarter(k).wait_recv()
    r.q_sum[...] = r.smf[g] + r.q_in[0] + r.q_in[1] + r.q_in[2]
    for k in range(7):
        eighth(k).start()
    ph2_a(4)
    ph1_a(6)
    ph3_a(2)
    for k in range(7):
        eighth(k).wait_recv()
    r.ag[g, s, pl.ds(0, 8)] = r.q_sum[at(s, 8)] + jnp.sum(r.o_in[...], axis=0)
    r.ag[g, s, pl.ds(8, 24)] = r.q_sum[pl.ds(64, 24)]
    for k in range(7):
        spread(k, False).start()
    ph2_a(5)
    ph3_a(4)
    ph1_a(3)
    ph2_a(6)
    ph3_a(5)
    for k in range(7):
        spread(k, True).wait_recv()
    y_send.start()
    ph2_a(3)
    ph3_a(6)
    ph4_b(0)
    ph4_b(1)
    ph4_b(2)
    ph3_a(3)
    zf5()
    ph4_a(0, r.o_gup, 6, 24)
    ph4_a(1, r.o_gup, 12, 24)
    ph4_a(2, r.o_gup, 18, 24)
    y_back.wait_recv()
    for copy in c_send:
        copy.start()
    ph4_a(4, r.o_gin, 0, 18)
    ph4_a(5, r.o_gin, 6, 18)
    ph4_a(6, r.o_gin, 12, 18)
    for copy in c_back:
        copy.wait_recv()
    r.o_small[...] = r.ag[...]
    ph4_a(3, r.o_gout, 0, 6)

    @pl.when(s < 7)
    def _():
        last_rows.wait_send()

    @pl.when(s > 0)
    def _():
        first_rows.wait_send()

    for copy in shares:
        copy.wait_send()

    @pl.loop(0, 4)
    def _(which):
        @pl.loop(1, 8)
        def _(k):
            remote(
                r.stage.at[which, pl.ds(0, 96)],
                r.gat.at[pl.ds(0, 96)],
                r.a2a_s.at[which, k - 1],
                r.a2a_r.at[which, k - 1],
                (s, other),
            ).wait_send()

    for copy in hops:
        copy.wait_send()

    @pl.loop(0, 7)
    def _(p):
        one_a(p).wait_send()
        two_a(p).wait_send()
        three_a(p).wait_send()
        four_a(p).wait_send()

    @pl.loop(0, 3)
    def _(p):
        two_b(p).wait_send()
        three_b(p).wait_send()
        four_b(p).wait_send()

    for k in range(1, 4):
        quarter(k).wait_send()

    for k in range(7):
        eighth(k).wait_send()
        spread(k, False).wait_send()

    y_send.wait_send()
    for copy in c_send:
        copy.wait_send()


def finish_kernel(
    i_out, i_gtok, i_gin, i_gout, i_gup, i_gdown, small,
    out, gtok, gain, shift, gin, in_b, conv_w, conv_b, first, hidden, bias, freq,
    last, decay, skip, gout, out_b, gup, up_b, gdown, down_b, sems,
):
    bulk = (
        (i_out, out.at[0]), (i_gtok, gtok.at[0]), (i_gin, gin), (i_gout, gout), (i_gup, gup), (i_gdown, gdown),
    )
    leave = [pltpu.make_async_copy(a, b, sems.at[i]) for i, (a, b) in enumerate(bulk)]
    for copy in leave:
        copy.start()
    rows = jnp.concatenate([small[i, j, 0:8, :] for i in range(4) for j in range(8)], axis=0)

    def fetch(at_row, dest, dest_row, wide):
        for j in range(wide):
            dest[dest_row : dest_row + 1, 128 * j : 128 * j + 128] = rows[at_row + j : at_row + j + 1]

    def line(at_row, dest):
        dest[...] = rows[at_row : at_row + dest.shape[0] // 128].reshape(dest.shape[0])

    for i in range(2):
        fetch(AT_GAIN + 6 * i, gain, i, 6)
        fetch(AT_SHIFT + 6 * i, shift, i, 6)
        hidden[i] = rows[AT_HID : AT_HID + 64, 64 * i : 64 * i + 64]
    for i in range(3):
        fetch(AT_CONVW + 18 * i, conv_w, i, 18)
    line(AT_IN, in_b)
    line(AT_CONVB, conv_b)
    line(AT_SKIP, skip)
    line(AT_OUTB, out_b)
    line(AT_UPB, up_b)
    line(AT_DOWNB, down_b)
    first[...] = rows[AT_FIRST : AT_FIRST + 33, 0:64]
    bias[...] = rows[AT_FIRST : AT_FIRST + 3, 64:128]
    freq[...] = rows[AT_FIRST + 3 : AT_FIRST + 6, 64:128]
    channels = jnp.transpose(
        jnp.concatenate([small[j, i, 8:32, :] for i in range(8) for j in range(4)], axis=0)
    )
    last[...] = channels[0:64]
    decay[...] = channels[64:65].reshape(768)
    for copy in leave:
        copy.wait()


def one_kernel_body(tokens, out_grad, norm_gain, norm_bias, in_weight, in_bias, conv_weight, conv_bias,
                    filt_first, filt_hidden, filt_bias, filt_freq, filt_last, decay_rates, skip_scale,
                    out_weight, out_bias, up_weight, up_bias, down_weight, down_bias):
    width, hidden = up_weight.shape
    length = tokens.shape[1] * lax.axis_size("seq")
    any_spec = pl.BlockSpec(memory_space=pl.ANY)
    vmem_spec = pl.BlockSpec(memory_space=pltpu.VMEM)

    def vm(*shape, dtype=f32):
        return pltpu.VMEM(shape, dtype)

    def dma(*shape):
        return pltpu.SemaphoreType.DMA(shape)

    def shape(*dims):
        return jax.ShapeDtypeStruct(dims, f32)

    outs = pl.pallas_call(
        step_kernel,
        out_shape=[
            vm(128, width), vm(128, width), vm(432, 128), vm(144, 128),
            vm(576, 128), vm(576, 128), vm(4, 8, 32, 128),
        ],
        in_specs=[any_spec] * 23,
        out_specs=[vmem_spec] * 7,
        scratch_shapes=[vm(*dims) for _, dims in SMALL_ARGS]
        + [vm(*dims, dtype=dtype) for _, dims, dtype in SCRATCH]
        + [dma(*dims) for _, dims in SEMAPHORES],
        compiler_params=pltpu.CompilerParams(
            collective_id=0, has_side_effects=True, vmem_limit_bytes=60 * 1024 * 1024
        ),
        name="hyena_step",
    )(
        tokens, out_grad, in_weight, out_weight, up_weight, down_weight,
        jnp.asarray(fourier_tables()),
        norm_gain, norm_bias, in_bias, conv_weight, conv_bias,
        jnp.asarray(feature_table(length, (filt_first.shape[0] - 1) // 2)),
        filt_first, filt_hidden, filt_bias, filt_freq, filt_last, decay_rates, skip_scale, out_bias,
        up_bias, down_bias,
    )
    done = pl.pallas_call(
        finish_kernel,
        out_shape=[
            shape(1, 128, width), shape(1, 128, width), shape(2, width), shape(2, width), shape(432, 128),
            shape(3 * width), shape(3, 3 * width), shape(3 * width), shape(33, 64), shape(2, 64, 64),
            shape(3, 64), shape(3, 64), shape(64, width), shape(width), shape(width), shape(144, 128),
            shape(width), shape(576, 128), shape(hidden), shape(576, 128), shape(width),
        ],
        in_specs=[vmem_spec] * 7,
        out_specs=[any_spec, any_spec, vmem_spec, vmem_spec, any_spec]
        + [vmem_spec] * 10
        + [any_spec, vmem_spec, any_spec, vmem_spec, any_spec, vmem_spec],
        scratch_shapes=[dma(6)],
        compiler_params=pltpu.CompilerParams(vmem_limit_bytes=32 * 1024 * 1024),
        name="hyena_finish",
    )(*outs)
    flat = (4, 15, 17, 19)
    return tuple(v.reshape(-1) if i in flat else v for i, v in enumerate(done))


def solution(mesh):
    small_mesh = mesh.shape["seq"] == 8 and mesh.shape["grp"] == 4
    return jax.shard_map(
        one_kernel_body if small_mesh else body,
        mesh=mesh,
        in_specs=(P("grp", "seq", None), P("grp", "seq", None)) + (P(),) * 19,
        out_specs=(
            P("grp", "seq", None),
            P("grp", "seq", None),
            P(),
            P(),
            P(("seq", "grp")),
        )
        + (P(),) * 10
        + (P(("seq", "grp")), P(), P(("seq", "grp")), P(), P(("seq", "grp")), P()),
        check_vma=False,
    )
```

```python
import math
import types

import jax
import jax.numpy as jnp
import ml_dtypes
import numpy as np
from jax import lax
from jax.experimental import pallas as pl
from jax.experimental.pallas import tpu as pltpu
from jax.sharding import PartitionSpec as P

epsilon = 1e-05


def shifted(array, axis, by):
    peers = lax.axis_size(axis)
    pairs = [(i, i + by) for i in range(peers) if 0 <= i + by < peers]
    return lax.ppermute(array, axis, pairs)


def highest(left_mat, right_mat):
    return jnp.dot(
        left_mat, right_mat, precision=lax.Precision.HIGHEST, preferred_element_type=jnp.float32
    )


def highest_t(left_mat, right_mat):
    return lax.dot_general(
        left_mat,
        right_mat,
        (((0,), (0,)), ((), ())),
        precision=lax.Precision.HIGHEST,
        preferred_element_type=jnp.float32,
    )


def rows_t(left_mat, right_mat):
    return lax.dot_general(
        left_mat, right_mat, (((0,), (0,)), ((), ())), preferred_element_type=jnp.float32
    )


def back_mul(grad_in, weight_mat):
    return lax.dot_general(
        grad_in, weight_mat, (((1,), (1,)), ((), ())), preferred_element_type=jnp.float32
    )


def layer_norm(values, gain_row, shift_row):
    row_mean = jnp.mean(values, axis=-1, keepdims=True)
    centred = values - row_mean
    inv_std = lax.rsqrt(jnp.mean(centred * centred, axis=-1, keepdims=True) + epsilon)
    normed = centred * inv_std
    return (normed * gain_row + shift_row, normed, inv_std)


def norm_back(grad_in, normed, inv_std, gain_row):
    scaled = grad_in * gain_row
    centred_grad = (
        scaled
        - jnp.mean(scaled, axis=-1, keepdims=True)
        - normed * jnp.mean(scaled * normed, axis=-1, keepdims=True)
    )
    return (centred_grad * inv_std, jnp.sum(grad_in * normed, axis=0), jnp.sum(grad_in, axis=0))


def smooth(values):
    return jax.nn.gelu(values, approximate=False)


def filter_rows(params, positions, length):
    filt_first, filt_hidden, filt_bias, filt_freq, filt_last, decay_rates = params
    place = positions.astype(jnp.float32)
    bands = (filt_first.shape[0] - 1) // 2
    band = 0.0001 + jnp.arange(bands, dtype=jnp.float32) * ((bands - 1 - 0.0001) / (bands - 1))
    omega = place[:, None] * (2.0 * math.pi / length)
    phase = omega * band[None, :]
    feats = jnp.concatenate(
        [place[:, None] / (length - 1), jnp.cos(phase), -jnp.sin(phase)], axis=1
    )
    act_one = jnp.sin(filt_freq[0] * (highest(feats, filt_first) + filt_bias[0]))
    act_two = jnp.sin(filt_freq[1] * (highest(act_one, filt_hidden[0]) + filt_bias[1]))
    act_three = jnp.sin(filt_freq[2] * (highest(act_two, filt_hidden[1]) + filt_bias[2]))
    window = jnp.exp(-decay_rates[None, :] * jnp.maximum(place, 0.0)[:, None])
    return highest(act_three, filt_last) * window


def body(
    tokens,
    out_grad,
    norm_gain,
    norm_bias,
    in_weight,
    in_bias,
    conv_weight,
    conv_bias,
    filt_first,
    filt_hidden,
    filt_bias,
    filt_freq,
    filt_last,
    decay_rates,
    skip_scale,
    out_weight,
    out_bias,
    up_weight,
    up_bias,
    down_weight,
    down_bias,
):
    row_count = tokens.shape[1]
    model_width = tokens.shape[2]
    seq_count = lax.axis_size("seq")
    length = row_count * seq_count
    fft_span = 2 * row_count
    fparams = (filt_first, filt_hidden, filt_bias, filt_freq, filt_last, decay_rates)
    fft_grid = jnp.arange(fft_span, dtype=jnp.int32)
    angles = (fft_grid[:, None] * fft_grid[None, :] % fft_span).astype(jnp.float32) * (
        2.0 * math.pi / fft_span
    )
    cos_full = jnp.cos(angles)
    sin_full = jnp.sin(angles)
    cos_left = cos_full[:, :row_count]
    sin_left = sin_full[:, :row_count]
    cos_low = cos_full[row_count:, :]
    sin_low = sin_full[row_count:, :]

    def segment(params, lag_step):
        positions = (lag_step - 1) * row_count + fft_grid
        keep_mask = (positions >= 0).astype(jnp.float32)
        return filter_rows(params, positions, length) * keep_mask[:, None]

    def forward_add(lag_step, source, totals):
        filter_taps = segment(fparams, lag_step)
        g_re = highest(cos_full, filter_taps)
        g_im = -highest(sin_full, filter_taps)
        source_f = source.astype(jnp.float32)
        s_re = highest(cos_left, source_f)
        s_im = -highest(sin_left, source_f)
        return (totals[0] + g_re * s_re - g_im * s_im, totals[1] + g_re * s_im + g_im * s_re)

    inputs = tokens[0].astype(jnp.float32)
    normed1, hat_one, std_one = layer_norm(inputs, norm_gain[0], norm_bias[0])
    normed1_b = normed1.astype(jnp.bfloat16)
    projected = (
        jnp.dot(normed1_b, in_weight, preferred_element_type=jnp.float32) + in_bias
    ).astype(jnp.bfloat16)
    before = shifted(projected[row_count - 2 :], "seq", 1)
    padded = jnp.concatenate([before, projected], axis=0).astype(jnp.float32)
    mixed_conv = (
        conv_weight[0] * padded[:row_count]
        + conv_weight[1] * padded[1 : row_count + 1]
        + conv_weight[2] * padded[2:]
        + conv_bias
    )
    outer_part = mixed_conv[:, :model_width]
    inner_part = mixed_conv[:, model_width : 2 * model_width]
    value_part = mixed_conv[:, 2 * model_width :]
    gated_b = (inner_part * value_part).astype(jnp.bfloat16)
    gated_f = gated_b.astype(jnp.float32)
    zero_totals = (
        jnp.zeros((fft_span, model_width), jnp.float32),
        jnp.zeros((fft_span, model_width), jnp.float32),
    )
    first_pass = forward_add(0, gated_b, zero_totals)

    def forward_step(lag_step, loop_carry):
        source, tot_re, tot_im = loop_carry
        source = shifted(source, "seq", 1)
        tot_re, tot_im = forward_add(lag_step, source, (tot_re, tot_im))
        return (source, tot_re, tot_im)

    unused_src, tot_re, tot_im = lax.fori_loop(
        1, seq_count, forward_step, (gated_b, first_pass[0], first_pass[1])
    )
    conv_out = (highest(cos_low, tot_re) - highest(sin_low, tot_im)) / fft_span
    summed = conv_out + skip_scale * gated_f
    mixed_out_b = (outer_part * summed).astype(jnp.bfloat16)
    residual = (
        inputs + jnp.dot(mixed_out_b, out_weight, preferred_element_type=jnp.float32) + out_bias
    )
    normed2, hat_two, std_two = layer_norm(residual, norm_gain[1], norm_bias[1])
    normed2_b = normed2.astype(jnp.bfloat16)
    pre_act = jnp.dot(normed2_b, up_weight, preferred_element_type=jnp.float32) + up_bias
    act_val, gelu_back = jax.vjp(smooth, pre_act)
    act_b = act_val.astype(jnp.bfloat16)
    result = residual + jnp.dot(act_b, down_weight, preferred_element_type=jnp.float32) + down_bias
    grad_out_b = out_grad[0]
    grad_out_f = grad_out_b.astype(jnp.float32)
    g_down = rows_t(act_b, grad_out_b)
    g_down_bias = jnp.sum(grad_out_f, axis=0)
    g_act = back_mul(grad_out_b, down_weight)
    g_pre_b = gelu_back(g_act)[0].astype(jnp.bfloat16)
    g_up = rows_t(normed2_b, g_pre_b)
    g_up_bias = jnp.sum(g_pre_b.astype(jnp.float32), axis=0)
    g_norm_two = back_mul(g_pre_b, up_weight)
    g_res_norm, g_gain_two, g_shift_two = norm_back(g_norm_two, hat_two, std_two, norm_gain[1])
    g_resid = grad_out_f + g_res_norm
    g_resid_b = g_resid.astype(jnp.bfloat16)
    g_outw = rows_t(mixed_out_b, g_resid_b)
    g_out_bias = jnp.sum(g_resid_b.astype(jnp.float32), axis=0)
    g_mixed = back_mul(g_resid_b, out_weight)
    g_outer = g_mixed * summed
    g_summed = g_mixed * outer_part
    g_skip = jnp.sum(g_summed * gated_f, axis=0)
    g_conv_b = g_summed.astype(jnp.bfloat16)
    v_re = highest(cos_left, gated_f)
    v_im = -highest(sin_left, gated_f)

    def backward_add(lag_step, source, loop_carry):
        tot_re, tot_im, grad_acc = loop_carry
        source_f = source.astype(jnp.float32)
        d_re = highest_t(cos_low, source_f) / fft_span
        d_im = -highest_t(sin_low, source_f) / fft_span

        def lag_taps(params):
            return segment(params, lag_step)

        filter_taps, taps_pull = jax.vjp(lag_taps, fparams)
        g_re = highest(cos_full, filter_taps)
        g_im = -highest(sin_full, filter_taps)
        tot_re = tot_re + g_re * d_re + g_im * d_im
        tot_im = tot_im - g_im * d_re + g_re * d_im
        s_re = v_re * d_re + v_im * d_im
        s_im = v_re * d_im - v_im * d_re
        d_taps = highest_t(cos_full, s_re) - highest_t(sin_full, s_im)
        more_grads = taps_pull(d_taps)[0]
        grad_acc = jax.tree.map(jnp.add, grad_acc, more_grads)
        return (tot_re, tot_im, grad_acc)

    zero_grads = jax.tree.map(jnp.zeros_like, fparams)
    start_carry = (zero_totals[0], zero_totals[1], zero_grads)
    first_back = backward_add(0, g_conv_b, start_carry)

    def backward_step(lag_step, loop_carry):
        source, tot_re, tot_im, grad_acc = loop_carry
        source = shifted(source, "seq", -1)
        tot_re, tot_im, grad_acc = backward_add(lag_step, source, (tot_re, tot_im, grad_acc))
        return (source, tot_re, tot_im, grad_acc)

    unused_src, back_re, back_im, cycle_grads = lax.fori_loop(
        1, seq_count, backward_step, (g_conv_b,) + first_back
    )
    g_long = highest_t(cos_left, back_re) - highest_t(sin_left, back_im)
    g_gated = g_summed * skip_scale + g_long
    g_mix = jnp.concatenate([g_outer, g_gated * value_part, g_gated * inner_part], axis=1)
    g_conv_bias = jnp.sum(g_mix, axis=0)
    g_conv_w = jnp.stack(
        [
            jnp.sum(g_mix * padded[tap_index : tap_index + row_count], axis=0)
            for tap_index in range(3)
        ]
    )
    g_pad = (
        jnp.pad(conv_weight[0] * g_mix, ((0, 2), (0, 0)))
        + jnp.pad(conv_weight[1] * g_mix, ((1, 1), (0, 0)))
        + jnp.pad(conv_weight[2] * g_mix, ((2, 0), (0, 0)))
    )
    after_rows = shifted(g_pad[:2], "seq", -1)
    g_proj_b = (g_pad[2:] + jnp.pad(after_rows, ((row_count - 2, 0), (0, 0)))).astype(jnp.bfloat16)
    g_inw = rows_t(normed1_b, g_proj_b)
    g_in_bias = jnp.sum(g_proj_b.astype(jnp.float32), axis=0)
    g_norm_one = back_mul(g_proj_b, in_weight)
    g_in_norm, g_gain_one, g_shift_one = norm_back(g_norm_one, hat_one, std_one, norm_gain[0])
    g_tokens = g_resid + g_in_norm
    small_grads = lax.psum(
        (
            jnp.stack([g_gain_one, g_gain_two]),
            jnp.stack([g_shift_one, g_shift_two]),
            g_in_bias,
            g_conv_w,
            g_conv_bias,
            cycle_grads[0],
            cycle_grads[1],
            cycle_grads[2],
            cycle_grads[3],
            cycle_grads[4],
            cycle_grads[5],
            g_skip,
            g_out_bias,
            g_up_bias,
            g_down_bias,
        ),
        ("seq", "grp"),
    )
    large_grads = (
        lax.psum_scatter(g_inw.reshape(-1), ("seq", "grp"), scatter_dimension=0, tiled=True),
        lax.psum_scatter(g_outw.reshape(-1), ("seq", "grp"), scatter_dimension=0, tiled=True),
        lax.psum_scatter(g_up.reshape(-1), ("seq", "grp"), scatter_dimension=0, tiled=True),
        lax.psum_scatter(g_down.reshape(-1), ("seq", "grp"), scatter_dimension=0, tiled=True),
    )
    return (
        result[None],
        g_tokens[None],
        small_grads[0],
        small_grads[1],
        large_grads[0],
        small_grads[2],
        small_grads[3],
        small_grads[4],
        small_grads[5],
        small_grads[6],
        small_grads[7],
        small_grads[8],
        small_grads[9],
        small_grads[10],
        small_grads[11],
        large_grads[1],
        small_grads[12],
        large_grads[2],
        small_grads[13],
        large_grads[3],
        small_grads[14],
    )


f32 = jnp.float32
bf16 = jnp.bfloat16
MESH_ID = pl.DeviceIdType.MESH
HIGH = lax.Precision.HIGHEST
ROWS = 128
HALO = 16


def nn(a, b):
    return jnp.dot(a, b, preferred_element_type=f32)


def nt(a, b):
    return lax.dot_general(a, b, (((1,), (1,)), ((), ())), preferred_element_type=f32)


def nn_high(a, b):
    return jnp.dot(a, b, precision=HIGH, preferred_element_type=f32)


def nt_high(a, b):
    return lax.dot_general(
        a, b, (((1,), (1,)), ((), ())), precision=HIGH, preferred_element_type=f32
    )


def tn_high(a, b):
    return lax.dot_general(
        a, b, (((0,), (0,)), ((), ())), precision=HIGH, preferred_element_type=f32
    )


def two(v):
    high = v.astype(bf16)
    return high, (v - high.astype(f32)).astype(bf16)


def sin_cos(v):
    k = jnp.floor(v * (1.0 / math.pi) + 0.5)
    r = ((v - k * 3.140625) - k * 0.0009670257568359375) - k * 6.2771141529083252e-07
    sign = 1.0 - 2.0 * (k - 2.0 * jnp.floor(k * 0.5))
    q = r * r
    s = 1.0 / math.factorial(13)
    for order in (11, 9, 7, 5, 3):
        s = 1.0 / math.factorial(order) - s * q
    s = r - r * q * s
    c = 1.0 / math.factorial(12)
    for order in (10, 8, 6, 4, 2):
        c = 1.0 / math.factorial(order) - c * q
    c = 1.0 - q * c
    return s * sign, c * sign


def gelu_both(v):
    a = jnp.abs(v)
    t = 1.0 / (1.0 + (0.3275911 / math.sqrt(2.0)) * a)
    poly = t * (
        0.254829592
        + t * (-0.284496736 + t * (1.421413741 + t * (-1.453152027 + t * 1.061405429)))
    )
    bell = jnp.exp(-0.5 * v * v)
    tail = 0.5 * poly * bell
    phi = jnp.where(v >= 0, 1.0 - tail, tail)
    return v * phi, phi + v * bell * (1.0 / math.sqrt(2.0 * math.pi))


def col_sum(v):
    return jnp.sum(v, axis=0, keepdims=True)


def row_mean(v):
    return jnp.mean(v, axis=1, keepdims=True)


def norm_rows(v):
    centred = v - row_mean(v)
    inv = lax.rsqrt(row_mean(centred * centred) + epsilon)
    return centred * inv, inv


def norm_rows_back(e, hat, inv, gain):
    k = e * gain
    return (k - row_mean(k) - hat * row_mean(k * hat)) * inv


def fourier_tables():
    bins = np.arange(128) + 0.5
    angle = 2.0 * np.pi * bins[:, None] * np.arange(256)[None, :] / 256
    full = np.concatenate([np.cos(angle), -np.sin(angle)], axis=0).astype(np.float32)
    out = []
    for mat in (full, full.T):
        high = mat.astype(ml_dtypes.bfloat16)
        out += [high, (mat - high.astype(np.float32)).astype(ml_dtypes.bfloat16)]
    return np.stack(out)


def feature_table(length, bands):
    place = np.arange(length)
    band = 1e-4 + np.arange(bands) * ((bands - 1 - 1e-4) / (bands - 1))
    phase = band[:, None] * (2.0 * np.pi * place / length)[None, :]
    return np.concatenate(
        [(place / (length - 1))[None], np.cos(phase), -np.sin(phase)], axis=0
    ).astype(np.float32)


AT_HID, AT_FIRST, AT_GAIN, AT_SHIFT, AT_IN, AT_CONVW, AT_CONVB = 0, 64, 97, 109, 121, 139, 193
AT_SKIP, AT_OUTB, AT_UPB, AT_DOWNB = 211, 217, 223, 247

SMALL_ARGS = (
    ("norm_gain", (2, 768)), ("norm_bias", (2, 768)), ("in_b1", (2304,)), ("conv_w", (3, 2304)),
    ("conv_b1", (2304,)), ("feats", (33, 1024)), ("filt_first", (33, 64)), ("filt_hidden", (2, 64, 64)),
    ("filt_bias", (3, 64)), ("filt_freq", (3, 64)), ("filt_last", (64, 768)), ("decay1", (768,)),
    ("skip1", (768,)), ("out_b1", (768,)), ("up_b1", (3072,)), ("down_b1", (768,)),
)

SCRATCH = (
    ("in_w", (768, 2304), bf16), ("out_w", (768, 768), bf16), ("up_w", (768, 3072), bf16),
    ("down_w", (3072, 768), bf16), ("tables", (4, 256, 256), bf16),
    ("in_b", (1, 2304), f32), ("conv_b", (1, 2304), f32), ("skip", (1, 768), f32),
    ("out_b", (1, 768), f32), ("up_b", (1, 3072), f32), ("down_b", (1, 768), f32),
    ("tok", (144, 768), bf16), ("n1", (144, 768), bf16), ("hat1", (128, 768), f32),
    ("std1", (128, 1), f32), ("pp", (144, 2304), f32), ("outer", (128, 768), f32),
    ("inner", (128, 768), f32), ("value", (128, 768), f32), ("gf", (128, 768), f32),
    ("stage", (4, 768, 128), bf16), ("gat", (768, 128), bf16), ("co_in", (768, 128), bf16),
    ("gc_in", (768, 128), bf16), ("gl_in", (768, 128), bf16),
    ("xs", (768, 256), f32), ("es", (768, 256), f32), ("ys", (768, 256), f32),
    ("hw_high", (768, 256), bf16), ("hw_low", (768, 256), bf16),
    ("taps", (96, 1024), f32), ("wind", (96, 1024), f32), ("dpre", (96, 1024), f32),
    ("last_t", (768, 64), f32), ("rate_t", (768, 8), f32),
    ("a1", (64, 1024), f32), ("a2", (64, 1024), f32), ("a3", (64, 1024), f32),
    ("c1", (64, 1024), f32), ("c2", (64, 1024), f32), ("c3", (64, 1024), f32),
    ("u1", (64, 1024), f32), ("u2", (64, 1024), f32), ("u3", (64, 1024), f32),
    ("g_act", (128, 3072), f32), ("act", (128, 3072), bf16), ("summed", (128, 768), f32),
    ("hat2", (128, 768), f32), ("std2", (128, 1), f32),
    ("g_sum", (128, 768), f32), ("g_outer", (128, 768), f32),
    ("gm", (136, 2304), f32),
    ("at_down", (2, 1536, 128), bf16), ("at_up", (2, 384, 128), bf16), ("at_upz", (2, 384, 128), bf16), ("at_in", (2, 384, 128), bf16),
    ("at_out", (2, 384, 128), bf16), ("lh_down", (768, 512), bf16), ("lh_up", (384, 256), bf16), ("lh_upz", (384, 256), bf16),
    ("lh_in", (384, 256), bf16), ("lh_out", (384, 256), bf16), ("rh_down", (512, 768), bf16),
    ("rh_up", (256, 3072), bf16), ("rh_in", (256, 2304), bf16), ("rh_out", (256, 768), bf16),
    ("s1a", (7, 192, 768), bf16), ("k1a", (7, 192, 768), f32), ("r1a", (7, 192, 768), bf16),
    ("s2a", (7, 96, 768), bf16), ("r2a", (7, 96, 768), bf16), ("s3a", (7, 4, 48, 384), bf16),
    ("r3a", (7, 2, 48, 384), bf16), ("s4a", (7, 48, 384), bf16), ("r4a", (7, 48, 384), bf16),
    ("s2b", (3, 384, 256), bf16), ("k2b", (3, 384, 256), f32), ("r2b", (3, 384, 256), bf16),
    ("s3b", (3, 4, 96, 256), bf16), ("r3b", (3, 2, 96, 256), bf16), ("s4b", (3, 96, 256), bf16),
    ("r4b", (3, 96, 256), bf16),
    ("s1z", (192, 768), bf16), ("k1z", (192, 768), f32), ("r1z", (192, 768), bf16),
    ("s2z", (96, 768), bf16), ("r2z", (96, 768), bf16), ("k3z", (48, 768), f32),
    ("s3z", (48, 768), bf16), ("r3z", (48, 768), bf16), ("k4z", (24, 768), f32),
    ("s4z", (48, 384), bf16), ("r4z", (48, 384), bf16),
    ("smf", (4, 88, 128), f32), ("q_in", (3, 88, 128), f32), ("q_sum", (88, 128), f32),
    ("o_in", (7, 8, 128), f32), ("ag", (4, 8, 32, 128), bf16),

)

SEMAPHORES = (
    ("ld", (8,)), ("ls", (16,)), ("a2a_s", (4, 7)), ("a2a_r", (4, 7)), ("halo_s", (2,)), ("halo_r", (2,)),
    ("pair_s", (13,)), ("pair_r", (13,)), ("p1_s", (8,)), ("p1_r", (8,)), ("p2_s", (11,)),
    ("p2_r", (11,)), ("p3_s", (11,)), ("p3_r", (11,)), ("p4_s", (11,)), ("p4_r", (11,)),
    ("zf_s", (4,)), ("zf_r", (4,)), ("q_s", (3,)), ("q_r", (3,)),
    ("o_s", (7,)), ("o_r", (7,)), ("ag_s", (10,)), ("ag_r", (10,)),
)


def step_kernel(*refs):
    names = ["tokens", "out_grad", "in_w_h", "out_w_h", "up_w_h", "down_w_h", "tables_h"]
    names += ["h_" + name for name, _ in SMALL_ARGS]
    names += ["o_out", "o_gtok", "o_gin", "o_gout", "o_gup", "o_gdown", "o_small"]
    names += [name for name, _ in SMALL_ARGS]
    names += [name for name, _, _ in SCRATCH] + [name for name, _ in SEMAPHORES]
    r = types.SimpleNamespace(**dict(zip(names, refs, strict=True)))

    s = lax.axis_index("seq")
    g = lax.axis_index("grp")
    z, x = lax.div(s, 2), lax.rem(s, 2)
    y, c = lax.div(g, 2), lax.rem(g, 2)
    other = g + 1 - 2 * c
    x_step, y_step = 1 - 2 * x, 2 * (1 - 2 * y)
    first = (s + (1 - c) * x_step, g + c * y_step)
    second = (s + c * x_step, g + (1 - c) * y_step)
    cross = (s + c * x_step, other + (1 - c) * y_step)
    b1 = (1 - c) * x + c * y
    b2 = (1 - c) * y + c * x
    z2, z1 = lax.div(z, 2), lax.rem(z, 2)
    near, far = (s + 2 - 4 * z1, g), (s + 4 - 8 * z2, g)

    def at(index, size):
        return pl.ds(pl.multiple_of(index * size, size), size)

    def remote(src, dst, ss, rs, where):
        return pltpu.make_async_remote_copy(
            src_ref=src,
            dst_ref=dst,
            send_sem=ss,
            recv_sem=rs,
            device_id=where,
            device_id_type=MESH_ID,
        )

    bar = pltpu.get_barrier_semaphore()

    @pl.loop(1, 8)
    def _(k):
        pl.semaphore_signal(
            bar, inc=1, device_id=(lax.rem(s + k, 8), g), device_id_type=MESH_ID
        )

    @pl.loop(1, 4)
    def _(k):
        pl.semaphore_signal(
            bar, inc=1, device_id=(s, lax.rem(g + k, 4)), device_id_type=MESH_ID
        )

    pl.semaphore_signal(bar, inc=1, device_id=(s + x_step, other), device_id_type=MESH_ID)

    own = pl.ds(0, ROWS)
    loads = [
        pltpu.make_async_copy(r.tokens.at[0], r.tok.at[pl.ds(HALO, ROWS)], r.ld.at[0]),
        pltpu.make_async_copy(r.in_w_h, r.in_w, r.ld.at[1]),
        pltpu.make_async_copy(r.out_grad.at[0], r.rh_down.at[own], r.ld.at[2]),
        pltpu.make_async_copy(r.tables_h, r.tables, r.ld.at[3]),
        pltpu.make_async_copy(r.down_w_h, r.down_w, r.ld.at[4]),
        pltpu.make_async_copy(r.out_w_h, r.out_w, r.ld.at[5]),
        pltpu.make_async_copy(r.up_w_h, r.up_w, r.ld.at[6]),
    ]
    small_loads = [
        pltpu.make_async_copy(getattr(r, "h_" + name), getattr(r, name), r.ls.at[i])
        for i, (name, _) in enumerate(SMALL_ARGS)
    ]
    loads[0].start()
    for copy in small_loads[:2]:
        copy.start()
    loads[1].start()
    for copy in small_loads[2:]:
        copy.start()
    loads[2].start()
    loads[3].start()

    def share(index, src, dst, where):
        return remote(src, dst, r.pair_s.at[index], r.pair_r.at[index], where)

    block2, block3, block4 = pl.ds(ROWS, ROWS), pl.ds(2 * ROWS, ROWS), pl.ds(3 * ROWS, ROWS)
    shares = [
        share(0, r.rh_down.at[own], r.rh_down.at[block2], (s, other)),
        share(1, r.rh_down.at[own], r.rh_down.at[block3], first),
        share(2, r.rh_down.at[own], r.rh_down.at[block4], cross),
        share(3, r.at_down.at[1 - c, at(b2, 768)], r.lh_down.at[:, block2], (s, other)),
        share(4, r.at_down.at[c, at(1 - b1, 768)], r.lh_down.at[:, block3], first),
        share(5, r.at_down.at[1 - c, at(1 - b2, 768)], r.lh_down.at[:, block4], cross),
        share(6, r.at_in.at[1 - c], r.lh_in.at[:, block2], (s, other)),
        share(7, r.at_out.at[1 - c], r.lh_out.at[:, block2], (s, other)),
        share(8, r.at_up.at[1 - c], r.lh_up.at[:, block2], (s, other)),
        share(9, r.rh_up.at[own], r.rh_up.at[block2], (s, other)),
        share(10, r.rh_out.at[own], r.rh_out.at[block2], (s, other)),
        share(11, r.rh_in.at[own], r.rh_in.at[block2], (s, other)),
        share(12, r.at_upz.at[1 - c], r.lh_upz.at[:, block2], (s, other)),
    ]

    def order_rows(v, halves, z_halves=None):
        t = jnp.transpose(v)
        bits = [(i, j) for i in range(2) for j in range(2)]
        for core in range(2):

            def block(i1, i2, iz):
                ix, iy = (i1, i2) if core == 0 else (i2, i1)
                at_row = 24 * (iz * 8 + ix * 4 + iy * 2 + core)
                return t[at_row : at_row + 24]

            blocks = [block(i1, i2, iz) for i1, i2 in bits for iz in range(4)]
            halves[core] = jnp.concatenate(blocks, axis=0).astype(bf16)
            if z_halves is not None:
                blocks = [block(i1, i2, 2 * j2 + j1) for j1, j2 in bits for i1, i2 in bits]
                z_halves[core] = jnp.concatenate(blocks, axis=0).astype(bf16)

    loads[0].wait()
    hat, inv = norm_rows(r.tok[pl.ds(HALO, ROWS)].astype(f32))
    r.hat1[...] = hat
    r.std1[...] = inv
    small_loads[0].wait()
    small_loads[1].wait()
    own_norm = (hat * r.norm_gain[0:1] + r.norm_bias[0:1]).astype(bf16)
    r.n1[pl.ds(HALO, ROWS)] = own_norm
    pl.semaphore_wait(bar, 11)
    last_rows = remote(
        r.tok.at[pl.ds(ROWS, HALO)],
        r.tok.at[pl.ds(0, HALO)],
        r.halo_s.at[0],
        r.halo_r.at[0],
        (s + 1, g),
    )

    @pl.when(s < 7)
    def _():
        last_rows.start()

    order_rows(own_norm.astype(f32), r.at_in)
    r.lh_in[:, own] = r.at_in[c]
    for copy in small_loads[2:]:
        copy.wait()
    for line, flat in (
        (r.in_b, r.in_b1), (r.conv_b, r.conv_b1), (r.skip, r.skip1),
        (r.out_b, r.out_b1), (r.up_b, r.up_b1), (r.down_b, r.down_b1),
    ):
        line[...] = flat[...].reshape(line.shape)

    @pl.when(s > 0)
    def _():
        last_rows.wait_recv()

    @pl.when(s == 0)
    def _():
        r.tok[pl.ds(0, HALO)] = jnp.zeros((HALO, r.tok.shape[1]), bf16)

    hat, inv = norm_rows(r.tok[pl.ds(0, HALO)].astype(f32))
    r.n1[pl.ds(0, HALO)] = (hat * r.norm_gain[0:1] + r.norm_bias[0:1]).astype(bf16)
    loads[1].wait()
    for copy in loads[4:]:
        copy.start()
    inside = jnp.where(s > 0, 1.0, 0.0).astype(f32)
    for part, dest in enumerate((r.outer, r.inner, r.value)):
        cols = pl.ds(768 * part, 768)
        proj = (nn(r.n1[...], r.in_w[:, cols]) + r.in_b[:, cols]).astype(bf16).astype(f32)
        r.pp[pl.ds(0, HALO), cols] = proj[:HALO] * inside
        r.pp[pl.ds(HALO, ROWS), cols] = proj[HALO:]
        dest[...] = (
            r.conv_w[0:1, cols] * r.pp[pl.ds(HALO - 2, ROWS), cols]
            + r.conv_w[1:2, cols] * r.pp[pl.ds(HALO - 1, ROWS), cols]
            + r.conv_w[2:3, cols] * r.pp[pl.ds(HALO, ROWS), cols]
            + r.conv_b[:, cols]
        )
    gated = (r.inner[...] * r.value[...]).astype(bf16).astype(f32)
    r.gf[...] = gated

    across, over_two, next_z = 3 - z, lax.rem(z + 2, 4), z + 1 - 2 * z1
    peers = [
        2 * to_z + to_x
        for to_z, to_x in (
            (across, 1 - x), (across, x), (over_two, 1 - x), (over_two, x),
            (next_z, 1 - x), (next_z, x), (z, 1 - x),
        )
    ]

    def swap(which, k, dst, slot):
        return remote(
            r.stage.at[which, at(peers[k], 96)],
            dst.at[at(slot, 96)],
            r.a2a_s.at[which, k],
            r.a2a_r.at[which, k],
            (peers[k], g),
        )

    def trade(which, dst):
        for k in range(7):
            swap(which, k, dst, s).start()
        dst[at(s, 96)] = r.stage[which, at(s, 96)]

    def arrive(which, dst):
        for k in range(7):
            swap(which, k, dst, peers[k]).wait_recv()

    r.stage[0] = jnp.transpose(gated).astype(bf16)
    trade(0, r.gat)

    bias_cols = jnp.transpose(r.filt_bias[...])
    freq_cols = jnp.transpose(r.filt_freq[...])
    below = r.feats[...]
    for i, (u_ref, a_ref, c_ref) in enumerate(
        ((r.u1, r.a1, r.c1), (r.u2, r.a2, r.c2), (r.u3, r.a3, r.c3))
    ):
        weights = r.filt_first[...] if i == 0 else r.filt_hidden[i - 1]
        u = tn_high(weights, below) + bias_cols[:, i : i + 1]
        u_ref[...] = u
        below, cosine = sin_cos(freq_cols[:, i : i + 1] * u)
        a_ref[...] = below
        c_ref[...] = cosine

    r.last_t[...] = jnp.transpose(r.filt_last[...])
    r.rate_t[...] = jnp.transpose(jnp.broadcast_to(r.decay1[...].reshape(1, 768), (8, 768)))
    last = r.last_t[at(s, 96)]
    rate = r.rate_t[at(s, 96), 0:1]
    place = lax.broadcasted_iota(jnp.int32, (1, 1024), 1).astype(f32)
    r.wind[...] = jnp.exp(-rate * place)
    r.taps[...] = nn_high(last, r.a3[...]) * r.wind[...]
    r.hw_high[pl.ds(0, 96), own] = jnp.zeros((96, 128), bf16)
    r.hw_low[pl.ds(0, 96), own] = jnp.zeros((96, 128), bf16)
    for b in range(8):
        high, low = two(r.taps[:, 128 * b : 128 * b + 128])
        for half, ref in ((high, r.hw_high), (low, r.hw_low)):
            ref[96 * b : 96 * b + 96, 128:256] = half
            if b < 7:
                ref[96 * b + 96 : 96 * b + 192, 0:128] = half

    def by_table(v, which, rows, cols):
        high, low = two(v)
        table = r.tables[which, rows, cols]
        return nn(high, table) + nn(low, table) + nn(high, r.tables[which + 1, rows, cols])

    every = pl.ds(0, 256)
    low_half, high_half = pl.ds(0, 128), pl.ds(128, 128)
    loads[3].wait()
    r.es[...] = (
        nn(r.hw_high[...], r.tables[2])
        + nn(r.hw_low[...], r.tables[2])
        + nn(r.hw_high[...], r.tables[3])
    )
    loads[2].wait()
    for copy in shares[0:3]:
        copy.start()
    shares[6].start()

    arrive(0, r.gat)
    r.xs[...] = nn(r.gat[...], r.tables[2, low_half]) + nn(r.gat[...], r.tables[3, low_half])

    def pick(ref, tile, b):
        rows = pl.ds(pl.multiple_of(96 * b + 8 * tile, 8), 8)
        return ref[rows, low_half], ref[rows, high_half]

    def keep(ref, tile, b, pair_of):
        rows = pl.ds(pl.multiple_of(96 * b + 8 * tile, 8), 8)
        ref[rows, low_half] = pair_of[0]
        ref[rows, high_half] = pair_of[1]

    @pl.loop(0, 12)
    def _(tile):
        e = [pick(r.es, tile, b) for b in range(8)]
        v = [pick(r.xs, tile, b) for b in range(8)]
        for b in range(8):
            re, im = 0.0, 0.0
            for lag in range(b + 1):
                er, ei = e[lag]
                vr, vi = v[b - lag]
                re = re + er * vr - ei * vi
                im = im + er * vi + ei * vr
            keep(r.ys, tile, b, (re, im))

    conv = by_table(r.ys[...], 0, every, high_half) * (1.0 / 128.0)
    r.stage[1] = conv.astype(bf16)
    trade(1, r.co_in)

    loads[4].wait()
    for t in range(4):
        cols = pl.ds(768 * t, 768)
        r.g_act[:, cols] = nt(r.rh_down[own], r.down_w[cols])

    arrive(1, r.co_in)
    sum_f = jnp.transpose(r.co_in[...].astype(f32)) + r.skip[...] * r.gf[...]
    r.summed[...] = sum_f
    mixed = (r.outer[...] * sum_f).astype(bf16)
    loads[5].wait()
    res = r.tok[pl.ds(HALO, ROWS)].astype(f32) + nn(mixed, r.out_w[...]) + r.out_b[...]
    r.o_out[...] = res
    hat, inv = norm_rows(res)
    r.hat2[...] = hat
    r.std2[...] = inv
    n2 = (hat * r.norm_gain[1:2] + r.norm_bias[1:2]).astype(bf16)
    loads[6].wait()
    for t in range(4):
        cols = pl.ds(768 * t, 768)
        act_f, slope = gelu_both(nn(n2, r.up_w[:, cols]) + r.up_b[:, cols])
        act_b = act_f.astype(bf16)
        r.act[:, cols] = act_b
        r.rh_up[own, cols] = (r.g_act[:, cols] * slope).astype(bf16)
        turned = jnp.transpose(act_b.astype(f32)).astype(bf16)
        for ix in range(2):
            for iy in range(2):
                for core in range(2):
                    i1, i2 = (ix, iy) if core == 0 else (iy, ix)
                    src = 96 * (ix * 4 + iy * 2 + core)
                    r.at_down[core, pl.ds(i1 * 768 + i2 * 384 + t * 96, 96)] = turned[src : src + 96]
    for copy in shares[3:6]:
        copy.start()
    shares[9].start()
    order_rows(n2.astype(f32), r.at_up, r.at_upz)
    shares[12].start()
    shares[8].start()
    r.lh_up[:, own] = r.at_up[c]
    r.lh_upz[:, own] = r.at_upz[c]
    order_rows(mixed.astype(f32), r.at_out)
    shares[7].start()
    r.lh_out[:, own] = r.at_out[c]
    r.lh_down[:, own] = r.at_down[c, at(b1, 768)]

    def one_a(p):
        return remote(r.s1a.at[p], r.r1a.at[p], r.p1_s.at[p], r.p1_r.at[p], first)

    def two_a(p):
        return remote(r.s2a.at[p], r.r2a.at[p], r.p2_s.at[p], r.p2_r.at[p], second)

    def three_a(p):
        return remote(
            r.s3a.at[p, at(1 - z1, 2)], r.r3a.at[p], r.p3_s.at[p], r.p3_r.at[p], near
        )

    def four_a(p):
        return remote(r.s4a.at[p], r.r4a.at[p], r.p4_s.at[p], r.p4_r.at[p], far)

    def two_b(p):
        return remote(r.s2b.at[p], r.r2b.at[p], r.p2_s.at[8 + p], r.p2_r.at[8 + p], second)

    def three_b(p):
        return remote(
            r.s3b.at[p, at(1 - z1, 2)], r.r3b.at[p], r.p3_s.at[8 + p], r.p3_r.at[8 + p], near
        )

    def four_b(p):
        return remote(r.s4b.at[p], r.r4b.at[p], r.p4_s.at[8 + p], r.p4_r.at[8 + p], far)

    def make_a(p0, count, lh, rh, c0=0):
        @pl.loop(0, count)
        def _(p):
            r.s1a[p0 + p] = nn(lh[at(1 - b1, 192)], rh[:, at(c0 + p, 768)]).astype(bf16)

    def stay_a(p0, count, lh, rh, c0=0):
        @pl.loop(0, count)
        def _(p):
            r.k1a[p0 + p] = nn(lh[at(b1, 192)], rh[:, at(c0 + p, 768)])

    def ph1_a(p):
        one_a(p).wait_recv()
        rows = at(1 - b2, 96)
        r.s2a[p] = (r.k1a[p, rows] + r.r1a[p, rows].astype(f32)).astype(bf16)
        two_a(p).start()

    def ph2_a(p):
        two_a(p).wait_recv()
        rows = at(b2, 96)
        v = r.k1a[p, rows] + r.r1a[p, rows].astype(f32) + r.r2a[p].astype(f32)
        for iz in range(4):
            block = v[24 * iz : 24 * iz + 24]
            r.s3a[p, 2 * (iz % 2) + iz // 2] = jnp.concatenate(
                [block[:, :384], block[:, 384:]], axis=0
            ).astype(bf16)
        three_a(p).start()

    def ph3_a(p):
        three_a(p).wait_recv()
        r.s4a[p] = (
            r.s3a[p, 2 * z1 + 1 - z2].astype(f32) + r.r3a[p, 1 - z2].astype(f32)
        ).astype(bf16)
        four_a(p).start()

    def ph4_a(p, dest, base, per_row):
        four_a(p).wait_recv()
        v = r.s3a[p, 2 * z1 + z2].astype(f32) + r.r3a[p, z2].astype(f32) + r.r4a[p].astype(f32)
        for h in range(2):
            for j in range(3):
                dest[pl.ds(base + 3 * h + j, 24, stride=per_row)] = v[
                    24 * h : 24 * h + 24, 128 * j : 128 * j + 128
                ]

    def ph2_b(p):
        two_b(p).wait_recv()
        v = r.k2b[p] + r.r2b[p].astype(f32)
        for iz in range(4):
            r.s3b[p, 2 * (iz % 2) + iz // 2] = v[96 * iz : 96 * iz + 96].astype(bf16)
        three_b(p).start()

    def ph3_b(p):
        three_b(p).wait_recv()
        r.s4b[p] = (
            r.s3b[p, 2 * z1 + 1 - z2].astype(f32) + r.r3b[p, 1 - z2].astype(f32)
        ).astype(bf16)
        four_b(p).start()

    def ph4_b(p):
        four_b(p).wait_recv()
        v = r.s3b[p, 2 * z1 + z2].astype(f32) + r.r3b[p, z2].astype(f32) + r.r4b[p].astype(f32)
        for j in range(2):
            r.o_gdown[pl.ds(2 * p + j, 96, stride=6)] = v[:, 128 * j : 128 * j + 128]

    hops = [
        remote(src, dst, r.zf_s.at[i], r.zf_r.at[i], where)
        for i, (src, dst, where) in enumerate(
            ((r.s1z, r.r1z, near), (r.s2z, r.r2z, far), (r.s3z, r.r3z, first), (r.s4z, r.r4z, second))
        )
    ]

    def zf1():
        r.s1z[...] = nn(r.lh_upz[at(1 - z1, 192)], r.rh_up[:, 0:768]).astype(bf16)
        hops[0].start()

    def zf2():
        hops[0].wait_recv()
        rows = at(1 - z2, 96)
        r.s2z[...] = (r.k1z[rows] + r.r1z[rows].astype(f32)).astype(bf16)
        hops[1].start()

    def zf3():
        hops[1].wait_recv()
        for ref, half in ((r.s3z, 1 - b1), (r.k3z, b1)):
            rows = pl.ds(pl.multiple_of(96 * z2 + 48 * half, 48), 48)
            v = r.k1z[rows] + r.r1z[rows].astype(f32) + r.r2z[at(half, 48)].astype(f32)
            ref[...] = v.astype(ref.dtype)
        hops[2].start()

    def zf4():
        hops[2].wait_recv()
        v = r.k3z[...] + r.r3z[...].astype(f32)
        lower, upper = v[:24], v[24:]
        sent = jnp.where(b2 == 0, upper, lower)
        r.k4z[...] = jnp.where(b2 == 0, lower, upper)
        r.s4z[...] = jnp.concatenate([sent[:, :384], sent[:, 384:]], axis=0).astype(bf16)
        hops[3].start()

    def zf5():
        hops[3].wait_recv()
        got = r.r4z[...].astype(f32)
        for h in range(2):
            for j in range(3):
                k = 3 * h + j
                r.o_gup[pl.ds(k, 24, stride=24)] = (
                    r.k4z[:, 128 * k : 128 * k + 128]
                    + got[24 * h : 24 * h + 24, 128 * j : 128 * j + 128]
                )

    def put(row, v):
        for j in range(v.shape[1] // 128):
            part, line = divmod(row + j, 64)
            r.smf[part, line : line + 1] = v[:, 128 * j : 128 * j + 128]

    e = nt(r.rh_up[own], r.up_w[...])
    hat = r.hat2[...]
    grad_f = r.rh_down[own].astype(f32)
    g_res = grad_f + norm_rows_back(e, hat, r.std2[...], r.norm_gain[1:2])
    r.o_gtok[...] = g_res
    g_res_b = g_res.astype(bf16)
    r.rh_out[own] = g_res_b
    shares[10].start()
    g_mixed = nt(g_res_b, r.out_w[...])
    r.g_outer[...] = g_mixed * r.summed[...]
    g_summed = g_mixed * r.outer[...]
    r.g_sum[...] = g_summed
    r.stage[2] = jnp.transpose(g_summed).astype(bf16)
    trade(2, r.gc_in)

    def quarter(k):
        t = lax.rem(g + k, 4)
        return remote(r.smf.at[t], r.q_in.at[k - 1], r.q_s.at[k - 1], r.q_r.at[k - 1], (s, t))

    def eighth(k):
        t = peers[k]
        return remote(r.q_sum.at[at(t, 8)], r.o_in.at[k], r.o_s.at[k], r.o_r.at[k], (t, g))

    def spread(k, back):
        slot = r.ag.at[g, peers[k] if back else s]
        return remote(slot, slot, r.ag_s.at[k], r.ag_r.at[k], (peers[k], g))

    over_y = g + y_step
    first_slot, second_slot = r.ag.at[g], r.ag.at[over_y]
    y_send = remote(first_slot, first_slot, r.ag_s.at[7], r.ag_r.at[7], (s, over_y))
    y_back = remote(second_slot, second_slot, r.ag_s.at[7], r.ag_r.at[7], (s, over_y))
    c_send = [
        remote(slot, slot, r.ag_s.at[8 + i], r.ag_r.at[8 + i], (s, other))
        for i, slot in enumerate((first_slot, second_slot))
    ]
    third_slot, fourth_slot = r.ag.at[other], r.ag.at[other + y_step]
    c_back = [
        remote(slot, slot, r.ag_s.at[8 + i], r.ag_r.at[8 + i], (s, other))
        for i, slot in enumerate((third_slot, fourth_slot))
    ]

    put(AT_GAIN + 6, col_sum(e * hat))
    put(AT_SHIFT + 6, col_sum(e))
    put(AT_DOWNB, col_sum(grad_f))
    put(AT_UPB, col_sum(r.rh_up[own].astype(f32)))
    put(AT_OUTB, col_sum(g_res_b.astype(f32)))
    put(AT_SKIP, col_sum(g_summed * r.gf[...]))
    shares[8].wait_recv()
    shares[9].wait_recv()
    shares[12].wait_recv()
    r.s1z[...] = nn(r.lh_upz[at(1 - z1, 192)], r.rh_up[:, 0:768]).astype(bf16)
    hops[0].start()
    make_a(0, 3, r.lh_up, r.rh_up, 1)
    one_a(0).start()
    for copy in shares[0:6]:
        copy.wait_recv()
    for p in range(3):
        cols = pl.ds(256 * p, 256)
        r.s2b[p] = nn(r.lh_down[at(1 - b2, 384)], r.rh_down[:, cols]).astype(bf16)
    two_b(0).start()
    for p in range(3):
        cols = pl.ds(256 * p, 256)
        r.k2b[p] = nn(r.lh_down[at(b2, 384)], r.rh_down[:, cols])
    shares[7].wait_recv()
    shares[10].wait_recv()
    make_a(3, 1, r.lh_out, r.rh_out)
    r.k1z[...] = nn(r.lh_upz[at(z1, 192)], r.rh_up[:, 0:768])
    arrive(2, r.gc_in)
    r.ys[...] = (
        nn(r.gc_in[...], r.tables[2, high_half]) + nn(r.gc_in[...], r.tables[3, high_half])
    ) * (1.0 / 128.0)

    @pl.loop(0, 12)
    def _(tile):
        e = [pick(r.es, tile, b) for b in range(8)]
        d = [pick(r.ys, tile, b) for b in range(8)]
        for b in range(8):
            re, im = 0.0, 0.0
            for lag in range(8 - b):
                er, ei = e[lag]
                dr, di = d[b + lag]
                re = re + er * dr + ei * di
                im = im + er * di - ei * dr
            keep(r.es, tile, b, (re, im))

    g_long = by_table(r.es[...], 0, every, low_half)
    r.stage[3] = g_long.astype(bf16)
    trade(3, r.gl_in)
    one_a(1).start()
    two_b(1).start()
    zf2()
    stay_a(0, 3, r.lh_up, r.rh_up, 1)
    stay_a(3, 1, r.lh_out, r.rh_out)
    ph2_b(0)
    ph1_a(0)
    r.o_out[...] = r.o_out[...] + nn(r.act[...], r.down_w[...]) + r.down_b[...]
    arrive(3, r.gl_in)
    g_gated = r.skip[...] * r.g_sum[...] + jnp.transpose(r.gl_in[...].astype(f32))
    mixes = (r.g_outer[...], g_gated * r.value[...], g_gated * r.inner[...])
    for part in range(3):
        r.gm[own, 768 * part : 768 * part + 768] = mixes[part]
    first_rows = remote(
        r.gm.at[pl.ds(0, 2)], r.gm.at[pl.ds(ROWS, 2)], r.halo_s.at[1], r.halo_r.at[1], (s - 1, g)
    )

    @pl.when(s > 0)
    def _():
        first_rows.start()

    one_a(2).start()
    two_b(2).start()
    for part in range(3):
        cols = pl.ds(768 * part, 768)
        mix = r.gm[own, cols]
        put(AT_CONVB + 6 * part, col_sum(mix))
        for tap in range(3):
            put(
                AT_CONVW + 18 * tap + 6 * part,
                col_sum(mix * r.pp[pl.ds(HALO - 2 + tap, ROWS), cols]),
            )

    @pl.when(s < 7)
    def _():
        first_rows.wait_recv()

    @pl.when(s == 7)
    def _():
        r.gm[pl.ds(ROWS, 8)] = jnp.zeros((8, r.gm.shape[1]), f32)

    for part in range(3):
        cols = pl.ds(768 * part, 768)
        r.rh_in[own, cols] = (
            r.conv_w[0:1, cols] * r.gm[pl.ds(2, ROWS), cols]
            + r.conv_w[1:2, cols] * r.gm[pl.ds(1, ROWS), cols]
            + r.conv_w[2:3, cols] * r.gm[pl.ds(0, ROWS), cols]
        ).astype(bf16)
    shares[11].start()
    r.g_sum[...] = nt(r.rh_in[own], r.in_w[...])
    shares[6].wait_recv()
    shares[11].wait_recv()
    make_a(4, 3, r.lh_in, r.rh_in)
    one_a(4).start()
    one_a(5).start()
    one_a(6).start()
    zf3()
    ph1_a(1)
    ph2_b(1)
    ph3_b(0)
    stay_a(4, 3, r.lh_in, r.rh_in)
    ph1_a(2)
    ph2_b(2)
    e = r.g_sum[...]
    hat = r.hat1[...]
    put(AT_IN, col_sum(r.rh_in[own].astype(f32)))
    put(AT_GAIN, col_sum(e * hat))
    put(AT_SHIFT, col_sum(e))
    r.o_gtok[...] = r.o_gtok[...] + norm_rows_back(e, hat, r.std1[...], r.norm_gain[0:1])
    ph2_a(0)
    ph3_b(1)
    @pl.loop(0, 12)
    def _(tile):
        v = [pick(r.xs, tile, b) for b in range(8)]
        d = [pick(r.ys, tile, b) for b in range(8)]
        for lag in range(8):
            re, im = 0.0, 0.0
            for b in range(8 - lag):
                vr, vi = v[b]
                dr, di = d[b + lag]
                re = re + vr * dr + vi * di
                im = im + vr * di - vi * dr
            keep(r.xs, tile, lag, (re, im))

    r.es[...] = by_table(r.xs[...], 0, every, every)
    ph1_a(4)
    ph2_a(1)
    ph3_a(0)
    ph3_b(2)
    for b in range(8):
        cols = pl.ds(128 * b, 128)
        gt = r.es[96 * b : 96 * b + 96, 128:256]
        if b < 7:
            gt = gt + r.es[96 * b + 96 : 96 * b + 192, 0:128]
        r.dpre[:, cols] = gt * r.wind[:, cols]
        r.taps[:, cols] = r.taps[:, cols] * gt
    g_rate = -jnp.sum(r.taps[...] * place, axis=1, keepdims=True)
    g_last = nt_high(r.dpre[...], r.a3[...])
    for j in range(4):
        r.smf[j, 64:88, 0:64] = g_last[24 * j : 24 * j + 24]
        r.smf[j, 64:88, 64:65] = g_rate[24 * j : 24 * j + 24]
    ones = jnp.ones((8, 1024), f32)
    g_a = tn_high(last, r.dpre[...])
    for i, (u_ref, c_ref, a_ref) in enumerate(
        ((r.u3, r.c3, r.a2), (r.u2, r.c2, r.a1), (r.u1, r.c1, None))
    ):
        layer = 2 - i
        g_arg = g_a * c_ref[...]
        g_freq = nt_high(ones, g_arg * u_ref[...])[0:1]
        g_u = g_arg * freq_cols[:, layer : layer + 1]
        g_bias = nt_high(ones, g_u)[0:1]
        r.smf[1, layer : layer + 1, 64:128] = g_bias
        r.smf[1, 3 + layer : 4 + layer, 64:128] = g_freq
        if layer > 0:
            r.smf[0, 0:64, 64 * (layer - 1) : 64 * layer] = nt_high(a_ref[...], g_u)
            g_a = nn_high(r.filt_hidden[layer - 1], g_u)
        else:
            r.smf[1, 0:33, 0:64] = nt_high(r.feats[...], g_u)

    for k in range(1, 4):
        quarter(k).start()
    one_a(3).start()
    zf4()
    ph1_a(5)
    ph2_a(2)
    ph3_a(1)
    for k in range(1, 4):
        quarter(k).wait_recv()
    r.q_sum[...] = r.smf[g] + r.q_in[0] + r.q_in[1] + r.q_in[2]
    for k in range(7):
        eighth(k).start()
    ph2_a(4)
    ph1_a(6)
    ph3_a(2)
    for k in range(7):
        eighth(k).wait_recv()
    eighth_sum = r.q_sum[at(s, 8)] + jnp.sum(r.o_in[...], axis=0)
    r.ag[g, s] = jnp.concatenate([eighth_sum, r.q_sum[pl.ds(64, 24)]], axis=0).astype(bf16)
    for k in range(7):
        spread(k, False).start()
    ph2_a(5)
    ph3_a(4)
    ph1_a(3)
    ph2_a(6)
    ph3_a(5)
    for k in range(7):
        spread(k, True).wait_recv()
    y_send.start()
    ph2_a(3)
    ph3_a(6)
    ph4_b(0)
    ph4_b(1)
    ph4_b(2)
    ph3_a(3)
    zf5()
    ph4_a(0, r.o_gup, 6, 24)
    ph4_a(1, r.o_gup, 12, 24)
    ph4_a(2, r.o_gup, 18, 24)
    y_back.wait_recv()
    for copy in c_send:
        copy.start()
    ph4_a(4, r.o_gin, 0, 18)
    ph4_a(5, r.o_gin, 6, 18)
    ph4_a(6, r.o_gin, 12, 18)
    for copy in c_back:
        copy.wait_recv()
    r.o_small[...] = r.ag[...]
    ph4_a(3, r.o_gout, 0, 6)

    @pl.when(s < 7)
    def _():
        last_rows.wait_send()

    @pl.when(s > 0)
    def _():
        first_rows.wait_send()

    for copy in shares:
        copy.wait_send()

    @pl.loop(0, 4)
    def _(which):
        @pl.loop(1, 8)
        def _(k):
            remote(
                r.stage.at[which, pl.ds(0, 96)],
                r.gat.at[pl.ds(0, 96)],
                r.a2a_s.at[which, k - 1],
                r.a2a_r.at[which, k - 1],
                (s, other),
            ).wait_send()

    for copy in hops:
        copy.wait_send()

    @pl.loop(0, 7)
    def _(p):
        one_a(p).wait_send()
        two_a(p).wait_send()
        three_a(p).wait_send()
        four_a(p).wait_send()

    @pl.loop(0, 3)
    def _(p):
        two_b(p).wait_send()
        three_b(p).wait_send()
        four_b(p).wait_send()

    for k in range(1, 4):
        quarter(k).wait_send()

    for k in range(7):
        eighth(k).wait_send()
        spread(k, False).wait_send()

    y_send.wait_send()
    for copy in c_send:
        copy.wait_send()


def finish_kernel(
    i_out, i_gtok, i_gin, i_gout, i_gup, i_gdown, small,
    out, gtok, gain, shift, gin, in_b, conv_w, conv_b, first, hidden, bias, freq,
    last, decay, skip, gout, out_b, gup, up_b, gdown, down_b, sems,
):
    bulk = (
        (i_out, out.at[0]), (i_gtok, gtok.at[0]), (i_gin, gin), (i_gout, gout), (i_gup, gup), (i_gdown, gdown),
    )
    leave = [pltpu.make_async_copy(a, b, sems.at[i]) for i, (a, b) in enumerate(bulk)]
    for copy in leave:
        copy.start()
    slots = [[small[i, j].astype(f32) for j in range(8)] for i in range(4)]
    rows = jnp.concatenate([slots[i][j][0:8] for i in range(4) for j in range(8)], axis=0)

    def fetch(at_row, dest, dest_row, wide):
        for j in range(wide):
            dest[dest_row : dest_row + 1, 128 * j : 128 * j + 128] = rows[at_row + j : at_row + j + 1]

    def line(at_row, dest):
        dest[...] = rows[at_row : at_row + dest.shape[0] // 128].reshape(dest.shape[0])

    for i in range(2):
        fetch(AT_GAIN + 6 * i, gain, i, 6)
        fetch(AT_SHIFT + 6 * i, shift, i, 6)
        hidden[i] = rows[AT_HID : AT_HID + 64, 64 * i : 64 * i + 64]
    for i in range(3):
        fetch(AT_CONVW + 18 * i, conv_w, i, 18)
    line(AT_IN, in_b)
    line(AT_CONVB, conv_b)
    line(AT_SKIP, skip)
    line(AT_OUTB, out_b)
    line(AT_UPB, up_b)
    line(AT_DOWNB, down_b)
    first[...] = rows[AT_FIRST : AT_FIRST + 33, 0:64]
    bias[...] = rows[AT_FIRST : AT_FIRST + 3, 64:128]
    freq[...] = rows[AT_FIRST + 3 : AT_FIRST + 6, 64:128]
    channels = jnp.transpose(
        jnp.concatenate([slots[j][i][8:32] for i in range(8) for j in range(4)], axis=0)
    )
    last[...] = channels[0:64]
    decay[...] = channels[64:65].reshape(768)
    for copy in leave:
        copy.wait()


def one_kernel_body(tokens, out_grad, norm_gain, norm_bias, in_weight, in_bias, conv_weight, conv_bias,
                    filt_first, filt_hidden, filt_bias, filt_freq, filt_last, decay_rates, skip_scale,
                    out_weight, out_bias, up_weight, up_bias, down_weight, down_bias):
    width, hidden = up_weight.shape
    length = tokens.shape[1] * lax.axis_size("seq")
    any_spec = pl.BlockSpec(memory_space=pl.ANY)
    vmem_spec = pl.BlockSpec(memory_space=pltpu.VMEM)

    def vm(*shape, dtype=f32):
        return pltpu.VMEM(shape, dtype)

    def dma(*shape):
        return pltpu.SemaphoreType.DMA(shape)

    def shape(*dims):
        return jax.ShapeDtypeStruct(dims, f32)

    outs = pl.pallas_call(
        step_kernel,
        out_shape=[
            vm(128, width), vm(128, width), vm(432, 128), vm(144, 128),
            vm(576, 128), vm(576, 128), vm(4, 8, 32, 128, dtype=bf16),
        ],
        in_specs=[any_spec] * 23,
        out_specs=[vmem_spec] * 7,
        scratch_shapes=[vm(*dims) for _, dims in SMALL_ARGS]
        + [vm(*dims, dtype=dtype) for _, dims, dtype in SCRATCH]
        + [dma(*dims) for _, dims in SEMAPHORES],
        compiler_params=pltpu.CompilerParams(
            collective_id=0, has_side_effects=True, vmem_limit_bytes=60 * 1024 * 1024
        ),
        name="hyena_step",
    )(
        tokens, out_grad, in_weight, out_weight, up_weight, down_weight,
        jnp.asarray(fourier_tables()),
        norm_gain, norm_bias, in_bias, conv_weight, conv_bias,
        jnp.asarray(feature_table(length, (filt_first.shape[0] - 1) // 2)),
        filt_first, filt_hidden, filt_bias, filt_freq, filt_last, decay_rates, skip_scale, out_bias,
        up_bias, down_bias,
    )
    done = pl.pallas_call(
        finish_kernel,
        out_shape=[
            shape(1, 128, width), shape(1, 128, width), shape(2, width), shape(2, width), shape(432, 128),
            shape(3 * width), shape(3, 3 * width), shape(3 * width), shape(33, 64), shape(2, 64, 64),
            shape(3, 64), shape(3, 64), shape(64, width), shape(width), shape(width), shape(144, 128),
            shape(width), shape(576, 128), shape(hidden), shape(576, 128), shape(width),
        ],
        in_specs=[vmem_spec] * 7,
        out_specs=[any_spec, any_spec, vmem_spec, vmem_spec, any_spec]
        + [vmem_spec] * 10
        + [any_spec, vmem_spec, any_spec, vmem_spec, any_spec, vmem_spec],
        scratch_shapes=[dma(6)],
        compiler_params=pltpu.CompilerParams(vmem_limit_bytes=32 * 1024 * 1024),
        name="hyena_finish",
    )(*outs)
    flat = (4, 15, 17, 19)
    return tuple(v.reshape(-1) if i in flat else v for i, v in enumerate(done))


def solution(mesh):
    small_mesh = mesh.shape["seq"] == 8 and mesh.shape["grp"] == 4
    return jax.shard_map(
        one_kernel_body if small_mesh else body,
        mesh=mesh,
        in_specs=(P("grp", "seq", None), P("grp", "seq", None)) + (P(),) * 19,
        out_specs=(
            P("grp", "seq", None),
            P("grp", "seq", None),
            P(),
            P(),
            P(("seq", "grp")),
        )
        + (P(),) * 10
        + (P(("seq", "grp")), P(), P(("seq", "grp")), P(), P(("seq", "grp")), P()),
        check_vma=False,
    )
```

```python
import math
import types

import jax
import jax.numpy as jnp
import ml_dtypes
import numpy as np
from jax import lax
from jax.experimental import pallas as pl
from jax.experimental.pallas import tpu as pltpu
from jax.sharding import PartitionSpec as P

epsilon = 1e-05


def shifted(array, axis, by):
    peers = lax.axis_size(axis)
    pairs = [(i, i + by) for i in range(peers) if 0 <= i + by < peers]
    return lax.ppermute(array, axis, pairs)


def highest(left_mat, right_mat):
    return jnp.dot(
        left_mat, right_mat, precision=lax.Precision.HIGHEST, preferred_element_type=jnp.float32
    )


def highest_t(left_mat, right_mat):
    return lax.dot_general(
        left_mat,
        right_mat,
        (((0,), (0,)), ((), ())),
        precision=lax.Precision.HIGHEST,
        preferred_element_type=jnp.float32,
    )


def rows_t(left_mat, right_mat):
    return lax.dot_general(
        left_mat, right_mat, (((0,), (0,)), ((), ())), preferred_element_type=jnp.float32
    )


def back_mul(grad_in, weight_mat):
    return lax.dot_general(
        grad_in, weight_mat, (((1,), (1,)), ((), ())), preferred_element_type=jnp.float32
    )


def layer_norm(values, gain_row, shift_row):
    row_mean = jnp.mean(values, axis=-1, keepdims=True)
    centred = values - row_mean
    inv_std = lax.rsqrt(jnp.mean(centred * centred, axis=-1, keepdims=True) + epsilon)
    normed = centred * inv_std
    return (normed * gain_row + shift_row, normed, inv_std)


def norm_back(grad_in, normed, inv_std, gain_row):
    scaled = grad_in * gain_row
    centred_grad = (
        scaled
        - jnp.mean(scaled, axis=-1, keepdims=True)
        - normed * jnp.mean(scaled * normed, axis=-1, keepdims=True)
    )
    return (centred_grad * inv_std, jnp.sum(grad_in * normed, axis=0), jnp.sum(grad_in, axis=0))


def smooth(values):
    return jax.nn.gelu(values, approximate=False)


def filter_rows(params, positions, length):
    filt_first, filt_hidden, filt_bias, filt_freq, filt_last, decay_rates = params
    place = positions.astype(jnp.float32)
    bands = (filt_first.shape[0] - 1) // 2
    band = 0.0001 + jnp.arange(bands, dtype=jnp.float32) * ((bands - 1 - 0.0001) / (bands - 1))
    omega = place[:, None] * (2.0 * math.pi / length)
    phase = omega * band[None, :]
    feats = jnp.concatenate(
        [place[:, None] / (length - 1), jnp.cos(phase), -jnp.sin(phase)], axis=1
    )
    act_one = jnp.sin(filt_freq[0] * (highest(feats, filt_first) + filt_bias[0]))
    act_two = jnp.sin(filt_freq[1] * (highest(act_one, filt_hidden[0]) + filt_bias[1]))
    act_three = jnp.sin(filt_freq[2] * (highest(act_two, filt_hidden[1]) + filt_bias[2]))
    window = jnp.exp(-decay_rates[None, :] * jnp.maximum(place, 0.0)[:, None])
    return highest(act_three, filt_last) * window


def body(
    tokens,
    out_grad,
    norm_gain,
    norm_bias,
    in_weight,
    in_bias,
    conv_weight,
    conv_bias,
    filt_first,
    filt_hidden,
    filt_bias,
    filt_freq,
    filt_last,
    decay_rates,
    skip_scale,
    out_weight,
    out_bias,
    up_weight,
    up_bias,
    down_weight,
    down_bias,
):
    row_count = tokens.shape[1]
    model_width = tokens.shape[2]
    seq_count = lax.axis_size("seq")
    length = row_count * seq_count
    fft_span = 2 * row_count
    fparams = (filt_first, filt_hidden, filt_bias, filt_freq, filt_last, decay_rates)
    fft_grid = jnp.arange(fft_span, dtype=jnp.int32)
    angles = (fft_grid[:, None] * fft_grid[None, :] % fft_span).astype(jnp.float32) * (
        2.0 * math.pi / fft_span
    )
    cos_full = jnp.cos(angles)
    sin_full = jnp.sin(angles)
    cos_left = cos_full[:, :row_count]
    sin_left = sin_full[:, :row_count]
    cos_low = cos_full[row_count:, :]
    sin_low = sin_full[row_count:, :]

    def segment(params, lag_step):
        positions = (lag_step - 1) * row_count + fft_grid
        keep_mask = (positions >= 0).astype(jnp.float32)
        return filter_rows(params, positions, length) * keep_mask[:, None]

    def forward_add(lag_step, source, totals):
        filter_taps = segment(fparams, lag_step)
        g_re = highest(cos_full, filter_taps)
        g_im = -highest(sin_full, filter_taps)
        source_f = source.astype(jnp.float32)
        s_re = highest(cos_left, source_f)
        s_im = -highest(sin_left, source_f)
        return (totals[0] + g_re * s_re - g_im * s_im, totals[1] + g_re * s_im + g_im * s_re)

    inputs = tokens[0].astype(jnp.float32)
    normed1, hat_one, std_one = layer_norm(inputs, norm_gain[0], norm_bias[0])
    normed1_b = normed1.astype(jnp.bfloat16)
    projected = (
        jnp.dot(normed1_b, in_weight, preferred_element_type=jnp.float32) + in_bias
    ).astype(jnp.bfloat16)
    before = shifted(projected[row_count - 2 :], "seq", 1)
    padded = jnp.concatenate([before, projected], axis=0).astype(jnp.float32)
    mixed_conv = (
        conv_weight[0] * padded[:row_count]
        + conv_weight[1] * padded[1 : row_count + 1]
        + conv_weight[2] * padded[2:]
        + conv_bias
    )
    outer_part = mixed_conv[:, :model_width]
    inner_part = mixed_conv[:, model_width : 2 * model_width]
    value_part = mixed_conv[:, 2 * model_width :]
    gated_b = (inner_part * value_part).astype(jnp.bfloat16)
    gated_f = gated_b.astype(jnp.float32)
    zero_totals = (
        jnp.zeros((fft_span, model_width), jnp.float32),
        jnp.zeros((fft_span, model_width), jnp.float32),
    )
    first_pass = forward_add(0, gated_b, zero_totals)

    def forward_step(lag_step, loop_carry):
        source, tot_re, tot_im = loop_carry
        source = shifted(source, "seq", 1)
        tot_re, tot_im = forward_add(lag_step, source, (tot_re, tot_im))
        return (source, tot_re, tot_im)

    unused_src, tot_re, tot_im = lax.fori_loop(
        1, seq_count, forward_step, (gated_b, first_pass[0], first_pass[1])
    )
    conv_out = (highest(cos_low, tot_re) - highest(sin_low, tot_im)) / fft_span
    summed = conv_out + skip_scale * gated_f
    mixed_out_b = (outer_part * summed).astype(jnp.bfloat16)
    residual = (
        inputs + jnp.dot(mixed_out_b, out_weight, preferred_element_type=jnp.float32) + out_bias
    )
    normed2, hat_two, std_two = layer_norm(residual, norm_gain[1], norm_bias[1])
    normed2_b = normed2.astype(jnp.bfloat16)
    pre_act = jnp.dot(normed2_b, up_weight, preferred_element_type=jnp.float32) + up_bias
    act_val, gelu_back = jax.vjp(smooth, pre_act)
    act_b = act_val.astype(jnp.bfloat16)
    result = residual + jnp.dot(act_b, down_weight, preferred_element_type=jnp.float32) + down_bias
    grad_out_b = out_grad[0]
    grad_out_f = grad_out_b.astype(jnp.float32)
    g_down = rows_t(act_b, grad_out_b)
    g_down_bias = jnp.sum(grad_out_f, axis=0)
    g_act = back_mul(grad_out_b, down_weight)
    g_pre_b = gelu_back(g_act)[0].astype(jnp.bfloat16)
    g_up = rows_t(normed2_b, g_pre_b)
    g_up_bias = jnp.sum(g_pre_b.astype(jnp.float32), axis=0)
    g_norm_two = back_mul(g_pre_b, up_weight)
    g_res_norm, g_gain_two, g_shift_two = norm_back(g_norm_two, hat_two, std_two, norm_gain[1])
    g_resid = grad_out_f + g_res_norm
    g_resid_b = g_resid.astype(jnp.bfloat16)
    g_outw = rows_t(mixed_out_b, g_resid_b)
    g_out_bias = jnp.sum(g_resid_b.astype(jnp.float32), axis=0)
    g_mixed = back_mul(g_resid_b, out_weight)
    g_outer = g_mixed * summed
    g_summed = g_mixed * outer_part
    g_skip = jnp.sum(g_summed * gated_f, axis=0)
    g_conv_b = g_summed.astype(jnp.bfloat16)
    v_re = highest(cos_left, gated_f)
    v_im = -highest(sin_left, gated_f)

    def backward_add(lag_step, source, loop_carry):
        tot_re, tot_im, grad_acc = loop_carry
        source_f = source.astype(jnp.float32)
        d_re = highest_t(cos_low, source_f) / fft_span
        d_im = -highest_t(sin_low, source_f) / fft_span

        def lag_taps(params):
            return segment(params, lag_step)

        filter_taps, taps_pull = jax.vjp(lag_taps, fparams)
        g_re = highest(cos_full, filter_taps)
        g_im = -highest(sin_full, filter_taps)
        tot_re = tot_re + g_re * d_re + g_im * d_im
        tot_im = tot_im - g_im * d_re + g_re * d_im
        s_re = v_re * d_re + v_im * d_im
        s_im = v_re * d_im - v_im * d_re
        d_taps = highest_t(cos_full, s_re) - highest_t(sin_full, s_im)
        more_grads = taps_pull(d_taps)[0]
        grad_acc = jax.tree.map(jnp.add, grad_acc, more_grads)
        return (tot_re, tot_im, grad_acc)

    zero_grads = jax.tree.map(jnp.zeros_like, fparams)
    start_carry = (zero_totals[0], zero_totals[1], zero_grads)
    first_back = backward_add(0, g_conv_b, start_carry)

    def backward_step(lag_step, loop_carry):
        source, tot_re, tot_im, grad_acc = loop_carry
        source = shifted(source, "seq", -1)
        tot_re, tot_im, grad_acc = backward_add(lag_step, source, (tot_re, tot_im, grad_acc))
        return (source, tot_re, tot_im, grad_acc)

    unused_src, back_re, back_im, cycle_grads = lax.fori_loop(
        1, seq_count, backward_step, (g_conv_b,) + first_back
    )
    g_long = highest_t(cos_left, back_re) - highest_t(sin_left, back_im)
    g_gated = g_summed * skip_scale + g_long
    g_mix = jnp.concatenate([g_outer, g_gated * value_part, g_gated * inner_part], axis=1)
    g_conv_bias = jnp.sum(g_mix, axis=0)
    g_conv_w = jnp.stack(
        [
            jnp.sum(g_mix * padded[tap_index : tap_index + row_count], axis=0)
            for tap_index in range(3)
        ]
    )
    g_pad = (
        jnp.pad(conv_weight[0] * g_mix, ((0, 2), (0, 0)))
        + jnp.pad(conv_weight[1] * g_mix, ((1, 1), (0, 0)))
        + jnp.pad(conv_weight[2] * g_mix, ((2, 0), (0, 0)))
    )
    after_rows = shifted(g_pad[:2], "seq", -1)
    g_proj_b = (g_pad[2:] + jnp.pad(after_rows, ((row_count - 2, 0), (0, 0)))).astype(jnp.bfloat16)
    g_inw = rows_t(normed1_b, g_proj_b)
    g_in_bias = jnp.sum(g_proj_b.astype(jnp.float32), axis=0)
    g_norm_one = back_mul(g_proj_b, in_weight)
    g_in_norm, g_gain_one, g_shift_one = norm_back(g_norm_one, hat_one, std_one, norm_gain[0])
    g_tokens = g_resid + g_in_norm
    small_grads = lax.psum(
        (
            jnp.stack([g_gain_one, g_gain_two]),
            jnp.stack([g_shift_one, g_shift_two]),
            g_in_bias,
            g_conv_w,
            g_conv_bias,
            cycle_grads[0],
            cycle_grads[1],
            cycle_grads[2],
            cycle_grads[3],
            cycle_grads[4],
            cycle_grads[5],
            g_skip,
            g_out_bias,
            g_up_bias,
            g_down_bias,
        ),
        ("seq", "grp"),
    )
    large_grads = (
        lax.psum_scatter(g_inw.reshape(-1), ("seq", "grp"), scatter_dimension=0, tiled=True),
        lax.psum_scatter(g_outw.reshape(-1), ("seq", "grp"), scatter_dimension=0, tiled=True),
        lax.psum_scatter(g_up.reshape(-1), ("seq", "grp"), scatter_dimension=0, tiled=True),
        lax.psum_scatter(g_down.reshape(-1), ("seq", "grp"), scatter_dimension=0, tiled=True),
    )
    return (
        result[None],
        g_tokens[None],
        small_grads[0],
        small_grads[1],
        large_grads[0],
        small_grads[2],
        small_grads[3],
        small_grads[4],
        small_grads[5],
        small_grads[6],
        small_grads[7],
        small_grads[8],
        small_grads[9],
        small_grads[10],
        small_grads[11],
        large_grads[1],
        small_grads[12],
        large_grads[2],
        small_grads[13],
        large_grads[3],
        small_grads[14],
    )


f32 = jnp.float32
bf16 = jnp.bfloat16
MESH_ID = pl.DeviceIdType.MESH
HIGH = lax.Precision.HIGHEST
ROWS = 128
HALO = 16


def nn(a, b):
    return jnp.dot(a, b, preferred_element_type=f32)


def nt(a, b):
    return lax.dot_general(a, b, (((1,), (1,)), ((), ())), preferred_element_type=f32)


def nn_high(a, b):
    return jnp.dot(a, b, precision=HIGH, preferred_element_type=f32)


def nt_high(a, b):
    return lax.dot_general(
        a, b, (((1,), (1,)), ((), ())), precision=HIGH, preferred_element_type=f32
    )


def tn_high(a, b):
    return lax.dot_general(
        a, b, (((0,), (0,)), ((), ())), precision=HIGH, preferred_element_type=f32
    )


def two(v):
    high = v.astype(bf16)
    return high, (v - high.astype(f32)).astype(bf16)


def sin_cos(v):
    k = jnp.floor(v * (1.0 / math.pi) + 0.5)
    r = ((v - k * 3.140625) - k * 0.0009670257568359375) - k * 6.2771141529083252e-07
    sign = 1.0 - 2.0 * (k - 2.0 * jnp.floor(k * 0.5))
    q = r * r
    s = 1.0 / math.factorial(13)
    for order in (11, 9, 7, 5, 3):
        s = 1.0 / math.factorial(order) - s * q
    s = r - r * q * s
    c = 1.0 / math.factorial(12)
    for order in (10, 8, 6, 4, 2):
        c = 1.0 / math.factorial(order) - c * q
    c = 1.0 - q * c
    return s * sign, c * sign


def gelu_both(v):
    a = jnp.abs(v)
    t = 1.0 / (1.0 + (0.3275911 / math.sqrt(2.0)) * a)
    poly = t * (
        0.254829592
        + t * (-0.284496736 + t * (1.421413741 + t * (-1.453152027 + t * 1.061405429)))
    )
    bell = jnp.exp(-0.5 * v * v)
    tail = 0.5 * poly * bell
    phi = jnp.where(v >= 0, 1.0 - tail, tail)
    return v * phi, phi + v * bell * (1.0 / math.sqrt(2.0 * math.pi))


def col_sum(v):
    return jnp.sum(v, axis=0, keepdims=True)


def row_mean(v):
    return jnp.mean(v, axis=1, keepdims=True)


def norm_rows(v):
    centred = v - row_mean(v)
    inv = lax.rsqrt(row_mean(centred * centred) + epsilon)
    return centred * inv, inv


def norm_rows_back(e, hat, inv, gain):
    k = e * gain
    return (k - row_mean(k) - hat * row_mean(k * hat)) * inv


def fourier_tables():
    bins = np.arange(128) + 0.5
    angle = 2.0 * np.pi * bins[:, None] * np.arange(256)[None, :] / 256
    full = np.concatenate([np.cos(angle), -np.sin(angle)], axis=0).astype(np.float32)
    out = []
    for mat in (full, full.T):
        high = mat.astype(ml_dtypes.bfloat16)
        out += [high, (mat - high.astype(np.float32)).astype(ml_dtypes.bfloat16)]
    return np.stack(out)


def feature_table(length, bands):
    place = np.arange(length)
    band = 1e-4 + np.arange(bands) * ((bands - 1 - 1e-4) / (bands - 1))
    phase = band[:, None] * (2.0 * np.pi * place / length)[None, :]
    return np.concatenate(
        [(place / (length - 1))[None], np.cos(phase), -np.sin(phase)], axis=0
    ).astype(np.float32)


AT_HID, AT_FIRST, AT_GAIN, AT_SHIFT, AT_IN, AT_CONVW, AT_CONVB = 0, 64, 97, 109, 121, 139, 193
AT_SKIP, AT_OUTB, AT_UPB, AT_DOWNB = 211, 217, 223, 247

SMALL_ARGS = (
    ("norm_gain", (2, 768)), ("norm_bias", (2, 768)), ("in_b1", (2304,)), ("conv_w", (3, 2304)),
    ("conv_b1", (2304,)), ("feats", (33, 1024)), ("filt_first", (33, 64)), ("filt_hidden", (2, 64, 64)),
    ("filt_bias", (3, 64)), ("filt_freq", (3, 64)), ("filt_last", (64, 768)), ("decay1", (768,)),
    ("skip1", (768,)), ("out_b1", (768,)), ("up_b1", (3072,)), ("down_b1", (768,)),
)

SCRATCH = (
    ("in_w", (768, 2304), bf16), ("out_w", (768, 768), bf16), ("up_w", (768, 3072), bf16),
    ("down_w", (3072, 768), bf16), ("tables", (4, 256, 256), bf16),
    ("in_b", (1, 2304), f32), ("conv_b", (1, 2304), f32), ("skip", (1, 768), f32),
    ("out_b", (1, 768), f32), ("up_b", (1, 3072), f32), ("down_b", (1, 768), f32),
    ("tok", (144, 768), bf16), ("n1", (144, 768), bf16), ("hat1", (128, 768), f32),
    ("std1", (128, 1), f32), ("pp", (144, 2304), f32), ("outer", (128, 768), f32),
    ("inner", (128, 768), f32), ("value", (128, 768), f32), ("gf", (128, 768), f32),
    ("stage", (4, 768, 128), bf16), ("gat", (768, 128), bf16), ("co_in", (768, 128), bf16),
    ("gc_in", (768, 128), bf16), ("gl_in", (768, 128), bf16),
    ("xs", (768, 256), f32), ("es", (768, 256), f32), ("ys", (768, 256), f32),
    ("hw_high", (768, 256), bf16), ("hw_low", (768, 256), bf16),
    ("taps", (96, 1024), f32), ("wind", (96, 1024), f32), ("dpre", (96, 1024), f32),
    ("last_t", (768, 64), f32), ("rate_t", (768, 8), f32),
    ("a1", (64, 1024), f32), ("a2", (64, 1024), f32), ("a3", (64, 1024), f32),
    ("c1", (64, 1024), f32), ("c2", (64, 1024), f32), ("c3", (64, 1024), f32),
    ("u1", (64, 1024), f32), ("u2", (64, 1024), f32), ("u3", (64, 1024), f32),
    ("g_act", (128, 3072), f32), ("act", (128, 3072), bf16), ("summed", (128, 768), f32),
    ("hat2", (128, 768), f32), ("std2", (128, 1), f32),
    ("g_sum", (128, 768), f32), ("g_outer", (128, 768), f32),
    ("gm", (136, 2304), f32),
    ("at_down", (2, 1536, 128), bf16), ("at_up", (2, 384, 128), bf16), ("at_upz", (2, 384, 128), bf16), ("at_in", (2, 384, 128), bf16),
    ("at_out", (2, 384, 128), bf16), ("lh_down", (768, 512), bf16), ("lh_up", (384, 256), bf16), ("lh_upz", (384, 256), bf16),
    ("lh_in", (384, 256), bf16), ("lh_out", (384, 256), bf16), ("rh_down", (512, 768), bf16),
    ("rh_up", (256, 3072), bf16), ("rh_in", (256, 2304), bf16), ("rh_out", (256, 768), bf16),
    ("s1a", (7, 192, 768), bf16), ("k1a", (7, 192, 768), f32), ("r1a", (7, 192, 768), bf16),
    ("s2a", (7, 96, 768), bf16), ("r2a", (7, 96, 768), bf16), ("s3a", (7, 4, 48, 384), bf16),
    ("r3a", (7, 2, 48, 384), bf16), ("s4a", (7, 48, 384), bf16), ("r4a", (7, 48, 384), bf16),
    ("s2b", (3, 384, 256), bf16), ("k2b", (3, 384, 256), f32), ("r2b", (3, 384, 256), bf16),
    ("s3b", (3, 4, 96, 256), bf16), ("r3b", (3, 2, 96, 256), bf16), ("s4b", (3, 96, 256), bf16),
    ("r4b", (3, 96, 256), bf16),
    ("s1z", (192, 768), bf16), ("k1z", (192, 768), f32), ("r1z", (192, 768), bf16),
    ("s2z", (96, 768), bf16), ("r2z", (96, 768), bf16), ("k3z", (48, 768), f32),
    ("s3z", (48, 768), bf16), ("r3z", (48, 768), bf16), ("k4z", (24, 768), f32),
    ("s4z", (48, 384), bf16), ("r4z", (48, 384), bf16),
    ("smf", (4, 88, 128), f32), ("q_in", (3, 88, 128), f32), ("q_sum", (88, 128), f32),
    ("o_in", (7, 8, 128), f32), ("ag", (4, 8, 32, 128), bf16),

)

SEMAPHORES = (
    ("ld", (8,)), ("ls", (16,)), ("a2a_s", (4, 7)), ("a2a_r", (4, 7)), ("halo_s", (2,)), ("halo_r", (2,)),
    ("pair_s", (13,)), ("pair_r", (13,)), ("p1_s", (8,)), ("p1_r", (8,)), ("p2_s", (11,)),
    ("p2_r", (11,)), ("p3_s", (11,)), ("p3_r", (11,)), ("p4_s", (11,)), ("p4_r", (11,)),
    ("zf_s", (4,)), ("zf_r", (4,)), ("q_s", (3,)), ("q_r", (3,)),
    ("o_s", (7,)), ("o_r", (7,)), ("ag_s", (10,)), ("ag_r", (10,)),
)


def step_kernel(*refs):
    names = ["tokens", "out_grad", "in_w_h", "out_w_h", "up_w_h", "down_w_h", "tables_h"]
    names += ["h_" + name for name, _ in SMALL_ARGS]
    names += ["o_out", "o_gtok", "o_gin", "o_gout", "o_gup", "o_gdown", "o_small"]
    names += [name for name, _ in SMALL_ARGS]
    names += [name for name, _, _ in SCRATCH] + [name for name, _ in SEMAPHORES]
    r = types.SimpleNamespace(**dict(zip(names, refs, strict=True)))

    s = lax.axis_index("seq")
    g = lax.axis_index("grp")
    z, x = lax.div(s, 2), lax.rem(s, 2)
    y, c = lax.div(g, 2), lax.rem(g, 2)
    other = g + 1 - 2 * c
    x_step, y_step = 1 - 2 * x, 2 * (1 - 2 * y)
    first = (s + (1 - c) * x_step, g + c * y_step)
    second = (s + c * x_step, g + (1 - c) * y_step)
    cross = (s + c * x_step, other + (1 - c) * y_step)
    b1 = (1 - c) * x + c * y
    b2 = (1 - c) * y + c * x
    z2, z1 = lax.div(z, 2), lax.rem(z, 2)
    near, far = (s + 2 - 4 * z1, g), (s + 4 - 8 * z2, g)

    def at(index, size):
        return pl.ds(pl.multiple_of(index * size, size), size)

    def remote(src, dst, ss, rs, where):
        return pltpu.make_async_remote_copy(
            src_ref=src,
            dst_ref=dst,
            send_sem=ss,
            recv_sem=rs,
            device_id=where,
            device_id_type=MESH_ID,
        )

    bar = pltpu.get_barrier_semaphore()

    @pl.loop(1, 8)
    def _(k):
        pl.semaphore_signal(
            bar, inc=1, device_id=(lax.rem(s + k, 8), g), device_id_type=MESH_ID
        )

    @pl.loop(1, 4)
    def _(k):
        pl.semaphore_signal(
            bar, inc=1, device_id=(s, lax.rem(g + k, 4)), device_id_type=MESH_ID
        )

    pl.semaphore_signal(bar, inc=1, device_id=(s + x_step, other), device_id_type=MESH_ID)

    own = pl.ds(0, ROWS)
    loads = [
        pltpu.make_async_copy(r.tokens.at[0], r.tok.at[pl.ds(HALO, ROWS)], r.ld.at[0]),
        pltpu.make_async_copy(r.in_w_h, r.in_w, r.ld.at[1]),
        pltpu.make_async_copy(r.out_grad.at[0], r.rh_down.at[own], r.ld.at[2]),
        pltpu.make_async_copy(r.tables_h, r.tables, r.ld.at[3]),
        pltpu.make_async_copy(r.down_w_h, r.down_w, r.ld.at[4]),
        pltpu.make_async_copy(r.out_w_h, r.out_w, r.ld.at[5]),
        pltpu.make_async_copy(r.up_w_h, r.up_w, r.ld.at[6]),
    ]
    small_loads = [
        pltpu.make_async_copy(getattr(r, "h_" + name), getattr(r, name), r.ls.at[i])
        for i, (name, _) in enumerate(SMALL_ARGS)
    ]
    loads[0].start()
    for copy in small_loads[:2]:
        copy.start()
    loads[1].start()
    for copy in small_loads[2:]:
        copy.start()
    loads[2].start()
    loads[3].start()

    def share(index, src, dst, where):
        return remote(src, dst, r.pair_s.at[index], r.pair_r.at[index], where)

    block2, block3, block4 = pl.ds(ROWS, ROWS), pl.ds(2 * ROWS, ROWS), pl.ds(3 * ROWS, ROWS)
    shares = [
        share(0, r.rh_down.at[own], r.rh_down.at[block2], (s, other)),
        share(1, r.rh_down.at[own], r.rh_down.at[block3], first),
        share(2, r.rh_down.at[own], r.rh_down.at[block4], cross),
        share(3, r.at_down.at[1 - c, at(b2, 768)], r.lh_down.at[:, block2], (s, other)),
        share(4, r.at_down.at[c, at(1 - b1, 768)], r.lh_down.at[:, block3], first),
        share(5, r.at_down.at[1 - c, at(1 - b2, 768)], r.lh_down.at[:, block4], cross),
        share(6, r.at_in.at[1 - c], r.lh_in.at[:, block2], (s, other)),
        share(7, r.at_out.at[1 - c], r.lh_out.at[:, block2], (s, other)),
        share(8, r.at_up.at[1 - c], r.lh_up.at[:, block2], (s, other)),
        share(9, r.rh_up.at[own], r.rh_up.at[block2], (s, other)),
        share(10, r.rh_out.at[own], r.rh_out.at[block2], (s, other)),
        share(11, r.rh_in.at[own], r.rh_in.at[block2], (s, other)),
        share(12, r.at_upz.at[1 - c], r.lh_upz.at[:, block2], (s, other)),
    ]

    def order_rows(v, halves, z_halves=None):
        t = jnp.transpose(v)
        bits = [(i, j) for i in range(2) for j in range(2)]
        for core in range(2):

            def block(i1, i2, iz):
                ix, iy = (i1, i2) if core == 0 else (i2, i1)
                at_row = 24 * (iz * 8 + ix * 4 + iy * 2 + core)
                return t[at_row : at_row + 24]

            blocks = [block(i1, i2, iz) for i1, i2 in bits for iz in range(4)]
            halves[core] = jnp.concatenate(blocks, axis=0).astype(bf16)
            if z_halves is not None:
                blocks = [block(i1, i2, 2 * j2 + j1) for j1, j2 in bits for i1, i2 in bits]
                z_halves[core] = jnp.concatenate(blocks, axis=0).astype(bf16)

    loads[0].wait()
    hat, inv = norm_rows(r.tok[pl.ds(HALO, ROWS)].astype(f32))
    r.hat1[...] = hat
    r.std1[...] = inv
    small_loads[0].wait()
    small_loads[1].wait()
    own_norm = (hat * r.norm_gain[0:1] + r.norm_bias[0:1]).astype(bf16)
    r.n1[pl.ds(HALO, ROWS)] = own_norm
    pl.semaphore_wait(bar, 11)
    last_rows = remote(
        r.tok.at[pl.ds(ROWS, HALO)],
        r.tok.at[pl.ds(0, HALO)],
        r.halo_s.at[0],
        r.halo_r.at[0],
        (s + 1, g),
    )

    @pl.when(s < 7)
    def _():
        last_rows.start()

    order_rows(own_norm.astype(f32), r.at_in)
    r.lh_in[:, own] = r.at_in[c]
    for copy in small_loads[2:]:
        copy.wait()
    for line, flat in (
        (r.in_b, r.in_b1), (r.conv_b, r.conv_b1), (r.skip, r.skip1),
        (r.out_b, r.out_b1), (r.up_b, r.up_b1), (r.down_b, r.down_b1),
    ):
        line[...] = flat[...].reshape(line.shape)

    @pl.when(s > 0)
    def _():
        last_rows.wait_recv()

    @pl.when(s == 0)
    def _():
        r.tok[pl.ds(0, HALO)] = jnp.zeros((HALO, r.tok.shape[1]), bf16)

    hat, inv = norm_rows(r.tok[pl.ds(0, HALO)].astype(f32))
    r.n1[pl.ds(0, HALO)] = (hat * r.norm_gain[0:1] + r.norm_bias[0:1]).astype(bf16)
    loads[1].wait()
    for copy in loads[4:]:
        copy.start()
    inside = jnp.where(s > 0, 1.0, 0.0).astype(f32)
    for part, dest in enumerate((r.outer, r.inner, r.value)):
        cols = pl.ds(768 * part, 768)
        proj = (nn(r.n1[...], r.in_w[:, cols]) + r.in_b[:, cols]).astype(bf16).astype(f32)
        r.pp[pl.ds(0, HALO), cols] = proj[:HALO] * inside
        r.pp[pl.ds(HALO, ROWS), cols] = proj[HALO:]
        dest[...] = (
            r.conv_w[0:1, cols] * r.pp[pl.ds(HALO - 2, ROWS), cols]
            + r.conv_w[1:2, cols] * r.pp[pl.ds(HALO - 1, ROWS), cols]
            + r.conv_w[2:3, cols] * r.pp[pl.ds(HALO, ROWS), cols]
            + r.conv_b[:, cols]
        )
    gated = (r.inner[...] * r.value[...]).astype(bf16).astype(f32)
    r.gf[...] = gated

    across, over_two, next_z = 3 - z, lax.rem(z + 2, 4), z + 1 - 2 * z1
    peers = [
        2 * to_z + to_x
        for to_z, to_x in (
            (across, 1 - x), (across, x), (over_two, 1 - x), (over_two, x),
            (next_z, 1 - x), (next_z, x), (z, 1 - x),
        )
    ]

    def swap(which, k, dst, slot):
        return remote(
            r.stage.at[which, at(peers[k], 96)],
            dst.at[at(slot, 96)],
            r.a2a_s.at[which, k],
            r.a2a_r.at[which, k],
            (peers[k], g),
        )

    def trade(which, dst):
        for k in range(7):
            swap(which, k, dst, s).start()
        dst[at(s, 96)] = r.stage[which, at(s, 96)]

    def arrive(which, dst):
        for k in range(7):
            swap(which, k, dst, peers[k]).wait_recv()

    r.stage[0] = jnp.transpose(gated).astype(bf16)
    trade(0, r.gat)

    bias_cols = jnp.transpose(r.filt_bias[...])
    freq_cols = jnp.transpose(r.filt_freq[...])
    below = r.feats[...]
    for i, (u_ref, a_ref, c_ref) in enumerate(
        ((r.u1, r.a1, r.c1), (r.u2, r.a2, r.c2), (r.u3, r.a3, r.c3))
    ):
        weights = r.filt_first[...] if i == 0 else r.filt_hidden[i - 1]
        u = tn_high(weights, below) + bias_cols[:, i : i + 1]
        u_ref[...] = u
        below, cosine = sin_cos(freq_cols[:, i : i + 1] * u)
        a_ref[...] = below
        c_ref[...] = cosine

    r.last_t[...] = jnp.transpose(r.filt_last[...])
    r.rate_t[...] = jnp.transpose(jnp.broadcast_to(r.decay1[...].reshape(1, 768), (8, 768)))
    last = r.last_t[at(s, 96)]
    rate = r.rate_t[at(s, 96), 0:1]
    place = lax.broadcasted_iota(jnp.int32, (1, 1024), 1).astype(f32)
    r.wind[...] = jnp.exp(-rate * place)
    r.taps[...] = nn_high(last, r.a3[...]) * r.wind[...]
    r.hw_high[pl.ds(0, 96), own] = jnp.zeros((96, 128), bf16)
    r.hw_low[pl.ds(0, 96), own] = jnp.zeros((96, 128), bf16)
    for b in range(8):
        high, low = two(r.taps[:, 128 * b : 128 * b + 128])
        for half, ref in ((high, r.hw_high), (low, r.hw_low)):
            ref[96 * b : 96 * b + 96, 128:256] = half
            if b < 7:
                ref[96 * b + 96 : 96 * b + 192, 0:128] = half

    def by_table(v, which, rows, cols):
        high, low = two(v)
        table = r.tables[which, rows, cols]
        return nn(high, table) + nn(low, table) + nn(high, r.tables[which + 1, rows, cols])

    every = pl.ds(0, 256)
    low_half, high_half = pl.ds(0, 128), pl.ds(128, 128)
    loads[3].wait()
    r.es[...] = (
        nn(r.hw_high[...], r.tables[2])
        + nn(r.hw_low[...], r.tables[2])
        + nn(r.hw_high[...], r.tables[3])
    )
    loads[2].wait()
    for copy in shares[0:3]:
        copy.start()
    shares[6].start()

    arrive(0, r.gat)
    r.xs[...] = nn(r.gat[...], r.tables[2, low_half]) + nn(r.gat[...], r.tables[3, low_half])

    def pick(ref, tile, b):
        rows = pl.ds(pl.multiple_of(96 * b + 8 * tile, 8), 8)
        return ref[rows, low_half], ref[rows, high_half]

    def keep(ref, tile, b, pair_of):
        rows = pl.ds(pl.multiple_of(96 * b + 8 * tile, 8), 8)
        ref[rows, low_half] = pair_of[0]
        ref[rows, high_half] = pair_of[1]

    @pl.loop(0, 12)
    def _(tile):
        e = [pick(r.es, tile, b) for b in range(8)]
        v = [pick(r.xs, tile, b) for b in range(8)]
        for b in range(8):
            re, im = 0.0, 0.0
            for lag in range(b + 1):
                er, ei = e[lag]
                vr, vi = v[b - lag]
                re = re + er * vr - ei * vi
                im = im + er * vi + ei * vr
            keep(r.ys, tile, b, (re, im))

    conv = by_table(r.ys[...], 0, every, high_half) * (1.0 / 128.0)
    r.stage[1] = conv.astype(bf16)
    trade(1, r.co_in)

    loads[4].wait()
    for t in range(4):
        cols = pl.ds(768 * t, 768)
        r.g_act[:, cols] = nt(r.rh_down[own], r.down_w[cols])

    arrive(1, r.co_in)
    sum_f = jnp.transpose(r.co_in[...].astype(f32)) + r.skip[...] * r.gf[...]
    r.summed[...] = sum_f
    mixed = (r.outer[...] * sum_f).astype(bf16)
    loads[5].wait()
    res = r.tok[pl.ds(HALO, ROWS)].astype(f32) + nn(mixed, r.out_w[...]) + r.out_b[...]
    r.o_out[...] = res
    hat, inv = norm_rows(res)
    r.hat2[...] = hat
    r.std2[...] = inv
    n2 = (hat * r.norm_gain[1:2] + r.norm_bias[1:2]).astype(bf16)
    loads[6].wait()
    for t in range(4):
        cols = pl.ds(768 * t, 768)
        act_f, slope = gelu_both(nn(n2, r.up_w[:, cols]) + r.up_b[:, cols])
        act_b = act_f.astype(bf16)
        r.act[:, cols] = act_b
        r.rh_up[own, cols] = (r.g_act[:, cols] * slope).astype(bf16)
        turned = jnp.transpose(act_b.astype(f32)).astype(bf16)
        for ix in range(2):
            for iy in range(2):
                for core in range(2):
                    i1, i2 = (ix, iy) if core == 0 else (iy, ix)
                    src = 96 * (ix * 4 + iy * 2 + core)
                    r.at_down[core, pl.ds(i1 * 768 + i2 * 384 + t * 96, 96)] = turned[src : src + 96]
    for copy in shares[3:6]:
        copy.start()
    shares[9].start()
    order_rows(n2.astype(f32), r.at_up, r.at_upz)
    shares[12].start()
    shares[8].start()
    r.lh_up[:, own] = r.at_up[c]
    r.lh_upz[:, own] = r.at_upz[c]
    order_rows(mixed.astype(f32), r.at_out)
    shares[7].start()
    r.lh_out[:, own] = r.at_out[c]
    r.lh_down[:, own] = r.at_down[c, at(b1, 768)]

    def one_a(p):
        return remote(r.s1a.at[p], r.r1a.at[p], r.p1_s.at[p], r.p1_r.at[p], first)

    def two_a(p):
        return remote(r.s2a.at[p], r.r2a.at[p], r.p2_s.at[p], r.p2_r.at[p], second)

    def three_a(p):
        return remote(
            r.s3a.at[p, at(1 - z1, 2)], r.r3a.at[p], r.p3_s.at[p], r.p3_r.at[p], near
        )

    def four_a(p):
        return remote(r.s4a.at[p], r.r4a.at[p], r.p4_s.at[p], r.p4_r.at[p], far)

    def two_b(p):
        return remote(r.s2b.at[p], r.r2b.at[p], r.p2_s.at[8 + p], r.p2_r.at[8 + p], second)

    def three_b(p):
        return remote(
            r.s3b.at[p, at(1 - z1, 2)], r.r3b.at[p], r.p3_s.at[8 + p], r.p3_r.at[8 + p], near
        )

    def four_b(p):
        return remote(r.s4b.at[p], r.r4b.at[p], r.p4_s.at[8 + p], r.p4_r.at[8 + p], far)

    def make_a(p0, count, lh, rh, c0=0):
        @pl.loop(0, count)
        def _(p):
            r.s1a[p0 + p] = nn(lh[at(1 - b1, 192)], rh[:, at(c0 + p, 768)]).astype(bf16)

    def stay_a(p0, count, lh, rh, c0=0):
        @pl.loop(0, count)
        def _(p):
            r.k1a[p0 + p] = nn(lh[at(b1, 192)], rh[:, at(c0 + p, 768)])

    def ph1_a(p):
        one_a(p).wait_recv()
        rows = at(1 - b2, 96)
        r.s2a[p] = (r.k1a[p, rows] + r.r1a[p, rows].astype(f32)).astype(bf16)
        two_a(p).start()

    def ph2_a(p):
        two_a(p).wait_recv()
        rows = at(b2, 96)
        v = r.k1a[p, rows] + r.r1a[p, rows].astype(f32) + r.r2a[p].astype(f32)
        for iz in range(4):
            block = v[24 * iz : 24 * iz + 24]
            r.s3a[p, 2 * (iz % 2) + iz // 2] = jnp.concatenate(
                [block[:, :384], block[:, 384:]], axis=0
            ).astype(bf16)
        three_a(p).start()

    def ph3_a(p):
        three_a(p).wait_recv()
        r.s4a[p] = (
            r.s3a[p, 2 * z1 + 1 - z2].astype(f32) + r.r3a[p, 1 - z2].astype(f32)
        ).astype(bf16)
        four_a(p).start()

    def ph4_a(p, dest, base, per_row):
        four_a(p).wait_recv()
        v = r.s3a[p, 2 * z1 + z2].astype(f32) + r.r3a[p, z2].astype(f32) + r.r4a[p].astype(f32)
        for h in range(2):
            for j in range(3):
                dest[pl.ds(base + 3 * h + j, 24, stride=per_row)] = v[
                    24 * h : 24 * h + 24, 128 * j : 128 * j + 128
                ]

    def ph2_b(p):
        two_b(p).wait_recv()
        v = r.k2b[p] + r.r2b[p].astype(f32)
        for iz in range(4):
            r.s3b[p, 2 * (iz % 2) + iz // 2] = v[96 * iz : 96 * iz + 96].astype(bf16)
        three_b(p).start()

    def ph3_b(p):
        three_b(p).wait_recv()
        r.s4b[p] = (
            r.s3b[p, 2 * z1 + 1 - z2].astype(f32) + r.r3b[p, 1 - z2].astype(f32)
        ).astype(bf16)
        four_b(p).start()

    def ph4_b(p):
        four_b(p).wait_recv()
        v = r.s3b[p, 2 * z1 + z2].astype(f32) + r.r3b[p, z2].astype(f32) + r.r4b[p].astype(f32)
        for j in range(2):
            r.o_gdown[pl.ds(2 * p + j, 96, stride=6)] = v[:, 128 * j : 128 * j + 128]

    hops = [
        remote(src, dst, r.zf_s.at[i], r.zf_r.at[i], where)
        for i, (src, dst, where) in enumerate(
            ((r.s1z, r.r1z, near), (r.s2z, r.r2z, far), (r.s3z, r.r3z, first), (r.s4z, r.r4z, second))
        )
    ]

    def zf1():
        r.s1z[...] = nn(r.lh_upz[at(1 - z1, 192)], r.rh_up[:, 0:768]).astype(bf16)
        hops[0].start()

    def zf2():
        hops[0].wait_recv()
        rows = at(1 - z2, 96)
        r.s2z[...] = (r.k1z[rows] + r.r1z[rows].astype(f32)).astype(bf16)
        hops[1].start()

    def zf3():
        hops[1].wait_recv()
        for ref, half in ((r.s3z, 1 - b1), (r.k3z, b1)):
            rows = pl.ds(pl.multiple_of(96 * z2 + 48 * half, 48), 48)
            v = r.k1z[rows] + r.r1z[rows].astype(f32) + r.r2z[at(half, 48)].astype(f32)
            ref[...] = v.astype(ref.dtype)
        hops[2].start()

    def zf4():
        hops[2].wait_recv()
        v = r.k3z[...] + r.r3z[...].astype(f32)
        lower, upper = v[:24], v[24:]
        sent = jnp.where(b2 == 0, upper, lower)
        r.k4z[...] = jnp.where(b2 == 0, lower, upper)
        r.s4z[...] = jnp.concatenate([sent[:, :384], sent[:, 384:]], axis=0).astype(bf16)
        hops[3].start()

    def zf5():
        hops[3].wait_recv()
        got = r.r4z[...].astype(f32)
        for h in range(2):
            for j in range(3):
                k = 3 * h + j
                r.o_gup[pl.ds(k, 24, stride=24)] = (
                    r.k4z[:, 128 * k : 128 * k + 128]
                    + got[24 * h : 24 * h + 24, 128 * j : 128 * j + 128]
                )

    def put(row, v):
        for j in range(v.shape[1] // 128):
            part, line = divmod(row + j, 64)
            r.smf[part, line : line + 1] = v[:, 128 * j : 128 * j + 128]

    e = nt(r.rh_up[own], r.up_w[...])
    hat = r.hat2[...]
    grad_f = r.rh_down[own].astype(f32)
    g_res = grad_f + norm_rows_back(e, hat, r.std2[...], r.norm_gain[1:2])
    r.o_gtok[...] = g_res
    g_res_b = g_res.astype(bf16)
    r.rh_out[own] = g_res_b
    shares[10].start()
    g_mixed = nt(g_res_b, r.out_w[...])
    r.g_outer[...] = g_mixed * r.summed[...]
    g_summed = g_mixed * r.outer[...]
    r.g_sum[...] = g_summed
    r.stage[2] = jnp.transpose(g_summed).astype(bf16)
    trade(2, r.gc_in)

    def quarter(k):
        t = lax.rem(g + k, 4)
        return remote(r.smf.at[t], r.q_in.at[k - 1], r.q_s.at[k - 1], r.q_r.at[k - 1], (s, t))

    def eighth(k):
        t = peers[k]
        return remote(r.q_sum.at[at(t, 8)], r.o_in.at[k], r.o_s.at[k], r.o_r.at[k], (t, g))

    def spread(k, back):
        slot = r.ag.at[g, peers[k] if back else s]
        return remote(slot, slot, r.ag_s.at[k], r.ag_r.at[k], (peers[k], g))

    over_y = g + y_step
    first_slot, second_slot = r.ag.at[g], r.ag.at[over_y]
    y_send = remote(first_slot, first_slot, r.ag_s.at[7], r.ag_r.at[7], (s, over_y))
    y_back = remote(second_slot, second_slot, r.ag_s.at[7], r.ag_r.at[7], (s, over_y))
    c_send = [
        remote(slot, slot, r.ag_s.at[8 + i], r.ag_r.at[8 + i], (s, other))
        for i, slot in enumerate((first_slot, second_slot))
    ]
    third_slot, fourth_slot = r.ag.at[other], r.ag.at[other + y_step]
    c_back = [
        remote(slot, slot, r.ag_s.at[8 + i], r.ag_r.at[8 + i], (s, other))
        for i, slot in enumerate((third_slot, fourth_slot))
    ]

    put(AT_GAIN + 6, col_sum(e * hat))
    put(AT_SHIFT + 6, col_sum(e))
    put(AT_DOWNB, col_sum(grad_f))
    put(AT_UPB, col_sum(r.rh_up[own].astype(f32)))
    put(AT_OUTB, col_sum(g_res_b.astype(f32)))
    put(AT_SKIP, col_sum(g_summed * r.gf[...]))
    shares[8].wait_recv()
    shares[9].wait_recv()
    shares[12].wait_recv()
    r.s1z[...] = nn(r.lh_upz[at(1 - z1, 192)], r.rh_up[:, 0:768]).astype(bf16)
    hops[0].start()
    make_a(0, 3, r.lh_up, r.rh_up, 1)
    one_a(0).start()
    for copy in shares[0:6]:
        copy.wait_recv()
    for p in range(3):
        cols = pl.ds(256 * p, 256)
        r.s2b[p] = nn(r.lh_down[at(1 - b2, 384)], r.rh_down[:, cols]).astype(bf16)
    two_b(0).start()
    for p in range(3):
        cols = pl.ds(256 * p, 256)
        r.k2b[p] = nn(r.lh_down[at(b2, 384)], r.rh_down[:, cols])
    shares[7].wait_recv()
    shares[10].wait_recv()
    make_a(3, 1, r.lh_out, r.rh_out)
    r.k1z[...] = nn(r.lh_upz[at(z1, 192)], r.rh_up[:, 0:768])
    arrive(2, r.gc_in)
    r.ys[...] = (
        nn(r.gc_in[...], r.tables[2, high_half]) + nn(r.gc_in[...], r.tables[3, high_half])
    ) * (1.0 / 128.0)

    @pl.loop(0, 12)
    def _(tile):
        e = [pick(r.es, tile, b) for b in range(8)]
        d = [pick(r.ys, tile, b) for b in range(8)]
        for b in range(8):
            re, im = 0.0, 0.0
            for lag in range(8 - b):
                er, ei = e[lag]
                dr, di = d[b + lag]
                re = re + er * dr + ei * di
                im = im + er * di - ei * dr
            keep(r.es, tile, b, (re, im))

    g_long = by_table(r.es[...], 0, every, low_half)
    r.stage[3] = g_long.astype(bf16)
    trade(3, r.gl_in)
    one_a(1).start()
    two_b(1).start()
    zf2()
    stay_a(0, 3, r.lh_up, r.rh_up, 1)
    stay_a(3, 1, r.lh_out, r.rh_out)
    ph2_b(0)
    ph1_a(0)
    r.o_out[...] = r.o_out[...] + nn(r.act[...], r.down_w[...]) + r.down_b[...]
    arrive(3, r.gl_in)
    g_gated = r.skip[...] * r.g_sum[...] + jnp.transpose(r.gl_in[...].astype(f32))
    mixes = (r.g_outer[...], g_gated * r.value[...], g_gated * r.inner[...])
    for part in range(3):
        r.gm[own, 768 * part : 768 * part + 768] = mixes[part]
    first_rows = remote(
        r.gm.at[pl.ds(0, 2)], r.gm.at[pl.ds(ROWS, 2)], r.halo_s.at[1], r.halo_r.at[1], (s - 1, g)
    )

    @pl.when(s > 0)
    def _():
        first_rows.start()

    one_a(2).start()
    two_b(2).start()
    for part in range(3):
        cols = pl.ds(768 * part, 768)
        mix = r.gm[own, cols]
        put(AT_CONVB + 6 * part, col_sum(mix))
        for tap in range(3):
            put(
                AT_CONVW + 18 * tap + 6 * part,
                col_sum(mix * r.pp[pl.ds(HALO - 2 + tap, ROWS), cols]),
            )

    @pl.when(s < 7)
    def _():
        first_rows.wait_recv()

    @pl.when(s == 7)
    def _():
        r.gm[pl.ds(ROWS, 8)] = jnp.zeros((8, r.gm.shape[1]), f32)

    for part in range(3):
        cols = pl.ds(768 * part, 768)
        r.rh_in[own, cols] = (
            r.conv_w[0:1, cols] * r.gm[pl.ds(2, ROWS), cols]
            + r.conv_w[1:2, cols] * r.gm[pl.ds(1, ROWS), cols]
            + r.conv_w[2:3, cols] * r.gm[pl.ds(0, ROWS), cols]
        ).astype(bf16)
    shares[11].start()
    r.g_sum[...] = nt(r.rh_in[own], r.in_w[...])
    shares[6].wait_recv()
    shares[11].wait_recv()
    make_a(4, 3, r.lh_in, r.rh_in)
    one_a(4).start()
    one_a(5).start()
    one_a(6).start()
    zf3()
    ph1_a(1)
    ph2_b(1)
    ph3_b(0)
    stay_a(4, 3, r.lh_in, r.rh_in)
    ph1_a(2)
    ph2_b(2)
    e = r.g_sum[...]
    hat = r.hat1[...]
    put(AT_IN, col_sum(r.rh_in[own].astype(f32)))
    put(AT_GAIN, col_sum(e * hat))
    put(AT_SHIFT, col_sum(e))
    r.o_gtok[...] = r.o_gtok[...] + norm_rows_back(e, hat, r.std1[...], r.norm_gain[0:1])
    ph2_a(0)
    ph3_b(1)
    @pl.loop(0, 12)
    def _(tile):
        v = [pick(r.xs, tile, b) for b in range(8)]
        d = [pick(r.ys, tile, b) for b in range(8)]
        for lag in range(8):
            re, im = 0.0, 0.0
            for b in range(8 - lag):
                vr, vi = v[b]
                dr, di = d[b + lag]
                re = re + vr * dr + vi * di
                im = im + vr * di - vi * dr
            keep(r.xs, tile, lag, (re, im))

    r.es[...] = by_table(r.xs[...], 0, every, every)
    ph1_a(4)
    ph2_a(1)
    ph3_a(0)
    ph3_b(2)
    for b in range(8):
        cols = pl.ds(128 * b, 128)
        gt = r.es[96 * b : 96 * b + 96, 128:256]
        if b < 7:
            gt = gt + r.es[96 * b + 96 : 96 * b + 192, 0:128]
        r.dpre[:, cols] = gt * r.wind[:, cols]
        r.taps[:, cols] = r.taps[:, cols] * gt
    g_rate = -jnp.sum(r.taps[...] * place, axis=1, keepdims=True)
    g_last = nt_high(r.dpre[...], r.a3[...])
    for j in range(4):
        r.smf[j, 64:88, 0:64] = g_last[24 * j : 24 * j + 24]
        r.smf[j, 64:88, 64:65] = g_rate[24 * j : 24 * j + 24]
    ones = jnp.ones((8, 1024), f32)
    g_a = tn_high(last, r.dpre[...])
    for i, (u_ref, c_ref, a_ref) in enumerate(
        ((r.u3, r.c3, r.a2), (r.u2, r.c2, r.a1), (r.u1, r.c1, None))
    ):
        layer = 2 - i
        g_arg = g_a * c_ref[...]
        g_freq = nt_high(ones, g_arg * u_ref[...])[0:1]
        g_u = g_arg * freq_cols[:, layer : layer + 1]
        g_bias = nt_high(ones, g_u)[0:1]
        r.smf[1, layer : layer + 1, 64:128] = g_bias
        r.smf[1, 3 + layer : 4 + layer, 64:128] = g_freq
        if layer > 0:
            r.smf[0, 0:64, 64 * (layer - 1) : 64 * layer] = nt_high(a_ref[...], g_u)
            g_a = nn_high(r.filt_hidden[layer - 1], g_u)
        else:
            r.smf[1, 0:33, 0:64] = nt_high(r.feats[...], g_u)

    for k in range(1, 4):
        quarter(k).start()
    one_a(3).start()
    zf4()
    ph1_a(5)
    ph2_a(2)
    ph3_a(1)
    for k in range(1, 4):
        quarter(k).wait_recv()
    r.q_sum[...] = r.smf[g] + r.q_in[0] + r.q_in[1] + r.q_in[2]
    for k in range(7):
        eighth(k).start()
    ph2_a(4)
    ph1_a(6)
    ph3_a(2)
    for k in range(7):
        eighth(k).wait_recv()
    eighth_sum = r.q_sum[at(s, 8)] + jnp.sum(r.o_in[...], axis=0)
    r.ag[g, s] = jnp.concatenate([eighth_sum, r.q_sum[pl.ds(64, 24)]], axis=0).astype(bf16)
    for k in range(7):
        spread(k, False).start()
    ph2_a(5)
    ph3_a(4)
    ph1_a(3)
    ph2_a(6)
    ph3_a(5)
    for k in range(7):
        spread(k, True).wait_recv()
    y_send.start()
    ph2_a(3)
    ph3_a(6)
    ph3_a(3)
    zf5()
    ph4_a(0, r.o_gup, 6, 24)
    ph4_a(1, r.o_gup, 12, 24)
    ph4_a(2, r.o_gup, 18, 24)
    y_back.wait_recv()
    for copy in c_send:
        copy.start()
    ph4_a(4, r.o_gin, 0, 18)
    ph4_a(5, r.o_gin, 6, 18)
    ph4_a(6, r.o_gin, 12, 18)
    ph4_b(0)
    ph4_b(1)
    ph4_b(2)
    for copy in c_back:
        copy.wait_recv()
    r.o_small[...] = r.ag[...]
    ph4_a(3, r.o_gout, 0, 6)

    @pl.when(s < 7)
    def _():
        last_rows.wait_send()

    @pl.when(s > 0)
    def _():
        first_rows.wait_send()

    for copy in shares:
        copy.wait_send()

    @pl.loop(0, 4)
    def _(which):
        @pl.loop(1, 8)
        def _(k):
            remote(
                r.stage.at[which, pl.ds(0, 96)],
                r.gat.at[pl.ds(0, 96)],
                r.a2a_s.at[which, k - 1],
                r.a2a_r.at[which, k - 1],
                (s, other),
            ).wait_send()

    for copy in hops:
        copy.wait_send()

    @pl.loop(0, 7)
    def _(p):
        one_a(p).wait_send()
        two_a(p).wait_send()
        three_a(p).wait_send()
        four_a(p).wait_send()

    @pl.loop(0, 3)
    def _(p):
        two_b(p).wait_send()
        three_b(p).wait_send()
        four_b(p).wait_send()

    for k in range(1, 4):
        quarter(k).wait_send()

    for k in range(7):
        eighth(k).wait_send()
        spread(k, False).wait_send()

    y_send.wait_send()
    for copy in c_send:
        copy.wait_send()


def finish_kernel(
    i_out, i_gtok, i_gin, i_gout, i_gup, i_gdown, small,
    out, gtok, gain, shift, gin, in_b, conv_w, conv_b, first, hidden, bias, freq,
    last, decay, skip, gout, out_b, gup, up_b, gdown, down_b, sems,
):
    bulk = (
        (i_out, out.at[0]), (i_gtok, gtok.at[0]), (i_gin, gin), (i_gout, gout), (i_gup, gup), (i_gdown, gdown),
    )
    leave = [pltpu.make_async_copy(a, b, sems.at[i]) for i, (a, b) in enumerate(bulk)]
    for copy in leave:
        copy.start()
    slots = [[small[i, j].astype(f32) for j in range(8)] for i in range(4)]
    rows = jnp.concatenate([slots[i][j][0:8] for i in range(4) for j in range(8)], axis=0)

    def fetch(at_row, dest, dest_row, wide):
        for j in range(wide):
            dest[dest_row : dest_row + 1, 128 * j : 128 * j + 128] = rows[at_row + j : at_row + j + 1]

    def line(at_row, dest):
        dest[...] = rows[at_row : at_row + dest.shape[0] // 128].reshape(dest.shape[0])

    for i in range(2):
        fetch(AT_GAIN + 6 * i, gain, i, 6)
        fetch(AT_SHIFT + 6 * i, shift, i, 6)
        hidden[i] = rows[AT_HID : AT_HID + 64, 64 * i : 64 * i + 64]
    for i in range(3):
        fetch(AT_CONVW + 18 * i, conv_w, i, 18)
    line(AT_IN, in_b)
    line(AT_CONVB, conv_b)
    line(AT_SKIP, skip)
    line(AT_OUTB, out_b)
    line(AT_UPB, up_b)
    line(AT_DOWNB, down_b)
    first[...] = rows[AT_FIRST : AT_FIRST + 33, 0:64]
    bias[...] = rows[AT_FIRST : AT_FIRST + 3, 64:128]
    freq[...] = rows[AT_FIRST + 3 : AT_FIRST + 6, 64:128]
    channels = jnp.transpose(
        jnp.concatenate([slots[j][i][8:32] for i in range(8) for j in range(4)], axis=0)
    )
    last[...] = channels[0:64]
    decay[...] = channels[64:65].reshape(768)
    for copy in leave:
        copy.wait()


def one_kernel_body(tokens, out_grad, norm_gain, norm_bias, in_weight, in_bias, conv_weight, conv_bias,
                    filt_first, filt_hidden, filt_bias, filt_freq, filt_last, decay_rates, skip_scale,
                    out_weight, out_bias, up_weight, up_bias, down_weight, down_bias):
    width, hidden = up_weight.shape
    length = tokens.shape[1] * lax.axis_size("seq")
    any_spec = pl.BlockSpec(memory_space=pl.ANY)
    vmem_spec = pl.BlockSpec(memory_space=pltpu.VMEM)

    def vm(*shape, dtype=f32):
        return pltpu.VMEM(shape, dtype)

    def dma(*shape):
        return pltpu.SemaphoreType.DMA(shape)

    def shape(*dims):
        return jax.ShapeDtypeStruct(dims, f32)

    outs = pl.pallas_call(
        step_kernel,
        out_shape=[
            vm(128, width), vm(128, width), vm(432, 128), vm(144, 128),
            vm(576, 128), vm(576, 128), vm(4, 8, 32, 128, dtype=bf16),
        ],
        in_specs=[any_spec] * 23,
        out_specs=[vmem_spec] * 7,
        scratch_shapes=[vm(*dims) for _, dims in SMALL_ARGS]
        + [vm(*dims, dtype=dtype) for _, dims, dtype in SCRATCH]
        + [dma(*dims) for _, dims in SEMAPHORES],
        compiler_params=pltpu.CompilerParams(
            collective_id=0, has_side_effects=True, vmem_limit_bytes=60 * 1024 * 1024
        ),
        name="hyena_step",
    )(
        tokens, out_grad, in_weight, out_weight, up_weight, down_weight,
        jnp.asarray(fourier_tables()),
        norm_gain, norm_bias, in_bias, conv_weight, conv_bias,
        jnp.asarray(feature_table(length, (filt_first.shape[0] - 1) // 2)),
        filt_first, filt_hidden, filt_bias, filt_freq, filt_last, decay_rates, skip_scale, out_bias,
        up_bias, down_bias,
    )
    done = pl.pallas_call(
        finish_kernel,
        out_shape=[
            shape(1, 128, width), shape(1, 128, width), shape(2, width), shape(2, width), shape(432, 128),
            shape(3 * width), shape(3, 3 * width), shape(3 * width), shape(33, 64), shape(2, 64, 64),
            shape(3, 64), shape(3, 64), shape(64, width), shape(width), shape(width), shape(144, 128),
            shape(width), shape(576, 128), shape(hidden), shape(576, 128), shape(width),
        ],
        in_specs=[vmem_spec] * 7,
        out_specs=[any_spec, any_spec, vmem_spec, vmem_spec, any_spec]
        + [vmem_spec] * 10
        + [any_spec, vmem_spec, any_spec, vmem_spec, any_spec, vmem_spec],
        scratch_shapes=[dma(6)],
        compiler_params=pltpu.CompilerParams(vmem_limit_bytes=32 * 1024 * 1024),
        name="hyena_finish",
    )(*outs)
    flat = (4, 15, 17, 19)
    return tuple(v.reshape(-1) if i in flat else v for i, v in enumerate(done))


def solution(mesh):
    small_mesh = mesh.shape["seq"] == 8 and mesh.shape["grp"] == 4
    return jax.shard_map(
        one_kernel_body if small_mesh else body,
        mesh=mesh,
        in_specs=(P("grp", "seq", None), P("grp", "seq", None)) + (P(),) * 19,
        out_specs=(
            P("grp", "seq", None),
            P("grp", "seq", None),
            P(),
            P(),
            P(("seq", "grp")),
        )
        + (P(),) * 10
        + (P(("seq", "grp")), P(), P(("seq", "grp")), P(), P(("seq", "grp")), P()),
        check_vma=False,
    )
```
